32 devices in a mesh: seq: 4 (over x, core), batch: 8 (over z, y).
Axes of the slice: x: 2, y: 2, z: 4, core: 2. Of those that a mesh axis runs over, the one named last changes fastest.
Arguments:
- block_input: bfloat16 [16, 1024, 768], P('batch', 'seq'), may hold values from -6 to 6
- lengths: int32 [16], P('batch'), may hold values from 1 to 1024, as said below
- pass_ids: int32 [16, 1024], P('batch', 'seq'), may hold values from 0 to 4
- pass_embed: float32 [5, 768], replicated, may hold values from -3 to 3
- ln1_gain: float32 [768], replicated, may hold values from 0.5 to 1.5
- ln1_bias: float32 [768], replicated, may hold values from -1.2 to 1.2
- w_qkv: bfloat16 [768, 2304], replicated, may hold values from -0.21875 to 0.21875
- w_out: bfloat16 [768, 768], replicated, may hold values from -1.75 to 1.75
- ln2_gain: float32 [768], replicated, may hold values from 0.5 to 1.5
- ln2_bias: float32 [768], replicated, may hold values from -1.2 to 1.2
- w_up: bfloat16 [768, 3072], replicated, may hold values from -0.21875 to 0.21875
- b_up: float32 [3072], replicated, may hold values from -1.8 to 1.8
- w_down: bfloat16 [3072, 768], replicated, may hold values from -0.109375 to 0.109375
- b_down: float32 [768], replicated, may hold values from -1.8 to 1.8
- cotangent: bfloat16 [16, 1024, 768], P('batch', 'seq'), may hold values from -6 to 6
Outputs:
- output: bfloat16 [16, 1024, 768], P('batch', 'seq')
- grad_input: bfloat16 [16, 1024, 768], P('batch', 'seq')
- grad_pass_embed: float32 [5, 768], replicated
- grad_ln1_gain: float32 [768], replicated
- grad_ln1_bias: float32 [768], replicated
- grad_w_qkv: float32 [768, 2304], P('seq', 'batch')
- grad_w_out: float32 [768, 768], P('seq', 'batch')
- grad_ln2_gain: float32 [768], replicated
- grad_ln2_bias: float32 [768], replicated
- grad_w_up: float32 [768, 3072], P('seq', 'batch')
- grad_b_up: float32 [3072], replicated
- grad_w_down: float32 [3072, 768], P('seq', 'batch')
- grad_b_down: float32 [768], replicated
The draws below stay inside these ranges and needn't reach their ends.
Inputs may be any that keep to these rules, and one draw needn't show every extreme that they name: `lengths`: in each aligned block of 2 rows one row, drawn from the seed, has all 1024 positions.
All inputs are finite; a program needn't handle non-finite values.
Results may differ from the reference program's by a relative error of at most 0.019.
Values may be sent and summed in bfloat16 or wider, within the bound.
A program may use at most 192 MiB of HBM per device.

```python
import jax
import jax.numpy as jnp
from jax import lax

D = 768
H = 12
FF = 3072
PASSES = 5
ROW_DEV = 2
SEQ = 1024
ROWS = 16


def draw_lengths(key, part):
    key = jax.random.fold_in(key, 7)
    key_short, key_pick = jax.random.split(key)
    groups = ROWS // ROW_DEV
    short = jax.random.randint(key_short, (groups, ROW_DEV), 1, SEQ + 1)
    picked = jax.random.randint(key_pick, (groups, 1), 0, ROW_DEV)
    chosen = jnp.arange(ROW_DEV, dtype=jnp.int32)[None, :] == picked
    return jnp.where(chosen, SEQ, short).reshape(ROWS).astype(jnp.int32)


def place_ends(entries, rng, low, top_value):
    index_at = [jax.random.randint(jax.random.fold_in(rng, axis), (), 0, length) for axis, length in enumerate(entries.shape)]
    longest = entries.shape.index(max(entries.shape))
    next_to = index_at[:longest] + [(index_at[longest] + 1) % entries.shape[longest]] + index_at[longest + 1:]
    return entries.at[tuple(index_at)].set(low).at[tuple(next_to)].set(top_value)


def levels(own_key, dims, cuts, smallest, largest):
    def one(axis_at, blocks):
        draws = jax.random.uniform(jax.random.fold_in(jax.random.fold_in(own_key, 6), axis_at), (blocks,), jnp.float32, smallest / len(cuts), largest / len(cuts))
        return jnp.repeat(jnp.exp(draws), dims[axis_at] // blocks).reshape((-1,) + (1,) * (len(dims) - axis_at - 1))

    level = one(*cuts[0])
    for cut in cuts[1:]:
        level = level * one(*cut)
    return level


def centred(key, extent, scale, reach, cuts=(), held_as=jnp.bfloat16):
    level = levels(key, extent, cuts, -0.22, 0.18) if cuts else 1.0
    entries = jax.random.normal(key, extent, jnp.float32) * scale * level
    return jnp.minimum(jnp.maximum(entries, -reach), reach).astype(held_as)


def setup_inputs(seed: int = 0) -> dict:
    arg_keys = jax.random.split(jax.random.key(seed), 16)
    block_input = centred(arg_keys[0], (ROWS, SEQ, D), 1.0, 6.0, ((0, 8), (1, 4)))
    lengths = draw_lengths(jax.random.fold_in(arg_keys[15], 71), 0)
    pass_ids = place_ends(jax.random.randint(arg_keys[2], (ROWS, SEQ), 0, PASSES), jax.random.fold_in(arg_keys[2], 1), 0, PASSES - 1).astype(jnp.int32)
    pass_embed = centred(arg_keys[3], (PASSES, D), 0.5, 3.0, (), jnp.float32)
    ln1_gain = jnp.clip(1.0 + 0.1 * jax.random.normal(arg_keys[4], (D,), jnp.float32), 0.5, 1.5)
    ln1_bias = centred(arg_keys[5], (D,), 0.2, 1.2, (), jnp.float32)
    w_qkv = centred(arg_keys[6], (D, 3 * D), D ** -0.5, 0.21875)
    w_out = centred(arg_keys[7], (D, D), (D // 64) ** -0.5, 1.75)
    ln2_gain = jnp.clip(1.0 + 0.1 * jax.random.normal(arg_keys[8], (D,), jnp.float32), 0.5, 1.5)
    ln2_bias = centred(arg_keys[9], (D,), 0.2, 1.2, (), jnp.float32)
    w_up = centred(arg_keys[10], (D, FF), D ** -0.5, 0.21875)
    b_up = centred(arg_keys[11], (FF,), 0.3, 1.8, (), jnp.float32)
    w_down = centred(arg_keys[12], (FF, D), FF ** -0.5, 0.109375)
    b_down = centred(arg_keys[13], (D,), 0.3, 1.8, (), jnp.float32)
    cotangent = centred(arg_keys[14], (ROWS, SEQ, D), 1.0, 6.0, ((0, 8), (1, 4)))
    return dict(block_input=block_input, lengths=lengths, pass_ids=pass_ids, pass_embed=pass_embed, ln1_gain=ln1_gain, ln1_bias=ln1_bias, w_qkv=w_qkv, w_out=w_out, ln2_gain=ln2_gain, ln2_bias=ln2_bias, w_up=w_up, b_up=b_up, w_down=w_down, b_down=b_down, cotangent=cotangent)


@jax.custom_vjp
def low(v):
    return lax.optimization_barrier(v.astype(jnp.bfloat16)).astype(jnp.float32)

@jax.custom_vjp
def low_back(v):
    return v

def low_keep(v):
    return (low(v), None)

def low_pass(kept, grad):
    return (grad,)

def back_keep(v):
    return (v, None)

def back_low(kept, grad):
    return (low(grad),)
low.defvjp(low_keep, low_pass)
low_back.defvjp(back_keep, back_low)
highest = lax.Precision.HIGHEST
negative = -1e+30

def layer_norm(hidden, gain, offset):
    centre = lax.optimization_barrier(jnp.mean(hidden, -1, keepdims=True))
    shifted = hidden - centre
    spread = lax.optimization_barrier(jnp.mean(shifted * shifted, -1, keepdims=True))
    return shifted * lax.rsqrt(spread + 1e-05) * gain + offset

def visible(query_place, query_pass, key_place, key_pass, length):
    earlier = key_place[None, :] < query_place[:, None]
    allowed = earlier & (key_pass[None, :] <= query_pass[:, None]) & (key_place[None, :] < length)
    return allowed | (key_place[None, :] == query_place[:, None])

def block_attend(index, query_all, key_all, value_all, passes, length):
    block_len = min(512, query_all.shape[0])
    start = (index * block_len).astype(jnp.int32)
    query_part = lax.dynamic_slice_in_dim(query_all, start, block_len, 0)
    pass_part = lax.dynamic_slice_in_dim(passes, start, block_len, 0)
    place_part = start + jnp.arange(block_len, dtype=jnp.int32)
    key_place = jnp.arange(key_all.shape[0], dtype=jnp.int32)
    factor = query_all.shape[-1] ** (-0.5)
    raw = jnp.einsum('qhd,khd->hqk', query_part, key_all, precision=highest) * factor
    scores = low_back(raw)
    seen = visible(place_part, pass_part, key_place, passes, length)
    scores = jnp.where(seen[None], scores, negative)
    peak = lax.optimization_barrier(jnp.max(scores, -1, keepdims=True))
    expo = jnp.exp(scores - peak)
    chance = expo / lax.optimization_barrier(jnp.sum(expo, -1, keepdims=True))
    return jnp.einsum('hqk,khd->qhd', low(chance), value_all, precision=highest)

def row_output(params, input_row, passes, length):
    pass_embed, ln1_gain, ln1_bias, w_qkv, w_out, ln2_gain, ln2_bias, w_up, b_up, w_down, b_down = params
    seq_len, width = input_row.shape
    head_size = width // H
    onehot = (passes[:, None] == jnp.arange(pass_embed.shape[0], dtype=jnp.int32)[None, :]).astype(jnp.float32)
    hidden = input_row + jnp.dot(onehot, pass_embed, precision=highest)
    normed = low(layer_norm(hidden, ln1_gain, ln1_bias))
    qkv = jnp.dot(normed, w_qkv, precision=highest)
    query_all = low_back(low(qkv[:, :width])).reshape(seq_len, H, head_size)
    key_all = low_back(low(qkv[:, width:2 * width])).reshape(seq_len, H, head_size)
    value_all = low_back(low(qkv[:, 2 * width:])).reshape(seq_len, H, head_size)
    checked = jax.checkpoint(block_attend)
    block_len = min(512, seq_len)

    def one_block(index):
        return checked(index, query_all, key_all, value_all, passes, length)
    attended = lax.map(one_block, jnp.arange(seq_len // block_len, dtype=jnp.int32))
    attended = low_back(low(attended.reshape(seq_len, width)))
    branch = low_back(jnp.dot(attended, w_out, precision=highest))
    middle = hidden + branch
    normed2 = low(layer_norm(middle, ln2_gain, ln2_bias))
    pre_act = low_back(jnp.dot(normed2, w_up, precision=highest) + b_up)
    active = low(jax.nn.gelu(pre_act, approximate=True))
    return middle + jnp.dot(active, w_down, precision=highest) + b_down

def reference(block_input, lengths, pass_ids, pass_embed, ln1_gain, ln1_bias, w_qkv, w_out, ln2_gain, ln2_bias, w_up, b_up, w_down, b_down, cotangent):
    params = tuple((p_arr.astype(jnp.float32) for p_arr in (pass_embed, ln1_gain, ln1_bias, w_qkv, w_out, ln2_gain, ln2_bias, w_up, b_up, w_down, b_down)))

    def step(totals, inputs):
        input_row, passes, length, cot_row = inputs

        def forward(prm, row_in):
            return row_output(prm, row_in, passes, length)
        y_row, backward = jax.vjp(forward, params, input_row.astype(jnp.float32))
        grad_params, grad_row = backward(cot_row.astype(jnp.float32))
        totals = jax.tree.map(jnp.add, totals, grad_params)
        return (totals, (y_row.astype(jnp.bfloat16), grad_row.astype(jnp.bfloat16)))
    zeros = jax.tree.map(jnp.zeros_like, params)
    totals, outputs = lax.scan(step, zeros, (block_input, pass_ids, lengths, cotangent))
    return (outputs[0], outputs[1], totals[0], totals[1], totals[2], totals[3], totals[4], totals[5], totals[6], totals[7], totals[8], totals[9], totals[10])
```

```python
import functools

import jax
import jax.numpy as jnp
from jax import lax
from jax.experimental import pallas as pl
from jax.experimental.pallas import tpu as pltpu
from jax.sharding import PartitionSpec as P

H = 12


negative = -1e30
key_block = 1024
query_block = 512
highest = lax.Precision.HIGHEST


def layer_norm(hidden, gain, offset):
    centre = jnp.mean(hidden, -1, keepdims=True)
    shifted = hidden - centre
    spread = jnp.mean(shifted * shifted, -1, keepdims=True)
    return shifted * lax.rsqrt(spread + 1e-05) * gain + offset


def gelu_tanh(values):
    return jax.nn.gelu(values, approximate=True)


def visible(query_place, query_pass, key_place, key_pass, length):
    earlier = key_place[None, :] < query_place[:, None]
    allowed = earlier & (key_pass[None, :] <= query_pass[:, None]) & (key_place[None, :] < length)
    return allowed | (key_place[None, :] == query_place[:, None])


def masked_scores(query_part, key_part, factor, seen):
    raw = (
        jnp.einsum("qhd,khd->hqk", query_part, key_part, preferred_element_type=jnp.float32)
        * factor
    )
    return jnp.where(seen[None], raw, negative)


def split_blocks(arrays, block_len):
    return tuple(
        (
            array.reshape((array.shape[0] // block_len, block_len) + array.shape[1:])
            for array in arrays
        )
    )


def chance_of(query_part, key_part, log_part, seen, factor):
    scores = masked_scores(query_part, key_part, factor, seen)
    return jnp.where(seen[None], jnp.exp(scores - log_part[..., None]), 0.0)


def grad_pieces(query_part, dout_part, log_part, delta_part, key_part, value_part, seen, factor):
    chance = chance_of(query_part, key_part, log_part, seen, factor)
    dprob = jnp.einsum("qhd,khd->hqk", dout_part, value_part, preferred_element_type=jnp.float32)
    dscore = (chance * (dprob - delta_part[..., None])).astype(jnp.bfloat16)
    return (dscore, chance.astype(jnp.bfloat16))


def attend_row(queries, query_place, query_pass, key_rows, value_rows, key_pass, length):
    factor = queries.shape[-1] ** (-0.5)
    places = jnp.arange(key_rows.shape[0], dtype=jnp.int32)
    key_parts = split_blocks(
        (key_rows, value_rows, key_pass, places), min(key_block, key_rows.shape[0])
    )
    query_len = min(query_block, queries.shape[0])
    query_parts = split_blocks((queries, query_place, query_pass), query_len)

    def attend_one_block(query_args):
        query_part, place_part, pass_part = query_args

        def running(carry, key_args):
            peak, summed, total_out = carry
            key_part, value_part, kpass_part, kplace_part = key_args
            seen = visible(place_part, pass_part, kplace_part, kpass_part, length)
            scores = masked_scores(query_part, key_part, factor, seen)
            new_peak = jnp.maximum(peak, jnp.max(scores, -1))
            terms = jnp.where(seen[None], jnp.exp(scores - new_peak[..., None]), 0.0)
            rescale = jnp.exp(peak - new_peak)
            summed = summed * rescale + jnp.sum(terms, -1)
            added = jnp.einsum(
                "hqk,khd->qhd",
                terms.astype(jnp.bfloat16),
                value_part,
                preferred_element_type=jnp.float32,
            )
            total_out = total_out * rescale.T[..., None] + added
            return ((new_peak, summed, total_out), None)

        heads_n = query_part.shape[1]
        start = (
            jnp.full((heads_n, query_len), negative, jnp.float32),
            jnp.zeros((heads_n, query_len), jnp.float32),
            jnp.zeros(query_part.shape, jnp.float32),
        )
        (peak, summed, total_out), _ = lax.scan(running, start, key_parts)
        log_total = peak + jnp.log(summed)
        result = total_out / summed.T[..., None]
        return (result, log_total)

    results, log_totals = lax.map(attend_one_block, query_parts)
    heads_n = queries.shape[1]
    return (
        results.reshape(queries.shape),
        jnp.moveaxis(log_totals, 1, 0).reshape(heads_n, queries.shape[0]),
    )


def backward_row(
    queries,
    douts,
    outs_kept,
    log_totals,
    query_place,
    query_pass,
    key_rows,
    value_rows,
    key_pass,
    length,
):
    factor = queries.shape[-1] ** (-0.5)
    places = jnp.arange(key_rows.shape[0], dtype=jnp.int32)
    key_parts = split_blocks(
        (key_rows, value_rows, key_pass, places), min(key_block, key_rows.shape[0])
    )
    query_len = min(query_block, queries.shape[0])
    heads_n = queries.shape[1]
    block_count = queries.shape[0] // query_len
    log_parts = jnp.moveaxis(log_totals.reshape(heads_n, block_count, query_len), 1, 0)
    query_parts = split_blocks((queries, douts, outs_kept, query_place, query_pass), query_len)

    def backward_one_block(carry, query_args):
        query_part, dout_part, kept_part, place_part, pass_part, log_part = query_args
        delta_part = jnp.einsum("qhd,qhd->hq", dout_part.astype(jnp.float32), kept_part)

        def add_grads(dquery, key_args):
            key_part, value_part, kpass_part, kplace_part = key_args
            seen = visible(place_part, pass_part, kplace_part, kpass_part, length)
            dscore, low_chance = grad_pieces(
                query_part, dout_part, log_part, delta_part, key_part, value_part, seen, factor
            )
            dquery = dquery + factor * jnp.einsum(
                "hqk,khd->qhd", dscore, key_part, preferred_element_type=jnp.float32
            )
            dkey = factor * jnp.einsum(
                "hqk,qhd->khd", dscore, query_part, preferred_element_type=jnp.float32
            )
            dvalue = jnp.einsum(
                "hqk,qhd->khd", low_chance, dout_part, preferred_element_type=jnp.float32
            )
            return (dquery, (dkey, dvalue))

        dquery, key_terms = lax.scan(add_grads, jnp.zeros(query_part.shape, jnp.float32), key_parts)
        carry = (
            carry[0] + key_terms[0].reshape(key_rows.shape),
            carry[1] + key_terms[1].reshape(value_rows.shape),
        )
        return (carry, (dquery, delta_part))

    start = (jnp.zeros(key_rows.shape, jnp.float32), jnp.zeros(value_rows.shape, jnp.float32))
    key_sums, (dqueries, deltas) = lax.scan(backward_one_block, start, query_parts + (log_parts,))
    return (
        dqueries.reshape(queries.shape),
        jnp.moveaxis(deltas, 1, 0).reshape(heads_n, queries.shape[0]),
        key_sums,
    )


def local(
    block_input,
    lengths,
    pass_ids,
    pass_embed,
    ln1_gain,
    ln1_bias,
    w_qkv,
    w_out,
    ln2_gain,
    ln2_bias,
    w_up,
    b_up,
    w_down,
    b_down,
    cotangent,
):
    row_count, seg_len, width = block_input.shape
    heads_n = H
    head_size = width // heads_n
    onehot = (
        pass_ids[..., None] == jnp.arange(pass_embed.shape[0], dtype=jnp.int32)[None, None, :]
    ).astype(jnp.float32)
    hidden_in = block_input.astype(jnp.float32) + jnp.einsum(
        "rsp,pd->rsd", onehot, pass_embed, precision=highest
    )
    normed, norm_back = jax.vjp(layer_norm, hidden_in, ln1_gain, ln1_bias)
    normed_low = normed.astype(jnp.bfloat16)
    qkv = jnp.einsum("rsd,de->rse", normed_low, w_qkv, preferred_element_type=jnp.float32)
    queries = qkv[..., :width].astype(jnp.bfloat16)
    key_flat = qkv[..., width : 2 * width].astype(jnp.bfloat16)
    value_flat = qkv[..., 2 * width :].astype(jnp.bfloat16)
    pass_low = pass_ids.astype(jnp.bfloat16)
    key_all, value_all, pass_all = (
        lax.all_gather(key_flat, "seq", axis=1, tiled=True),
        lax.all_gather(value_flat, "seq", axis=1, tiled=True),
        lax.all_gather(pass_low, "seq", axis=1, tiled=True),
    )
    total_len = key_all.shape[1]
    key_all = key_all.reshape(row_count, total_len, heads_n, head_size)
    value_all = value_all.reshape(row_count, total_len, heads_n, head_size)
    pass_all = pass_all.astype(jnp.float32)
    offset = lax.axis_index("seq") * seg_len
    query_place = offset + jnp.arange(seg_len, dtype=jnp.int32)
    query_pass = pass_ids.astype(jnp.float32)
    query_heads = queries.reshape(row_count, seg_len, heads_n, head_size)
    attended_rows = []
    log_rows = []
    for row in range(row_count):
        attended, log_total = attend_row(
            query_heads[row],
            query_place,
            query_pass[row],
            key_all[row],
            value_all[row],
            pass_all[row],
            lengths[row],
        )
        attended_rows.append(attended)
        log_rows.append(log_total)
    attended_low = jnp.stack(attended_rows).astype(jnp.bfloat16).reshape(row_count, seg_len, width)
    branch = jnp.einsum("rsd,de->rse", attended_low, w_out, preferred_element_type=jnp.float32)
    middle = hidden_in + branch
    normed2, norm2_back = jax.vjp(layer_norm, middle, ln2_gain, ln2_bias)
    normed2_low = normed2.astype(jnp.bfloat16)
    pre_act = (
        jnp.einsum("rsd,df->rsf", normed2_low, w_up, preferred_element_type=jnp.float32) + b_up
    )
    active, active_back = jax.vjp(gelu_tanh, pre_act)
    active_low = active.astype(jnp.bfloat16)
    result = (
        middle
        + jnp.einsum("rsf,fd->rsd", active_low, w_down, preferred_element_type=jnp.float32)
        + b_down
    )
    output = result.astype(jnp.bfloat16)
    cot_f = cotangent.astype(jnp.float32)
    grad_active = jnp.einsum("rsd,fd->rsf", cotangent, w_down, preferred_element_type=jnp.float32)
    grad_w_down = jnp.einsum(
        "rsf,rsd->fd", active_low, cotangent, preferred_element_type=jnp.float32
    )
    grad_b_down = jnp.sum(cot_f, (0, 1))
    grad_pre = active_back(grad_active)[0].astype(jnp.bfloat16)
    grad_b_up = jnp.sum(grad_pre.astype(jnp.float32), (0, 1))
    grad_w_up = jnp.einsum("rsd,rsf->df", normed2_low, grad_pre, preferred_element_type=jnp.float32)
    grad_normed2 = jnp.einsum("rsf,df->rsd", grad_pre, w_up, preferred_element_type=jnp.float32)
    grad_mid_norm, grad_ln2_gain, grad_ln2_bias = norm2_back(grad_normed2)
    grad_middle = cot_f + grad_mid_norm
    grad_branch = grad_middle.astype(jnp.bfloat16)
    grad_w_out = jnp.einsum(
        "rsd,rse->de", attended_low, grad_branch, preferred_element_type=jnp.float32
    )
    grad_attended = jnp.einsum(
        "rse,de->rsd", grad_branch, w_out, preferred_element_type=jnp.float32
    ).astype(jnp.bfloat16)
    dout_heads = grad_attended.reshape(row_count, seg_len, heads_n, head_size)
    dquery_rows = []
    dkey_rows = []
    dvalue_rows = []
    for row in range(row_count):
        dquery, _, key_sums = backward_row(
            query_heads[row],
            dout_heads[row],
            attended_rows[row],
            log_rows[row],
            query_place,
            query_pass[row],
            key_all[row],
            value_all[row],
            pass_all[row],
            lengths[row],
        )
        dquery_rows.append(dquery)
        dkey_rows.append(key_sums[0].reshape(total_len, width))
        dvalue_rows.append(key_sums[1].reshape(total_len, width))
    dkey_sum, dvalue_sum = (
        lax.psum_scatter(
            jnp.stack(dkey_rows).astype(jnp.bfloat16), "seq", scatter_dimension=1, tiled=True
        ).astype(jnp.float32),
        lax.psum_scatter(
            jnp.stack(dvalue_rows).astype(jnp.bfloat16), "seq", scatter_dimension=1, tiled=True
        ).astype(jnp.float32),
    )
    dquery_all = jnp.stack(dquery_rows).reshape(row_count, seg_len, width)
    grad_qkv = jnp.concatenate(
        [
            dquery_all.astype(jnp.bfloat16),
            dkey_sum.astype(jnp.bfloat16),
            dvalue_sum.astype(jnp.bfloat16),
        ],
        -1,
    )
    grad_w_qkv = jnp.einsum("rsd,rse->de", normed_low, grad_qkv, preferred_element_type=jnp.float32)
    grad_normed = jnp.einsum("rse,de->rsd", grad_qkv, w_qkv, preferred_element_type=jnp.float32)
    grad_in_norm, grad_ln1_gain, grad_ln1_bias = norm_back(grad_normed)
    grad_hidden = grad_middle + grad_in_norm
    grad_input = grad_hidden.astype(jnp.bfloat16)
    grad_pass = jnp.einsum("rsp,rsd->pd", onehot, grad_hidden, precision=highest)
    matrices = (
        lax.psum_scatter(
            grad_w_qkv.astype(jnp.bfloat16), "seq", scatter_dimension=0, tiled=True
        ).astype(jnp.float32),
        lax.psum_scatter(
            grad_w_out.astype(jnp.bfloat16), "seq", scatter_dimension=0, tiled=True
        ).astype(jnp.float32),
        lax.psum_scatter(
            grad_w_up.astype(jnp.bfloat16), "seq", scatter_dimension=0, tiled=True
        ).astype(jnp.float32),
        lax.psum_scatter(
            grad_w_down.astype(jnp.bfloat16), "seq", scatter_dimension=0, tiled=True
        ).astype(jnp.float32),
    )
    matrices = (
        lax.psum_scatter(
            matrices[0].astype(jnp.bfloat16), "batch", scatter_dimension=1, tiled=True
        ).astype(jnp.float32),
        lax.psum_scatter(
            matrices[1].astype(jnp.bfloat16), "batch", scatter_dimension=1, tiled=True
        ).astype(jnp.float32),
        lax.psum_scatter(
            matrices[2].astype(jnp.bfloat16), "batch", scatter_dimension=1, tiled=True
        ).astype(jnp.float32),
        lax.psum_scatter(
            matrices[3].astype(jnp.bfloat16), "batch", scatter_dimension=1, tiled=True
        ).astype(jnp.float32),
    )
    vectors = lax.psum(
        (
            grad_pass,
            grad_ln1_gain,
            grad_ln1_bias,
            grad_ln2_gain,
            grad_ln2_bias,
            grad_b_up,
            grad_b_down,
        ),
        ("seq", "batch"),
    )
    return (
        output,
        grad_input,
        vectors[0],
        vectors[1],
        vectors[2],
        matrices[0],
        matrices[1],
        vectors[3],
        vectors[4],
        matrices[2],
        vectors[5],
        matrices[3],
        vectors[6],
    )


NN = (((1,), (0,)), ((), ()))
NT = (((1,), (1,)), ((), ()))
TN = (((0,), (0,)), ((), ()))
vmem_bytes = 60 << 20
block = 256


def dot(left, right, form):
    return lax.dot_general(left, right, form, preferred_element_type=jnp.float32)


def lane_loop(total, width, body):
    def step(i, carry):
        body(pl.ds(pl.multiple_of(i * width, width), width))
        return carry

    lax.fori_loop(0, total // width, step, 0)


def attend_kernel(
    info, b0, b1, b2, b3, emb, vecs, wqkv, ht, at, qt, kt, vt, ot, kept, inv, bias, prow, pcol
):
    width, total = ht.shape
    half = qt.shape[0]
    core = info[4]

    @pl.when(pl.program_id(0) == 0)
    def _():
        for k, ref in enumerate((b0, b1, b2, b3)):
            place = pl.ds(pl.multiple_of(info[k] * block, block), block)
            passes = ref[block : block + 16, 0:block].astype(jnp.float32)
            prow[:, place] = passes[0:8, :]
            pcol[place, :] = jnp.transpose(passes)[:, 0:8]
            kind = (lax.broadcasted_iota(jnp.int32, (16, block), 0) % 5).astype(jnp.float32)
            line = lax.broadcasted_iota(jnp.int32, (16, block), 0)
            onehot = jnp.where((kind == passes[0:1, :]) & (line < 15), 1.0, 0.0)
            added = dot(emb[...], onehot.astype(jnp.bfloat16), NN)
            ht[:, place] = jnp.transpose(ref[0:block, :]).astype(jnp.float32) + added

        def norm(cols):
            h = ht[:, cols]
            shifted = h - jnp.sum(h, 0, keepdims=True) * (1.0 / width)
            spread = jnp.sum(shifted * shifted, 0, keepdims=True) * (1.0 / width)
            scaled = shifted * lax.rsqrt(spread + 1e-05)
            at[:, cols] = (scaled * vecs[:, 0:1] + vecs[:, 1:2]).astype(jnp.bfloat16)

        lane_loop(total, 128, norm)
        for j, (ref, factor) in enumerate(((qt, 0.125), (kt, 1.0), (vt, 1.0))):
            cols = pl.ds(pl.multiple_of(j * width + core * half, 128), half)
            part = dot(wqkv[:, cols], at[...], TN).astype(jnp.bfloat16)
            ref[...] = part if factor == 1.0 else part * jnp.bfloat16(factor)
        length = info[5]
        for qb in range(total // block):
            n = (qb + 1) * block
            keys = lax.broadcasted_iota(jnp.int32, (n, block), 0)
            place = lax.broadcasted_iota(jnp.int32, (n, block), 1) + qb * block
            allowed = (pcol[0:n, 0:1] <= prow[0:1, qb * block : n]) & (keys < length)
            allowed = (allowed & (keys < place)) | (keys == place)
            at_row = qb * (qb + 1) // 2 * block
            bias[at_row : at_row + n, :] = jnp.where(allowed, 0.0, negative)

    head = pl.program_id(0)
    rows = pl.ds(pl.multiple_of(head * 64, 64), 64)
    keyn = jnp.transpose(kt[rows, :])
    for qb in range(total // block):
        n = (qb + 1) * block
        at_row = qb * (qb + 1) // 2 * block
        scores = dot(keyn[0:n, :], qt[rows, qb * block : n], NN) + bias[at_row : at_row + n, :]
        peak = jnp.max(scores, 0, keepdims=True)
        expo = jnp.exp(scores - peak)
        over = 1.0 / jnp.sum(expo, 0, keepdims=True)
        low = expo.astype(jnp.bfloat16)
        kept[0, at_row : at_row + n, :] = low
        inv[0, :, qb * block : n] = jnp.broadcast_to(over, (8, block))
        result = dot(vt[rows, 0:n], low, NN) * over
        ot[rows, qb * block : n] = result.astype(jnp.bfloat16)


def mlp_kernel(
    info, ot_own, ot_recv, ht, c0, c1, c2, c3, w_out, vecs, w_up, b_up, w_down,
    midt, mt, gt, dut, bdown, otf, ct
):
    width, total = ht.shape
    half = ot_own.shape[0]
    core = info[4]
    otf[pl.ds(pl.multiple_of(core * half, 64), half), :] = ot_own[...]
    otf[pl.ds(pl.multiple_of((1 - core) * half, 64), half), :] = ot_recv[...]
    for k, ref in enumerate((c0, c1, c2, c3)):
        place = pl.ds(pl.multiple_of(info[k] * block, block), block)
        ct[:, place] = jnp.transpose(ref[...])

    def mix(cols):
        mid = ht[:, cols] + dot(w_out[...], otf[:, cols], TN)
        midt[:, cols] = mid
        shifted = mid - jnp.sum(mid, 0, keepdims=True) * (1.0 / width)
        spread = jnp.sum(shifted * shifted, 0, keepdims=True) * (1.0 / width)
        scaled = shifted * lax.rsqrt(spread + 1e-05)
        mt[:, cols] = (scaled * vecs[:, 2:3] + vecs[:, 3:4]).astype(jnp.bfloat16)

    lane_loop(total, 256, mix)
    part = 192
    inner = gt.shape[0]

    def hidden(i, carry):
        rows = pl.ds(pl.multiple_of(i * part, part), part)
        u = dot(w_up[rows, :], mt[...], NN) + b_up[rows, 0:1]
        back = dot(w_down[rows, :], ct[...], NN)
        square = u * u
        t = jnp.tanh(u * (0.7978845608028654 + 0.035677408136300125 * square))
        gate = 0.5 + 0.5 * t
        gt[rows, :] = (u * gate).astype(jnp.bfloat16)
        slope = gate + (0.5 * u) * (1.0 - t * t) * (
            0.7978845608028654 + 0.10703222440890037 * square
        )
        dut[rows, :] = (back * slope).astype(jnp.bfloat16)
        return carry

    lax.fori_loop(0, inner // part, hidden, 0)
    lanes = bdown.shape[-1]
    bs = bdown.shape[1]
    band = width // bs
    for x in range(2):
        for j in range(2):
            at_row = (2 * x + j) * lanes
            grad = dot(ct[...], gt[at_row : at_row + lanes, :], NT).astype(jnp.bfloat16)
            for b in range(bs):
                bdown[x, b, j * band : (j + 1) * band, :] = grad[b * band : (b + 1) * band, :]


def up_kernel(dut, mt, w_up, bup, dmt, bsum):
    width, total = mt.shape
    inner = dut.shape[0]
    bs = bup.shape[1]
    band = inner // bs
    lanes = bup.shape[-1]
    dmt[...] = dot(w_up[...], dut[...], TN).astype(jnp.bfloat16)
    for x in range(2):
        grad = dot(dut[...], mt[x * lanes : (x + 1) * lanes, :], NT).astype(jnp.bfloat16)
        for b in range(bs):
            bup[x, b] = grad[b * band : (b + 1) * band, :]
    for i in range(4):
        rows = slice(i * inner // 4, (i + 1) * inner // 4)
        bsum[rows, :] = jnp.broadcast_to(
            jnp.sum(dut[rows, :].astype(jnp.float32), 1, keepdims=True), (inner // 4, 8)
        )


def down_kernel(info, gt, w_down, midt, vecs, keep, send):
    core = info[4]
    for k in range(2):
        mine = pl.ds(pl.multiple_of(core * block + k * 2 * block, block), block)
        other = pl.ds(pl.multiple_of((1 - core) * block + k * 2 * block, block), block)
        to = slice(k * block, (k + 1) * block)
        keep[:, to] = midt[:, mine] + vecs[:, 4:5] + dot(w_down[...], gt[:, mine], TN)
        send[:, to] = dot(w_down[...], gt[:, other], TN).astype(jnp.bfloat16)


def middle_kernel(
    info, dm_own, dm_recv, midt, vecs, c0, c1, c2, c3, ot_own, ot_recv, w_out,
    dmidt, dot_own, bout, sums, dat, otf, picked
):
    width, total = midt.shape
    half = ot_own.shape[0]
    core = info[4]
    otf[pl.ds(pl.multiple_of(core * half, 64), half), :] = ot_own[...]
    otf[pl.ds(pl.multiple_of((1 - core) * half, 64), half), :] = ot_recv[...]
    sums[...] = jnp.zeros_like(sums)
    for k, ref in enumerate((c0, c1, c2, c3)):
        place = pl.ds(pl.multiple_of(info[k] * block, block), block)
        cot = jnp.transpose(ref[...]).astype(jnp.float32)
        mid = midt[:, place]
        shifted = mid - jnp.sum(mid, 0, keepdims=True) * (1.0 / width)
        spread = jnp.sum(shifted * shifted, 0, keepdims=True) * (1.0 / width)
        r = lax.rsqrt(spread + 1e-05)
        n = shifted * r
        dm = dm_own[:, place].astype(jnp.float32) + dm_recv[:, place].astype(jnp.float32)
        e = dm * vecs[:, 2:3]
        mean_e = jnp.sum(e, 0, keepdims=True) * (1.0 / width)
        mean_en = jnp.sum(e * n, 0, keepdims=True) * (1.0 / width)
        dmid = cot + r * (e - mean_e - n * mean_en)
        dmidt[:, place] = dmid
        dat[:, place] = dmid.astype(jnp.bfloat16)
        sums[:, 0:1] += jnp.sum(dm * n, 1, keepdims=True)
        sums[:, 1:2] += jnp.sum(dm, 1, keepdims=True)
        sums[:, 2:3] += jnp.sum(cot, 1, keepdims=True)
    own = pl.ds(pl.multiple_of(core * half, 64), half)
    dot_own[...] = dot(w_out[own, :], dat[...], NN).astype(jnp.bfloat16)
    bs = bout.shape[1]
    band = width // bs
    small = band // 2
    lanes = bout.shape[-1]
    for b in range(bs):
        picked[b * small : (b + 1) * small, :] = dat[
            pl.ds(pl.multiple_of(b * band + core * small, 16), small), :
        ]
    for x in range(2):
        grad = dot(picked[...], otf[x * lanes : (x + 1) * lanes, :], NT).astype(jnp.bfloat16)
        for b in range(bs):
            bout[x, b] = grad[b * small : (b + 1) * small, :]


def attend_back_kernel(qt, kt, vt, ot, dout, kept, inv, dq, dk, dv, ksum, vsum):
    total = qt.shape[1]
    valn = jnp.transpose(vt[...])
    scaled = dout[...].astype(jnp.float32) * inv[0, 0:1, :]
    grads = scaled.astype(jnp.bfloat16)
    delta = jnp.sum(grads.astype(jnp.float32) * ot[...].astype(jnp.float32), 0, keepdims=True)
    ksum[...] = jnp.zeros_like(ksum)
    vsum[...] = jnp.zeros_like(vsum)
    for qb in range(total // block):
        n = (qb + 1) * block
        at_row = qb * (qb + 1) // 2 * block
        cols = slice(qb * block, n)
        low = kept[0, at_row : at_row + n, :]
        dprob = dot(valn[0:n, :], grads[:, cols], NN)
        dscore = (low.astype(jnp.float32) * (dprob - delta[:, cols])).astype(jnp.bfloat16)
        dq[:, cols] = (dot(kt[:, 0:n], dscore, NN) * 0.125).astype(jnp.bfloat16)
        ksum[:, 0:n] += dot(qt[:, cols], dscore, NT)
        vsum[:, 0:n] += dot(grads[:, cols], low, NT)
    dk[...] = ksum[...].astype(jnp.bfloat16)
    dv[...] = vsum[...].astype(jnp.bfloat16)


def qkv_grad_kernel(info, own, recv, at, bqkv, full, picked):
    width, total = at.shape
    half = own.shape[0] // 3
    core = info[4]
    for j in range(3):
        rows = slice(j * half, (j + 1) * half)
        full[pl.ds(pl.multiple_of(j * width + core * half, 64), half), :] = own[rows, :]
        full[pl.ds(pl.multiple_of(j * width + (1 - core) * half, 64), half), :] = recv[rows, :]
    bs = bqkv.shape[1]
    band = 3 * width // bs
    small = band // 2
    lanes = bqkv.shape[-1]
    for b in range(bs):
        picked[b * small : (b + 1) * small, :] = full[
            pl.ds(pl.multiple_of(b * band + core * small, 16), small), :
        ]
    for x in range(2):
        grad = dot(picked[...], at[x * lanes : (x + 1) * lanes, :], NT).astype(jnp.bfloat16)
        for b in range(bs):
            bqkv[x, b] = grad[b * small : (b + 1) * small, :]


def input_grad_kernel(info, full, w_qkv, ht, dmidt, vecs, prow, gin, sums, gpass):
    width, total = ht.shape
    core = info[4]
    sums[...] = jnp.zeros_like(sums)
    gpass[...] = jnp.zeros_like(gpass)
    for k in range(2):
        mine = pl.ds(pl.multiple_of(core * block + k * 2 * block, block), block)
        da = dot(w_qkv[...], full[:, mine], NN)
        h = ht[:, mine]
        shifted = h - jnp.sum(h, 0, keepdims=True) * (1.0 / width)
        spread = jnp.sum(shifted * shifted, 0, keepdims=True) * (1.0 / width)
        r = lax.rsqrt(spread + 1e-05)
        n = shifted * r
        e = da * vecs[:, 0:1]
        mean_e = jnp.sum(e, 0, keepdims=True) * (1.0 / width)
        mean_en = jnp.sum(e * n, 0, keepdims=True) * (1.0 / width)
        dh = dmidt[:, mine] + r * (e - mean_e - n * mean_en)
        gin[k] = jnp.transpose(dh).astype(jnp.bfloat16)
        sums[:, 0:1] += jnp.sum(da * n, 1, keepdims=True)
        sums[:, 1:2] += jnp.sum(da, 1, keepdims=True)
        kind = lax.broadcasted_iota(jnp.int32, (16, block), 0).astype(jnp.float32)
        onehot = jnp.where(kind == prow[0:1, mine], 1.0, 0.0).astype(jnp.bfloat16)
        high = dh.astype(jnp.bfloat16)
        rest = dh - high.astype(jnp.float32)
        mid = rest.astype(jnp.bfloat16)
        tail = (rest - mid.astype(jnp.float32)).astype(jnp.bfloat16)
        gpass[...] += dot(high, onehot, NT) + dot(mid, onehot, NT) + dot(tail, onehot, NT)


def call(kernel, outs, scratch=(), smem=True, n_in=0, name=None, flops=0, **kw):
    in_specs = [pl.BlockSpec(memory_space=pltpu.VMEM)] * n_in
    if smem:
        in_specs[0] = pl.BlockSpec(memory_space=pltpu.SMEM)
    return pl.pallas_call(
        kernel,
        out_shape=outs,
        in_specs=in_specs,
        out_specs=[pl.BlockSpec(memory_space=pltpu.VMEM)] * len(outs),
        scratch_shapes=list(scratch),
        compiler_params=pltpu.CompilerParams(vmem_limit_bytes=vmem_bytes),
        cost_estimate=pl.CostEstimate(flops=int(flops), bytes_accessed=0, transcendentals=0),
        name=name,
        **kw,
    )


def shaped(*dims, kind=jnp.bfloat16):
    return jax.ShapeDtypeStruct(dims, kind)


def pick(array, axis, index):
    return lax.dynamic_index_in_dim(array, index, axis, keepdims=False)


def swap(array, axis, size, distance):
    return lax.ppermute(array, axis, [(i, i ^ distance) for i in range(size)])


def regrouped(
    block_input, lengths, pass_ids, pass_embed, ln1_gain, ln1_bias, w_qkv, w_out,
    ln2_gain, ln2_bias, w_up, b_up, w_down, b_down, cotangent, batch_n, y_n
):
    row_count, seg_len, width = block_input.shape
    total = 4 * seg_len
    inner = w_up.shape[1]
    own_in = inner // 2
    heads_own = H // 2
    half = width // 2
    z_n = batch_n // y_n
    s = lax.axis_index("seq")
    x, core = s // 2, s % 2
    bat = lax.axis_index("batch")
    z, y = bat // y_n, bat % y_n

    def by_x(array):
        return swap(array, "seq", 4, 2)

    def by_core(array):
        return swap(array, "seq", 4, 1)

    def by_y(array):
        return swap(array, "batch", batch_n, 1)

    pass_rows = jnp.zeros((row_count, 16, width), jnp.bfloat16)
    pass_rows = lax.dynamic_update_slice(
        pass_rows,
        jnp.broadcast_to(pass_ids.astype(jnp.bfloat16)[:, None, :], (row_count, 16, seg_len)),
        (0, 0, 0),
    )
    packed = jnp.concatenate([block_input, pass_rows], 1)
    x_own = pick(packed, 0, x)
    x_far = by_x(pick(packed, 0, 1 - x))
    x_near = by_core(x_own)
    x_cross = by_core(x_far)
    c_own = pick(cotangent, 0, x)
    c_far = by_x(pick(cotangent, 0, 1 - x))
    c_near = by_core(c_own)
    c_cross = by_core(c_far)
    length = pick(lengths, 0, x)
    info = jnp.stack(
        [2 * x + core, 2 * (1 - x) + core, 2 * x + 1 - core, 2 * (1 - x) + 1 - core, core, length]
    ).astype(jnp.int32)

    embed_t = jnp.transpose(pass_embed)
    first = embed_t.astype(jnp.bfloat16)
    rest = embed_t - first.astype(jnp.float32)
    second = rest.astype(jnp.bfloat16)
    third = (rest - second.astype(jnp.float32)).astype(jnp.bfloat16)
    emb = jnp.concatenate([first, second, third, jnp.zeros((width, 1), jnp.bfloat16)], 1)
    zero = jnp.zeros_like(ln1_gain)
    vecs = jnp.stack([ln1_gain, ln1_bias, ln2_gain, ln2_bias, b_down, zero, zero, zero], 1)
    band = inner // batch_n // 2
    w_up_own = pick(w_up.reshape(width, batch_n, 2, band), 2, core).reshape(width, own_in)
    w_up_t = jnp.transpose(w_up_own)
    w_down_own = pick(w_down.reshape(batch_n, 2, band, width), 1, core).reshape(own_in, width)
    b_up_own = pick(b_up.reshape(batch_n, 2, band), 1, core).reshape(own_in, 1)
    b_up_own = jnp.broadcast_to(b_up_own, (own_in, 8))

    blocks_n = total // block
    kept_rows = blocks_n * (blocks_n + 1) // 2 * block
    whole = pl.BlockSpec(memory_space=pltpu.VMEM)

    def fixed(*dims):
        return pl.BlockSpec(dims, lambda i: (0,) * len(dims))

    ht, at, qt, kt, vt, ot, kept, inv, prow = pl.pallas_call(
        lambda *refs: attend_kernel(*refs[:8], *refs[8:16], refs[17], refs[16], refs[18]),
        out_shape=[
            shaped(width, total, kind=jnp.float32),
            shaped(width, total),
            shaped(half, total),
            shaped(half, total),
            shaped(half, total),
            shaped(half, total),
            shaped(heads_own, kept_rows, block),
            shaped(heads_own, 8, total, kind=jnp.float32),
            shaped(8, total, kind=jnp.float32),
        ],
        grid=(heads_own,),
        in_specs=[pl.BlockSpec(memory_space=pltpu.SMEM)]
        + [fixed(seg_len + 16, width)] * 4
        + [fixed(width, 16), fixed(width, 8), fixed(width, 3 * width)],
        out_specs=[
            fixed(width, total),
            fixed(width, total),
            fixed(half, total),
            fixed(half, total),
            fixed(half, total),
            fixed(half, total),
            pl.BlockSpec((1, kept_rows, block), lambda i: (i, 0, 0)),
            pl.BlockSpec((1, 8, total), lambda i: (i, 0, 0)),
            fixed(8, total),
        ],
        scratch_shapes=[
            pltpu.VMEM((kept_rows, block), jnp.float32),
            pltpu.VMEM((total, 8), jnp.float32),
        ],
        compiler_params=pltpu.CompilerParams(vmem_limit_bytes=vmem_bytes),
        cost_estimate=pl.CostEstimate(flops=int(12e9), bytes_accessed=0, transcendentals=0),
        name="attend",
    )(info, x_own, x_far, x_near, x_cross, emb, vecs, w_qkv)

    ot_recv = by_core(ot)
    lanes = width // 2
    row_down = 2 * (width // batch_n)
    midt, mt, gt, dut, bdown = call(
        mlp_kernel,
        [
            shaped(width, total, kind=jnp.float32),
            shaped(width, total),
            shaped(own_in, total),
            shaped(own_in, total),
            shaped(2, batch_n, row_down, own_in // 4),
        ],
        [pltpu.VMEM((width, total), jnp.bfloat16), pltpu.VMEM((width, total), jnp.bfloat16)],
        n_in=13,
        name="mlp",
        flops=18e9,
    )(info, ot, ot_recv, ht, c_own, c_far, c_near, c_cross, w_out, vecs, w_up_t, b_up_own, w_down_own)
    bup, dmt, bsum = call(
        up_kernel,
        [
            shaped(2, batch_n, band, lanes),
            shaped(width, total),
            shaped(own_in, 8, kind=jnp.float32),
        ],
        smem=False,
        n_in=3,
        name="up",
        flops=5e9,
    )(dut, mt, w_up_t)
    dm_recv = by_core(dmt)
    keep, give = call(
        down_kernel,
        [shaped(width, 2 * block, kind=jnp.float32), shaped(width, 2 * block)],
        n_in=5,
        name="down",
        flops=3e9,
    )(info, gt, w_down_own, midt, vecs)
    out_recv = by_core(give)
    out_rows = jnp.transpose((keep + out_recv.astype(jnp.float32)).astype(jnp.bfloat16))
    out_rows = out_rows.reshape(2, block, width)

    dmidt, dout, bout, sums2 = call(
        middle_kernel,
        [
            shaped(width, total, kind=jnp.float32),
            shaped(half, total),
            shaped(2, batch_n, width // batch_n // 2, lanes),
            shaped(width, 8, kind=jnp.float32),
        ],
        [
            pltpu.VMEM((width, total), jnp.bfloat16),
            pltpu.VMEM((width, total), jnp.bfloat16),
            pltpu.VMEM((half, total), jnp.bfloat16),
        ],
        n_in=12,
        name="middle",
        flops=4e9,
    )(info, dmt, dm_recv, midt, vecs, c_own, c_far, c_near, c_cross, ot, ot_recv, w_out)

    def head_rows():
        return pl.BlockSpec((64, total), lambda i: (i, 0))

    dq, dk, dv = pl.pallas_call(
        attend_back_kernel,
        out_shape=[shaped(half, total)] * 3,
        grid=(heads_own,),
        in_specs=[head_rows()] * 5
        + [
            pl.BlockSpec((1, kept_rows, block), lambda i: (i, 0, 0)),
            pl.BlockSpec((1, 8, total), lambda i: (i, 0, 0)),
        ],
        out_specs=[head_rows()] * 3,
        scratch_shapes=[pltpu.VMEM((64, total), jnp.float32)] * 2,
        compiler_params=pltpu.CompilerParams(vmem_limit_bytes=vmem_bytes),
        cost_estimate=pl.CostEstimate(flops=int(15e9), bytes_accessed=0, transcendentals=0),
        name="attend_back",
    )(qt, kt, vt, ot, dout, kept, inv)
    dqkv = jnp.concatenate([dq, dk, dv], 0)
    dqkv_recv = by_core(dqkv)
    small = 3 * width // batch_n // 2
    bqkv, full = call(
        lambda *refs: qkv_grad_kernel(*refs[:5], refs[5], refs[6]),
        [shaped(2, batch_n, small, lanes), shaped(3 * width, total)],
        [pltpu.VMEM((3 * half, total), jnp.bfloat16)],
        n_in=4,
        name="qkv_grad",
        flops=2e9,
    )(info, dqkv, dqkv_recv, at)
    gin_rows, sums1, gpass = call(
        input_grad_kernel,
        [
            shaped(2, block, width),
            shaped(width, 8, kind=jnp.float32),
            shaped(width, 16, kind=jnp.float32),
        ],
        n_in=7,
        name="input_grad",
        flops=3e9,
    )(info, full, w_qkv, ht, dmidt, vecs, prow)

    def hand_back(rows):
        mine, far = pick(rows, 0, x), by_x(pick(rows, 0, 1 - x))
        both = jnp.stack([mine, far])
        return jnp.where(x == 0, both, both[::-1])

    output = hand_back(out_rows)
    grad_input = hand_back(gin_rows)

    def halve(array, axis, index, send):
        return pick(array, axis, index) + send(pick(array, axis, 1 - index))

    def along_z(array):
        right, left = None, None
        for t in range(z_n - 1):
            ahead = pick(array, 0, jnp.minimum(z_n - 1 - t + z, z_n - 1))
            back = pick(array, 0, jnp.maximum(t - (z_n - 1 - z), 0))
            if t:
                ahead, back = ahead + right, back + left
            up = [(a, a + 1) for a in range(t + 1)]
            pairs = [(a * y_n + k, b * y_n + k) for a, b in up for k in range(y_n)]
            mirror = [
                ((z_n - 1 - a) * y_n + k, (z_n - 1 - b) * y_n + k) for a, b in up for k in range(y_n)
            ]
            right = lax.ppermute(ahead, "batch", pairs)
            left = lax.ppermute(back, "batch", mirror)
        return pick(array, 0, z) + right + left

    def reduce_scatter(array):
        rows = array.shape[2]
        array = array.reshape(2, z_n, y_n, rows, array.shape[3])
        cut = rows // 2 // 16 * 16
        one, two = array[..., :cut, :], array[..., cut:, :]
        one = halve(halve(one, 0, x, by_x), 1, y, by_y)
        two = halve(halve(two, 2, y, by_y), 0, x, by_x)
        return jnp.concatenate([along_z(one), along_z(two)], 0)

    gdown = reduce_scatter(bdown)
    gup = reduce_scatter(bup)
    gout = reduce_scatter(bout)
    gqkv = reduce_scatter(bqkv)

    def across(array):
        wide = array.shape[1] // 2
        parts = array.reshape(array.shape[0], 2, wide)
        mine, got = pick(parts, 1, core), by_core(pick(parts, 1, 1 - core))
        return jnp.where(core == 0, jnp.stack([mine, got]), jnp.stack([got, mine]))

    def finish(array):
        both = across(array)
        return jnp.transpose(both.reshape(-1, both.shape[2])).astype(jnp.float32)

    parts = gdown.reshape(2, row_down // 2, own_in // 4)
    mine, got = pick(parts, 0, core), by_core(pick(parts, 0, 1 - core))
    both = jnp.where(core == 0, jnp.stack([mine, got]), jnp.stack([got, mine]))
    both = both.reshape(2, row_down // 2, own_in // 4 // band, band)
    grad_down = jnp.transpose(both, (2, 0, 3, 1)).reshape(inner // 4, row_down // 2)
    grad_down = grad_down.astype(jnp.float32)
    grad_up, grad_out, grad_qkv = finish(gup), finish(gout), finish(gqkv)

    bsum_own = bsum[:, 0].reshape(batch_n, 1, band)
    spread_up = jnp.where(
        lax.broadcasted_iota(jnp.int32, (batch_n, 2, band), 1) == core, bsum_own, 0.0
    )
    vector = jnp.concatenate(
        [
            jnp.transpose(gpass[:, :5]).reshape(-1),
            sums1[:, 0],
            sums1[:, 1],
            sums2[:, 0] * 0.5,
            sums2[:, 1] * 0.5,
            sums2[:, 2] * 0.5,
            spread_up.reshape(-1),
        ]
    ).reshape(-1, width)
    vector = vector + by_core(vector)
    vector = vector + by_x(vector)
    step = 1
    while step < batch_n:
        vector = vector + swap(vector, "batch", batch_n, step)
        step *= 2
    return (
        output,
        grad_input,
        vector[0:5],
        vector[5],
        vector[6],
        grad_qkv,
        grad_out,
        vector[7],
        vector[8],
        grad_up,
        vector[10:].reshape(-1),
        grad_down,
        vector[9],
    )


def solution(mesh):
    batch_n = mesh.shape["batch"]
    few = mesh.shape["seq"] == 4 and batch_n % 2 == 0
    plan = functools.partial(regrouped, batch_n=batch_n, y_n=2) if few else local
    return jax.shard_map(
        plan,
        mesh=mesh,
        in_specs=(
            P("batch", "seq", None),
            P("batch"),
            P("batch", "seq"),
            P(),
            P(),
            P(),
            P(),
            P(),
            P(),
            P(),
            P(),
            P(),
            P(),
            P(),
            P("batch", "seq", None),
        ),
        out_specs=(
            P("batch", "seq", None),
            P("batch", "seq", None),
            P(),
            P(),
            P(),
            P("seq", "batch"),
            P("seq", "batch"),
            P(),
            P(),
            P("seq", "batch"),
            P(),
            P("seq", "batch"),
            P(),
        ),
        check_vma=False,
    )
```

```python
import functools

import jax
import jax.numpy as jnp
from jax import lax
from jax.experimental import pallas as pl
from jax.experimental.pallas import tpu as pltpu
from jax.sharding import PartitionSpec as P

H = 12


negative = -1e30
key_block = 1024
query_block = 512
highest = lax.Precision.HIGHEST


def layer_norm(hidden, gain, offset):
    centre = jnp.mean(hidden, -1, keepdims=True)
    shifted = hidden - centre
    spread = jnp.mean(shifted * shifted, -1, keepdims=True)
    return shifted * lax.rsqrt(spread + 1e-05) * gain + offset


def gelu_tanh(values):
    return jax.nn.gelu(values, approximate=True)


def visible(query_place, query_pass, key_place, key_pass, length):
    earlier = key_place[None, :] < query_place[:, None]
    allowed = earlier & (key_pass[None, :] <= query_pass[:, None]) & (key_place[None, :] < length)
    return allowed | (key_place[None, :] == query_place[:, None])


def masked_scores(query_part, key_part, factor, seen):
    raw = (
        jnp.einsum("qhd,khd->hqk", query_part, key_part, preferred_element_type=jnp.float32)
        * factor
    )
    return jnp.where(seen[None], raw, negative)


def split_blocks(arrays, block_len):
    return tuple(
        (
            array.reshape((array.shape[0] // block_len, block_len) + array.shape[1:])
            for array in arrays
        )
    )


def chance_of(query_part, key_part, log_part, seen, factor):
    scores = masked_scores(query_part, key_part, factor, seen)
    return jnp.where(seen[None], jnp.exp(scores - log_part[..., None]), 0.0)


def grad_pieces(query_part, dout_part, log_part, delta_part, key_part, value_part, seen, factor):
    chance = chance_of(query_part, key_part, log_part, seen, factor)
    dprob = jnp.einsum("qhd,khd->hqk", dout_part, value_part, preferred_element_type=jnp.float32)
    dscore = (chance * (dprob - delta_part[..., None])).astype(jnp.bfloat16)
    return (dscore, chance.astype(jnp.bfloat16))


def attend_row(queries, query_place, query_pass, key_rows, value_rows, key_pass, length):
    factor = queries.shape[-1] ** (-0.5)
    places = jnp.arange(key_rows.shape[0], dtype=jnp.int32)
    key_parts = split_blocks(
        (key_rows, value_rows, key_pass, places), min(key_block, key_rows.shape[0])
    )
    query_len = min(query_block, queries.shape[0])
    query_parts = split_blocks((queries, query_place, query_pass), query_len)

    def attend_one_block(query_args):
        query_part, place_part, pass_part = query_args

        def running(carry, key_args):
            peak, summed, total_out = carry
            key_part, value_part, kpass_part, kplace_part = key_args
            seen = visible(place_part, pass_part, kplace_part, kpass_part, length)
            scores = masked_scores(query_part, key_part, factor, seen)
            new_peak = jnp.maximum(peak, jnp.max(scores, -1))
            terms = jnp.where(seen[None], jnp.exp(scores - new_peak[..., None]), 0.0)
            rescale = jnp.exp(peak - new_peak)
            summed = summed * rescale + jnp.sum(terms, -1)
            added = jnp.einsum(
                "hqk,khd->qhd",
                terms.astype(jnp.bfloat16),
                value_part,
                preferred_element_type=jnp.float32,
            )
            total_out = total_out * rescale.T[..., None] + added
            return ((new_peak, summed, total_out), None)

        heads_n = query_part.shape[1]
        start = (
            jnp.full((heads_n, query_len), negative, jnp.float32),
            jnp.zeros((heads_n, query_len), jnp.float32),
            jnp.zeros(query_part.shape, jnp.float32),
        )
        (peak, summed, total_out), _ = lax.scan(running, start, key_parts)
        log_total = peak + jnp.log(summed)
        result = total_out / summed.T[..., None]
        return (result, log_total)

    results, log_totals = lax.map(attend_one_block, query_parts)
    heads_n = queries.shape[1]
    return (
        results.reshape(queries.shape),
        jnp.moveaxis(log_totals, 1, 0).reshape(heads_n, queries.shape[0]),
    )


def backward_row(
    queries,
    douts,
    outs_kept,
    log_totals,
    query_place,
    query_pass,
    key_rows,
    value_rows,
    key_pass,
    length,
):
    factor = queries.shape[-1] ** (-0.5)
    places = jnp.arange(key_rows.shape[0], dtype=jnp.int32)
    key_parts = split_blocks(
        (key_rows, value_rows, key_pass, places), min(key_block, key_rows.shape[0])
    )
    query_len = min(query_block, queries.shape[0])
    heads_n = queries.shape[1]
    block_count = queries.shape[0] // query_len
    log_parts = jnp.moveaxis(log_totals.reshape(heads_n, block_count, query_len), 1, 0)
    query_parts = split_blocks((queries, douts, outs_kept, query_place, query_pass), query_len)

    def backward_one_block(carry, query_args):
        query_part, dout_part, kept_part, place_part, pass_part, log_part = query_args
        delta_part = jnp.einsum("qhd,qhd->hq", dout_part.astype(jnp.float32), kept_part)

        def add_grads(dquery, key_args):
            key_part, value_part, kpass_part, kplace_part = key_args
            seen = visible(place_part, pass_part, kplace_part, kpass_part, length)
            dscore, low_chance = grad_pieces(
                query_part, dout_part, log_part, delta_part, key_part, value_part, seen, factor
            )
            dquery = dquery + factor * jnp.einsum(
                "hqk,khd->qhd", dscore, key_part, preferred_element_type=jnp.float32
            )
            dkey = factor * jnp.einsum(
                "hqk,qhd->khd", dscore, query_part, preferred_element_type=jnp.float32
            )
            dvalue = jnp.einsum(
                "hqk,qhd->khd", low_chance, dout_part, preferred_element_type=jnp.float32
            )
            return (dquery, (dkey, dvalue))

        dquery, key_terms = lax.scan(add_grads, jnp.zeros(query_part.shape, jnp.float32), key_parts)
        carry = (
            carry[0] + key_terms[0].reshape(key_rows.shape),
            carry[1] + key_terms[1].reshape(value_rows.shape),
        )
        return (carry, (dquery, delta_part))

    start = (jnp.zeros(key_rows.shape, jnp.float32), jnp.zeros(value_rows.shape, jnp.float32))
    key_sums, (dqueries, deltas) = lax.scan(backward_one_block, start, query_parts + (log_parts,))
    return (
        dqueries.reshape(queries.shape),
        jnp.moveaxis(deltas, 1, 0).reshape(heads_n, queries.shape[0]),
        key_sums,
    )


def local(
    block_input,
    lengths,
    pass_ids,
    pass_embed,
    ln1_gain,
    ln1_bias,
    w_qkv,
    w_out,
    ln2_gain,
    ln2_bias,
    w_up,
    b_up,
    w_down,
    b_down,
    cotangent,
):
    row_count, seg_len, width = block_input.shape
    heads_n = H
    head_size = width // heads_n
    onehot = (
        pass_ids[..., None] == jnp.arange(pass_embed.shape[0], dtype=jnp.int32)[None, None, :]
    ).astype(jnp.float32)
    hidden_in = block_input.astype(jnp.float32) + jnp.einsum(
        "rsp,pd->rsd", onehot, pass_embed, precision=highest
    )
    normed, norm_back = jax.vjp(layer_norm, hidden_in, ln1_gain, ln1_bias)
    normed_low = normed.astype(jnp.bfloat16)
    qkv = jnp.einsum("rsd,de->rse", normed_low, w_qkv, preferred_element_type=jnp.float32)
    queries = qkv[..., :width].astype(jnp.bfloat16)
    key_flat = qkv[..., width : 2 * width].astype(jnp.bfloat16)
    value_flat = qkv[..., 2 * width :].astype(jnp.bfloat16)
    pass_low = pass_ids.astype(jnp.bfloat16)
    key_all, value_all, pass_all = (
        lax.all_gather(key_flat, "seq", axis=1, tiled=True),
        lax.all_gather(value_flat, "seq", axis=1, tiled=True),
        lax.all_gather(pass_low, "seq", axis=1, tiled=True),
    )
    total_len = key_all.shape[1]
    key_all = key_all.reshape(row_count, total_len, heads_n, head_size)
    value_all = value_all.reshape(row_count, total_len, heads_n, head_size)
    pass_all = pass_all.astype(jnp.float32)
    offset = lax.axis_index("seq") * seg_len
    query_place = offset + jnp.arange(seg_len, dtype=jnp.int32)
    query_pass = pass_ids.astype(jnp.float32)
    query_heads = queries.reshape(row_count, seg_len, heads_n, head_size)
    attended_rows = []
    log_rows = []
    for row in range(row_count):
        attended, log_total = attend_row(
            query_heads[row],
            query_place,
            query_pass[row],
            key_all[row],
            value_all[row],
            pass_all[row],
            lengths[row],
        )
        attended_rows.append(attended)
        log_rows.append(log_total)
    attended_low = jnp.stack(attended_rows).astype(jnp.bfloat16).reshape(row_count, seg_len, width)
    branch = jnp.einsum("rsd,de->rse", attended_low, w_out, preferred_element_type=jnp.float32)
    middle = hidden_in + branch
    normed2, norm2_back = jax.vjp(layer_norm, middle, ln2_gain, ln2_bias)
    normed2_low = normed2.astype(jnp.bfloat16)
    pre_act = (
        jnp.einsum("rsd,df->rsf", normed2_low, w_up, preferred_element_type=jnp.float32) + b_up
    )
    active, active_back = jax.vjp(gelu_tanh, pre_act)
    active_low = active.astype(jnp.bfloat16)
    result = (
        middle
        + jnp.einsum("rsf,fd->rsd", active_low, w_down, preferred_element_type=jnp.float32)
        + b_down
    )
    output = result.astype(jnp.bfloat16)
    cot_f = cotangent.astype(jnp.float32)
    grad_active = jnp.einsum("rsd,fd->rsf", cotangent, w_down, preferred_element_type=jnp.float32)
    grad_w_down = jnp.einsum(
        "rsf,rsd->fd", active_low, cotangent, preferred_element_type=jnp.float32
    )
    grad_b_down = jnp.sum(cot_f, (0, 1))
    grad_pre = active_back(grad_active)[0].astype(jnp.bfloat16)
    grad_b_up = jnp.sum(grad_pre.astype(jnp.float32), (0, 1))
    grad_w_up = jnp.einsum("rsd,rsf->df", normed2_low, grad_pre, preferred_element_type=jnp.float32)
    grad_normed2 = jnp.einsum("rsf,df->rsd", grad_pre, w_up, preferred_element_type=jnp.float32)
    grad_mid_norm, grad_ln2_gain, grad_ln2_bias = norm2_back(grad_normed2)
    grad_middle = cot_f + grad_mid_norm
    grad_branch = grad_middle.astype(jnp.bfloat16)
    grad_w_out = jnp.einsum(
        "rsd,rse->de", attended_low, grad_branch, preferred_element_type=jnp.float32
    )
    grad_attended = jnp.einsum(
        "rse,de->rsd", grad_branch, w_out, preferred_element_type=jnp.float32
    ).astype(jnp.bfloat16)
    dout_heads = grad_attended.reshape(row_count, seg_len, heads_n, head_size)
    dquery_rows = []
    dkey_rows = []
    dvalue_rows = []
    for row in range(row_count):
        dquery, _, key_sums = backward_row(
            query_heads[row],
            dout_heads[row],
            attended_rows[row],
            log_rows[row],
            query_place,
            query_pass[row],
            key_all[row],
            value_all[row],
            pass_all[row],
            lengths[row],
        )
        dquery_rows.append(dquery)
        dkey_rows.append(key_sums[0].reshape(total_len, width))
        dvalue_rows.append(key_sums[1].reshape(total_len, width))
    dkey_sum, dvalue_sum = (
        lax.psum_scatter(
            jnp.stack(dkey_rows).astype(jnp.bfloat16), "seq", scatter_dimension=1, tiled=True
        ).astype(jnp.float32),
        lax.psum_scatter(
            jnp.stack(dvalue_rows).astype(jnp.bfloat16), "seq", scatter_dimension=1, tiled=True
        ).astype(jnp.float32),
    )
    dquery_all = jnp.stack(dquery_rows).reshape(row_count, seg_len, width)
    grad_qkv = jnp.concatenate(
        [
            dquery_all.astype(jnp.bfloat16),
            dkey_sum.astype(jnp.bfloat16),
            dvalue_sum.astype(jnp.bfloat16),
        ],
        -1,
    )
    grad_w_qkv = jnp.einsum("rsd,rse->de", normed_low, grad_qkv, preferred_element_type=jnp.float32)
    grad_normed = jnp.einsum("rse,de->rsd", grad_qkv, w_qkv, preferred_element_type=jnp.float32)
    grad_in_norm, grad_ln1_gain, grad_ln1_bias = norm_back(grad_normed)
    grad_hidden = grad_middle + grad_in_norm
    grad_input = grad_hidden.astype(jnp.bfloat16)
    grad_pass = jnp.einsum("rsp,rsd->pd", onehot, grad_hidden, precision=highest)
    matrices = (
        lax.psum_scatter(
            grad_w_qkv.astype(jnp.bfloat16), "seq", scatter_dimension=0, tiled=True
        ).astype(jnp.float32),
        lax.psum_scatter(
            grad_w_out.astype(jnp.bfloat16), "seq", scatter_dimension=0, tiled=True
        ).astype(jnp.float32),
        lax.psum_scatter(
            grad_w_up.astype(jnp.bfloat16), "seq", scatter_dimension=0, tiled=True
        ).astype(jnp.float32),
        lax.psum_scatter(
            grad_w_down.astype(jnp.bfloat16), "seq", scatter_dimension=0, tiled=True
        ).astype(jnp.float32),
    )
    matrices = (
        lax.psum_scatter(
            matrices[0].astype(jnp.bfloat16), "batch", scatter_dimension=1, tiled=True
        ).astype(jnp.float32),
        lax.psum_scatter(
            matrices[1].astype(jnp.bfloat16), "batch", scatter_dimension=1, tiled=True
        ).astype(jnp.float32),
        lax.psum_scatter(
            matrices[2].astype(jnp.bfloat16), "batch", scatter_dimension=1, tiled=True
        ).astype(jnp.float32),
        lax.psum_scatter(
            matrices[3].astype(jnp.bfloat16), "batch", scatter_dimension=1, tiled=True
        ).astype(jnp.float32),
    )
    vectors = lax.psum(
        (
            grad_pass,
            grad_ln1_gain,
            grad_ln1_bias,
            grad_ln2_gain,
            grad_ln2_bias,
            grad_b_up,
            grad_b_down,
        ),
        ("seq", "batch"),
    )
    return (
        output,
        grad_input,
        vectors[0],
        vectors[1],
        vectors[2],
        matrices[0],
        matrices[1],
        vectors[3],
        vectors[4],
        matrices[2],
        vectors[5],
        matrices[3],
        vectors[6],
    )


NN = (((1,), (0,)), ((), ()))
NT = (((1,), (1,)), ((), ()))
TN = (((0,), (0,)), ((), ()))
vmem_bytes = 60 << 20
block = 256


def dot(left, right, form):
    return lax.dot_general(left, right, form, preferred_element_type=jnp.float32)


def lane_loop(total, width, body):
    def step(i, carry):
        body(pl.ds(pl.multiple_of(i * width, width), width))
        return carry

    lax.fori_loop(0, total // width, step, 0)


def attend_kernel(
    info, b0, b1, b2, b3, emb, vecs, wqkv, ht, at, qt, kt, vt, ot, kept, inv, bias, prow, pcol
):
    width, total = ht.shape
    half = qt.shape[0]
    core = info[4]

    @pl.when(pl.program_id(0) == 0)
    def _():
        for k, ref in enumerate((b0, b1, b2, b3)):
            place = pl.ds(pl.multiple_of(info[k] * block, block), block)
            passes = ref[block : block + 16, 0:block].astype(jnp.float32)
            prow[:, place] = passes[0:8, :]
            pcol[place, :] = jnp.transpose(passes)[:, 0:8]
            kind = (lax.broadcasted_iota(jnp.int32, (16, block), 0) % 5).astype(jnp.float32)
            line = lax.broadcasted_iota(jnp.int32, (16, block), 0)
            onehot = jnp.where((kind == passes[0:1, :]) & (line < 15), 1.0, 0.0)
            added = dot(emb[...], onehot.astype(jnp.bfloat16), NN)
            ht[:, place] = jnp.transpose(ref[0:block, :]).astype(jnp.float32) + added

        def norm(cols):
            h = ht[:, cols]
            shifted = h - jnp.sum(h, 0, keepdims=True) * (1.0 / width)
            spread = jnp.sum(shifted * shifted, 0, keepdims=True) * (1.0 / width)
            scaled = shifted * lax.rsqrt(spread + 1e-05)
            at[:, cols] = (scaled * vecs[:, 0:1] + vecs[:, 1:2]).astype(jnp.bfloat16)

        lane_loop(total, 128, norm)
        for j, (ref, factor) in enumerate(((qt, 0.125), (kt, 1.0), (vt, 1.0))):
            cols = pl.ds(pl.multiple_of(j * width + core * half, 128), half)
            part = dot(wqkv[:, cols], at[...], TN).astype(jnp.bfloat16)
            ref[...] = part if factor == 1.0 else part * jnp.bfloat16(factor)
        length = info[5]
        for qb in range(total // block):
            n = (qb + 1) * block
            keys = lax.broadcasted_iota(jnp.int32, (n, block), 0)
            place = lax.broadcasted_iota(jnp.int32, (n, block), 1) + qb * block
            allowed = (pcol[0:n, 0:1] <= prow[0:1, qb * block : n]) & (keys < length)
            allowed = (allowed & (keys < place)) | (keys == place)
            at_row = qb * (qb + 1) // 2 * block
            bias[at_row : at_row + n, :] = jnp.where(allowed, 0.0, negative)

    head = pl.program_id(0)
    rows = pl.ds(pl.multiple_of(head * 64, 64), 64)
    keyn = jnp.transpose(kt[rows, :])
    for qb in range(total // block):
        n = (qb + 1) * block
        at_row = qb * (qb + 1) // 2 * block
        scores = dot(keyn[0:n, :], qt[rows, qb * block : n], NN) + bias[at_row : at_row + n, :]
        peak = jnp.max(scores, 0, keepdims=True)
        expo = jnp.exp(scores - peak)
        over = 1.0 / jnp.sum(expo, 0, keepdims=True)
        low = expo.astype(jnp.bfloat16)
        kept[0, at_row : at_row + n, :] = low
        inv[0, :, qb * block : n] = jnp.broadcast_to(over, (8, block))
        result = dot(vt[rows, 0:n], low, NN) * over
        ot[rows, qb * block : n] = result.astype(jnp.bfloat16)


mesh_ids = pl.DeviceIdType.MESH


def prepare_kernel(info, w_up, w_up_t):
    width, inner = w_up.shape
    bands = 8
    band = inner // bands
    for b in range(bands):
        turned = jnp.transpose(w_up[:, b * band : (b + 1) * band])
        w_up_t[b * band // 2 : (b + 1) * band // 2, :] = jnp.where(
            info[4] == 0, turned[: band // 2], turned[band // 2 :]
        )


def turn_kernel(info, c0, c1, c2, c3, ct):
    for k, ref in enumerate((c0, c1, c2, c3)):
        place = pl.ds(pl.multiple_of(info[k] * block, block), block)
        ct[:, place] = jnp.transpose(ref[...])


def back_kernel(
    ot_own, ot_recv, ht_in, at_in, qt_in, kt_in, vt_in, kept_in, ct_in,
    w_out_in, w_qkv_in, w_up_in, w_down_in,
    inv, prow, b_up, vecs,
    out, gin, vector, gqkv, gout, gup, gdown,
    mid, keep, at, qkv, otf, ct, mt, gd, far, dm, kept, w_out, w_up, w_down,
    bsum, r1a, r2a, r1c, r2c, rz, osend, orecv, hand, sums, gpass, vrecv, ksum, vsum,
    stage_send, stage_recv, down_recv,
    lsem, ssem, rsem,
    *, chunks, plan, rest_plan,
):
    seq, bat = lax.axis_index("seq"), lax.axis_index("batch")
    x, core = seq // 2, seq % 2
    z, y = bat // 2, bat % 2
    to_core, to_x, to_y = (seq + 1 - 2 * core, bat), (seq + 2 - 4 * x, bat), (seq, bat + 1 - 2 * y)
    to_z = [(seq, ((z + i) % 4) * 2 + y) for i in (1, 2, 3)]
    up_z, low_z = (seq, bat + 2), (seq, bat - 2)

    barrier = pltpu.get_barrier_semaphore()
    for peer in [to_core, to_x, to_y] + to_z:
        pl.semaphore_signal(barrier, inc=1, device_id=peer, device_id_type=mesh_ids)

    width, total = mid.shape
    half = width // 2
    inner = w_up.shape[0]
    blocks_n = total // block
    heads = kept_in.shape[0]

    def rows_at(first, count):
        return pl.ds(pl.multiple_of(first, 16), count)

    def local(i, src, dst):
        return pltpu.make_async_copy(src, dst, lsem.at[i])

    loads = {
        "o1": local(0, ot_own, otf.at[rows_at(core * half, half), :]),
        "o2": local(1, ot_recv, otf.at[rows_at((1 - core) * half, half), :]),
        "w_out": local(2, w_out_in, w_out),
        "h": local(3, ht_in, mid),
        "w_up": local(4, w_up_in, w_up),
        "ct": local(5, ct_in, ct),
        "at": local(7, at_in, at),
        "q": local(8, qt_in, qkv.at[0:half, :]),
        "k": local(9, kt_in, qkv.at[half : 2 * half, :]),
        "v": local(10, vt_in, qkv.at[2 * half : 3 * half, :]),
    }
    part = w_down_in.shape[2]
    for i in range(w_down_in.shape[0]):
        loads["w_down%d" % i] = local(
            18 + i, w_down_in.at[i, core], w_down.at[i * part : (i + 1) * part, :]
        )
    for load in loads.values():
        load.start()

    def kept_load(h, slot):
        return pltpu.make_async_copy(kept_in.at[h], kept.at[slot], lsem.at[11 + slot])

    kept_load(0, 0).start()
    kept_load(1, 1).start()

    def remote(i, src, dst, peer):
        return pltpu.make_async_remote_copy(
            src_ref=src, dst_ref=dst, send_sem=ssem.at[i], recv_sem=rsem.at[i],
            device_id=peer, device_id_type=mesh_ids,
        )

    def first(k):
        r0, ra, r1, a0, c0 = chunks[k]
        na, nc = ra - r0, r1 - ra
        return (
            remote(12 * k, bsum.at[1 - x, :, :, r0:ra, :], r1a.at[:, :, a0 : a0 + na, :], to_x),
            remote(
                12 * k + 1, bsum.at[:, :, 1 - y, ra:r1, :], r1c.at[:, :, c0 : c0 + nc, :], to_y
            ),
        )

    def second(k):
        r0, ra, r1, a0, c0 = chunks[k]
        na, nc = ra - r0, r1 - ra
        return (
            remote(12 * k + 2, bsum.at[x, :, 1 - y, r0:ra, :], r2a.at[:, a0 : a0 + na, :], to_y),
            remote(12 * k + 3, bsum.at[1 - x, :, y, ra:r1, :], r2c.at[:, c0 : c0 + nc, :], to_x),
        )

    def up_copy(k, d):
        r0, _, r1, _, _ = chunks[k]
        return remote(12 * k + 4 + d, bsum.at[x, d, y, r0:r1, :], rz.at[d, r0:r1, :], up_z)

    def low_copy(k, d):
        r0, _, r1, _, _ = chunks[k]
        slot = jnp.where(z - 1 == d, 4, d)
        return remote(12 * k + 8 + d, bsum.at[x, d, y, r0:r1, :], rz.at[slot, r0:r1, :], low_z)

    def add_z(k, d, slot):
        r0, _, r1, _, _ = chunks[k]
        bsum[x, d, y, r0:r1, :] = bsum[x, d, y, r0:r1, :] + rz[slot, r0:r1, :]

    def step_start(k):
        for copy in first(k):
            copy.start()

    def step_second(k):
        r0, ra, r1, a0, c0 = chunks[k]
        na, nc = ra - r0, r1 - ra
        one, two = first(k)
        three, four = second(k)
        one.wait()
        bsum[x, :, :, r0:ra, :] = bsum[x, :, :, r0:ra, :] + r1a[:, :, a0 : a0 + na, :]
        three.start()
        two.wait()
        bsum[:, :, y, ra:r1, :] = bsum[:, :, y, ra:r1, :] + r1c[:, :, c0 : c0 + nc, :]
        four.start()

    def step_line(k):
        r0, ra, r1, a0, c0 = chunks[k]
        na, nc = ra - r0, r1 - ra
        three, four = second(k)
        three.wait()
        bsum[x, :, y, r0:ra, :] = bsum[x, :, y, r0:ra, :] + r2a[:, a0 : a0 + na, :]
        four.wait()
        bsum[x, :, y, ra:r1, :] = bsum[x, :, y, ra:r1, :] + r2c[:, c0 : c0 + nc, :]

        @pl.when(z == 0)
        def _():
            for d in (3, 2, 1):
                up_copy(k, d).start()

        @pl.when(z == 3)
        def _():
            for d in (0, 1, 2):
                low_copy(k, d).start()

    def pass_up(k, d):
        up_copy(k, d).wait_recv()
        add_z(k, d, d)
        up_copy(k, d).start()

    def pass_low(k, d):
        low_copy(k, d).wait_recv()
        add_z(k, d, d)
        low_copy(k, d).start()

    def step_pass(k):
        @pl.when(z == 1)
        def _():
            pass_up(k, 3)

        @pl.when(z == 2)
        def _():
            pass_low(k, 0)

    def step_pass_more(k):
        @pl.when(z == 1)
        def _():
            pass_up(k, 2)
            pass_low(k, 0)

        @pl.when(z == 2)
        def _():
            pass_low(k, 1)
            pass_up(k, 3)

    def step_last(k):
        for d in range(4):

            @pl.when(z == d)
            def _():
                if d > 0:
                    up_copy(k, d).wait_recv()
                    add_z(k, d, d)
                if d < 3:
                    low_copy(k, d).wait_recv()
                    add_z(k, d, 4)
                for e in range(4):
                    if e > d:
                        up_copy(k, e).wait_send()
                    if e < d:
                        low_copy(k, e).wait_send()

    steps = (step_start, step_second, step_line, step_pass, step_pass_more, step_last)

    loads["o1"].wait()
    loads["o2"].wait()
    loads["w_out"].wait()
    loads["h"].wait()

    def mix(i, carry):
        cols = pl.ds(pl.multiple_of(i * block, block), block)
        m = mid[:, cols] + dot(w_out[...], otf[:, cols], TN)
        mid[:, cols] = m
        shifted = m - jnp.sum(m, 0, keepdims=True) * (1.0 / width)
        spread = jnp.sum(shifted * shifted, 0, keepdims=True) * (1.0 / width)
        scaled = shifted * lax.rsqrt(spread + 1e-05)
        mt[:, cols] = (scaled * vecs[:, 2:3] + vecs[:, 3:4]).astype(jnp.bfloat16)
        return carry

    lax.fori_loop(0, blocks_n, mix, 0)
    loads["w_up"].wait()
    loads["ct"].wait()
    for i in range(w_down_in.shape[0]):
        loads["w_down%d" % i].wait()

    def hidden(i, carry):
        rows = pl.ds(pl.multiple_of(i * part, part), part)
        below = pl.ds(pl.multiple_of(inner + i * part, part), part)
        u = dot(w_up[rows, :], mt[...], NN) + b_up[rows, 0:1]
        back = dot(w_down[rows, :], ct[...], NN)
        square = u * u
        t = jnp.tanh(u * (0.7978845608028654 + 0.035677408136300125 * square))
        gate = 0.5 + 0.5 * t
        gd[rows, :] = (u * gate).astype(jnp.bfloat16)
        slope = gate + (0.5 * u) * (1.0 - t * t) * (
            0.7978845608028654 + 0.10703222440890037 * square
        )
        gd[below, :] = (back * slope).astype(jnp.bfloat16)
        return carry

    lax.fori_loop(0, inner // part, hidden, 0)
    lanes = bsum.shape[-1]
    bs = 8
    band = width // bs
    for xx in range(2):
        for j in range(2):
            at_row = (2 * xx + j) * lanes
            grad = dot(ct[...], gd[at_row : at_row + lanes, :], NT).astype(jnp.bfloat16)
            for b in range(bs):
                bsum[xx, b // 2, b % 2, j * band : (j + 1) * band, :] = grad[
                    b * band : (b + 1) * band, :
                ]
    pl.semaphore_wait(barrier, 6)
    steps[0](0)

    base = 12 * len(chunks)
    dm_copy = remote(base, dm.at[0:width, :], dm.at[width : 2 * width, :], to_core)

    def back_up(i, carry):
        cols = pl.ds(pl.multiple_of(i * block, block), block)
        dm[0:width, cols] = dot(w_up[...], gd[inner : 2 * inner, cols], TN).astype(jnp.bfloat16)
        return carry

    lax.fori_loop(0, blocks_n, back_up, 0)
    dm_copy.start()
    first_up = 2 * band
    up_band = part
    for xx in range(2):
        for i in range(2):
            low, high = inner + i * inner // 2, inner + (i + 1) * inner // 2
            grad = dot(gd[low:high, :], mt[xx * lanes : (xx + 1) * lanes, :], NT)
            grad = grad.astype(jnp.bfloat16)
            for b in range(bs // 2):
                bb = i * bs // 2 + b
                bsum[xx, bb // 2, bb % 2, first_up : first_up + up_band, :] = grad[
                    b * up_band : (b + 1) * up_band, :
                ]
    ones = jnp.ones((8, total), jnp.bfloat16)
    up_sum = dot(ones, gd[inner : 2 * inner, :], NT)
    vector[...] = jnp.zeros_like(vector)
    for c in range(2):
        for i in range(2):
            line = up_sum[0:1, i * width : (i + 1) * width]
            vector[10 + 2 * c + i : 11 + 2 * c + i, :] = jnp.where(core == c, line, 0.0)
    out_copy = remote(base + 1, osend, orecv, to_core)
    for k in range(2):
        mine = pl.ds(pl.multiple_of(core * block + k * 2 * block, block), block)
        other = pl.ds(pl.multiple_of((1 - core) * block + k * 2 * block, block), block)
        to = slice(k * block, (k + 1) * block)
        osend[:, to] = dot(w_down[...], gd[0:inner, other], TN).astype(jnp.bfloat16)
        keep[:, to] = mid[:, mine] + vecs[:, 4:5] + dot(w_down[...], gd[0:inner, mine], TN)
    out_copy.start()

    dm_copy.wait()
    sums[...] = jnp.zeros_like(sums)

    def middle(i, carry):
        cols = pl.ds(pl.multiple_of(i * block, block), block)
        cot = ct[:, cols].astype(jnp.float32)
        m = mid[:, cols]
        shifted = m - jnp.sum(m, 0, keepdims=True) * (1.0 / width)
        spread = jnp.sum(shifted * shifted, 0, keepdims=True) * (1.0 / width)
        r = lax.rsqrt(spread + 1e-05)
        n = shifted * r
        d = dm[0:width, cols].astype(jnp.float32) + dm[width : 2 * width, cols].astype(jnp.float32)
        e = d * vecs[:, 2:3]
        mean_e = jnp.sum(e, 0, keepdims=True) * (1.0 / width)
        mean_en = jnp.sum(e * n, 0, keepdims=True) * (1.0 / width)
        dmid = cot + r * (e - mean_e - n * mean_en)
        mid[:, cols] = dmid
        dm[width : 2 * width, cols] = dmid.astype(jnp.bfloat16)
        sums[:, 0:1] += jnp.sum(d * n, 1, keepdims=True)
        sums[:, 1:2] += jnp.sum(d, 1, keepdims=True)
        sums[:, 2:3] += jnp.sum(cot, 1, keepdims=True)
        return carry

    lax.fori_loop(0, blocks_n, middle, 0)
    small = band // 2
    for b in range(bs):
        dm[half + b * small : half + (b + 1) * small, :] = dm[
            rows_at(width + b * band + core * small, small), :
        ]
    first_out = first_up + up_band
    for xx in range(2):
        grad = dot(dm[half:width, :], otf[xx * lanes : (xx + 1) * lanes, :], NT)
        grad = grad.astype(jnp.bfloat16)
        for b in range(bs):
            bsum[xx, b // 2, b % 2, first_out : first_out + small, :] = grad[
                b * small : (b + 1) * small, :
            ]
    steps[0](1)
    dm[0:half, :] = dot(
        w_out[rows_at(core * half, half), :], dm[width : 2 * width, :], NN
    ).astype(jnp.bfloat16)

    whole_loads = [
        local(13, w_qkv_in.at[:, 0:width], w_up.at[0:width, :]),
        local(14, w_qkv_in.at[:, width : 2 * width], w_up.at[width : 2 * width, :]),
        local(15, w_qkv_in.at[:, 2 * width : 3 * width], w_down.at[0:width, :]),
    ]
    for load in whole_loads:
        load.start()

    out_copy.wait()
    hand_out = remote(base + 2, hand.at[0], out.at[x], to_x)
    for k in range(2):
        cols = slice(k * block, (k + 1) * block)
        rows = jnp.transpose(
            (keep[:, cols] + orecv[:, cols].astype(jnp.float32)).astype(jnp.bfloat16)
        )

        @pl.when(x == k)
        def _():
            out[k] = rows

        @pl.when(x != k)
        def _():
            hand[0] = rows

    hand_out.start()
    own_loads = [
        local(16 + k, ht_in.at[:, pl.ds(pl.multiple_of(core * block + k * 2 * block, block), block)],
              keep.at[:, k * block : (k + 1) * block])
        for k in range(2)
    ]
    for load in own_loads:
        load.start()

    for name in ("at", "q", "k", "v"):
        loads[name].wait()

    def far_copy(h, j):
        mine = rows_at(j * width + core * half + h * 64, 64)
        return remote(
            base + 3 + h * 3 + j, gd.at[mine, :], far.at[rows_at(j * half + h * 64, 64), :], to_core
        )

    def one_head(h, carry):
        slot = h % 2
        kept_load(h, slot).wait()
        qrow, krow, vrow = (rows_at(j * half + h * 64, 64) for j in range(3))
        mine = [rows_at(j * width + core * half + h * 64, 64) for j in range(3)]
        valn = jnp.transpose(qkv[vrow, :])
        grads = (dm[rows_at(h * 64, 64), :].astype(jnp.float32) * inv[h, 0:1, :]).astype(
            jnp.bfloat16
        )
        o_rows = otf[rows_at(core * half + h * 64, 64), :]
        delta = jnp.sum(grads.astype(jnp.float32) * o_rows.astype(jnp.float32), 0, keepdims=True)
        ksum[...] = jnp.zeros_like(ksum)
        vsum[...] = jnp.zeros_like(vsum)
        for qb in range(blocks_n):
            n = (qb + 1) * block
            at_row = qb * (qb + 1) // 2 * block
            cols = slice(qb * block, n)
            low = kept[slot, at_row : at_row + n, :]
            dprob = dot(valn[0:n, :], grads[:, cols], NN)
            dscore = (low.astype(jnp.float32) * (dprob - delta[:, cols])).astype(jnp.bfloat16)
            gd[mine[0], cols] = (dot(qkv[krow, 0:n], dscore, NN) * 0.125).astype(jnp.bfloat16)
            ksum[:, 0:n] += dot(qkv[qrow, cols], dscore, NT)
            vsum[:, 0:n] += dot(grads[:, cols], low, NT)
        gd[mine[1], :] = ksum[...].astype(jnp.bfloat16)
        gd[mine[2], :] = vsum[...].astype(jnp.bfloat16)
        for j in range(3):
            far_copy(h, j).start()

        @pl.when(h + 2 < heads)
        def _():
            kept_load(h + 2, slot).start()

        for at_head, which, k in plan:

            @pl.when(h == at_head)
            def _():
                steps[which](k)

        return carry

    lax.fori_loop(0, heads, one_head, 0)

    for h in range(heads):
        for j in range(3):
            far_copy(h, j).wait()
    for j in range(3):
        gd[rows_at(j * width + (1 - core) * half, half), :] = far[j * half : (j + 1) * half, :]
    qkv_band = 3 * width // bs
    qkv_small = qkv_band // 2
    for b in range(bs):
        dm[b * qkv_small : (b + 1) * qkv_small, :] = gd[
            rows_at(b * qkv_band + core * qkv_small, qkv_small), :
        ]
    first_qkv = first_out + small
    for xx in range(2):
        grad = dot(dm[0 : bs * qkv_small, :], at[xx * lanes : (xx + 1) * lanes, :], NT)
        grad = grad.astype(jnp.bfloat16)
        for b in range(bs):
            bsum[xx, b // 2, b % 2, first_qkv : first_qkv + qkv_small, :] = grad[
                b * qkv_small : (b + 1) * qkv_small, :
            ]
    steps[0](2)

    for load in whole_loads + own_loads:
        load.wait()
    gpass[...] = jnp.zeros_like(gpass)
    hand_in = remote(base + 21, hand.at[1], gin.at[x], to_x)
    for k in range(2):
        mine = pl.ds(pl.multiple_of(core * block + k * 2 * block, block), block)
        da = dot(w_up[0:width, :], gd[0:width, mine], NN)
        da += dot(w_up[width : 2 * width, :], gd[width : 2 * width, mine], NN)
        da += dot(w_down[0:width, :], gd[2 * width : 3 * width, mine], NN)
        h = keep[:, k * block : (k + 1) * block]
        shifted = h - jnp.sum(h, 0, keepdims=True) * (1.0 / width)
        spread = jnp.sum(shifted * shifted, 0, keepdims=True) * (1.0 / width)
        r = lax.rsqrt(spread + 1e-05)
        n = shifted * r
        e = da * vecs[:, 0:1]
        mean_e = jnp.sum(e, 0, keepdims=True) * (1.0 / width)
        mean_en = jnp.sum(e * n, 0, keepdims=True) * (1.0 / width)
        dh = mid[:, mine] + r * (e - mean_e - n * mean_en)
        rows = jnp.transpose(dh).astype(jnp.bfloat16)

        @pl.when(x == k)
        def _():
            gin[k] = rows

        @pl.when(x != k)
        def _():
            hand[1] = rows
            hand_in.start()

        sums[:, 3:4] += jnp.sum(da * n, 1, keepdims=True)
        sums[:, 4:5] += jnp.sum(da, 1, keepdims=True)
        kind = lax.broadcasted_iota(jnp.int32, (16, block), 0).astype(jnp.float32)
        onehot = jnp.where(kind == prow[0:1, mine], 1.0, 0.0).astype(jnp.bfloat16)
        high = dh.astype(jnp.bfloat16)
        rest = dh - high.astype(jnp.float32)
        second_part = rest.astype(jnp.bfloat16)
        tail = (rest - second_part.astype(jnp.float32)).astype(jnp.bfloat16)
        gpass[...] += dot(onehot, high, NT) + dot(onehot, second_part, NT) + dot(onehot, tail, NT)

    lines = jnp.transpose(sums[...])
    vector[0:5, :] = gpass[0:5, :]
    vector[5:7, :] = lines[3:5, :]
    vector[7:10, :] = lines[0:3, :] * 0.5
    for i, peer in enumerate((to_core, to_x, to_y)):
        copy = remote(base + 22 + i, vector, vrecv.at[i], peer)
        copy.start()
        copy.wait()
        vector[...] = vector[...] + vrecv[i]
        for which, k in rest_plan[i]:
            steps[which](k)
    copies = [
        remote(base + 25 + i, vector, vrecv.at[3 + z], peer) for i, peer in enumerate(to_z)
    ]
    for copy in copies:
        copy.start()
    vrecv[3 + z] = vector[...]

    own_rows = down_recv.shape[0]
    down_copy = remote(
        base + 28, bsum.at[x, z, y, rows_at((1 - core) * own_rows, own_rows), :], down_recv, to_core
    )

    def swap_lanes(i, r0, r1):
        wide = lanes // 2
        v = bsum[x, z, y, r0:r1, :]
        stage_send[r0 - first_up : r1 - first_up, 0:wide] = jnp.where(
            core == 0, v[:, wide:lanes], v[:, 0:wide]
        )
        at_rows = slice(r0 - first_up, r1 - first_up)
        return remote(base + i, stage_send.at[at_rows, :], stage_recv.at[at_rows, :], to_core)

    def both_cores(mine, got):
        return jnp.where(core == 0, mine, got), jnp.where(core == 0, got, mine)

    def put(result, r0, r1):
        wide = lanes // 2
        v = bsum[x, z, y, r0:r1, :].astype(jnp.float32)
        mine = jnp.where(core == 0, v[:, 0:wide], v[:, wide:lanes])
        got = stage_recv[r0 - first_up : r1 - first_up, 0:wide].astype(jnp.float32)
        result[...] = jnp.transpose(jnp.concatenate(both_cores(mine, got), 0))

    swaps = []
    for which, k in rest_plan[3]:
        steps[which](k)
        if which == 5:
            if k == 0:
                swaps.append(down_copy)
            else:
                swaps.append(swap_lanes(28 + k, chunks[k][0], chunks[k][2]))
            swaps[-1].start()
    swaps[0].wait()
    mine = bsum[x, z, y, rows_at(core * own_rows, own_rows), :].astype(jnp.float32)
    for c, piece in enumerate(both_cores(mine, down_recv[...].astype(jnp.float32))):
        turned = jnp.transpose(piece)
        for i in range(lanes // part):
            at_row = (2 * i + c) * part
            gdown[at_row : at_row + part, :] = turned[i * part : (i + 1) * part, :]
    swaps[1].wait()
    put(gup, first_up, first_out)
    put(gout, first_out, first_qkv)
    for copy in copies:
        copy.wait()
    vector[...] = (vrecv[3] + vrecv[4]) + (vrecv[5] + vrecv[6])
    hand_out.wait()
    hand_in.wait()
    swaps[2].wait()
    put(gqkv, first_qkv, first_qkv + qkv_small)


def call(kernel, outs, scratch=(), smem=True, n_in=0, name=None, flops=0, **kw):
    in_specs = [pl.BlockSpec(memory_space=pltpu.VMEM)] * n_in
    if smem:
        in_specs[0] = pl.BlockSpec(memory_space=pltpu.SMEM)
    return pl.pallas_call(
        kernel,
        out_shape=outs,
        in_specs=in_specs,
        out_specs=[pl.BlockSpec(memory_space=pltpu.VMEM)] * len(outs),
        scratch_shapes=list(scratch),
        compiler_params=pltpu.CompilerParams(vmem_limit_bytes=vmem_bytes),
        cost_estimate=pl.CostEstimate(flops=int(flops), bytes_accessed=0, transcendentals=0),
        name=name,
        **kw,
    )


def shaped(*dims, kind=jnp.bfloat16):
    return jax.ShapeDtypeStruct(dims, kind)


def pick(array, axis, index):
    return lax.dynamic_index_in_dim(array, index, axis, keepdims=False)


def swap(array, axis, size, distance):
    return lax.ppermute(array, axis, [(i, i ^ distance) for i in range(size)])


def regrouped(
    block_input, lengths, pass_ids, pass_embed, ln1_gain, ln1_bias, w_qkv, w_out,
    ln2_gain, ln2_bias, w_up, b_up, w_down, b_down, cotangent, batch_n, y_n
):
    row_count, seg_len, width = block_input.shape
    total = 4 * seg_len
    inner = w_up.shape[1]
    own_in = inner // 2
    heads_own = H // 2
    half = width // 2
    z_n = batch_n // y_n
    s = lax.axis_index("seq")
    x, core = s // 2, s % 2
    bat = lax.axis_index("batch")
    z, y = bat // y_n, bat % y_n

    def by_x(array):
        return swap(array, "seq", 4, 2)

    def by_core(array):
        return swap(array, "seq", 4, 1)

    def by_y(array):
        return swap(array, "batch", batch_n, 1)

    pass_rows = jnp.zeros((row_count, 16, width), jnp.bfloat16)
    pass_rows = lax.dynamic_update_slice(
        pass_rows,
        jnp.broadcast_to(pass_ids.astype(jnp.bfloat16)[:, None, :], (row_count, 16, seg_len)),
        (0, 0, 0),
    )
    packed = jnp.concatenate([block_input, pass_rows], 1)
    x_own = pick(packed, 0, x)
    x_far = by_x(pick(packed, 0, 1 - x))
    x_near = by_core(x_own)
    x_cross = by_core(x_far)
    c_own = pick(cotangent, 0, x)
    c_far = by_x(pick(cotangent, 0, 1 - x))
    c_near = by_core(c_own)
    c_cross = by_core(c_far)
    length = pick(lengths, 0, x)
    info = jnp.stack(
        [2 * x + core, 2 * (1 - x) + core, 2 * x + 1 - core, 2 * (1 - x) + 1 - core, core, length]
    ).astype(jnp.int32)

    embed_t = jnp.transpose(pass_embed)
    first = embed_t.astype(jnp.bfloat16)
    rest = embed_t - first.astype(jnp.float32)
    second = rest.astype(jnp.bfloat16)
    third = (rest - second.astype(jnp.float32)).astype(jnp.bfloat16)
    emb = jnp.concatenate([first, second, third, jnp.zeros((width, 1), jnp.bfloat16)], 1)
    zero = jnp.zeros_like(ln1_gain)
    vecs = jnp.stack([ln1_gain, ln1_bias, ln2_gain, ln2_bias, b_down, zero, zero, zero], 1)
    band = inner // batch_n // 2
    (w_up_t,) = call(
        prepare_kernel, [shaped(own_in, width)], n_in=2, name="prepare", flops=2e9
    )(info, w_up)
    w_down_parts = w_down.reshape(batch_n, 2, band, width)
    b_up_own = pick(b_up.reshape(batch_n, 2, band), 1, core).reshape(own_in, 1)
    b_up_own = jnp.broadcast_to(b_up_own, (own_in, 8))

    blocks_n = total // block
    kept_rows = blocks_n * (blocks_n + 1) // 2 * block
    whole = pl.BlockSpec(memory_space=pltpu.VMEM)

    def fixed(*dims):
        return pl.BlockSpec(dims, lambda i: (0,) * len(dims))

    ht, at, qt, kt, vt, ot, kept, inv, prow = pl.pallas_call(
        lambda *refs: attend_kernel(*refs[:8], *refs[8:16], refs[17], refs[16], refs[18]),
        out_shape=[
            shaped(width, total, kind=jnp.float32),
            shaped(width, total),
            shaped(half, total),
            shaped(half, total),
            shaped(half, total),
            shaped(half, total),
            shaped(heads_own, kept_rows, block),
            shaped(heads_own, 8, total, kind=jnp.float32),
            shaped(8, total, kind=jnp.float32),
        ],
        grid=(heads_own,),
        in_specs=[pl.BlockSpec(memory_space=pltpu.SMEM)]
        + [fixed(seg_len + 16, width)] * 4
        + [fixed(width, 16), fixed(width, 8), fixed(width, 3 * width)],
        out_specs=[
            fixed(width, total),
            fixed(width, total),
            fixed(half, total),
            fixed(half, total),
            fixed(half, total),
            fixed(half, total),
            pl.BlockSpec((1, kept_rows, block), lambda i: (i, 0, 0)),
            pl.BlockSpec((1, 8, total), lambda i: (i, 0, 0)),
            fixed(8, total),
        ],
        scratch_shapes=[
            pltpu.VMEM((kept_rows, block), jnp.float32),
            pltpu.VMEM((total, 8), jnp.float32),
        ],
        compiler_params=pltpu.CompilerParams(vmem_limit_bytes=vmem_bytes),
        cost_estimate=pl.CostEstimate(flops=int(12e9), bytes_accessed=0, transcendentals=0),
        name="attend",
    )(info, x_own, x_far, x_near, x_cross, emb, vecs, w_qkv)

    ot_recv = by_core(ot)
    (ct,) = call(turn_kernel, [shaped(width, total)], n_in=5, name="turn", flops=1e9)(
        info, c_own, c_far, c_near, c_cross
    )
    lanes = width // 2
    down_n, up_n, out_n, qkv_n = 2 * width // batch_n, band, width // batch_n // 2, 3 * width // batch_n // 2
    chunks, a0, c0, r0 = [], 0, 0, 0
    for count in (down_n, up_n + out_n, qkv_n):
        na = max(count // 3 // 16 * 16, 16)
        chunks.append((r0, r0 + na, r0 + count, a0, c0))
        r0, a0, c0 = r0 + count, a0 + na, c0 + count - na
    plan = ((0, 1, 0), (4, 2, 0), (5, 3, 0))
    rest_plan = (
        ((4, 0), (1, 1)),
        (),
        (),
        ((5, 0), (2, 1), (3, 1), (1, 2), (4, 1), (2, 2), (5, 1), (3, 2), (4, 2), (5, 2)),
    )
    anywhere = pl.BlockSpec(memory_space=pl.ANY)
    whole = pl.BlockSpec(memory_space=pltpu.VMEM)
    low, full = jnp.bfloat16, jnp.float32
    copies_n = 12 * len(chunks) + 31
    output, grad_input, vector, grad_qkv, grad_out, grad_up, grad_down = pl.pallas_call(
        functools.partial(back_kernel, chunks=tuple(chunks), plan=plan, rest_plan=rest_plan),
        out_shape=[
            shaped(2, block, width),
            shaped(2, block, width),
            shaped(16, width, kind=full),
            shaped(width // 4, 3 * width // batch_n, kind=full),
            shaped(width // 4, width // batch_n, kind=full),
            shaped(width // 4, inner // batch_n, kind=full),
            shaped(inner // 4, width // batch_n, kind=full),
        ],
        in_specs=[anywhere] * 13 + [whole] * 4,
        out_specs=[whole] * 7,
        scratch_shapes=[
            pltpu.VMEM((width, total), full),
            pltpu.VMEM((width, 2 * block), full),
            pltpu.VMEM((width, total), low),
            pltpu.VMEM((3 * half, total), low),
            pltpu.VMEM((width, total), low),
            pltpu.VMEM((width, total), low),
            pltpu.VMEM((width, total), low),
            pltpu.VMEM((2 * own_in, total), low),
            pltpu.VMEM((3 * half, total), low),
            pltpu.VMEM((2 * width, total), low),
            pltpu.VMEM((2, kept_rows, block), low),
            pltpu.VMEM((width, width), low),
            pltpu.VMEM((own_in, width), low),
            pltpu.VMEM((own_in, width), low),
            pltpu.VMEM((2, z_n, 2, r0, lanes), low),
            pltpu.VMEM((z_n, 2, a0, lanes), low),
            pltpu.VMEM((z_n, a0, lanes), low),
            pltpu.VMEM((2, z_n, c0, lanes), low),
            pltpu.VMEM((z_n, c0, lanes), low),
            pltpu.VMEM((z_n + 1, r0, lanes), low),
            pltpu.VMEM((width, 2 * block), low),
            pltpu.VMEM((width, 2 * block), low),
            pltpu.VMEM((2, block, width), low),
            pltpu.VMEM((width, 128), full),
            pltpu.VMEM((16, width), full),
            pltpu.VMEM((7, 16, width), full),
            pltpu.VMEM((64, total), full),
            pltpu.VMEM((64, total), full),
            pltpu.VMEM((r0 - down_n, 256), low),
            pltpu.VMEM((r0 - down_n, 256), low),
            pltpu.VMEM((down_n // 2, lanes), low),
            pltpu.SemaphoreType.DMA((26,)),
            pltpu.SemaphoreType.DMA((copies_n,)),
            pltpu.SemaphoreType.DMA((copies_n,)),
        ],
        compiler_params=pltpu.CompilerParams(
            vmem_limit_bytes=62 << 20, collective_id=0, has_side_effects=True
        ),
        cost_estimate=pl.CostEstimate(flops=int(60e9), bytes_accessed=0, transcendentals=0),
        name="back",
    )(
        ot, ot_recv, ht, at, qt, kt, vt, kept, ct, w_out, w_qkv, w_up_t, w_down_parts,
        inv, prow, b_up_own, vecs,
    )
    grad_b_up = jnp.transpose(vector[10:14].reshape(2, batch_n, band), (1, 0, 2)).reshape(inner)
    return (
        output,
        grad_input,
        vector[0:5],
        vector[5],
        vector[6],
        grad_qkv,
        grad_out,
        vector[7],
        vector[8],
        grad_up,
        grad_b_up,
        grad_down,
        vector[9],
    )


def solution(mesh):
    batch_n = mesh.shape["batch"]
    few = mesh.shape["seq"] == 4 and batch_n == 8
    plan = functools.partial(regrouped, batch_n=batch_n, y_n=2) if few else local
    return jax.shard_map(
        plan,
        mesh=mesh,
        in_specs=(
            P("batch", "seq", None),
            P("batch"),
            P("batch", "seq"),
            P(),
            P(),
            P(),
            P(),
            P(),
            P(),
            P(),
            P(),
            P(),
            P(),
            P(),
            P("batch", "seq", None),
        ),
        out_specs=(
            P("batch", "seq", None),
            P("batch", "seq", None),
            P(),
            P(),
            P(),
            P("seq", "batch"),
            P("seq", "batch"),
            P(),
            P(),
            P("seq", "batch"),
            P(),
            P("seq", "batch"),
            P(),
        ),
        check_vma=False,
    )
```

```python
import functools

import jax
import jax.numpy as jnp
from jax import lax
from jax.experimental import pallas as pl
from jax.experimental.pallas import tpu as pltpu
from jax.sharding import PartitionSpec as P

H = 12


negative = -1e30
key_block = 1024
query_block = 512
highest = lax.Precision.HIGHEST


def layer_norm(hidden, gain, offset):
    centre = jnp.mean(hidden, -1, keepdims=True)
    shifted = hidden - centre
    spread = jnp.mean(shifted * shifted, -1, keepdims=True)
    return shifted * lax.rsqrt(spread + 1e-05) * gain + offset


def gelu_tanh(values):
    return jax.nn.gelu(values, approximate=True)


def visible(query_place, query_pass, key_place, key_pass, length):
    earlier = key_place[None, :] < query_place[:, None]
    allowed = earlier & (key_pass[None, :] <= query_pass[:, None]) & (key_place[None, :] < length)
    return allowed | (key_place[None, :] == query_place[:, None])


def masked_scores(query_part, key_part, factor, seen):
    raw = (
        jnp.einsum("qhd,khd->hqk", query_part, key_part, preferred_element_type=jnp.float32)
        * factor
    )
    return jnp.where(seen[None], raw, negative)


def split_blocks(arrays, block_len):
    return tuple(
        (
            array.reshape((array.shape[0] // block_len, block_len) + array.shape[1:])
            for array in arrays
        )
    )


def chance_of(query_part, key_part, log_part, seen, factor):
    scores = masked_scores(query_part, key_part, factor, seen)
    return jnp.where(seen[None], jnp.exp(scores - log_part[..., None]), 0.0)


def grad_pieces(query_part, dout_part, log_part, delta_part, key_part, value_part, seen, factor):
    chance = chance_of(query_part, key_part, log_part, seen, factor)
    dprob = jnp.einsum("qhd,khd->hqk", dout_part, value_part, preferred_element_type=jnp.float32)
    dscore = (chance * (dprob - delta_part[..., None])).astype(jnp.bfloat16)
    return (dscore, chance.astype(jnp.bfloat16))


def attend_row(queries, query_place, query_pass, key_rows, value_rows, key_pass, length):
    factor = queries.shape[-1] ** (-0.5)
    places = jnp.arange(key_rows.shape[0], dtype=jnp.int32)
    key_parts = split_blocks(
        (key_rows, value_rows, key_pass, places), min(key_block, key_rows.shape[0])
    )
    query_len = min(query_block, queries.shape[0])
    query_parts = split_blocks((queries, query_place, query_pass), query_len)

    def attend_one_block(query_args):
        query_part, place_part, pass_part = query_args

        def running(carry, key_args):
            peak, summed, total_out = carry
            key_part, value_part, kpass_part, kplace_part = key_args
            seen = visible(place_part, pass_part, kplace_part, kpass_part, length)
            scores = masked_scores(query_part, key_part, factor, seen)
            new_peak = jnp.maximum(peak, jnp.max(scores, -1))
            terms = jnp.where(seen[None], jnp.exp(scores - new_peak[..., None]), 0.0)
            rescale = jnp.exp(peak - new_peak)
            summed = summed * rescale + jnp.sum(terms, -1)
            added = jnp.einsum(
                "hqk,khd->qhd",
                terms.astype(jnp.bfloat16),
                value_part,
                preferred_element_type=jnp.float32,
            )
            total_out = total_out * rescale.T[..., None] + added
            return ((new_peak, summed, total_out), None)

        heads_n = query_part.shape[1]
        start = (
            jnp.full((heads_n, query_len), negative, jnp.float32),
            jnp.zeros((heads_n, query_len), jnp.float32),
            jnp.zeros(query_part.shape, jnp.float32),
        )
        (peak, summed, total_out), _ = lax.scan(running, start, key_parts)
        log_total = peak + jnp.log(summed)
        result = total_out / summed.T[..., None]
        return (result, log_total)

    results, log_totals = lax.map(attend_one_block, query_parts)
    heads_n = queries.shape[1]
    return (
        results.reshape(queries.shape),
        jnp.moveaxis(log_totals, 1, 0).reshape(heads_n, queries.shape[0]),
    )


def backward_row(
    queries,
    douts,
    outs_kept,
    log_totals,
    query_place,
    query_pass,
    key_rows,
    value_rows,
    key_pass,
    length,
):
    factor = queries.shape[-1] ** (-0.5)
    places = jnp.arange(key_rows.shape[0], dtype=jnp.int32)
    key_parts = split_blocks(
        (key_rows, value_rows, key_pass, places), min(key_block, key_rows.shape[0])
    )
    query_len = min(query_block, queries.shape[0])
    heads_n = queries.shape[1]
    block_count = queries.shape[0] // query_len
    log_parts = jnp.moveaxis(log_totals.reshape(heads_n, block_count, query_len), 1, 0)
    query_parts = split_blocks((queries, douts, outs_kept, query_place, query_pass), query_len)

    def backward_one_block(carry, query_args):
        query_part, dout_part, kept_part, place_part, pass_part, log_part = query_args
        delta_part = jnp.einsum("qhd,qhd->hq", dout_part.astype(jnp.float32), kept_part)

        def add_grads(dquery, key_args):
            key_part, value_part, kpass_part, kplace_part = key_args
            seen = visible(place_part, pass_part, kplace_part, kpass_part, length)
            dscore, low_chance = grad_pieces(
                query_part, dout_part, log_part, delta_part, key_part, value_part, seen, factor
            )
            dquery = dquery + factor * jnp.einsum(
                "hqk,khd->qhd", dscore, key_part, preferred_element_type=jnp.float32
            )
            dkey = factor * jnp.einsum(
                "hqk,qhd->khd", dscore, query_part, preferred_element_type=jnp.float32
            )
            dvalue = jnp.einsum(
                "hqk,qhd->khd", low_chance, dout_part, preferred_element_type=jnp.float32
            )
            return (dquery, (dkey, dvalue))

        dquery, key_terms = lax.scan(add_grads, jnp.zeros(query_part.shape, jnp.float32), key_parts)
        carry = (
            carry[0] + key_terms[0].reshape(key_rows.shape),
            carry[1] + key_terms[1].reshape(value_rows.shape),
        )
        return (carry, (dquery, delta_part))

    start = (jnp.zeros(key_rows.shape, jnp.float32), jnp.zeros(value_rows.shape, jnp.float32))
    key_sums, (dqueries, deltas) = lax.scan(backward_one_block, start, query_parts + (log_parts,))
    return (
        dqueries.reshape(queries.shape),
        jnp.moveaxis(deltas, 1, 0).reshape(heads_n, queries.shape[0]),
        key_sums,
    )


def local(
    block_input,
    lengths,
    pass_ids,
    pass_embed,
    ln1_gain,
    ln1_bias,
    w_qkv,
    w_out,
    ln2_gain,
    ln2_bias,
    w_up,
    b_up,
    w_down,
    b_down,
    cotangent,
):
    row_count, seg_len, width = block_input.shape
    heads_n = H
    head_size = width // heads_n
    onehot = (
        pass_ids[..., None] == jnp.arange(pass_embed.shape[0], dtype=jnp.int32)[None, None, :]
    ).astype(jnp.float32)
    hidden_in = block_input.astype(jnp.float32) + jnp.einsum(
        "rsp,pd->rsd", onehot, pass_embed, precision=highest
    )
    normed, norm_back = jax.vjp(layer_norm, hidden_in, ln1_gain, ln1_bias)
    normed_low = normed.astype(jnp.bfloat16)
    qkv = jnp.einsum("rsd,de->rse", normed_low, w_qkv, preferred_element_type=jnp.float32)
    queries = qkv[..., :width].astype(jnp.bfloat16)
    key_flat = qkv[..., width : 2 * width].astype(jnp.bfloat16)
    value_flat = qkv[..., 2 * width :].astype(jnp.bfloat16)
    pass_low = pass_ids.astype(jnp.bfloat16)
    key_all, value_all, pass_all = (
        lax.all_gather(key_flat, "seq", axis=1, tiled=True),
        lax.all_gather(value_flat, "seq", axis=1, tiled=True),
        lax.all_gather(pass_low, "seq", axis=1, tiled=True),
    )
    total_len = key_all.shape[1]
    key_all = key_all.reshape(row_count, total_len, heads_n, head_size)
    value_all = value_all.reshape(row_count, total_len, heads_n, head_size)
    pass_all = pass_all.astype(jnp.float32)
    offset = lax.axis_index("seq") * seg_len
    query_place = offset + jnp.arange(seg_len, dtype=jnp.int32)
    query_pass = pass_ids.astype(jnp.float32)
    query_heads = queries.reshape(row_count, seg_len, heads_n, head_size)
    attended_rows = []
    log_rows = []
    for row in range(row_count):
        attended, log_total = attend_row(
            query_heads[row],
            query_place,
            query_pass[row],
            key_all[row],
            value_all[row],
            pass_all[row],
            lengths[row],
        )
        attended_rows.append(attended)
        log_rows.append(log_total)
    attended_low = jnp.stack(attended_rows).astype(jnp.bfloat16).reshape(row_count, seg_len, width)
    branch = jnp.einsum("rsd,de->rse", attended_low, w_out, preferred_element_type=jnp.float32)
    middle = hidden_in + branch
    normed2, norm2_back = jax.vjp(layer_norm, middle, ln2_gain, ln2_bias)
    normed2_low = normed2.astype(jnp.bfloat16)
    pre_act = (
        jnp.einsum("rsd,df->rsf", normed2_low, w_up, preferred_element_type=jnp.float32) + b_up
    )
    active, active_back = jax.vjp(gelu_tanh, pre_act)
    active_low = active.astype(jnp.bfloat16)
    result = (
        middle
        + jnp.einsum("rsf,fd->rsd", active_low, w_down, preferred_element_type=jnp.float32)
        + b_down
    )
    output = result.astype(jnp.bfloat16)
    cot_f = cotangent.astype(jnp.float32)
    grad_active = jnp.einsum("rsd,fd->rsf", cotangent, w_down, preferred_element_type=jnp.float32)
    grad_w_down = jnp.einsum(
        "rsf,rsd->fd", active_low, cotangent, preferred_element_type=jnp.float32
    )
    grad_b_down = jnp.sum(cot_f, (0, 1))
    grad_pre = active_back(grad_active)[0].astype(jnp.bfloat16)
    grad_b_up = jnp.sum(grad_pre.astype(jnp.float32), (0, 1))
    grad_w_up = jnp.einsum("rsd,rsf->df", normed2_low, grad_pre, preferred_element_type=jnp.float32)
    grad_normed2 = jnp.einsum("rsf,df->rsd", grad_pre, w_up, preferred_element_type=jnp.float32)
    grad_mid_norm, grad_ln2_gain, grad_ln2_bias = norm2_back(grad_normed2)
    grad_middle = cot_f + grad_mid_norm
    grad_branch = grad_middle.astype(jnp.bfloat16)
    grad_w_out = jnp.einsum(
        "rsd,rse->de", attended_low, grad_branch, preferred_element_type=jnp.float32
    )
    grad_attended = jnp.einsum(
        "rse,de->rsd", grad_branch, w_out, preferred_element_type=jnp.float32
    ).astype(jnp.bfloat16)
    dout_heads = grad_attended.reshape(row_count, seg_len, heads_n, head_size)
    dquery_rows = []
    dkey_rows = []
    dvalue_rows = []
    for row in range(row_count):
        dquery, _, key_sums = backward_row(
            query_heads[row],
            dout_heads[row],
            attended_rows[row],
            log_rows[row],
            query_place,
            query_pass[row],
            key_all[row],
            value_all[row],
            pass_all[row],
            lengths[row],
        )
        dquery_rows.append(dquery)
        dkey_rows.append(key_sums[0].reshape(total_len, width))
        dvalue_rows.append(key_sums[1].reshape(total_len, width))
    dkey_sum, dvalue_sum = (
        lax.psum_scatter(
            jnp.stack(dkey_rows).astype(jnp.bfloat16), "seq", scatter_dimension=1, tiled=True
        ).astype(jnp.float32),
        lax.psum_scatter(
            jnp.stack(dvalue_rows).astype(jnp.bfloat16), "seq", scatter_dimension=1, tiled=True
        ).astype(jnp.float32),
    )
    dquery_all = jnp.stack(dquery_rows).reshape(row_count, seg_len, width)
    grad_qkv = jnp.concatenate(
        [
            dquery_all.astype(jnp.bfloat16),
            dkey_sum.astype(jnp.bfloat16),
            dvalue_sum.astype(jnp.bfloat16),
        ],
        -1,
    )
    grad_w_qkv = jnp.einsum("rsd,rse->de", normed_low, grad_qkv, preferred_element_type=jnp.float32)
    grad_normed = jnp.einsum("rse,de->rsd", grad_qkv, w_qkv, preferred_element_type=jnp.float32)
    grad_in_norm, grad_ln1_gain, grad_ln1_bias = norm_back(grad_normed)
    grad_hidden = grad_middle + grad_in_norm
    grad_input = grad_hidden.astype(jnp.bfloat16)
    grad_pass = jnp.einsum("rsp,rsd->pd", onehot, grad_hidden, precision=highest)
    matrices = (
        lax.psum_scatter(
            grad_w_qkv.astype(jnp.bfloat16), "seq", scatter_dimension=0, tiled=True
        ).astype(jnp.float32),
        lax.psum_scatter(
            grad_w_out.astype(jnp.bfloat16), "seq", scatter_dimension=0, tiled=True
        ).astype(jnp.float32),
        lax.psum_scatter(
            grad_w_up.astype(jnp.bfloat16), "seq", scatter_dimension=0, tiled=True
        ).astype(jnp.float32),
        lax.psum_scatter(
            grad_w_down.astype(jnp.bfloat16), "seq", scatter_dimension=0, tiled=True
        ).astype(jnp.float32),
    )
    matrices = (
        lax.psum_scatter(
            matrices[0].astype(jnp.bfloat16), "batch", scatter_dimension=1, tiled=True
        ).astype(jnp.float32),
        lax.psum_scatter(
            matrices[1].astype(jnp.bfloat16), "batch", scatter_dimension=1, tiled=True
        ).astype(jnp.float32),
        lax.psum_scatter(
            matrices[2].astype(jnp.bfloat16), "batch", scatter_dimension=1, tiled=True
        ).astype(jnp.float32),
        lax.psum_scatter(
            matrices[3].astype(jnp.bfloat16), "batch", scatter_dimension=1, tiled=True
        ).astype(jnp.float32),
    )
    vectors = lax.psum(
        (
            grad_pass,
            grad_ln1_gain,
            grad_ln1_bias,
            grad_ln2_gain,
            grad_ln2_bias,
            grad_b_up,
            grad_b_down,
        ),
        ("seq", "batch"),
    )
    return (
        output,
        grad_input,
        vectors[0],
        vectors[1],
        vectors[2],
        matrices[0],
        matrices[1],
        vectors[3],
        vectors[4],
        matrices[2],
        vectors[5],
        matrices[3],
        vectors[6],
    )


NN = (((1,), (0,)), ((), ()))
NT = (((1,), (1,)), ((), ()))
TN = (((0,), (0,)), ((), ()))
vmem_bytes = 60 << 20
block = 256


def dot(left, right, form):
    return lax.dot_general(left, right, form, preferred_element_type=jnp.float32)


mesh_ids = pl.DeviceIdType.MESH


def block_kernel(
    lengths,
    block_in, cot_in, w_up_in, w_qkv_in, w_out_in, w_down_in,
    pass_in, embed_in, gain1, bias1, gain2, bias2, b_up_in, b_down_in,
    out, gin, vector, gqkv, gout, gup, gdown,
    kept_far, h_far,
    mid, keep, at, qkv, otf, ct, mt, gd, far, dm, kept, w_out, w_up, w_down,
    bsum, r1a, r2a, r1c, r2c, r2e, r3e, rz, rze,
    osend, orecv, hand, sums, gpass, vrecv, ksum, vsum, stage_send, stage_recv, down_recv,
    params, vecs, bcol, inv, prow, kmask, qhot, passes,
    lsem, ssem, rsem,
    *, chunks, plan,
):
    seq, bat = lax.axis_index("seq"), lax.axis_index("batch")
    x, core = seq // 2, seq % 2
    z, y = bat // 2, bat % 2
    to_core, to_x, to_y = (seq + 1 - 2 * core, bat), (seq + 2 - 4 * x, bat), (seq, bat + 1 - 2 * y)
    to_cross = (3 - seq, bat)
    to_z = [(seq, ((z + i) % 4) * 2 + y) for i in (1, 2, 3)]
    up_z, low_z = (seq, bat + 2), (seq, bat - 2)

    barrier = pltpu.get_barrier_semaphore()
    for peer in [to_core, to_x, to_y, to_cross] + to_z:
        pl.semaphore_signal(barrier, inc=1, device_id=peer, device_id_type=mesh_ids)

    width, total = mid.shape
    half = width // 2
    inner = w_up.shape[0]
    blocks_n = total // block
    heads = half // 64
    bs = 8

    def rows_at(first, count):
        return pl.ds(pl.multiple_of(first, 16), count)

    def lanes_at(first, count):
        return pl.ds(pl.multiple_of(first, 128), count)

    def own_cols(k):
        return lanes_at(core * block + k * 2 * block, block)

    def local(i, src, dst):
        return pltpu.make_async_copy(src, dst, lsem.at[i])

    def remote(i, src, dst, peer):
        return pltpu.make_async_remote_copy(
            src_ref=src, dst_ref=dst, send_sem=ssem.at[i], recv_sem=rsem.at[i],
            device_id=peer, device_id_type=mesh_ids,
        )

    part = w_down_in.shape[2]
    own_x = local(0, block_in.at[x], far.at[0:block, 0:width])
    own_c = local(1, cot_in.at[x], dm.at[0:block, 0:width])
    out_load = local(2, w_out_in, w_out)
    up_loads = [
        local(3 + p, w_up_in.at[:, p * width : (p + 1) * width],
              gd.at[p * width : (p + 1) * width, 0:width])
        for p in range(4)
    ]
    down_loads = [
        local(7 + i, w_down_in.at[i, core], w_down.at[i * part : (i + 1) * part, :])
        for i in range(bs)
    ]
    qkv_loads = [
        local(15 + j, w_qkv_in.at[:, j * width : (j + 1) * width],
              gd.at[j * width : (j + 1) * width, 0:width])
        for j in range(3)
    ]
    for load in [own_x] + up_loads + [own_c, out_load] + down_loads:
        load.start()

    base = 22 * len(chunks)
    x_far = remote(base, block_in.at[1 - x], far.at[block : 2 * block, 0:width], to_x)
    x_near = remote(base + 1, block_in.at[x], far.at[2 * block : 3 * block, 0:width], to_core)
    x_cross = remote(
        base + 2, far.at[block : 2 * block, 0:width], far.at[3 * block : 4 * block, 0:width], to_core
    )
    c_far = remote(base + 3, cot_in.at[1 - x], dm.at[block : 2 * block, 0:width], to_x)
    c_near = remote(base + 4, cot_in.at[x], dm.at[2 * block : 3 * block, 0:width], to_core)
    c_cross = remote(
        base + 5, dm.at[block : 2 * block, 0:width], dm.at[3 * block : 4 * block, 0:width], to_core
    )
    p_far = remote(base + 6, pass_in, passes.at[1], to_x)
    p_near = remote(base + 7, pass_in, passes.at[2], to_core)
    p_cross = remote(base + 8, pass_in, passes.at[3], to_cross)
    base += 9
    pl.semaphore_wait(barrier, 7)
    for copy in (p_far, x_far, x_near, p_near, p_cross, c_near):
        copy.start()


    def line_copy(i, d, up, part, slots):
        slot = d if up else jnp.where(z - 1 == d, 4, d)
        return remote(i + (d if up else 4 + d), part(d), slots(slot), up_z if up else low_z)

    def line_add(d, slot, part, slots):
        here, got = part(d), slots(slot)
        here[...] = here[...] + got[...]

    def line_start(i, part, slots):
        @pl.when(z == 0)
        def _():
            for d in (3, 2, 1):
                line_copy(i, d, True, part, slots).start()

        @pl.when(z == 3)
        def _():
            for d in (0, 1, 2):
                line_copy(i, d, False, part, slots).start()

    def line_pass(i, d, up, part, slots):
        copy = line_copy(i, d, up, part, slots)
        copy.wait_recv()
        line_add(d, d, part, slots)
        copy.start()

    def line_one(i, part, slots):
        @pl.when(z == 1)
        def _():
            line_pass(i, 3, True, part, slots)

        @pl.when(z == 2)
        def _():
            line_pass(i, 0, False, part, slots)

    def line_two(i, part, slots):
        @pl.when(z == 1)
        def _():
            line_pass(i, 2, True, part, slots)
            line_pass(i, 0, False, part, slots)

        @pl.when(z == 2)
        def _():
            line_pass(i, 1, False, part, slots)
            line_pass(i, 3, True, part, slots)

    def line_last(i, part, slots):
        for d in range(4):

            @pl.when(z == d)
            def _():
                if d > 0:
                    line_copy(i, d, True, part, slots).wait_recv()
                    line_add(d, d, part, slots)
                if d < 3:
                    line_copy(i, d, False, part, slots).wait_recv()
                    line_add(d, 4, part, slots)
                for e in range(4):
                    if e > d:
                        line_copy(i, e, True, part, slots).wait_send()
                    if e < d:
                        line_copy(i, e, False, part, slots).wait_send()

    class Chunk:
        def __init__(self, k):
            r0, rc, ra, r1, a0, c0, e0 = chunks[k]
            ne, nc, na = rc - r0, ra - rc, r1 - ra
            i = 22 * k
            rows_e, rows_c, rows_a = pl.ds(r0, ne), pl.ds(rc, nc), pl.ds(ra, na)
            got_a, got_c, got_e = pl.ds(a0, na), pl.ds(c0, nc), pl.ds(e0, ne)
            sub = bsum.at
            self.one_a = remote(i, sub[1 - x, :, :, rows_a, :], r1a.at[:, :, got_a, :], to_x)
            self.one_c = remote(i + 1, sub[:, :, 1 - y, rows_c, :], r1c.at[:, :, got_c, :], to_y)
            self.two_a = remote(i + 2, sub[x, :, 1 - y, rows_a, :], r2a.at[:, got_a, :], to_y)
            self.two_c = remote(i + 3, sub[1 - x, :, y, rows_c, :], r2c.at[:, got_c, :], to_x)
            self.two_e = remote(i + 4, sub[:, z, 1 - y, rows_e, :], r2e.at[:, got_e, :], to_y)
            self.three_e = remote(i + 5, sub[1 - x, z, y, rows_e, :], r3e.at[got_e, :], to_x)
            self.adds = [
                (sub[x, :, :, rows_a, :], r1a.at[:, :, got_a, :]),
                (sub[:, :, y, rows_c, :], r1c.at[:, :, got_c, :]),
                (sub[x, :, y, rows_a, :], r2a.at[:, got_a, :]),
                (sub[x, :, y, rows_c, :], r2c.at[:, got_c, :]),
                (sub[:, z, y, rows_e, :], r2e.at[:, got_e, :]),
                (sub[x, z, y, rows_e, :], r3e.at[got_e, :]),
            ]
            both, low = pl.ds(rc, na + nc), pl.ds(a0 + c0, na + nc)
            self.line_ac = (
                i + 6, lambda d: sub[x, d, y, both, :], lambda s: rz.at[s, low, :]
            )
            self.line_e = (
                i + 14, lambda d: sub[:, d, :, rows_e, :], lambda s: rze.at[s, :, :, got_e, :]
            )

        def add(self, j):
            here, got = self.adds[j]
            here[...] = here[...] + got[...]

        def start(self):
            line_start(*self.line_e)
            self.one_c.start()
            self.one_a.start()

        def start_a(self):
            self.one_a.start()

        def start_c(self):
            self.one_c.start()

        def start_e(self):
            line_start(*self.line_e)

        def e1(self):
            line_one(*self.line_e)

        def e2(self):
            line_two(*self.line_e)

        def e3(self):
            line_last(*self.line_e)
            self.two_e.start()

        def a2(self):
            self.one_a.wait()
            self.add(0)
            self.two_a.start()

        def c2(self):
            self.one_c.wait()
            self.add(1)
            self.two_c.start()

        def e4(self):
            self.two_e.wait()
            self.add(4)
            self.three_e.start()

        def z0(self):
            self.two_a.wait()
            self.add(2)
            self.two_c.wait()
            self.add(3)
            line_start(*self.line_ac)

        def z1(self):
            line_one(*self.line_ac)

        def z2(self):
            line_two(*self.line_ac)

        def z3(self):
            line_last(*self.line_ac)
            self.three_e.wait()
            self.add(5)
    steps = [Chunk(k) for k in range(len(chunks))]

    def serve(slot):
        for k, name in plan[slot]:
            getattr(steps[k], name)()

    params[...] = jnp.zeros_like(params)
    params[0:5, :] = embed_in[...]
    for i, ref in enumerate((gain1, bias1, gain2, bias2, b_down_in)):
        params[5 + i, :] = ref[...]
    for i in range(4):
        params[10 + i, :] = b_up_in[pl.ds(i * width, width)]
    vecs[...] = jnp.transpose(params[...])
    for b in range(bs):
        i, low = 10 + b // 2, b % 2 * 2 * part
        bcol[b * part : (b + 1) * part, :] = jnp.broadcast_to(
            jnp.where(
                core == 0,
                vecs[low : low + part, i : i + 1],
                vecs[low + part : low + 2 * part, i : i + 1],
            ),
            (part, 8),
        )
    for b in range(bs):
        p, low = b // 2, b % 2 * 2 * part
        if b % 2 == 0:
            up_loads[p].wait()
        turned = jnp.transpose(gd[p * width : (p + 1) * width, low : low + 2 * part])
        w_up[b * part : (b + 1) * part, :] = jnp.where(core == 0, turned[:part], turned[part:])
    for load in qkv_loads:
        load.start()
    passes[0] = pass_in[...]
    places = (2 * x + core, 2 * (1 - x) + core, 2 * x + 1 - core, 2 * (1 - x) + 1 - core)
    length = lengths[x]
    emb = jnp.where(lax.broadcasted_iota(jnp.int32, (8, width), 0) < 5, params[0:8, :], 0.0)
    emb_a = emb.astype(jnp.bfloat16)
    rest = emb - emb_a.astype(jnp.float32)
    emb_b = rest.astype(jnp.bfloat16)
    emb_c = (rest - emb_b.astype(jnp.float32)).astype(jnp.bfloat16)

    def take(k):
        cols = lanes_at(places[k] * block, block)
        rows = rows_at(places[k] * block, block)
        got = passes[k]
        line = jnp.where(x == 0, got[0:1, :], got[1:2, :])
        prow[:, cols] = jnp.broadcast_to(line.astype(jnp.float32), (8, block))
        kind = lax.broadcasted_iota(jnp.int32, (16, block), 0)
        spot = lax.broadcasted_iota(jnp.int32, (16, block), 1) + places[k] * block
        onehot = jnp.where(kind == line, 1.0, 0.0).astype(jnp.bfloat16)
        qhot[:, cols] = onehot
        hidden = jnp.where((line > kind) | (spot >= length), negative, 0.0)
        kmask[rows, :] = jnp.transpose(hidden).astype(jnp.bfloat16)
        hot = onehot[0:8, :]
        added = dot(emb_a, hot, TN) + dot(emb_b, hot, TN) + dot(emb_c, hot, TN)
        h = jnp.transpose(far[k * block : (k + 1) * block, 0:width]).astype(jnp.float32) + added
        mid[:, cols] = h
        shifted = h - jnp.sum(h, 0, keepdims=True) * (1.0 / width)
        spread = jnp.sum(shifted * shifted, 0, keepdims=True) * (1.0 / width)
        scaled = shifted * lax.rsqrt(spread + 1e-05)
        at[:, cols] = (scaled * vecs[:, 5:6] + vecs[:, 6:7]).astype(jnp.bfloat16)
        for j in range(3):
            res = dot(
                gd[j * width : (j + 1) * width, lanes_at(core * half, half)], at[:, cols], TN
            ).astype(jnp.bfloat16)
            qkv[j * half : (j + 1) * half, cols] = res * jnp.bfloat16(0.125) if j == 0 else res

    own_x.wait()
    for load in qkv_loads:
        load.wait()
    take(0)
    x_near.wait()
    p_near.wait()
    take(2)
    p_far.wait()
    x_far.wait()
    x_cross.start()
    c_far.start()
    take(1)
    x_cross.wait()
    p_cross.wait()
    take(3)
    h_saves = [local(18 + k, mid.at[:, own_cols(k)], h_far.at[k]) for k in range(2)]
    for save in h_saves:
        save.start()

    for qb in range(blocks_n):
        cols = slice(qb * block, (qb + 1) * block)
        key = lax.broadcasted_iota(jnp.int32, (block, block), 0)
        place = lax.broadcasted_iota(jnp.int32, (block, block), 1)
        cover = dot(kmask[cols, :], qhot[:, cols], NN)
        cover = jnp.where(key < place, cover, negative)
        at_row, at_col = qb // 2 * block, qb % 2 * block
        keep[at_row : at_row + block, at_col : at_col + block] = jnp.where(key == place, 0.0, cover)

    def kept_save(h, slot):
        return pltpu.make_async_copy(kept.at[slot], kept_far.at[h], lsem.at[20 + slot])

    def o_copy(h):
        mine = rows_at(core * half + h * 64, 64)
        return remote(base + h, otf.at[mine, :], otf.at[mine, :], to_core)

    def turn(k):
        ct[:, lanes_at(places[k] * block, block)] = jnp.transpose(
            dm[k * block : (k + 1) * block, 0:width]
        )

    def one_head(h, carry):
        slot = h % 2

        @pl.when(h >= 2)
        def _():
            kept_save(h - 2, slot).wait()

        qrow, krow, vrow = (rows_at(j * half + h * 64, 64) for j in range(3))
        mine = rows_at(core * half + h * 64, 64)
        keyn = jnp.concatenate([jnp.transpose(qkv[krow, :]), kmask[...]], 1)
        query = jnp.concatenate([qkv[qrow, :], qhot[...]], 0)
        for qb in range(blocks_n):
            below, n = qb * block, (qb + 1) * block
            at_row = qb * (qb + 1) // 2 * block
            cols = slice(below, n)
            to_row, to_col = qb // 2 * block, qb % 2 * block
            diag = dot(keyn[cols, 0:64], query[0:64, cols], NN)
            diag = diag + keep[to_row : to_row + block, to_col : to_col + block]
            peak = jnp.max(diag, 0, keepdims=True)
            if qb:
                scores = dot(keyn[0:below, :], query[:, cols], NN)
                peak = jnp.maximum(peak, jnp.max(scores, 0, keepdims=True))
                expo = jnp.exp(scores - peak)
                count = jnp.sum(expo, 0, keepdims=True)
                kept[slot, at_row : at_row + below, :] = expo.astype(jnp.bfloat16)
            last = jnp.exp(diag - peak)
            kept[slot, at_row + below : at_row + n, :] = last.astype(jnp.bfloat16)
            last_sum = jnp.sum(last, 0, keepdims=True)
            over = 1.0 / (count + last_sum if qb else last_sum)
            inv[h, :, cols] = jnp.broadcast_to(over, (8, block))
            result = dot(qkv[vrow, 0:n], kept[slot, at_row : at_row + n, :], NN) * over
            otf[mine, cols] = result.astype(jnp.bfloat16)
        kept_save(h, slot).start()

        @pl.when(h == heads - 2)
        def _():
            c_near.wait()
            c_far.wait()
            c_cross.start()
            own_c.wait()
            for k in (0, 2, 1):
                turn(k)

        @pl.when(h == heads - 1)
        def _():
            c_cross.wait()
            turn(3)

        o_copy(h).start()
        return carry

    lax.fori_loop(0, heads, one_head, 0)
    kept_save(heads - 2, heads % 2).wait()
    kept_save(heads - 1, (heads - 1) % 2).wait()

    def kept_load(h, slot):
        return pltpu.make_async_copy(kept_far.at[h], kept.at[slot], lsem.at[22 + slot])

    kept_load(0, 0).start()
    kept_load(1, 1).start()
    for h in range(heads):
        o_copy(h).wait()
    base += heads

    for save in h_saves:
        save.wait()
    out_load.wait()

    def mix(i, carry):
        cols = lanes_at(i * block, block)
        m = mid[:, cols] + dot(w_out[...], otf[:, cols], TN)
        mid[:, cols] = m
        shifted = m - jnp.sum(m, 0, keepdims=True) * (1.0 / width)
        spread = jnp.sum(shifted * shifted, 0, keepdims=True) * (1.0 / width)
        scaled = shifted * lax.rsqrt(spread + 1e-05)
        mt[:, cols] = (scaled * vecs[:, 7:8] + vecs[:, 8:9]).astype(jnp.bfloat16)
        return carry

    lax.fori_loop(0, blocks_n, mix, 0)

    def hidden_at(first):
        def hidden(i, carry):
            rows = rows_at(first + i * part, part)
            below = rows_at(inner + first + i * part, part)
            u = dot(w_up[rows, :], mt[...], NN) + bcol[rows, 0:1]
            square = u * u
            t = jnp.tanh(u * (0.7978845608028654 + 0.035677408136300125 * square))
            gate = 0.5 + 0.5 * t
            gd[rows, :] = (u * gate).astype(jnp.bfloat16)
            slope = gate + (0.5 * u) * (1.0 - t * t) * (
                0.7978845608028654 + 0.10703222440890037 * square
            )
            gd[below, :] = slope.astype(jnp.bfloat16)
            return carry

        lax.fori_loop(0, 2, hidden, 0)

    lanes = bsum.shape[-1]
    band = width // bs
    for j in range(2):
        for xx in range(2):
            at_row = (2 * xx + j) * lanes
            hidden_at(at_row)
            grad = dot(ct[...], gd[at_row : at_row + lanes, :], NT).astype(jnp.bfloat16)
            for b in range(bs):
                bsum[xx, b // 2, b % 2, j * band : (j + 1) * band, :] = grad[
                    b * band : (b + 1) * band, :
                ]
        serve("down%d" % j)
    for load in down_loads:
        load.wait()

    def hidden_back(i, carry):
        rows = rows_at(i * part, part)
        below = rows_at(inner + i * part, part)
        back = dot(w_down[rows, :], ct[...], NN)
        gd[below, :] = (back * gd[below, :].astype(jnp.float32)).astype(jnp.bfloat16)
        return carry

    lax.fori_loop(0, bs, hidden_back, 0)
    serve("hidden")

    dm_copy = remote(base, dm.at[0:width, :], dm.at[width : 2 * width, :], to_core)

    def back_up(i, carry):
        cols = lanes_at(i * block, block)
        dm[0:width, cols] = dot(w_up[...], gd[inner : 2 * inner, cols], TN).astype(jnp.bfloat16)
        return carry

    lax.fori_loop(0, blocks_n, back_up, 0)
    dm_copy.start()
    serve("dm")
    first_up = 2 * band
    up_band = part
    for xx in range(2):
        for i in range(2):
            low, high = inner + i * inner // 2, inner + (i + 1) * inner // 2
            grad = dot(gd[low:high, :], mt[xx * lanes : (xx + 1) * lanes, :], NT)
            grad = grad.astype(jnp.bfloat16)
            for b in range(bs // 2):
                bb = i * bs // 2 + b
                bsum[xx, bb // 2, bb % 2, first_up : first_up + up_band, :] = grad[
                    b * up_band : (b + 1) * up_band, :
                ]
        serve("up%d" % xx)
    ones = jnp.ones((8, total), jnp.bfloat16)
    up_sum = dot(ones, gd[inner : 2 * inner, :], NT)
    vector[...] = jnp.zeros_like(vector)
    for i in range(4):
        one, two = (up_sum[0:1, (2 * i + e) * part : (2 * i + e + 1) * part] for e in range(2))
        none = jnp.zeros_like(one)
        vector[10 + i : 11 + i, :] = jnp.where(
            core == 0,
            jnp.concatenate([one, none, two, none], 1),
            jnp.concatenate([none, one, none, two], 1),
        )

    out_copy = remote(base + 1, osend, orecv, to_core)
    for k in range(2):
        other = lanes_at((1 - core) * block + k * 2 * block, block)
        to = slice(k * block, (k + 1) * block)
        osend[:, to] = dot(w_down[...], gd[0:inner, other], TN).astype(jnp.bfloat16)
        keep[:, to] = mid[:, own_cols(k)] + vecs[:, 9:10] + dot(
            w_down[...], gd[0:inner, own_cols(k)], TN
        )
    out_copy.start()
    serve("out")

    dm_copy.wait()
    sums[...] = jnp.zeros_like(sums)

    def middle(i, carry):
        cols = lanes_at(i * block, block)
        cot = ct[:, cols].astype(jnp.float32)
        m = mid[:, cols]
        shifted = m - jnp.sum(m, 0, keepdims=True) * (1.0 / width)
        spread = jnp.sum(shifted * shifted, 0, keepdims=True) * (1.0 / width)
        r = lax.rsqrt(spread + 1e-05)
        n = shifted * r
        d = dm[0:width, cols].astype(jnp.float32) + dm[width : 2 * width, cols].astype(jnp.float32)
        e = d * vecs[:, 7:8]
        mean_e = jnp.sum(e, 0, keepdims=True) * (1.0 / width)
        mean_en = jnp.sum(e * n, 0, keepdims=True) * (1.0 / width)
        dmid = cot + r * (e - mean_e - n * mean_en)
        mid[:, cols] = dmid
        dm[width : 2 * width, cols] = dmid.astype(jnp.bfloat16)
        sums[:, 0:1] += jnp.sum(d * n, 1, keepdims=True)
        sums[:, 1:2] += jnp.sum(d, 1, keepdims=True)
        sums[:, 2:3] += jnp.sum(cot, 1, keepdims=True)
        return carry

    lax.fori_loop(0, blocks_n, middle, 0)
    serve("middle")
    small = band // 2
    for b in range(bs):
        dm[half + b * small : half + (b + 1) * small, :] = dm[
            rows_at(width + b * band + core * small, small), :
        ]
    first_out = first_up + up_band
    for xx in range(2):
        grad = dot(dm[half:width, :], otf[xx * lanes : (xx + 1) * lanes, :], NT)
        grad = grad.astype(jnp.bfloat16)
        for b in range(bs):
            bsum[xx, b // 2, b % 2, first_out : first_out + small, :] = grad[
                b * small : (b + 1) * small, :
            ]
    dm[0:half, :] = dot(
        w_out[rows_at(core * half, half), :], dm[width : 2 * width, :], NN
    ).astype(jnp.bfloat16)
    serve("w_out")

    whole_loads = [
        local(24, w_qkv_in.at[:, 0:width], w_up.at[0:width, :]),
        local(25, w_qkv_in.at[:, width : 2 * width], w_up.at[width : 2 * width, :]),
        local(26, w_qkv_in.at[:, 2 * width : 3 * width], w_down.at[0:width, :]),
    ]
    for load in whole_loads:
        load.start()
    hand_out = remote(base + 2, hand.at[0], out.at[x], to_x)

    def give_output():
        out_copy.wait()
        for k in range(2):
            cols = slice(k * block, (k + 1) * block)
            rows = jnp.transpose(
                (keep[:, cols] + orecv[:, cols].astype(jnp.float32)).astype(jnp.bfloat16)
            )

            @pl.when(x == k)
            def _():
                out[k] = rows

            @pl.when(x != k)
            def _():
                hand[0] = rows

        hand_out.start()

    def far_copy(h, j):
        mine = rows_at(j * width + core * half + h * 64, 64)
        return remote(
            base + 3 + h * 3 + j, gd.at[mine, :], far.at[rows_at(j * half + h * 64, 64), :], to_core
        )

    def head_back(h, carry):
        slot = h % 2
        kept_load(h, slot).wait()
        qrow, krow, vrow = (rows_at(j * half + h * 64, 64) for j in range(3))
        mine = [rows_at(j * width + core * half + h * 64, 64) for j in range(3)]
        valn = jnp.transpose(qkv[vrow, :])
        grads = (dm[rows_at(h * 64, 64), :].astype(jnp.float32) * inv[h, 0:1, :]).astype(
            jnp.bfloat16
        )
        o_rows = otf[rows_at(core * half + h * 64, 64), :]
        delta = jnp.sum(grads.astype(jnp.float32) * o_rows.astype(jnp.float32), 0, keepdims=True)
        ksum[...] = jnp.zeros_like(ksum)
        vsum[...] = jnp.zeros_like(vsum)
        for qb in range(blocks_n):
            n = (qb + 1) * block
            at_row = qb * (qb + 1) // 2 * block
            cols = slice(qb * block, n)
            low = kept[slot, at_row : at_row + n, :]
            dprob = dot(valn[0:n, :], grads[:, cols], NN)
            dscore = (low.astype(jnp.float32) * (dprob - delta[:, cols])).astype(jnp.bfloat16)
            gd[mine[0], cols] = (dot(qkv[krow, 0:n], dscore, NN) * 0.125).astype(jnp.bfloat16)
            ksum[:, 0:n] += dot(qkv[qrow, cols], dscore, NT)
            vsum[:, 0:n] += dot(grads[:, cols], low, NT)
        gd[mine[1], :] = ksum[...].astype(jnp.bfloat16)
        gd[mine[2], :] = vsum[...].astype(jnp.bfloat16)
        for j in range(3):
            far_copy(h, j).start()

        @pl.when(h + 2 < heads)
        def _():
            kept_load(h + 2, slot).start()

        for at_head in range(heads):

            @pl.when(h == at_head)
            def _():
                serve("head%d" % at_head)

        return carry

    lax.fori_loop(0, heads, head_back, 0)
    give_output()
    serve("given")
    own_loads = [local(18 + k, h_far.at[k], keep.at[:, k * block : (k + 1) * block]) for k in range(2)]
    for load in own_loads:
        load.start()

    for h in range(heads):
        for j in range(3):
            far_copy(h, j).wait()
    for j in range(3):
        gd[rows_at(j * width + (1 - core) * half, half), :] = far[j * half : (j + 1) * half, :]
    qkv_band = 3 * width // bs
    qkv_small = qkv_band // 2
    for b in range(bs):
        dm[b * qkv_small : (b + 1) * qkv_small, :] = gd[
            rows_at(b * qkv_band + core * qkv_small, qkv_small), :
        ]
    first_qkv = first_out + small
    for xx in range(2):
        grad = dot(dm[0 : bs * qkv_small, :], at[xx * lanes : (xx + 1) * lanes, :], NT)
        grad = grad.astype(jnp.bfloat16)
        for b in range(bs):
            bsum[xx, b // 2, b % 2, first_qkv : first_qkv + qkv_small, :] = grad[
                b * qkv_small : (b + 1) * qkv_small, :
            ]
    serve("qkv")

    for load in whole_loads + own_loads:
        load.wait()
    gpass[...] = jnp.zeros_like(gpass)
    hand_in = remote(base + 21, hand.at[1], gin.at[x], to_x)
    for k in range(2):
        mine = own_cols(k)
        da = dot(w_up[0:width, :], gd[0:width, mine], NN)
        da += dot(w_up[width : 2 * width, :], gd[width : 2 * width, mine], NN)
        da += dot(w_down[0:width, :], gd[2 * width : 3 * width, mine], NN)
        h = keep[:, k * block : (k + 1) * block]
        shifted = h - jnp.sum(h, 0, keepdims=True) * (1.0 / width)
        spread = jnp.sum(shifted * shifted, 0, keepdims=True) * (1.0 / width)
        r = lax.rsqrt(spread + 1e-05)
        n = shifted * r
        e = da * vecs[:, 5:6]
        mean_e = jnp.sum(e, 0, keepdims=True) * (1.0 / width)
        mean_en = jnp.sum(e * n, 0, keepdims=True) * (1.0 / width)
        dh = mid[:, mine] + r * (e - mean_e - n * mean_en)
        rows = jnp.transpose(dh).astype(jnp.bfloat16)

        @pl.when(x == k)
        def _():
            gin[k] = rows

        @pl.when(x != k)
        def _():
            hand[1] = rows
            hand_in.start()

        sums[:, 3:4] += jnp.sum(da * n, 1, keepdims=True)
        sums[:, 4:5] += jnp.sum(da, 1, keepdims=True)
        kind = lax.broadcasted_iota(jnp.int32, (16, block), 0).astype(jnp.float32)
        onehot = jnp.where(kind == prow[0:1, mine], 1.0, 0.0).astype(jnp.bfloat16)
        high = dh.astype(jnp.bfloat16)
        rest = dh - high.astype(jnp.float32)
        second_part = rest.astype(jnp.bfloat16)
        tail = (rest - second_part.astype(jnp.float32)).astype(jnp.bfloat16)
        gpass[...] += dot(onehot, high, NT) + dot(onehot, second_part, NT) + dot(onehot, tail, NT)
        serve("input%d" % k)

    lines = jnp.transpose(sums[...])
    vector[0:5, :] = gpass[0:5, :]
    vector[5:7, :] = lines[3:5, :]
    vector[7:10, :] = lines[0:3, :] * 0.5
    for i, peer in enumerate((to_core, to_x, to_y)):
        copy = remote(base + 22 + i, vector, vrecv.at[i], peer)
        copy.start()
        copy.wait()
        vector[...] = vector[...] + vrecv[i]
        serve("sum%d" % i)
    copies = [
        remote(base + 25 + i, vector, vrecv.at[3 + z], peer) for i, peer in enumerate(to_z)
    ]
    for copy in copies:
        copy.start()
    vrecv[3 + z] = vector[...]

    own_rows = down_recv.shape[0]
    down_copy = remote(
        base + 28, bsum.at[x, z, y, rows_at((1 - core) * own_rows, own_rows), :], down_recv, to_core
    )

    def swap_lanes(i, r0, r1):
        wide = lanes // 2
        v = bsum[x, z, y, r0:r1, :]
        stage_send[r0 - first_up : r1 - first_up, 0:wide] = jnp.where(
            core == 0, v[:, wide:lanes], v[:, 0:wide]
        )
        at_rows = slice(r0 - first_up, r1 - first_up)
        return remote(base + i, stage_send.at[at_rows, :], stage_recv.at[at_rows, :], to_core)

    def both_cores(mine, got):
        return jnp.where(core == 0, mine, got), jnp.where(core == 0, got, mine)

    def put(result, r0, r1):
        wide = lanes // 2
        v = bsum[x, z, y, r0:r1, :].astype(jnp.float32)
        mine = jnp.where(core == 0, v[:, 0:wide], v[:, wide:lanes])
        got = stage_recv[r0 - first_up : r1 - first_up, 0:wide].astype(jnp.float32)
        result[...] = jnp.transpose(jnp.concatenate(both_cores(mine, got), 0))

    serve("end0")
    down_copy.start()
    serve("end1")
    up_copy = swap_lanes(29, first_up, first_qkv)
    up_copy.start()
    serve("end2")
    qkv_copy = swap_lanes(30, first_qkv, first_qkv + qkv_small)
    qkv_copy.start()
    down_copy.wait()
    mine = bsum[x, z, y, rows_at(core * own_rows, own_rows), :].astype(jnp.float32)
    for c, piece in enumerate(both_cores(mine, down_recv[...].astype(jnp.float32))):
        turned = jnp.transpose(piece)
        for i in range(lanes // part):
            at_row = (2 * i + c) * part
            gdown[at_row : at_row + part, :] = turned[i * part : (i + 1) * part, :]
    up_copy.wait()
    put(gup, first_up, first_out)
    put(gout, first_out, first_qkv)
    for copy in copies:
        copy.wait()
    vector[...] = (vrecv[3] + vrecv[4]) + (vrecv[5] + vrecv[6])
    hand_out.wait()
    hand_in.wait()
    qkv_copy.wait()
    put(gqkv, first_qkv, first_qkv + qkv_small)


def finish_kernel(
    out_in, gin_in, vector, gqkv_in, gout_in, gup_in, gdown_in,
    out, gin, gpass, gain1, bias1, gqkv, gout, gain2, bias2, gup, gb_up, gdown, gb_down,
):
    pairs = (
        (out_in, out), (gin_in, gin), (gqkv_in, gqkv), (gout_in, gout), (gup_in, gup), (gdown_in, gdown)
    )
    for a, b in pairs:
        b[...] = a[...]
    width = vector.shape[1]
    gpass[...] = vector[0:5, :]
    for i, ref in enumerate((gain1, bias1, gain2, bias2, gb_down)):
        ref[...] = vector[5 + i, :]
    for i in range(4):
        gb_up[pl.ds(i * width, width)] = vector[10 + i, :]


def shaped(*dims, kind=jnp.bfloat16):
    return jax.ShapeDtypeStruct(dims, kind)


shares = ((64, 80, 48), (64, 80, 48), (16, 16, 16), (48, 64, 32))
plan = {
    "down0": ((0, "start_e"),),
    "down1": ((0, "start_c"), (0, "start_a")),
    "hidden": ((0, "e1"),),
    "dm": ((0, "a2"),),
    "up0": ((0, "e2"),),
    "up1": ((1, "start"), (0, "c2")),
    "out": (),
    "middle": ((0, "e3"),),
    "w_out": ((2, "start"),),
    "head0": ((0, "z0"), (1, "e1")),
    "head1": ((0, "e4"),),
    "head2": ((0, "z1"), (1, "a2")),
    "head3": ((1, "e2"),),
    "head4": ((0, "z2"), (1, "c2"), (2, "e1")),
    "head5": ((1, "e3"), (2, "a2"), (2, "c2")),
    "given": ((0, "z3"), (1, "z0")),
    "qkv": ((3, "start"), (1, "e4"), (2, "e2")),
    "input0": ((1, "z1"), (2, "e3"), (3, "e1")),
    "input1": ((1, "z2"), (2, "z0"), (2, "e4"), (3, "a2")),
    "sum0": ((3, "e2"), (2, "z1")),
    "sum1": ((1, "z3"), (3, "c2")),
    "sum2": ((2, "z2"), (3, "e3")),
    "end0": (),
    "end1": ((2, "z3"), (3, "z0")),
    "end2": ((3, "e4"), (3, "z1"), (3, "z2"), (3, "z3")),
}


def regrouped(
    block_input, lengths, pass_ids, pass_embed, ln1_gain, ln1_bias, w_qkv, w_out,
    ln2_gain, ln2_bias, w_up, b_up, w_down, b_down, cotangent, batch_n
):
    width = block_input.shape[2]
    total = 4 * block_input.shape[1]
    inner = w_up.shape[1]
    own_in, half, lanes = inner // 2, width // 2, width // 2
    band = inner // batch_n // 2
    z_n = batch_n // 2
    blocks_n = total // block
    kept_rows = blocks_n * (blocks_n + 1) // 2 * block
    chunks, a0, c0, e0, r0 = [], 0, 0, 0, 0
    for ne, nc, na in shares:
        chunks.append((r0, r0 + ne, r0 + ne + nc, r0 + ne + nc + na, a0, c0, e0))
        r0, a0, c0, e0 = r0 + ne + nc + na, a0 + na, c0 + nc, e0 + ne
    down_n = 2 * width // batch_n
    anywhere = pl.BlockSpec(memory_space=pl.ANY)
    whole = pl.BlockSpec(memory_space=pltpu.VMEM)
    low, full = jnp.bfloat16, jnp.float32
    copies_n = 22 * len(chunks) + 9 + half // 64 + 31
    output, grad_input, vector, grad_qkv, grad_out, grad_up, grad_down, _, _ = pl.pallas_call(
        functools.partial(block_kernel, chunks=tuple(chunks), plan=plan),
        out_shape=[
            shaped(2, block, width),
            shaped(2, block, width),
            shaped(16, width, kind=full),
            shaped(width // 4, 3 * width // batch_n, kind=full),
            shaped(width // 4, width // batch_n, kind=full),
            shaped(width // 4, inner // batch_n, kind=full),
            shaped(inner // 4, width // batch_n, kind=full),
            shaped(half // 64, kept_rows, block),
            shaped(2, width, block, kind=full),
        ],
        in_specs=[pl.BlockSpec(memory_space=pltpu.SMEM)] + [anywhere] * 6 + [whole] * 8,
        out_specs=[whole] * 7 + [anywhere] * 2,
        scratch_shapes=[
            pltpu.VMEM((width, total), full),
            pltpu.VMEM((width, 2 * block), full),
            pltpu.VMEM((width, total), low),
            pltpu.VMEM((3 * half, total), low),
            pltpu.VMEM((width, total), low),
            pltpu.VMEM((width, total), low),
            pltpu.VMEM((width, total), low),
            pltpu.VMEM((2 * own_in, total), low),
            pltpu.VMEM((3 * half, total), low),
            pltpu.VMEM((2 * width, total), low),
            pltpu.VMEM((2, kept_rows, block), low),
            pltpu.VMEM((width, width), low),
            pltpu.VMEM((own_in, width), low),
            pltpu.VMEM((own_in, width), low),
            pltpu.VMEM((2, z_n, 2, r0, lanes), low),
            pltpu.VMEM((z_n, 2, a0, lanes), low),
            pltpu.VMEM((z_n, a0, lanes), low),
            pltpu.VMEM((2, z_n, c0, lanes), low),
            pltpu.VMEM((z_n, c0, lanes), low),
            pltpu.VMEM((2, e0, lanes), low),
            pltpu.VMEM((e0, lanes), low),
            pltpu.VMEM((z_n + 1, a0 + c0, lanes), low),
            pltpu.VMEM((z_n + 1, 2, 2, e0, lanes), low),
            pltpu.VMEM((width, 2 * block), low),
            pltpu.VMEM((width, 2 * block), low),
            pltpu.VMEM((2, block, width), low),
            pltpu.VMEM((width, 128), full),
            pltpu.VMEM((16, width), full),
            pltpu.VMEM((7, 16, width), full),
            pltpu.VMEM((64, total), full),
            pltpu.VMEM((64, total), full),
            pltpu.VMEM((r0 - down_n, 256), low),
            pltpu.VMEM((r0 - down_n, 256), low),
            pltpu.VMEM((down_n // 2, lanes), low),
            pltpu.VMEM((16, width), full),
            pltpu.VMEM((width, 16), full),
            pltpu.VMEM((own_in, 8), full),
            pltpu.VMEM((half // 64, 8, total), full),
            pltpu.VMEM((8, total), full),
            pltpu.VMEM((total, 16), low),
            pltpu.VMEM((16, total), low),
            pltpu.VMEM((4, 2, block), jnp.int32),
            pltpu.SemaphoreType.DMA((27,)),
            pltpu.SemaphoreType.DMA((copies_n,)),
            pltpu.SemaphoreType.DMA((copies_n,)),
        ],
        compiler_params=pltpu.CompilerParams(
            vmem_limit_bytes=63 << 20, collective_id=0, has_side_effects=True
        ),
        cost_estimate=pl.CostEstimate(flops=int(60e9), bytes_accessed=0, transcendentals=0),
        name="block",
    )(
        lengths, block_input, cotangent, w_up, w_qkv, w_out,
        w_down.reshape(batch_n, 2, band, width), pass_ids, pass_embed,
        ln1_gain, ln1_bias, ln2_gain, ln2_bias, b_up, b_down,
    )
    results = [output, grad_input, vector, grad_qkv, grad_out, grad_up, grad_down]
    line = jax.ShapeDtypeStruct((width,), full)
    return pl.pallas_call(
        finish_kernel,
        out_shape=[
            shaped(2, block, width),
            shaped(2, block, width),
            shaped(5, width, kind=full),
            line,
            line,
            jax.ShapeDtypeStruct(grad_qkv.shape, full),
            jax.ShapeDtypeStruct(grad_out.shape, full),
            line,
            line,
            jax.ShapeDtypeStruct(grad_up.shape, full),
            jax.ShapeDtypeStruct((inner,), full),
            jax.ShapeDtypeStruct(grad_down.shape, full),
            line,
        ],
        in_specs=[whole] * 7,
        out_specs=[whole] * 13,
        compiler_params=pltpu.CompilerParams(vmem_limit_bytes=16 << 20),
        name="finish",
    )(*results)


def solution(mesh):
    batch_n = mesh.shape["batch"]
    few = mesh.shape["seq"] == 4 and batch_n == 8
    body = functools.partial(regrouped, batch_n=batch_n) if few else local
    return jax.shard_map(
        body,
        mesh=mesh,
        in_specs=(
            P("batch", "seq", None),
            P("batch"),
            P("batch", "seq"),
            P(),
            P(),
            P(),
            P(),
            P(),
            P(),
            P(),
            P(),
            P(),
            P(),
            P(),
            P("batch", "seq", None),
        ),
        out_specs=(
            P("batch", "seq", None),
            P("batch", "seq", None),
            P(),
            P(),
            P(),
            P("seq", "batch"),
            P("seq", "batch"),
            P(),
            P(),
            P("seq", "batch"),
            P(),
            P("seq", "batch"),
            P(),
        ),
        check_vma=False,
    )
```

```python
import functools

import jax
import jax.numpy as jnp
from jax import lax
from jax.experimental import pallas as pl
from jax.experimental.pallas import tpu as pltpu
from jax.sharding import PartitionSpec as P

H = 12


negative = -1e30
key_block = 1024
query_block = 512
highest = lax.Precision.HIGHEST


def layer_norm(hidden, gain, offset):
    centre = jnp.mean(hidden, -1, keepdims=True)
    shifted = hidden - centre
    spread = jnp.mean(shifted * shifted, -1, keepdims=True)
    return shifted * lax.rsqrt(spread + 1e-05) * gain + offset


def gelu_tanh(values):
    return jax.nn.gelu(values, approximate=True)


def visible(query_place, query_pass, key_place, key_pass, length):
    earlier = key_place[None, :] < query_place[:, None]
    allowed = earlier & (key_pass[None, :] <= query_pass[:, None]) & (key_place[None, :] < length)
    return allowed | (key_place[None, :] == query_place[:, None])


def masked_scores(query_part, key_part, factor, seen):
    raw = (
        jnp.einsum("qhd,khd->hqk", query_part, key_part, preferred_element_type=jnp.float32)
        * factor
    )
    return jnp.where(seen[None], raw, negative)


def split_blocks(arrays, block_len):
    return tuple(
        (
            array.reshape((array.shape[0] // block_len, block_len) + array.shape[1:])
            for array in arrays
        )
    )


def chance_of(query_part, key_part, log_part, seen, factor):
    scores = masked_scores(query_part, key_part, factor, seen)
    return jnp.where(seen[None], jnp.exp(scores - log_part[..., None]), 0.0)


def grad_pieces(query_part, dout_part, log_part, delta_part, key_part, value_part, seen, factor):
    chance = chance_of(query_part, key_part, log_part, seen, factor)
    dprob = jnp.einsum("qhd,khd->hqk", dout_part, value_part, preferred_element_type=jnp.float32)
    dscore = (chance * (dprob - delta_part[..., None])).astype(jnp.bfloat16)
    return (dscore, chance.astype(jnp.bfloat16))


def attend_row(queries, query_place, query_pass, key_rows, value_rows, key_pass, length):
    factor = queries.shape[-1] ** (-0.5)
    places = jnp.arange(key_rows.shape[0], dtype=jnp.int32)
    key_parts = split_blocks(
        (key_rows, value_rows, key_pass, places), min(key_block, key_rows.shape[0])
    )
    query_len = min(query_block, queries.shape[0])
    query_parts = split_blocks((queries, query_place, query_pass), query_len)

    def attend_one_block(query_args):
        query_part, place_part, pass_part = query_args

        def running(carry, key_args):
            peak, summed, total_out = carry
            key_part, value_part, kpass_part, kplace_part = key_args
            seen = visible(place_part, pass_part, kplace_part, kpass_part, length)
            scores = masked_scores(query_part, key_part, factor, seen)
            new_peak = jnp.maximum(peak, jnp.max(scores, -1))
            terms = jnp.where(seen[None], jnp.exp(scores - new_peak[..., None]), 0.0)
            rescale = jnp.exp(peak - new_peak)
            summed = summed * rescale + jnp.sum(terms, -1)
            added = jnp.einsum(
                "hqk,khd->qhd",
                terms.astype(jnp.bfloat16),
                value_part,
                preferred_element_type=jnp.float32,
            )
            total_out = total_out * rescale.T[..., None] + added
            return ((new_peak, summed, total_out), None)

        heads_n = query_part.shape[1]
        start = (
            jnp.full((heads_n, query_len), negative, jnp.float32),
            jnp.zeros((heads_n, query_len), jnp.float32),
            jnp.zeros(query_part.shape, jnp.float32),
        )
        (peak, summed, total_out), _ = lax.scan(running, start, key_parts)
        log_total = peak + jnp.log(summed)
        result = total_out / summed.T[..., None]
        return (result, log_total)

    results, log_totals = lax.map(attend_one_block, query_parts)
    heads_n = queries.shape[1]
    return (
        results.reshape(queries.shape),
        jnp.moveaxis(log_totals, 1, 0).reshape(heads_n, queries.shape[0]),
    )


def backward_row(
    queries,
    douts,
    outs_kept,
    log_totals,
    query_place,
    query_pass,
    key_rows,
    value_rows,
    key_pass,
    length,
):
    factor = queries.shape[-1] ** (-0.5)
    places = jnp.arange(key_rows.shape[0], dtype=jnp.int32)
    key_parts = split_blocks(
        (key_rows, value_rows, key_pass, places), min(key_block, key_rows.shape[0])
    )
    query_len = min(query_block, queries.shape[0])
    heads_n = queries.shape[1]
    block_count = queries.shape[0] // query_len
    log_parts = jnp.moveaxis(log_totals.reshape(heads_n, block_count, query_len), 1, 0)
    query_parts = split_blocks((queries, douts, outs_kept, query_place, query_pass), query_len)

    def backward_one_block(carry, query_args):
        query_part, dout_part, kept_part, place_part, pass_part, log_part = query_args
        delta_part = jnp.einsum("qhd,qhd->hq", dout_part.astype(jnp.float32), kept_part)

        def add_grads(dquery, key_args):
            key_part, value_part, kpass_part, kplace_part = key_args
            seen = visible(place_part, pass_part, kplace_part, kpass_part, length)
            dscore, low_chance = grad_pieces(
                query_part, dout_part, log_part, delta_part, key_part, value_part, seen, factor
            )
            dquery = dquery + factor * jnp.einsum(
                "hqk,khd->qhd", dscore, key_part, preferred_element_type=jnp.float32
            )
            dkey = factor * jnp.einsum(
                "hqk,qhd->khd", dscore, query_part, preferred_element_type=jnp.float32
            )
            dvalue = jnp.einsum(
                "hqk,qhd->khd", low_chance, dout_part, preferred_element_type=jnp.float32
            )
            return (dquery, (dkey, dvalue))

        dquery, key_terms = lax.scan(add_grads, jnp.zeros(query_part.shape, jnp.float32), key_parts)
        carry = (
            carry[0] + key_terms[0].reshape(key_rows.shape),
            carry[1] + key_terms[1].reshape(value_rows.shape),
        )
        return (carry, (dquery, delta_part))

    start = (jnp.zeros(key_rows.shape, jnp.float32), jnp.zeros(value_rows.shape, jnp.float32))
    key_sums, (dqueries, deltas) = lax.scan(backward_one_block, start, query_parts + (log_parts,))
    return (
        dqueries.reshape(queries.shape),
        jnp.moveaxis(deltas, 1, 0).reshape(heads_n, queries.shape[0]),
        key_sums,
    )


def local(
    block_input,
    lengths,
    pass_ids,
    pass_embed,
    ln1_gain,
    ln1_bias,
    w_qkv,
    w_out,
    ln2_gain,
    ln2_bias,
    w_up,
    b_up,
    w_down,
    b_down,
    cotangent,
):
    row_count, seg_len, width = block_input.shape
    heads_n = H
    head_size = width // heads_n
    onehot = (
        pass_ids[..., None] == jnp.arange(pass_embed.shape[0], dtype=jnp.int32)[None, None, :]
    ).astype(jnp.float32)
    hidden_in = block_input.astype(jnp.float32) + jnp.einsum(
        "rsp,pd->rsd", onehot, pass_embed, precision=highest
    )
    normed, norm_back = jax.vjp(layer_norm, hidden_in, ln1_gain, ln1_bias)
    normed_low = normed.astype(jnp.bfloat16)
    qkv = jnp.einsum("rsd,de->rse", normed_low, w_qkv, preferred_element_type=jnp.float32)
    queries = qkv[..., :width].astype(jnp.bfloat16)
    key_flat = qkv[..., width : 2 * width].astype(jnp.bfloat16)
    value_flat = qkv[..., 2 * width :].astype(jnp.bfloat16)
    pass_low = pass_ids.astype(jnp.bfloat16)
    key_all, value_all, pass_all = (
        lax.all_gather(key_flat, "seq", axis=1, tiled=True),
        lax.all_gather(value_flat, "seq", axis=1, tiled=True),
        lax.all_gather(pass_low, "seq", axis=1, tiled=True),
    )
    total_len = key_all.shape[1]
    key_all = key_all.reshape(row_count, total_len, heads_n, head_size)
    value_all = value_all.reshape(row_count, total_len, heads_n, head_size)
    pass_all = pass_all.astype(jnp.float32)
    offset = lax.axis_index("seq") * seg_len
    query_place = offset + jnp.arange(seg_len, dtype=jnp.int32)
    query_pass = pass_ids.astype(jnp.float32)
    query_heads = queries.reshape(row_count, seg_len, heads_n, head_size)
    attended_rows = []
    log_rows = []
    for row in range(row_count):
        attended, log_total = attend_row(
            query_heads[row],
            query_place,
            query_pass[row],
            key_all[row],
            value_all[row],
            pass_all[row],
            lengths[row],
        )
        attended_rows.append(attended)
        log_rows.append(log_total)
    attended_low = jnp.stack(attended_rows).astype(jnp.bfloat16).reshape(row_count, seg_len, width)
    branch = jnp.einsum("rsd,de->rse", attended_low, w_out, preferred_element_type=jnp.float32)
    middle = hidden_in + branch
    normed2, norm2_back = jax.vjp(layer_norm, middle, ln2_gain, ln2_bias)
    normed2_low = normed2.astype(jnp.bfloat16)
    pre_act = (
        jnp.einsum("rsd,df->rsf", normed2_low, w_up, preferred_element_type=jnp.float32) + b_up
    )
    active, active_back = jax.vjp(gelu_tanh, pre_act)
    active_low = active.astype(jnp.bfloat16)
    result = (
        middle
        + jnp.einsum("rsf,fd->rsd", active_low, w_down, preferred_element_type=jnp.float32)
        + b_down
    )
    output = result.astype(jnp.bfloat16)
    cot_f = cotangent.astype(jnp.float32)
    grad_active = jnp.einsum("rsd,fd->rsf", cotangent, w_down, preferred_element_type=jnp.float32)
    grad_w_down = jnp.einsum(
        "rsf,rsd->fd", active_low, cotangent, preferred_element_type=jnp.float32
    )
    grad_b_down = jnp.sum(cot_f, (0, 1))
    grad_pre = active_back(grad_active)[0].astype(jnp.bfloat16)
    grad_b_up = jnp.sum(grad_pre.astype(jnp.float32), (0, 1))
    grad_w_up = jnp.einsum("rsd,rsf->df", normed2_low, grad_pre, preferred_element_type=jnp.float32)
    grad_normed2 = jnp.einsum("rsf,df->rsd", grad_pre, w_up, preferred_element_type=jnp.float32)
    grad_mid_norm, grad_ln2_gain, grad_ln2_bias = norm2_back(grad_normed2)
    grad_middle = cot_f + grad_mid_norm
    grad_branch = grad_middle.astype(jnp.bfloat16)
    grad_w_out = jnp.einsum(
        "rsd,rse->de", attended_low, grad_branch, preferred_element_type=jnp.float32
    )
    grad_attended = jnp.einsum(
        "rse,de->rsd", grad_branch, w_out, preferred_element_type=jnp.float32
    ).astype(jnp.bfloat16)
    dout_heads = grad_attended.reshape(row_count, seg_len, heads_n, head_size)
    dquery_rows = []
    dkey_rows = []
    dvalue_rows = []
    for row in range(row_count):
        dquery, _, key_sums = backward_row(
            query_heads[row],
            dout_heads[row],
            attended_rows[row],
            log_rows[row],
            query_place,
            query_pass[row],
            key_all[row],
            value_all[row],
            pass_all[row],
            lengths[row],
        )
        dquery_rows.append(dquery)
        dkey_rows.append(key_sums[0].reshape(total_len, width))
        dvalue_rows.append(key_sums[1].reshape(total_len, width))
    dkey_sum, dvalue_sum = (
        lax.psum_scatter(
            jnp.stack(dkey_rows).astype(jnp.bfloat16), "seq", scatter_dimension=1, tiled=True
        ).astype(jnp.float32),
        lax.psum_scatter(
            jnp.stack(dvalue_rows).astype(jnp.bfloat16), "seq", scatter_dimension=1, tiled=True
        ).astype(jnp.float32),
    )
    dquery_all = jnp.stack(dquery_rows).reshape(row_count, seg_len, width)
    grad_qkv = jnp.concatenate(
        [
            dquery_all.astype(jnp.bfloat16),
            dkey_sum.astype(jnp.bfloat16),
            dvalue_sum.astype(jnp.bfloat16),
        ],
        -1,
    )
    grad_w_qkv = jnp.einsum("rsd,rse->de", normed_low, grad_qkv, preferred_element_type=jnp.float32)
    grad_normed = jnp.einsum("rse,de->rsd", grad_qkv, w_qkv, preferred_element_type=jnp.float32)
    grad_in_norm, grad_ln1_gain, grad_ln1_bias = norm_back(grad_normed)
    grad_hidden = grad_middle + grad_in_norm
    grad_input = grad_hidden.astype(jnp.bfloat16)
    grad_pass = jnp.einsum("rsp,rsd->pd", onehot, grad_hidden, precision=highest)
    matrices = (
        lax.psum_scatter(
            grad_w_qkv.astype(jnp.bfloat16), "seq", scatter_dimension=0, tiled=True
        ).astype(jnp.float32),
        lax.psum_scatter(
            grad_w_out.astype(jnp.bfloat16), "seq", scatter_dimension=0, tiled=True
        ).astype(jnp.float32),
        lax.psum_scatter(
            grad_w_up.astype(jnp.bfloat16), "seq", scatter_dimension=0, tiled=True
        ).astype(jnp.float32),
        lax.psum_scatter(
            grad_w_down.astype(jnp.bfloat16), "seq", scatter_dimension=0, tiled=True
        ).astype(jnp.float32),
    )
    matrices = (
        lax.psum_scatter(
            matrices[0].astype(jnp.bfloat16), "batch", scatter_dimension=1, tiled=True
        ).astype(jnp.float32),
        lax.psum_scatter(
            matrices[1].astype(jnp.bfloat16), "batch", scatter_dimension=1, tiled=True
        ).astype(jnp.float32),
        lax.psum_scatter(
            matrices[2].astype(jnp.bfloat16), "batch", scatter_dimension=1, tiled=True
        ).astype(jnp.float32),
        lax.psum_scatter(
            matrices[3].astype(jnp.bfloat16), "batch", scatter_dimension=1, tiled=True
        ).astype(jnp.float32),
    )
    vectors = lax.psum(
        (
            grad_pass,
            grad_ln1_gain,
            grad_ln1_bias,
            grad_ln2_gain,
            grad_ln2_bias,
            grad_b_up,
            grad_b_down,
        ),
        ("seq", "batch"),
    )
    return (
        output,
        grad_input,
        vectors[0],
        vectors[1],
        vectors[2],
        matrices[0],
        matrices[1],
        vectors[3],
        vectors[4],
        matrices[2],
        vectors[5],
        matrices[3],
        vectors[6],
    )


NN = (((1,), (0,)), ((), ()))
NT = (((1,), (1,)), ((), ()))
TN = (((0,), (0,)), ((), ()))
vmem_bytes = 60 << 20
block = 256


def dot(left, right, form):
    return lax.dot_general(left, right, form, preferred_element_type=jnp.float32)


mesh_ids = pl.DeviceIdType.MESH


def block_kernel(
    lengths,
    block_in, cot_in, w_up_in, w_qkv_in, w_out_in, w_down_in,
    pass_in, embed_in, gain1, bias1, gain2, bias2, b_up_in, b_down_in,
    out, gin, vector, gqkv, gout, gup, gdown,
    kept_far, h_far,
    mid, keep, at, qkv, otf, ct, mt, gd, far, dm, kept, w_out, w_up, w_down,
    bsum, r1a, r2a, r1c, r2c, r2e, r3e, rz, rze,
    osend, orecv, hand, sums, gpass, vrecv, ksum, vsum, stage_send, stage_recv, down_recv,
    params, vecs, bcol, inv, prow, kmask, qhot, passes,
    lsem, ssem, rsem,
    *, chunks, plan,
):
    seq, bat = lax.axis_index("seq"), lax.axis_index("batch")
    x, core = seq // 2, seq % 2
    z, y = bat // 2, bat % 2
    to_core, to_x, to_y = (seq + 1 - 2 * core, bat), (seq + 2 - 4 * x, bat), (seq, bat + 1 - 2 * y)
    to_cross = (3 - seq, bat)
    to_z = [(seq, ((z + i) % 4) * 2 + y) for i in (1, 2, 3)]
    up_z, low_z = (seq, bat + 2), (seq, bat - 2)

    barrier = pltpu.get_barrier_semaphore()
    for peer in [to_core, to_x, to_y, to_cross] + to_z:
        pl.semaphore_signal(barrier, inc=1, device_id=peer, device_id_type=mesh_ids)

    width, total = mid.shape
    half = width // 2
    inner = w_up.shape[0]
    blocks_n = total // block
    heads = half // 64
    bs = 8

    def rows_at(first, count):
        return pl.ds(pl.multiple_of(first, 16), count)

    def lanes_at(first, count):
        return pl.ds(pl.multiple_of(first, 128), count)

    def own_cols(k):
        return lanes_at(core * block + k * 2 * block, block)

    def local(i, src, dst):
        return pltpu.make_async_copy(src, dst, lsem.at[i])

    def remote(i, src, dst, peer):
        return pltpu.make_async_remote_copy(
            src_ref=src, dst_ref=dst, send_sem=ssem.at[i], recv_sem=rsem.at[i],
            device_id=peer, device_id_type=mesh_ids,
        )

    part = w_down_in.shape[2]
    own_x = local(0, block_in.at[x], far.at[0:block, 0:width])
    own_c = local(1, cot_in.at[x], dm.at[0:block, 0:width])
    out_load = local(2, w_out_in, w_out)
    up_loads = [
        local(3 + p, w_up_in.at[:, p * width : (p + 1) * width],
              gd.at[p * width : (p + 1) * width, 0:width])
        for p in range(4)
    ]
    down_loads = [
        local(7 + i, w_down_in.at[i, core], w_down.at[i * part : (i + 1) * part, :])
        for i in range(bs)
    ]
    qkv_loads = [
        local(15 + j, w_qkv_in.at[:, j * width : (j + 1) * width],
              gd.at[j * width : (j + 1) * width, 0:width])
        for j in range(3)
    ]
    for load in [own_x] + up_loads + [own_c, out_load] + down_loads:
        load.start()

    base = 22 * len(chunks)
    x_far = remote(base, block_in.at[1 - x], far.at[block : 2 * block, 0:width], to_x)
    x_near = remote(base + 1, block_in.at[x], far.at[2 * block : 3 * block, 0:width], to_core)
    x_cross = remote(
        base + 2, far.at[block : 2 * block, 0:width], far.at[3 * block : 4 * block, 0:width], to_core
    )
    c_far = remote(base + 3, cot_in.at[1 - x], dm.at[block : 2 * block, 0:width], to_x)
    c_near = remote(base + 4, cot_in.at[x], dm.at[2 * block : 3 * block, 0:width], to_core)
    c_cross = remote(
        base + 5, dm.at[block : 2 * block, 0:width], dm.at[3 * block : 4 * block, 0:width], to_core
    )
    p_far = remote(base + 6, pass_in, passes.at[1], to_x)
    p_near = remote(base + 7, pass_in, passes.at[2], to_core)
    p_cross = remote(base + 8, pass_in, passes.at[3], to_cross)
    base += 9
    pl.semaphore_wait(barrier, 7)
    for copy in (p_far, x_far, x_near, p_near, p_cross, c_near):
        copy.start()


    def line_copy(i, d, up, part, slots):
        slot = d if up else jnp.where(z - 1 == d, 4, d)
        return remote(i + (d if up else 4 + d), part(d), slots(slot), up_z if up else low_z)

    def line_add(d, slot, part, slots):
        here, got = part(d), slots(slot)
        here[...] = here[...] + got[...]

    def line_start(i, part, slots):
        @pl.when(z == 0)
        def _():
            for d in (3, 2, 1):
                line_copy(i, d, True, part, slots).start()

        @pl.when(z == 3)
        def _():
            for d in (0, 1, 2):
                line_copy(i, d, False, part, slots).start()

    def line_pass(i, d, up, part, slots):
        copy = line_copy(i, d, up, part, slots)
        copy.wait_recv()
        line_add(d, d, part, slots)
        copy.start()

    def line_one(i, part, slots):
        @pl.when(z == 1)
        def _():
            line_pass(i, 3, True, part, slots)

        @pl.when(z == 2)
        def _():
            line_pass(i, 0, False, part, slots)

    def line_two(i, part, slots):
        @pl.when(z == 1)
        def _():
            line_pass(i, 2, True, part, slots)
            line_pass(i, 0, False, part, slots)

        @pl.when(z == 2)
        def _():
            line_pass(i, 1, False, part, slots)
            line_pass(i, 3, True, part, slots)

    def line_last(i, part, slots):
        for d in range(4):

            @pl.when(z == d)
            def _():
                if d > 0:
                    line_copy(i, d, True, part, slots).wait_recv()
                    line_add(d, d, part, slots)
                if d < 3:
                    line_copy(i, d, False, part, slots).wait_recv()
                    line_add(d, 4, part, slots)
                for e in range(4):
                    if e > d:
                        line_copy(i, e, True, part, slots).wait_send()
                    if e < d:
                        line_copy(i, e, False, part, slots).wait_send()

    class Chunk:
        def __init__(self, k):
            r0, rc, ra, r1, a0, c0, e0 = chunks[k]
            ne, nc, na = rc - r0, ra - rc, r1 - ra
            i = 22 * k
            rows_e, rows_c, rows_a = pl.ds(r0, ne), pl.ds(rc, nc), pl.ds(ra, na)
            got_a, got_c, got_e = pl.ds(a0, na), pl.ds(c0, nc), pl.ds(e0, ne)
            sub = bsum.at
            self.one_a = remote(i, sub[1 - x, :, :, rows_a, :], r1a.at[:, :, got_a, :], to_x)
            self.one_c = remote(i + 1, sub[:, :, 1 - y, rows_c, :], r1c.at[:, :, got_c, :], to_y)
            self.two_a = remote(i + 2, sub[x, :, 1 - y, rows_a, :], r2a.at[:, got_a, :], to_y)
            self.two_c = remote(i + 3, sub[1 - x, :, y, rows_c, :], r2c.at[:, got_c, :], to_x)
            self.two_e = remote(i + 4, sub[:, z, 1 - y, rows_e, :], r2e.at[:, got_e, :], to_y)
            self.three_e = remote(i + 5, sub[1 - x, z, y, rows_e, :], r3e.at[got_e, :], to_x)
            self.adds = [
                (sub[x, :, :, rows_a, :], r1a.at[:, :, got_a, :]),
                (sub[:, :, y, rows_c, :], r1c.at[:, :, got_c, :]),
                (sub[x, :, y, rows_a, :], r2a.at[:, got_a, :]),
                (sub[x, :, y, rows_c, :], r2c.at[:, got_c, :]),
                (sub[:, z, y, rows_e, :], r2e.at[:, got_e, :]),
                (sub[x, z, y, rows_e, :], r3e.at[got_e, :]),
            ]
            both, low = pl.ds(rc, na + nc), pl.ds(a0 + c0, na + nc)
            self.line_ac = (
                i + 6, lambda d: sub[x, d, y, both, :], lambda s: rz.at[s, low, :]
            )
            self.line_e = (
                i + 14, lambda d: sub[:, d, :, rows_e, :], lambda s: rze.at[s, :, :, got_e, :]
            )

        def add(self, j):
            here, got = self.adds[j]
            here[...] = here[...] + got[...]

        def start(self):
            line_start(*self.line_e)
            self.one_c.start()
            self.one_a.start()

        def start_a(self):
            self.one_a.start()

        def start_c(self):
            self.one_c.start()

        def start_e(self):
            line_start(*self.line_e)

        def e1(self):
            line_one(*self.line_e)

        def e2(self):
            line_two(*self.line_e)

        def e3(self):
            line_last(*self.line_e)
            self.two_e.start()

        def a2(self):
            self.one_a.wait()
            self.add(0)
            self.two_a.start()

        def c2(self):
            self.one_c.wait()
            self.add(1)
            self.two_c.start()

        def e4(self):
            self.two_e.wait()
            self.add(4)
            self.three_e.start()

        def z0(self):
            self.two_a.wait()
            self.add(2)
            self.two_c.wait()
            self.add(3)
            line_start(*self.line_ac)

        def z1(self):
            line_one(*self.line_ac)

        def z2(self):
            line_two(*self.line_ac)

        def z3(self):
            line_last(*self.line_ac)
            self.three_e.wait()
            self.add(5)
    steps = [Chunk(k) for k in range(len(chunks))]

    def serve(slot):
        for k, name in plan[slot]:
            getattr(steps[k], name)()

    params[...] = jnp.zeros_like(params)
    params[0:5, :] = embed_in[...]
    for i, ref in enumerate((gain1, bias1, gain2, bias2, b_down_in)):
        params[5 + i, :] = ref[...]
    for i in range(4):
        params[10 + i, :] = b_up_in[pl.ds(i * width, width)]
    vecs[...] = jnp.transpose(params[...])
    for b in range(bs):
        i, low = 10 + b // 2, b % 2 * 2 * part
        bcol[b * part : (b + 1) * part, :] = jnp.broadcast_to(
            jnp.where(
                core == 0,
                vecs[low : low + part, i : i + 1],
                vecs[low + part : low + 2 * part, i : i + 1],
            ),
            (part, 8),
        )
    for b in range(bs):
        p, low = b // 2, b % 2 * 2 * part
        if b % 2 == 0:
            up_loads[p].wait()
        turned = jnp.transpose(gd[p * width : (p + 1) * width, low : low + 2 * part])
        w_up[b * part : (b + 1) * part, :] = jnp.where(core == 0, turned[:part], turned[part:])
    for load in qkv_loads:
        load.start()
    passes[0] = pass_in[...]
    places = (2 * x + core, 2 * (1 - x) + core, 2 * x + 1 - core, 2 * (1 - x) + 1 - core)
    length = lengths[x]
    emb = jnp.where(lax.broadcasted_iota(jnp.int32, (8, width), 0) < 5, params[0:8, :], 0.0)
    emb_a = emb.astype(jnp.bfloat16)
    rest = emb - emb_a.astype(jnp.float32)
    emb_b = rest.astype(jnp.bfloat16)
    emb_c = (rest - emb_b.astype(jnp.float32)).astype(jnp.bfloat16)

    def take(k):
        cols = lanes_at(places[k] * block, block)
        rows = rows_at(places[k] * block, block)
        got = passes[k]
        line = jnp.where(x == 0, got[0:1, :], got[1:2, :])
        prow[:, cols] = jnp.broadcast_to(line.astype(jnp.float32), (8, block))
        kind = lax.broadcasted_iota(jnp.int32, (16, block), 0)
        spot = lax.broadcasted_iota(jnp.int32, (16, block), 1) + places[k] * block
        onehot = jnp.where(kind == line, 1.0, 0.0).astype(jnp.bfloat16)
        qhot[:, cols] = onehot
        hidden = jnp.where((line > kind) | (spot >= length), negative, 0.0)
        kmask[rows, :] = jnp.transpose(hidden).astype(jnp.bfloat16)
        hot = onehot[0:8, :]
        added = dot(emb_a, hot, TN) + dot(emb_b, hot, TN) + dot(emb_c, hot, TN)
        h = jnp.transpose(far[k * block : (k + 1) * block, 0:width]).astype(jnp.float32) + added
        mid[:, cols] = h
        shifted = h - jnp.sum(h, 0, keepdims=True) * (1.0 / width)
        spread = jnp.sum(shifted * shifted, 0, keepdims=True) * (1.0 / width)
        scaled = shifted * lax.rsqrt(spread + 1e-05)
        at[:, cols] = (scaled * vecs[:, 5:6] + vecs[:, 6:7]).astype(jnp.bfloat16)
        for j in range(3):
            res = dot(
                gd[j * width : (j + 1) * width, lanes_at(core * half, half)], at[:, cols], TN
            ).astype(jnp.bfloat16)
            qkv[j * half : (j + 1) * half, cols] = res * jnp.bfloat16(0.125) if j == 0 else res

    own_x.wait()
    for load in qkv_loads:
        load.wait()
    take(0)
    x_near.wait()
    p_near.wait()
    take(2)
    p_far.wait()
    x_far.wait()
    x_cross.start()
    c_far.start()
    take(1)
    x_cross.wait()
    p_cross.wait()
    take(3)
    h_saves = [local(18 + k, mid.at[:, own_cols(k)], h_far.at[k]) for k in range(2)]
    for save in h_saves:
        save.start()

    for qb in range(blocks_n):
        cols = slice(qb * block, (qb + 1) * block)
        key = lax.broadcasted_iota(jnp.int32, (block, block), 0)
        place = lax.broadcasted_iota(jnp.int32, (block, block), 1)
        cover = dot(kmask[cols, :], qhot[:, cols], NN)
        cover = jnp.where(key < place, cover, negative)
        at_row, at_col = qb // 2 * block, qb % 2 * block
        keep[at_row : at_row + block, at_col : at_col + block] = jnp.where(key == place, 0.0, cover)

    def kept_save(h, slot):
        return pltpu.make_async_copy(kept.at[slot], kept_far.at[h], lsem.at[20 + slot])

    def o_copy(h):
        mine = rows_at(core * half + h * 64, 64)
        return remote(base + h, otf.at[mine, :], otf.at[mine, :], to_core)

    def turn(k):
        ct[:, lanes_at(places[k] * block, block)] = jnp.transpose(
            dm[k * block : (k + 1) * block, 0:width]
        )

    def one_head(h, carry):
        slot = h % 2

        @pl.when(h >= 2)
        def _():
            kept_save(h - 2, slot).wait()

        qrow, krow, vrow = (rows_at(j * half + h * 64, 64) for j in range(3))
        mine = rows_at(core * half + h * 64, 64)
        keyn = jnp.concatenate([jnp.transpose(qkv[krow, :]), kmask[...]], 1)
        query = jnp.concatenate([qkv[qrow, :], qhot[...]], 0)
        for qb in range(blocks_n):
            below, n = qb * block, (qb + 1) * block
            at_row = qb * (qb + 1) // 2 * block
            cols = slice(below, n)
            to_row, to_col = qb // 2 * block, qb % 2 * block
            diag = dot(keyn[cols, 0:64], query[0:64, cols], NN)
            diag = diag + keep[to_row : to_row + block, to_col : to_col + block]
            peak = jnp.max(diag, 0, keepdims=True)
            if qb:
                scores = dot(keyn[0:below, :], query[:, cols], NN)
                peak = jnp.maximum(peak, jnp.max(scores, 0, keepdims=True))
                expo = jnp.exp(scores - peak)
                count = jnp.sum(expo, 0, keepdims=True)
                kept[slot, at_row : at_row + below, :] = expo.astype(jnp.bfloat16)
            last = jnp.exp(diag - peak)
            kept[slot, at_row + below : at_row + n, :] = last.astype(jnp.bfloat16)
            last_sum = jnp.sum(last, 0, keepdims=True)
            over = 1.0 / (count + last_sum if qb else last_sum)
            inv[h, :, cols] = jnp.broadcast_to(over, (8, block))
            result = dot(qkv[vrow, 0:n], kept[slot, at_row : at_row + n, :], NN) * over
            otf[mine, cols] = result.astype(jnp.bfloat16)
        kept_save(h, slot).start()

        @pl.when(h == heads - 2)
        def _():
            c_near.wait()
            c_far.wait()
            c_cross.start()
            own_c.wait()
            for k in (0, 2, 1):
                turn(k)

        @pl.when(h == heads - 1)
        def _():
            c_cross.wait()
            turn(3)

        o_copy(h).start()
        return carry

    lax.fori_loop(0, heads, one_head, 0)
    kept_save(heads - 2, heads % 2).wait()
    kept_save(heads - 1, (heads - 1) % 2).wait()

    def kept_load(h, slot):
        return pltpu.make_async_copy(kept_far.at[h], kept.at[slot], lsem.at[22 + slot])

    kept_load(0, 0).start()
    kept_load(1, 1).start()
    for h in range(heads):
        o_copy(h).wait()
    base += heads

    for save in h_saves:
        save.wait()
    out_load.wait()

    def mix(i, carry):
        cols = lanes_at(i * block, block)
        m = mid[:, cols] + dot(w_out[...], otf[:, cols], TN)
        mid[:, cols] = m
        shifted = m - jnp.sum(m, 0, keepdims=True) * (1.0 / width)
        spread = jnp.sum(shifted * shifted, 0, keepdims=True) * (1.0 / width)
        scaled = shifted * lax.rsqrt(spread + 1e-05)
        mt[:, cols] = (scaled * vecs[:, 7:8] + vecs[:, 8:9]).astype(jnp.bfloat16)
        return carry

    lax.fori_loop(0, blocks_n, mix, 0)

    def hidden_at(first):
        def hidden(i, carry):
            rows = rows_at(first + i * part, part)
            below = rows_at(inner + first + i * part, part)
            u = dot(w_up[rows, :], mt[...], NN) + bcol[rows, 0:1]
            square = u * u
            t = jnp.tanh(u * (0.7978845608028654 + 0.035677408136300125 * square))
            gate = 0.5 + 0.5 * t
            gd[rows, :] = (u * gate).astype(jnp.bfloat16)
            slope = gate + (0.5 * u) * (1.0 - t * t) * (
                0.7978845608028654 + 0.10703222440890037 * square
            )
            gd[below, :] = slope.astype(jnp.bfloat16)
            return carry

        lax.fori_loop(0, 2, hidden, 0)

    lanes = bsum.shape[-1]
    band = width // bs
    for j in range(2):
        for xx in range(2):
            at_row = (2 * xx + j) * lanes
            hidden_at(at_row)
            grad = dot(ct[...], gd[at_row : at_row + lanes, :], NT).astype(jnp.bfloat16)
            for b in range(bs):
                bsum[xx, b // 2, b % 2, j * band : (j + 1) * band, :] = grad[
                    b * band : (b + 1) * band, :
                ]
        serve("down%d" % j)
    for load in down_loads:
        load.wait()

    def hidden_back(i, carry):
        rows = rows_at(i * part, part)
        below = rows_at(inner + i * part, part)
        back = dot(w_down[rows, :], ct[...], NN)
        gd[below, :] = (back * gd[below, :].astype(jnp.float32)).astype(jnp.bfloat16)
        return carry

    lax.fori_loop(0, bs, hidden_back, 0)
    serve("hidden")

    dm_copy = remote(base, dm.at[0:width, :], dm.at[width : 2 * width, :], to_core)

    def back_up(i, carry):
        cols = lanes_at(i * block, block)
        dm[0:width, cols] = dot(w_up[...], gd[inner : 2 * inner, cols], TN).astype(jnp.bfloat16)
        return carry

    lax.fori_loop(0, blocks_n, back_up, 0)
    dm_copy.start()
    serve("dm")
    first_up = 2 * band
    up_band = part
    for xx in range(2):
        for i in range(2):
            low, high = inner + i * inner // 2, inner + (i + 1) * inner // 2
            grad = dot(gd[low:high, :], mt[xx * lanes : (xx + 1) * lanes, :], NT)
            grad = grad.astype(jnp.bfloat16)
            for b in range(bs // 2):
                bb = i * bs // 2 + b
                bsum[xx, bb // 2, bb % 2, first_up : first_up + up_band, :] = grad[
                    b * up_band : (b + 1) * up_band, :
                ]
        serve("up%d" % xx)
    ones = jnp.ones((8, total), jnp.bfloat16)
    up_sum = dot(ones, gd[inner : 2 * inner, :], NT)
    vector[...] = jnp.zeros_like(vector)
    for i in range(4):
        one, two = (up_sum[0:1, (2 * i + e) * part : (2 * i + e + 1) * part] for e in range(2))
        none = jnp.zeros_like(one)
        vector[10 + i : 11 + i, :] = jnp.where(
            core == 0,
            jnp.concatenate([one, none, two, none], 1),
            jnp.concatenate([none, one, none, two], 1),
        )

    out_copy = remote(base + 1, osend, orecv, to_core)
    for k in range(2):
        other = lanes_at((1 - core) * block + k * 2 * block, block)
        to = slice(k * block, (k + 1) * block)
        osend[:, to] = dot(w_down[...], gd[0:inner, other], TN).astype(jnp.bfloat16)
        keep[:, to] = mid[:, own_cols(k)] + vecs[:, 9:10] + dot(
            w_down[...], gd[0:inner, own_cols(k)], TN
        )
    out_copy.start()
    serve("out")

    dm_copy.wait()
    sums[...] = jnp.zeros_like(sums)

    def middle(i, carry):
        cols = lanes_at(i * block, block)
        cot = ct[:, cols].astype(jnp.float32)
        m = mid[:, cols]
        shifted = m - jnp.sum(m, 0, keepdims=True) * (1.0 / width)
        spread = jnp.sum(shifted * shifted, 0, keepdims=True) * (1.0 / width)
        r = lax.rsqrt(spread + 1e-05)
        n = shifted * r
        d = dm[0:width, cols].astype(jnp.float32) + dm[width : 2 * width, cols].astype(jnp.float32)
        e = d * vecs[:, 7:8]
        mean_e = jnp.sum(e, 0, keepdims=True) * (1.0 / width)
        mean_en = jnp.sum(e * n, 0, keepdims=True) * (1.0 / width)
        dmid = cot + r * (e - mean_e - n * mean_en)
        mid[:, cols] = dmid
        dm[width : 2 * width, cols] = dmid.astype(jnp.bfloat16)
        sums[:, 0:1] += jnp.sum(d * n, 1, keepdims=True)
        sums[:, 1:2] += jnp.sum(d, 1, keepdims=True)
        sums[:, 2:3] += jnp.sum(cot, 1, keepdims=True)
        return carry

    lax.fori_loop(0, blocks_n, middle, 0)
    serve("middle")
    small = band // 2
    for b in range(bs):
        dm[half + b * small : half + (b + 1) * small, :] = dm[
            rows_at(width + b * band + core * small, small), :
        ]
    first_out = first_up + up_band
    for xx in range(2):
        grad = dot(dm[half:width, :], otf[xx * lanes : (xx + 1) * lanes, :], NT)
        grad = grad.astype(jnp.bfloat16)
        for b in range(bs):
            bsum[xx, b // 2, b % 2, first_out : first_out + small, :] = grad[
                b * small : (b + 1) * small, :
            ]
    dm[0:half, :] = dot(
        w_out[rows_at(core * half, half), :], dm[width : 2 * width, :], NN
    ).astype(jnp.bfloat16)
    serve("w_out")

    whole_loads = [
        local(24, w_qkv_in.at[:, 0:width], w_up.at[0:width, :]),
        local(25, w_qkv_in.at[:, width : 2 * width], w_up.at[width : 2 * width, :]),
        local(26, w_qkv_in.at[:, 2 * width : 3 * width], w_down.at[0:width, :]),
    ]
    for load in whole_loads:
        load.start()
    hand_out = remote(base + 2, hand.at[0], out.at[x], to_x)

    def give_output():
        out_copy.wait()
        for k in range(2):
            cols = slice(k * block, (k + 1) * block)
            rows = jnp.transpose(
                (keep[:, cols] + orecv[:, cols].astype(jnp.float32)).astype(jnp.bfloat16)
            )

            @pl.when(x == k)
            def _():
                out[k] = rows

            @pl.when(x != k)
            def _():
                hand[0] = rows

        hand_out.start()

    def far_copy(h, j):
        mine = rows_at(j * width + core * half + h * 64, 64)
        return remote(
            base + 3 + h * 3 + j, gd.at[mine, :], far.at[rows_at(j * half + h * 64, 64), :], to_core
        )

    def head_back(h, carry):
        slot = h % 2
        kept_load(h, slot).wait()
        qrow, krow, vrow = (rows_at(j * half + h * 64, 64) for j in range(3))
        mine = [rows_at(j * width + core * half + h * 64, 64) for j in range(3)]
        valn = jnp.transpose(qkv[vrow, :])
        grads = (dm[rows_at(h * 64, 64), :].astype(jnp.float32) * inv[h, 0:1, :]).astype(
            jnp.bfloat16
        )
        o_rows = otf[rows_at(core * half + h * 64, 64), :]
        delta = jnp.sum(grads.astype(jnp.float32) * o_rows.astype(jnp.float32), 0, keepdims=True)
        ksum[...] = jnp.zeros_like(ksum)
        vsum[...] = jnp.zeros_like(vsum)
        for qb in range(blocks_n):
            n = (qb + 1) * block
            at_row = qb * (qb + 1) // 2 * block
            cols = slice(qb * block, n)
            low = kept[slot, at_row : at_row + n, :]
            dprob = dot(valn[0:n, :], grads[:, cols], NN)
            dscore = (low.astype(jnp.float32) * (dprob - delta[:, cols])).astype(jnp.bfloat16)
            gd[mine[0], cols] = (dot(qkv[krow, 0:n], dscore, NN) * 0.125).astype(jnp.bfloat16)
            ksum[:, 0:n] += dot(qkv[qrow, cols], dscore, NT)
            vsum[:, 0:n] += dot(grads[:, cols], low, NT)
        gd[mine[1], :] = ksum[...].astype(jnp.bfloat16)
        gd[mine[2], :] = vsum[...].astype(jnp.bfloat16)
        for j in range(3):
            far_copy(h, j).start()

        @pl.when(h + 2 < heads)
        def _():
            kept_load(h + 2, slot).start()

        for at_head in range(heads):

            @pl.when(h == at_head)
            def _():
                serve("head%d" % at_head)

        return carry

    lax.fori_loop(0, heads, head_back, 0)
    give_output()
    serve("given")
    own_loads = [local(18 + k, h_far.at[k], keep.at[:, k * block : (k + 1) * block]) for k in range(2)]
    for load in own_loads:
        load.start()

    for h in range(heads):
        for j in range(3):
            far_copy(h, j).wait()
    for j in range(3):
        gd[rows_at(j * width + (1 - core) * half, half), :] = far[j * half : (j + 1) * half, :]
    qkv_band = 3 * width // bs
    qkv_small = qkv_band // 2
    for b in range(bs):
        dm[b * qkv_small : (b + 1) * qkv_small, :] = gd[
            rows_at(b * qkv_band + core * qkv_small, qkv_small), :
        ]
    first_qkv = first_out + small
    for xx in range(2):
        grad = dot(dm[0 : bs * qkv_small, :], at[xx * lanes : (xx + 1) * lanes, :], NT)
        grad = grad.astype(jnp.bfloat16)
        for b in range(bs):
            bsum[xx, b // 2, b % 2, first_qkv : first_qkv + qkv_small, :] = grad[
                b * qkv_small : (b + 1) * qkv_small, :
            ]
    serve("qkv")

    for load in whole_loads + own_loads:
        load.wait()
    gpass[...] = jnp.zeros_like(gpass)
    hand_in = remote(base + 21, hand.at[1], gin.at[x], to_x)
    for k in range(2):
        mine = own_cols(k)
        da = dot(w_up[0:width, :], gd[0:width, mine], NN)
        da += dot(w_up[width : 2 * width, :], gd[width : 2 * width, mine], NN)
        da += dot(w_down[0:width, :], gd[2 * width : 3 * width, mine], NN)
        h = keep[:, k * block : (k + 1) * block]
        shifted = h - jnp.sum(h, 0, keepdims=True) * (1.0 / width)
        spread = jnp.sum(shifted * shifted, 0, keepdims=True) * (1.0 / width)
        r = lax.rsqrt(spread + 1e-05)
        n = shifted * r
        e = da * vecs[:, 5:6]
        mean_e = jnp.sum(e, 0, keepdims=True) * (1.0 / width)
        mean_en = jnp.sum(e * n, 0, keepdims=True) * (1.0 / width)
        dh = mid[:, mine] + r * (e - mean_e - n * mean_en)
        rows = jnp.transpose(dh).astype(jnp.bfloat16)

        @pl.when(x == k)
        def _():
            gin[k] = rows

        @pl.when(x != k)
        def _():
            hand[1] = rows
            hand_in.start()

        sums[:, 3:4] += jnp.sum(da * n, 1, keepdims=True)
        sums[:, 4:5] += jnp.sum(da, 1, keepdims=True)
        kind = lax.broadcasted_iota(jnp.int32, (16, block), 0).astype(jnp.float32)
        onehot = jnp.where(kind == prow[0:1, mine], 1.0, 0.0).astype(jnp.bfloat16)
        high = dh.astype(jnp.bfloat16)
        rest = dh - high.astype(jnp.float32)
        second_part = rest.astype(jnp.bfloat16)
        tail = (rest - second_part.astype(jnp.float32)).astype(jnp.bfloat16)
        gpass[...] += dot(onehot, high, NT) + dot(onehot, second_part, NT) + dot(onehot, tail, NT)
        serve("input%d" % k)

    lines = jnp.transpose(sums[...])
    vector[0:5, :] = gpass[0:5, :]
    vector[5:7, :] = lines[3:5, :]
    vector[7:10, :] = lines[0:3, :] * 0.5
    for i, peer in enumerate((to_core, to_x, to_y)):
        copy = remote(base + 22 + i, vector, vrecv.at[i], peer)
        copy.start()
        copy.wait()
        vector[...] = vector[...] + vrecv[i]
        serve("sum%d" % i)
    copies = [
        remote(base + 25 + i, vector, vrecv.at[3 + z], peer) for i, peer in enumerate(to_z)
    ]
    for copy in copies:
        copy.start()
    vrecv[3 + z] = vector[...]

    own_rows = down_recv.shape[0]
    down_copy = remote(
        base + 28, bsum.at[x, z, y, rows_at((1 - core) * own_rows, own_rows), :], down_recv, to_core
    )

    def swap_lanes(i, r0, r1):
        wide = lanes // 2
        v = bsum[x, z, y, r0:r1, :]
        stage_send[r0 - first_up : r1 - first_up, 0:wide] = jnp.where(
            core == 0, v[:, wide:lanes], v[:, 0:wide]
        )
        at_rows = slice(r0 - first_up, r1 - first_up)
        return remote(base + i, stage_send.at[at_rows, :], stage_recv.at[at_rows, :], to_core)

    def both_cores(mine, got):
        return jnp.where(core == 0, mine, got), jnp.where(core == 0, got, mine)

    def put(result, r0, r1):
        wide = lanes // 2
        v = bsum[x, z, y, r0:r1, :].astype(jnp.float32)
        mine = jnp.where(core == 0, v[:, 0:wide], v[:, wide:lanes])
        got = stage_recv[r0 - first_up : r1 - first_up, 0:wide].astype(jnp.float32)
        result[...] = jnp.transpose(jnp.concatenate(both_cores(mine, got), 0))

    serve("end0")
    down_copy.start()
    serve("end1")
    up_copy = swap_lanes(29, first_up, first_qkv)
    up_copy.start()
    serve("end2")
    qkv_copy = swap_lanes(30, first_qkv, first_qkv + qkv_small)
    qkv_copy.start()
    down_copy.wait()
    mine = bsum[x, z, y, rows_at(core * own_rows, own_rows), :].astype(jnp.float32)
    for c, piece in enumerate(both_cores(mine, down_recv[...].astype(jnp.float32))):
        for i in range(lanes // part):
            at_row = (2 * i + c) * part
            gdown[:, at_row : at_row + part] = piece[:, i * part : (i + 1) * part]
    up_copy.wait()
    put(gup, first_up, first_out)
    put(gout, first_out, first_qkv)
    for copy in copies:
        copy.wait()
    vector[...] = (vrecv[3] + vrecv[4]) + (vrecv[5] + vrecv[6])
    hand_out.wait()
    hand_in.wait()
    qkv_copy.wait()
    put(gqkv, first_qkv, first_qkv + qkv_small)


def finish_kernel(
    out_in, gin_in, vector_in, gqkv_in, gout_in, gup_in, gdown_in,
    out, gin, gpass, gain1, bias1, gqkv, gout, gain2, bias2, gup, gb_up, gdown, gb_down,
    vector, sem,
):
    pairs = (
        (out_in, out), (gin_in, gin), (gqkv_in, gqkv), (gout_in, gout), (gup_in, gup), (gdown_in, gdown),
        (vector_in, vector),
    )
    copies = [pltpu.make_async_copy(a, b, sem.at[i]) for i, (a, b) in enumerate(pairs)]
    for copy in copies:
        copy.start()
    for copy in copies:
        copy.wait()
    width = vector.shape[1]
    gpass[...] = vector[0:5, :]
    for i, ref in enumerate((gain1, bias1, gain2, bias2, gb_down)):
        ref[...] = vector[5 + i, :]
    for i in range(4):
        gb_up[pl.ds(i * width, width)] = vector[10 + i, :]


def shaped(*dims, kind=jnp.bfloat16):
    return jax.ShapeDtypeStruct(dims, kind)


shares = ((64, 80, 48), (64, 80, 48), (16, 16, 16), (48, 64, 32))
plan = {
    "down0": ((0, "start_e"),),
    "down1": ((0, "start_c"), (0, "start_a")),
    "hidden": ((0, "e1"),),
    "dm": ((0, "a2"),),
    "up0": ((0, "e2"),),
    "up1": ((1, "start"), (0, "c2")),
    "out": (),
    "middle": ((0, "e3"),),
    "w_out": ((2, "start"),),
    "head0": ((0, "z0"), (1, "e1")),
    "head1": ((0, "e4"),),
    "head2": ((0, "z1"), (1, "a2")),
    "head3": ((1, "e2"),),
    "head4": ((0, "z2"), (1, "c2"), (2, "e1")),
    "head5": ((1, "e3"), (2, "a2"), (2, "c2")),
    "given": ((0, "z3"), (1, "z0")),
    "qkv": ((3, "start"), (1, "e4"), (2, "e2")),
    "input0": ((1, "z1"), (2, "e3"), (3, "e1")),
    "input1": ((1, "z2"), (2, "z0"), (2, "e4"), (3, "a2")),
    "sum0": ((3, "e2"), (2, "z1")),
    "sum1": ((1, "z3"), (3, "c2")),
    "sum2": ((2, "z2"), (3, "e3")),
    "end0": (),
    "end1": ((2, "z3"), (3, "z0")),
    "end2": ((3, "e4"), (3, "z1"), (3, "z2"), (3, "z3")),
}


def regrouped(
    block_input, lengths, pass_ids, pass_embed, ln1_gain, ln1_bias, w_qkv, w_out,
    ln2_gain, ln2_bias, w_up, b_up, w_down, b_down, cotangent, batch_n
):
    width = block_input.shape[2]
    total = 4 * block_input.shape[1]
    inner = w_up.shape[1]
    own_in, half, lanes = inner // 2, width // 2, width // 2
    band = inner // batch_n // 2
    z_n = batch_n // 2
    blocks_n = total // block
    kept_rows = blocks_n * (blocks_n + 1) // 2 * block
    chunks, a0, c0, e0, r0 = [], 0, 0, 0, 0
    for ne, nc, na in shares:
        chunks.append((r0, r0 + ne, r0 + ne + nc, r0 + ne + nc + na, a0, c0, e0))
        r0, a0, c0, e0 = r0 + ne + nc + na, a0 + na, c0 + nc, e0 + ne
    down_n = 2 * width // batch_n
    anywhere = pl.BlockSpec(memory_space=pl.ANY)
    whole = pl.BlockSpec(memory_space=pltpu.VMEM)
    low, full = jnp.bfloat16, jnp.float32
    copies_n = 22 * len(chunks) + 9 + half // 64 + 31
    output, grad_input, vector, grad_qkv, grad_out, grad_up, grad_down, _, _ = pl.pallas_call(
        functools.partial(block_kernel, chunks=tuple(chunks), plan=plan),
        out_shape=[
            shaped(2, block, width),
            shaped(2, block, width),
            shaped(16, width, kind=full),
            shaped(width // 4, 3 * width // batch_n, kind=full),
            shaped(width // 4, width // batch_n, kind=full),
            shaped(width // 4, inner // batch_n, kind=full),
            shaped(width // batch_n, inner // 4, kind=full),
            shaped(half // 64, kept_rows, block),
            shaped(2, width, block, kind=full),
        ],
        in_specs=[pl.BlockSpec(memory_space=pltpu.SMEM)] + [anywhere] * 6 + [whole] * 8,
        out_specs=[whole] * 7 + [anywhere] * 2,
        scratch_shapes=[
            pltpu.VMEM((width, total), full),
            pltpu.VMEM((width, 2 * block), full),
            pltpu.VMEM((width, total), low),
            pltpu.VMEM((3 * half, total), low),
            pltpu.VMEM((width, total), low),
            pltpu.VMEM((width, total), low),
            pltpu.VMEM((width, total), low),
            pltpu.VMEM((2 * own_in, total), low),
            pltpu.VMEM((3 * half, total), low),
            pltpu.VMEM((2 * width, total), low),
            pltpu.VMEM((2, kept_rows, block), low),
            pltpu.VMEM((width, width), low),
            pltpu.VMEM((own_in, width), low),
            pltpu.VMEM((own_in, width), low),
            pltpu.VMEM((2, z_n, 2, r0, lanes), low),
            pltpu.VMEM((z_n, 2, a0, lanes), low),
            pltpu.VMEM((z_n, a0, lanes), low),
            pltpu.VMEM((2, z_n, c0, lanes), low),
            pltpu.VMEM((z_n, c0, lanes), low),
            pltpu.VMEM((2, e0, lanes), low),
            pltpu.VMEM((e0, lanes), low),
            pltpu.VMEM((z_n + 1, a0 + c0, lanes), low),
            pltpu.VMEM((z_n + 1, 2, 2, e0, lanes), low),
            pltpu.VMEM((width, 2 * block), low),
            pltpu.VMEM((width, 2 * block), low),
            pltpu.VMEM((2, block, width), low),
            pltpu.VMEM((width, 128), full),
            pltpu.VMEM((16, width), full),
            pltpu.VMEM((7, 16, width), full),
            pltpu.VMEM((64, total), full),
            pltpu.VMEM((64, total), full),
            pltpu.VMEM((r0 - down_n, 256), low),
            pltpu.VMEM((r0 - down_n, 256), low),
            pltpu.VMEM((down_n // 2, lanes), low),
            pltpu.VMEM((16, width), full),
            pltpu.VMEM((width, 16), full),
            pltpu.VMEM((own_in, 8), full),
            pltpu.VMEM((half // 64, 8, total), full),
            pltpu.VMEM((8, total), full),
            pltpu.VMEM((total, 16), low),
            pltpu.VMEM((16, total), low),
            pltpu.VMEM((4, 2, block), jnp.int32),
            pltpu.SemaphoreType.DMA((27,)),
            pltpu.SemaphoreType.DMA((copies_n,)),
            pltpu.SemaphoreType.DMA((copies_n,)),
        ],
        compiler_params=pltpu.CompilerParams(
            vmem_limit_bytes=63 << 20, collective_id=0, has_side_effects=True
        ),
        cost_estimate=pl.CostEstimate(flops=int(60e9), bytes_accessed=0, transcendentals=0),
        name="block",
    )(
        lengths, block_input, cotangent, w_up, w_qkv, w_out,
        w_down.reshape(batch_n, 2, band, width), pass_ids, pass_embed,
        ln1_gain, ln1_bias, ln2_gain, ln2_bias, b_up, b_down,
    )
    results = [output, grad_input, vector, grad_qkv, grad_out, grad_up, grad_down]
    line = jax.ShapeDtypeStruct((width,), full)
    done = pl.pallas_call(
        finish_kernel,
        out_shape=[
            shaped(2, block, width),
            shaped(2, block, width),
            shaped(5, width, kind=full),
            line,
            line,
            jax.ShapeDtypeStruct(grad_qkv.shape, full),
            jax.ShapeDtypeStruct(grad_out.shape, full),
            line,
            line,
            jax.ShapeDtypeStruct(grad_up.shape, full),
            jax.ShapeDtypeStruct((inner,), full),
            jax.ShapeDtypeStruct(grad_down.shape, full),
            line,
        ],
        in_specs=[anywhere] * 7,
        out_specs=[whole] * 13,
        scratch_shapes=[pltpu.VMEM((16, width), full), pltpu.SemaphoreType.DMA((7,))],
        compiler_params=pltpu.CompilerParams(vmem_limit_bytes=62 << 20),
        name="finish",
    )(*results)
    done = list(done)
    done[11] = jnp.transpose(done[11])
    return tuple(done)


def solution(mesh):
    batch_n = mesh.shape["batch"]
    few = mesh.shape["seq"] == 4 and batch_n == 8
    body = functools.partial(regrouped, batch_n=batch_n) if few else local
    return jax.shard_map(
        body,
        mesh=mesh,
        in_specs=(
            P("batch", "seq", None),
            P("batch"),
            P("batch", "seq"),
            P(),
            P(),
            P(),
            P(),
            P(),
            P(),
            P(),
            P(),
            P(),
            P(),
            P(),
            P("batch", "seq", None),
        ),
        out_specs=(
            P("batch", "seq", None),
            P("batch", "seq", None),
            P(),
            P(),
            P(),
            P("seq", "batch"),
            P("seq", "batch"),
            P(),
            P(),
            P("seq", "batch"),
            P(),
            P("seq", "batch"),
            P(),
        ),
        check_vma=False,
    )
```

```python
import functools

import jax
import jax.numpy as jnp
from jax import lax
from jax.experimental import pallas as pl
from jax.experimental.pallas import tpu as pltpu
from jax.sharding import PartitionSpec as P

H = 12


negative = -1e30
key_block = 1024
query_block = 512
highest = lax.Precision.HIGHEST


def layer_norm(hidden, gain, offset):
    centre = jnp.mean(hidden, -1, keepdims=True)
    shifted = hidden - centre
    spread = jnp.mean(shifted * shifted, -1, keepdims=True)
    return shifted * lax.rsqrt(spread + 1e-05) * gain + offset


def gelu_tanh(values):
    return jax.nn.gelu(values, approximate=True)


def visible(query_place, query_pass, key_place, key_pass, length):
    earlier = key_place[None, :] < query_place[:, None]
    allowed = earlier & (key_pass[None, :] <= query_pass[:, None]) & (key_place[None, :] < length)
    return allowed | (key_place[None, :] == query_place[:, None])


def masked_scores(query_part, key_part, factor, seen):
    raw = (
        jnp.einsum("qhd,khd->hqk", query_part, key_part, preferred_element_type=jnp.float32)
        * factor
    )
    return jnp.where(seen[None], raw, negative)


def split_blocks(arrays, block_len):
    return tuple(
        (
            array.reshape((array.shape[0] // block_len, block_len) + array.shape[1:])
            for array in arrays
        )
    )


def chance_of(query_part, key_part, log_part, seen, factor):
    scores = masked_scores(query_part, key_part, factor, seen)
    return jnp.where(seen[None], jnp.exp(scores - log_part[..., None]), 0.0)


def grad_pieces(query_part, dout_part, log_part, delta_part, key_part, value_part, seen, factor):
    chance = chance_of(query_part, key_part, log_part, seen, factor)
    dprob = jnp.einsum("qhd,khd->hqk", dout_part, value_part, preferred_element_type=jnp.float32)
    dscore = (chance * (dprob - delta_part[..., None])).astype(jnp.bfloat16)
    return (dscore, chance.astype(jnp.bfloat16))


def attend_row(queries, query_place, query_pass, key_rows, value_rows, key_pass, length):
    factor = queries.shape[-1] ** (-0.5)
    places = jnp.arange(key_rows.shape[0], dtype=jnp.int32)
    key_parts = split_blocks(
        (key_rows, value_rows, key_pass, places), min(key_block, key_rows.shape[0])
    )
    query_len = min(query_block, queries.shape[0])
    query_parts = split_blocks((queries, query_place, query_pass), query_len)

    def attend_one_block(query_args):
        query_part, place_part, pass_part = query_args

        def running(carry, key_args):
            peak, summed, total_out = carry
            key_part, value_part, kpass_part, kplace_part = key_args
            seen = visible(place_part, pass_part, kplace_part, kpass_part, length)
            scores = masked_scores(query_part, key_part, factor, seen)
            new_peak = jnp.maximum(peak, jnp.max(scores, -1))
            terms = jnp.where(seen[None], jnp.exp(scores - new_peak[..., None]), 0.0)
            rescale = jnp.exp(peak - new_peak)
            summed = summed * rescale + jnp.sum(terms, -1)
            added = jnp.einsum(
                "hqk,khd->qhd",
                terms.astype(jnp.bfloat16),
                value_part,
                preferred_element_type=jnp.float32,
            )
            total_out = total_out * rescale.T[..., None] + added
            return ((new_peak, summed, total_out), None)

        heads_n = query_part.shape[1]
        start = (
            jnp.full((heads_n, query_len), negative, jnp.float32),
            jnp.zeros((heads_n, query_len), jnp.float32),
            jnp.zeros(query_part.shape, jnp.float32),
        )
        (peak, summed, total_out), _ = lax.scan(running, start, key_parts)
        log_total = peak + jnp.log(summed)
        result = total_out / summed.T[..., None]
        return (result, log_total)

    results, log_totals = lax.map(attend_one_block, query_parts)
    heads_n = queries.shape[1]
    return (
        results.reshape(queries.shape),
        jnp.moveaxis(log_totals, 1, 0).reshape(heads_n, queries.shape[0]),
    )


def backward_row(
    queries,
    douts,
    outs_kept,
    log_totals,
    query_place,
    query_pass,
    key_rows,
    value_rows,
    key_pass,
    length,
):
    factor = queries.shape[-1] ** (-0.5)
    places = jnp.arange(key_rows.shape[0], dtype=jnp.int32)
    key_parts = split_blocks(
        (key_rows, value_rows, key_pass, places), min(key_block, key_rows.shape[0])
    )
    query_len = min(query_block, queries.shape[0])
    heads_n = queries.shape[1]
    block_count = queries.shape[0] // query_len
    log_parts = jnp.moveaxis(log_totals.reshape(heads_n, block_count, query_len), 1, 0)
    query_parts = split_blocks((queries, douts, outs_kept, query_place, query_pass), query_len)

    def backward_one_block(carry, query_args):
        query_part, dout_part, kept_part, place_part, pass_part, log_part = query_args
        delta_part = jnp.einsum("qhd,qhd->hq", dout_part.astype(jnp.float32), kept_part)

        def add_grads(dquery, key_args):
            key_part, value_part, kpass_part, kplace_part = key_args
            seen = visible(place_part, pass_part, kplace_part, kpass_part, length)
            dscore, low_chance = grad_pieces(
                query_part, dout_part, log_part, delta_part, key_part, value_part, seen, factor
            )
            dquery = dquery + factor * jnp.einsum(
                "hqk,khd->qhd", dscore, key_part, preferred_element_type=jnp.float32
            )
            dkey = factor * jnp.einsum(
                "hqk,qhd->khd", dscore, query_part, preferred_element_type=jnp.float32
            )
            dvalue = jnp.einsum(
                "hqk,qhd->khd", low_chance, dout_part, preferred_element_type=jnp.float32
            )
            return (dquery, (dkey, dvalue))

        dquery, key_terms = lax.scan(add_grads, jnp.zeros(query_part.shape, jnp.float32), key_parts)
        carry = (
            carry[0] + key_terms[0].reshape(key_rows.shape),
            carry[1] + key_terms[1].reshape(value_rows.shape),
        )
        return (carry, (dquery, delta_part))

    start = (jnp.zeros(key_rows.shape, jnp.float32), jnp.zeros(value_rows.shape, jnp.float32))
    key_sums, (dqueries, deltas) = lax.scan(backward_one_block, start, query_parts + (log_parts,))
    return (
        dqueries.reshape(queries.shape),
        jnp.moveaxis(deltas, 1, 0).reshape(heads_n, queries.shape[0]),
        key_sums,
    )


def local(
    block_input,
    lengths,
    pass_ids,
    pass_embed,
    ln1_gain,
    ln1_bias,
    w_qkv,
    w_out,
    ln2_gain,
    ln2_bias,
    w_up,
    b_up,
    w_down,
    b_down,
    cotangent,
):
    row_count, seg_len, width = block_input.shape
    heads_n = H
    head_size = width // heads_n
    onehot = (
        pass_ids[..., None] == jnp.arange(pass_embed.shape[0], dtype=jnp.int32)[None, None, :]
    ).astype(jnp.float32)
    hidden_in = block_input.astype(jnp.float32) + jnp.einsum(
        "rsp,pd->rsd", onehot, pass_embed, precision=highest
    )
    normed, norm_back = jax.vjp(layer_norm, hidden_in, ln1_gain, ln1_bias)
    normed_low = normed.astype(jnp.bfloat16)
    qkv = jnp.einsum("rsd,de->rse", normed_low, w_qkv, preferred_element_type=jnp.float32)
    queries = qkv[..., :width].astype(jnp.bfloat16)
    key_flat = qkv[..., width : 2 * width].astype(jnp.bfloat16)
    value_flat = qkv[..., 2 * width :].astype(jnp.bfloat16)
    pass_low = pass_ids.astype(jnp.bfloat16)
    key_all, value_all, pass_all = (
        lax.all_gather(key_flat, "seq", axis=1, tiled=True),
        lax.all_gather(value_flat, "seq", axis=1, tiled=True),
        lax.all_gather(pass_low, "seq", axis=1, tiled=True),
    )
    total_len = key_all.shape[1]
    key_all = key_all.reshape(row_count, total_len, heads_n, head_size)
    value_all = value_all.reshape(row_count, total_len, heads_n, head_size)
    pass_all = pass_all.astype(jnp.float32)
    offset = lax.axis_index("seq") * seg_len
    query_place = offset + jnp.arange(seg_len, dtype=jnp.int32)
    query_pass = pass_ids.astype(jnp.float32)
    query_heads = queries.reshape(row_count, seg_len, heads_n, head_size)
    attended_rows = []
    log_rows = []
    for row in range(row_count):
        attended, log_total = attend_row(
            query_heads[row],
            query_place,
            query_pass[row],
            key_all[row],
            value_all[row],
            pass_all[row],
            lengths[row],
        )
        attended_rows.append(attended)
        log_rows.append(log_total)
    attended_low = jnp.stack(attended_rows).astype(jnp.bfloat16).reshape(row_count, seg_len, width)
    branch = jnp.einsum("rsd,de->rse", attended_low, w_out, preferred_element_type=jnp.float32)
    middle = hidden_in + branch
    normed2, norm2_back = jax.vjp(layer_norm, middle, ln2_gain, ln2_bias)
    normed2_low = normed2.astype(jnp.bfloat16)
    pre_act = (
        jnp.einsum("rsd,df->rsf", normed2_low, w_up, preferred_element_type=jnp.float32) + b_up
    )
    active, active_back = jax.vjp(gelu_tanh, pre_act)
    active_low = active.astype(jnp.bfloat16)
    result = (
        middle
        + jnp.einsum("rsf,fd->rsd", active_low, w_down, preferred_element_type=jnp.float32)
        + b_down
    )
    output = result.astype(jnp.bfloat16)
    cot_f = cotangent.astype(jnp.float32)
    grad_active = jnp.einsum("rsd,fd->rsf", cotangent, w_down, preferred_element_type=jnp.float32)
    grad_w_down = jnp.einsum(
        "rsf,rsd->fd", active_low, cotangent, preferred_element_type=jnp.float32
    )
    grad_b_down = jnp.sum(cot_f, (0, 1))
    grad_pre = active_back(grad_active)[0].astype(jnp.bfloat16)
    grad_b_up = jnp.sum(grad_pre.astype(jnp.float32), (0, 1))
    grad_w_up = jnp.einsum("rsd,rsf->df", normed2_low, grad_pre, preferred_element_type=jnp.float32)
    grad_normed2 = jnp.einsum("rsf,df->rsd", grad_pre, w_up, preferred_element_type=jnp.float32)
    grad_mid_norm, grad_ln2_gain, grad_ln2_bias = norm2_back(grad_normed2)
    grad_middle = cot_f + grad_mid_norm
    grad_branch = grad_middle.astype(jnp.bfloat16)
    grad_w_out = jnp.einsum(
        "rsd,rse->de", attended_low, grad_branch, preferred_element_type=jnp.float32
    )
    grad_attended = jnp.einsum(
        "rse,de->rsd", grad_branch, w_out, preferred_element_type=jnp.float32
    ).astype(jnp.bfloat16)
    dout_heads = grad_attended.reshape(row_count, seg_len, heads_n, head_size)
    dquery_rows = []
    dkey_rows = []
    dvalue_rows = []
    for row in range(row_count):
        dquery, _, key_sums = backward_row(
            query_heads[row],
            dout_heads[row],
            attended_rows[row],
            log_rows[row],
            query_place,
            query_pass[row],
            key_all[row],
            value_all[row],
            pass_all[row],
            lengths[row],
        )
        dquery_rows.append(dquery)
        dkey_rows.append(key_sums[0].reshape(total_len, width))
        dvalue_rows.append(key_sums[1].reshape(total_len, width))
    dkey_sum, dvalue_sum = (
        lax.psum_scatter(
            jnp.stack(dkey_rows).astype(jnp.bfloat16), "seq", scatter_dimension=1, tiled=True
        ).astype(jnp.float32),
        lax.psum_scatter(
            jnp.stack(dvalue_rows).astype(jnp.bfloat16), "seq", scatter_dimension=1, tiled=True
        ).astype(jnp.float32),
    )
    dquery_all = jnp.stack(dquery_rows).reshape(row_count, seg_len, width)
    grad_qkv = jnp.concatenate(
        [
            dquery_all.astype(jnp.bfloat16),
            dkey_sum.astype(jnp.bfloat16),
            dvalue_sum.astype(jnp.bfloat16),
        ],
        -1,
    )
    grad_w_qkv = jnp.einsum("rsd,rse->de", normed_low, grad_qkv, preferred_element_type=jnp.float32)
    grad_normed = jnp.einsum("rse,de->rsd", grad_qkv, w_qkv, preferred_element_type=jnp.float32)
    grad_in_norm, grad_ln1_gain, grad_ln1_bias = norm_back(grad_normed)
    grad_hidden = grad_middle + grad_in_norm
    grad_input = grad_hidden.astype(jnp.bfloat16)
    grad_pass = jnp.einsum("rsp,rsd->pd", onehot, grad_hidden, precision=highest)
    matrices = (
        lax.psum_scatter(
            grad_w_qkv.astype(jnp.bfloat16), "seq", scatter_dimension=0, tiled=True
        ).astype(jnp.float32),
        lax.psum_scatter(
            grad_w_out.astype(jnp.bfloat16), "seq", scatter_dimension=0, tiled=True
        ).astype(jnp.float32),
        lax.psum_scatter(
            grad_w_up.astype(jnp.bfloat16), "seq", scatter_dimension=0, tiled=True
        ).astype(jnp.float32),
        lax.psum_scatter(
            grad_w_down.astype(jnp.bfloat16), "seq", scatter_dimension=0, tiled=True
        ).astype(jnp.float32),
    )
    matrices = (
        lax.psum_scatter(
            matrices[0].astype(jnp.bfloat16), "batch", scatter_dimension=1, tiled=True
        ).astype(jnp.float32),
        lax.psum_scatter(
            matrices[1].astype(jnp.bfloat16), "batch", scatter_dimension=1, tiled=True
        ).astype(jnp.float32),
        lax.psum_scatter(
            matrices[2].astype(jnp.bfloat16), "batch", scatter_dimension=1, tiled=True
        ).astype(jnp.float32),
        lax.psum_scatter(
            matrices[3].astype(jnp.bfloat16), "batch", scatter_dimension=1, tiled=True
        ).astype(jnp.float32),
    )
    vectors = lax.psum(
        (
            grad_pass,
            grad_ln1_gain,
            grad_ln1_bias,
            grad_ln2_gain,
            grad_ln2_bias,
            grad_b_up,
            grad_b_down,
        ),
        ("seq", "batch"),
    )
    return (
        output,
        grad_input,
        vectors[0],
        vectors[1],
        vectors[2],
        matrices[0],
        matrices[1],
        vectors[3],
        vectors[4],
        matrices[2],
        vectors[5],
        matrices[3],
        vectors[6],
    )


NN = (((1,), (0,)), ((), ()))
NT = (((1,), (1,)), ((), ()))
TN = (((0,), (0,)), ((), ()))
vmem_bytes = 60 << 20
block = 256


def dot(left, right, form):
    return lax.dot_general(left, right, form, preferred_element_type=jnp.float32)


mesh_ids = pl.DeviceIdType.MESH


def block_kernel(
    lengths,
    block_in, cot_in, w_up_in, w_qkv_in, w_out_in, w_down_in,
    pass_in, embed_in, gain1, bias1, gain2, bias2, b_up_in, b_down_in,
    out, gin, vector, gqkv, gout, gup, gdown,
    kept_far, h_far,
    mid, keep, at, qkv, otf, ct, mt, gd, far, dm, kept, w_out, w_up, w_down,
    bsum, r1a, r2a, r1c, r2c, r2e, r3e, rz, rze,
    osend, orecv, hand, sums, gpass, vrecv, ksum, vsum, stage_send, stage_recv, down_recv,
    params, vecs, bcol, inv, prow, kmask, qhot, passes,
    lsem, ssem, rsem,
    *, chunks, plan,
):
    seq, bat = lax.axis_index("seq"), lax.axis_index("batch")
    x, core = seq // 2, seq % 2
    z, y = bat // 2, bat % 2
    to_core, to_x, to_y = (seq + 1 - 2 * core, bat), (seq + 2 - 4 * x, bat), (seq, bat + 1 - 2 * y)
    to_cross = (3 - seq, bat)
    to_z = [(seq, ((z + i) % 4) * 2 + y) for i in (1, 2, 3)]
    up_z, low_z = (seq, bat + 2), (seq, bat - 2)

    barrier = pltpu.get_barrier_semaphore()
    for peer in [to_core, to_x, to_y, to_cross] + to_z:
        pl.semaphore_signal(barrier, inc=1, device_id=peer, device_id_type=mesh_ids)

    width, total = mid.shape
    half = width // 2
    inner = w_up.shape[0]
    blocks_n = total // block
    heads = half // 64
    bs = 8

    def rows_at(first, count):
        return pl.ds(pl.multiple_of(first, 16), count)

    def lanes_at(first, count):
        return pl.ds(pl.multiple_of(first, 128), count)

    def own_cols(k):
        return lanes_at(core * block + k * 2 * block, block)

    def local(i, src, dst):
        return pltpu.make_async_copy(src, dst, lsem.at[i])

    def remote(i, src, dst, peer):
        return pltpu.make_async_remote_copy(
            src_ref=src, dst_ref=dst, send_sem=ssem.at[i], recv_sem=rsem.at[i],
            device_id=peer, device_id_type=mesh_ids,
        )

    part = w_down_in.shape[2]
    own_x = local(0, block_in.at[x], far.at[0:block, 0:width])
    own_c = local(1, cot_in.at[x], dm.at[0:block, 0:width])
    out_load = local(2, w_out_in, w_out)
    up_loads = [
        local(3 + p, w_up_in.at[:, p * width : (p + 1) * width],
              gd.at[p * width : (p + 1) * width, 0:width])
        for p in range(4)
    ]
    down_loads = [
        local(7 + i, w_down_in.at[i, core], w_down.at[i * part : (i + 1) * part, :])
        for i in range(bs)
    ]
    qkv_loads = [
        local(15 + j, w_qkv_in.at[:, j * width : (j + 1) * width],
              gd.at[j * width : (j + 1) * width, 0:width])
        for j in range(3)
    ]
    for load in [own_x] + up_loads + [own_c, out_load] + down_loads:
        load.start()

    base = 22 * len(chunks)
    x_far = remote(base, block_in.at[1 - x], far.at[block : 2 * block, 0:width], to_x)
    x_near = remote(base + 1, block_in.at[x], far.at[2 * block : 3 * block, 0:width], to_core)
    x_cross = remote(
        base + 2, far.at[block : 2 * block, 0:width], far.at[3 * block : 4 * block, 0:width], to_core
    )
    c_far = remote(base + 3, cot_in.at[1 - x], dm.at[block : 2 * block, 0:width], to_x)
    c_near = remote(base + 4, cot_in.at[x], dm.at[2 * block : 3 * block, 0:width], to_core)
    c_cross = remote(
        base + 5, dm.at[block : 2 * block, 0:width], dm.at[3 * block : 4 * block, 0:width], to_core
    )
    p_far = remote(base + 6, pass_in, passes.at[1], to_x)
    p_near = remote(base + 7, pass_in, passes.at[2], to_core)
    p_cross = remote(base + 8, pass_in, passes.at[3], to_cross)
    base += 9
    pl.semaphore_wait(barrier, 7)
    for copy in (p_far, x_far, x_near, p_near, p_cross, c_near):
        copy.start()


    def line_copy(i, d, up, part, slots):
        slot = d if up else jnp.where(z - 1 == d, 4, d)
        return remote(i + (d if up else 4 + d), part(d), slots(slot), up_z if up else low_z)

    def line_add(d, slot, part, slots):
        here, got = part(d), slots(slot)
        here[...] = here[...] + got[...]

    def line_start(i, part, slots):
        @pl.when(z == 0)
        def _():
            for d in (3, 2, 1):
                line_copy(i, d, True, part, slots).start()

        @pl.when(z == 3)
        def _():
            for d in (0, 1, 2):
                line_copy(i, d, False, part, slots).start()

    def line_pass(i, d, up, part, slots):
        copy = line_copy(i, d, up, part, slots)
        copy.wait_recv()
        line_add(d, d, part, slots)
        copy.start()

    def line_one(i, part, slots):
        @pl.when(z == 1)
        def _():
            line_pass(i, 3, True, part, slots)

        @pl.when(z == 2)
        def _():
            line_pass(i, 0, False, part, slots)

    def line_two(i, part, slots):
        @pl.when(z == 1)
        def _():
            line_pass(i, 2, True, part, slots)
            line_pass(i, 0, False, part, slots)

        @pl.when(z == 2)
        def _():
            line_pass(i, 1, False, part, slots)
            line_pass(i, 3, True, part, slots)

    def line_last(i, part, slots):
        for d in range(4):

            @pl.when(z == d)
            def _():
                if d > 0:
                    line_copy(i, d, True, part, slots).wait_recv()
                    line_add(d, d, part, slots)
                if d < 3:
                    line_copy(i, d, False, part, slots).wait_recv()
                    line_add(d, 4, part, slots)
                for e in range(4):
                    if e > d:
                        line_copy(i, e, True, part, slots).wait_send()
                    if e < d:
                        line_copy(i, e, False, part, slots).wait_send()

    class Chunk:
        def __init__(self, k):
            r0, rc, ra, r1, a0, c0, e0 = chunks[k]
            ne, nc, na = rc - r0, ra - rc, r1 - ra
            i = 22 * k
            rows_e, rows_c, rows_a = pl.ds(r0, ne), pl.ds(rc, nc), pl.ds(ra, na)
            got_a, got_c, got_e = pl.ds(a0, na), pl.ds(c0, nc), pl.ds(e0, ne)
            sub = bsum.at
            self.one_a = remote(i, sub[1 - x, :, :, rows_a, :], r1a.at[:, :, got_a, :], to_x)
            self.one_c = remote(i + 1, sub[:, :, 1 - y, rows_c, :], r1c.at[:, :, got_c, :], to_y)
            self.two_a = remote(i + 2, sub[x, :, 1 - y, rows_a, :], r2a.at[:, got_a, :], to_y)
            self.two_c = remote(i + 3, sub[1 - x, :, y, rows_c, :], r2c.at[:, got_c, :], to_x)
            self.two_e = remote(i + 4, sub[:, z, 1 - y, rows_e, :], r2e.at[:, got_e, :], to_y)
            self.three_e = remote(i + 5, sub[1 - x, z, y, rows_e, :], r3e.at[got_e, :], to_x)
            self.adds = [
                (sub[x, :, :, rows_a, :], r1a.at[:, :, got_a, :]),
                (sub[:, :, y, rows_c, :], r1c.at[:, :, got_c, :]),
                (sub[x, :, y, rows_a, :], r2a.at[:, got_a, :]),
                (sub[x, :, y, rows_c, :], r2c.at[:, got_c, :]),
                (sub[:, z, y, rows_e, :], r2e.at[:, got_e, :]),
                (sub[x, z, y, rows_e, :], r3e.at[got_e, :]),
            ]
            both, low = pl.ds(rc, na + nc), pl.ds(a0 + c0, na + nc)
            self.line_ac = (
                i + 6, lambda d: sub[x, d, y, both, :], lambda s: rz.at[s, low, :]
            )
            self.line_e = (
                i + 14, lambda d: sub[:, d, :, rows_e, :], lambda s: rze.at[s, :, :, got_e, :]
            )

        def add(self, j):
            here, got = self.adds[j]
            here[...] = here[...] + got[...]

        def start(self):
            line_start(*self.line_e)
            self.one_c.start()
            self.one_a.start()

        def start_a(self):
            self.one_a.start()

        def start_c(self):
            self.one_c.start()

        def start_e(self):
            line_start(*self.line_e)

        def e1(self):
            line_one(*self.line_e)

        def e2(self):
            line_two(*self.line_e)

        def e3(self):
            line_last(*self.line_e)
            self.two_e.start()

        def a2(self):
            self.one_a.wait()
            self.add(0)
            self.two_a.start()

        def c2(self):
            self.one_c.wait()
            self.add(1)
            self.two_c.start()

        def e4(self):
            self.two_e.wait()
            self.add(4)
            self.three_e.start()

        def z0(self):
            self.two_a.wait()
            self.add(2)
            self.two_c.wait()
            self.add(3)
            line_start(*self.line_ac)

        def z1(self):
            line_one(*self.line_ac)

        def z2(self):
            line_two(*self.line_ac)

        def z3(self):
            line_last(*self.line_ac)
            self.three_e.wait()
            self.add(5)
    steps = [Chunk(k) for k in range(len(chunks))]

    def serve(slot):
        for k, name in plan[slot]:
            getattr(steps[k], name)()

    params[...] = jnp.zeros_like(params)
    params[0:5, :] = embed_in[...]
    for i, ref in enumerate((gain1, bias1, gain2, bias2, b_down_in)):
        params[5 + i, :] = ref[...]
    for i in range(4):
        params[10 + i, :] = b_up_in[pl.ds(i * width, width)]
    vecs[...] = jnp.transpose(params[...])
    for b in range(bs):
        i, low = 10 + b // 2, b % 2 * 2 * part
        bcol[b * part : (b + 1) * part, :] = jnp.broadcast_to(
            jnp.where(
                core == 0,
                vecs[low : low + part, i : i + 1],
                vecs[low + part : low + 2 * part, i : i + 1],
            ),
            (part, 8),
        )
    for b in range(bs):
        p, low = b // 2, b % 2 * 2 * part
        if b % 2 == 0:
            up_loads[p].wait()
        turned = jnp.transpose(gd[p * width : (p + 1) * width, low : low + 2 * part])
        w_up[b * part : (b + 1) * part, :] = jnp.where(core == 0, turned[:part], turned[part:])
    for load in qkv_loads:
        load.start()
    passes[0] = pass_in[...]
    places = (2 * x + core, 2 * (1 - x) + core, 2 * x + 1 - core, 2 * (1 - x) + 1 - core)
    length = lengths[x]
    emb = jnp.where(lax.broadcasted_iota(jnp.int32, (8, width), 0) < 5, params[0:8, :], 0.0)
    emb_a = emb.astype(jnp.bfloat16)
    rest = emb - emb_a.astype(jnp.float32)
    emb_b = rest.astype(jnp.bfloat16)
    emb_c = (rest - emb_b.astype(jnp.float32)).astype(jnp.bfloat16)

    def take(k):
        cols = lanes_at(places[k] * block, block)
        rows = rows_at(places[k] * block, block)
        got = passes[k]
        line = jnp.where(x == 0, got[0:1, :], got[1:2, :])
        prow[:, cols] = jnp.broadcast_to(line.astype(jnp.float32), (8, block))
        kind = lax.broadcasted_iota(jnp.int32, (16, block), 0)
        spot = lax.broadcasted_iota(jnp.int32, (16, block), 1) + places[k] * block
        onehot = jnp.where(kind == line, 1.0, 0.0).astype(jnp.bfloat16)
        qhot[:, cols] = onehot
        hidden = jnp.where((line > kind) | (spot >= length), negative, 0.0)
        kmask[rows, :] = jnp.transpose(hidden).astype(jnp.bfloat16)
        hot = onehot[0:8, :]
        added = dot(emb_a, hot, TN) + dot(emb_b, hot, TN) + dot(emb_c, hot, TN)
        h = jnp.transpose(far[k * block : (k + 1) * block, 0:width]).astype(jnp.float32) + added
        mid[:, cols] = h
        shifted = h - jnp.sum(h, 0, keepdims=True) * (1.0 / width)
        spread = jnp.sum(shifted * shifted, 0, keepdims=True) * (1.0 / width)
        scaled = shifted * lax.rsqrt(spread + 1e-05)
        at[:, cols] = (scaled * vecs[:, 5:6] + vecs[:, 6:7]).astype(jnp.bfloat16)
        for j in range(3):
            res = dot(
                gd[j * width : (j + 1) * width, lanes_at(core * half, half)], at[:, cols], TN
            ).astype(jnp.bfloat16)
            qkv[j * half : (j + 1) * half, cols] = res * jnp.bfloat16(0.125) if j == 0 else res

    own_x.wait()
    for load in qkv_loads:
        load.wait()
    take(0)
    x_near.wait()
    p_near.wait()
    take(2)
    p_far.wait()
    x_far.wait()
    x_cross.start()
    c_far.start()
    take(1)
    x_cross.wait()
    p_cross.wait()
    take(3)
    h_saves = [local(18 + k, mid.at[:, own_cols(k)], h_far.at[k]) for k in range(2)]
    for save in h_saves:
        save.start()

    pairs_n = blocks_n // 2
    wide = 2 * block

    def cover(first_key, first_query, queries):
        key = lax.broadcasted_iota(jnp.int32, (block, queries), 0) + first_key
        place = lax.broadcasted_iota(jnp.int32, (block, queries), 1) + first_query
        hidden = dot(
            kmask[first_key : first_key + block, :], qhot[:, first_query : first_query + queries], NN
        )
        hidden = jnp.where(key < place, hidden, negative)
        return jnp.where(key == place, 0.0, hidden)

    for p in range(pairs_n):
        keep[p * block : (p + 1) * block, :] = cover(p * wide, p * wide, wide)
        keep[wide : wide + block, p * block : (p + 1) * block] = cover(
            p * wide + block, p * wide + block, block
        )

    def kept_save(h, slot):
        return pltpu.make_async_copy(kept.at[slot], kept_far.at[h], lsem.at[20 + slot])

    def o_copy(h):
        mine = rows_at(core * half + h * 64, 64)
        return remote(base + h, otf.at[mine, :], otf.at[mine, :], to_core)

    def turn(k):
        ct[:, lanes_at(places[k] * block, block)] = jnp.transpose(
            dm[k * block : (k + 1) * block, 0:width]
        )

    def one_head(h, slot):
        @pl.when(h >= 2)
        def _():
            kept_save(h - 2, slot).wait()

        qrow, krow, vrow = (rows_at(j * half + h * 64, 64) for j in range(3))
        mine = rows_at(core * half + h * 64, 64)
        keyn = jnp.concatenate([jnp.transpose(qkv[krow, :]), kmask[...]], 1)
        query = jnp.concatenate([qkv[qrow, :], qhot[...]], 0)
        for p in range(pairs_n):
            before, split, after = p * wide, p * wide + block, (p + 1) * wide
            at_row = p * p * block
            cols, late = slice(before, after), slice(split, after)
            side = slice(p * block, (p + 1) * block)
            near = dot(keyn[before:split, 0:64], query[0:64, cols], NN)
            near = near + keep[p * block : (p + 1) * block, :]
            peak = jnp.max(near, 0, keepdims=True)
            last = dot(keyn[late, 0:64], query[0:64, late], NN) + keep[wide : wide + block, side]
            last_peak = jnp.maximum(peak[:, block:], jnp.max(last, 0, keepdims=True))
            peak = jnp.concatenate([peak[:, :block], last_peak], 1)
            if p:
                scores = dot(keyn[0:before, :], query[:, cols], NN)
                peak = jnp.maximum(peak, jnp.max(scores, 0, keepdims=True))
                expo = jnp.exp(scores - peak)
                count = jnp.sum(expo, 0, keepdims=True)
                low = expo.astype(jnp.bfloat16)
                kept[slot, at_row : at_row + before, :] = low
                result = dot(qkv[vrow, 0:before], low, NN)
            near = jnp.exp(near - peak)
            near_sum = jnp.sum(near, 0, keepdims=True)
            count = count + near_sum if p else near_sum
            low = near.astype(jnp.bfloat16)
            kept[slot, at_row + before : at_row + split, :] = low
            near_result = dot(qkv[vrow, before:split], low, NN)
            result = result + near_result if p else near_result
            last = jnp.exp(last - peak[:, block:])
            low = last.astype(jnp.bfloat16)
            kept[slot, kept.shape[1] - block : kept.shape[1], side] = low
            last_result = dot(qkv[vrow, late], low, NN)
            over = 1.0 / jnp.concatenate(
                [count[:, :block], count[:, block:] + jnp.sum(last, 0, keepdims=True)], 1
            )
            result = jnp.concatenate([result[:, :block], result[:, block:] + last_result], 1)
            inv[h, :, cols] = jnp.broadcast_to(over, (8, wide))
            otf[mine, cols] = (result * over).astype(jnp.bfloat16)
        kept_save(h, slot).start()

        @pl.when(h == heads - 2)
        def _():
            c_near.wait()
            c_far.wait()
            c_cross.start()
            own_c.wait()
            for k in (0, 2, 1):
                turn(k)

        @pl.when(h == heads - 1)
        def _():
            c_cross.wait()
            turn(3)

        o_copy(h).start()

    def head_pair(i, carry):
        for e in range(2):
            one_head(2 * i + e, e)
        return carry

    lax.fori_loop(0, heads // 2, head_pair, 0)
    kept_save(heads - 2, heads % 2).wait()
    kept_save(heads - 1, (heads - 1) % 2).wait()

    def kept_load(h, slot):
        return pltpu.make_async_copy(kept_far.at[h], kept.at[slot], lsem.at[22 + slot])

    kept_load(0, 0).start()
    kept_load(1, 1).start()
    for h in range(heads):
        o_copy(h).wait()
    base += heads

    for save in h_saves:
        save.wait()
    out_load.wait()

    def mix(i, carry):
        cols = lanes_at(i * block, block)
        m = mid[:, cols] + dot(w_out[...], otf[:, cols], TN)
        mid[:, cols] = m
        shifted = m - jnp.sum(m, 0, keepdims=True) * (1.0 / width)
        spread = jnp.sum(shifted * shifted, 0, keepdims=True) * (1.0 / width)
        scaled = shifted * lax.rsqrt(spread + 1e-05)
        mt[:, cols] = (scaled * vecs[:, 7:8] + vecs[:, 8:9]).astype(jnp.bfloat16)
        return carry

    lax.fori_loop(0, blocks_n, mix, 0)

    def hidden_at(first):
        for i in range(2):
            rows = slice(first + i * part, first + (i + 1) * part)
            below = slice(inner + first + i * part, inner + first + (i + 1) * part)
            u = dot(w_up[rows, :], mt[...], NN) + bcol[rows, 0:1]
            square = u * u
            t = jnp.tanh(u * (0.7978845608028654 + 0.035677408136300125 * square))
            gate = 0.5 + 0.5 * t
            gd[rows, :] = (u * gate).astype(jnp.bfloat16)
            slope = gate + (0.5 * u) * (1.0 - t * t) * (
                0.7978845608028654 + 0.10703222440890037 * square
            )
            gd[below, :] = slope.astype(jnp.bfloat16)

    lanes = bsum.shape[-1]
    band = width // bs
    for j in range(2):
        for xx in range(2):
            at_row = (2 * xx + j) * lanes
            hidden_at(at_row)
            grad = dot(ct[...], gd[at_row : at_row + lanes, :], NT).astype(jnp.bfloat16)
            for b in range(bs):
                bsum[xx, b // 2, b % 2, j * band : (j + 1) * band, :] = grad[
                    b * band : (b + 1) * band, :
                ]
        serve("down%d" % j)
    for load in down_loads:
        load.wait()

    for i in range(bs):
        rows = slice(i * part, (i + 1) * part)
        below = slice(inner + i * part, inner + (i + 1) * part)
        back = dot(w_down[rows, :], ct[...], NN)
        gd[below, :] = (back * gd[below, :].astype(jnp.float32)).astype(jnp.bfloat16)
    serve("hidden")

    dm_copy = remote(base, dm.at[0:width, :], dm.at[width : 2 * width, :], to_core)

    for i in range(blocks_n):
        cols = slice(i * block, (i + 1) * block)
        dm[0:width, cols] = dot(w_up[...], gd[inner : 2 * inner, cols], TN).astype(jnp.bfloat16)
    dm_copy.start()
    serve("dm")
    first_up = 2 * band
    up_band = part
    for xx in range(2):
        for i in range(2):
            low, high = inner + i * inner // 2, inner + (i + 1) * inner // 2
            grad = dot(gd[low:high, :], mt[xx * lanes : (xx + 1) * lanes, :], NT)
            grad = grad.astype(jnp.bfloat16)
            for b in range(bs // 2):
                bb = i * bs // 2 + b
                bsum[xx, bb // 2, bb % 2, first_up : first_up + up_band, :] = grad[
                    b * up_band : (b + 1) * up_band, :
                ]
        serve("up%d" % xx)
    ones = jnp.ones((8, total), jnp.bfloat16)
    up_sum = dot(ones, gd[inner : 2 * inner, :], NT)
    vector[...] = jnp.zeros_like(vector)
    for i in range(4):
        one, two = (up_sum[0:1, (2 * i + e) * part : (2 * i + e + 1) * part] for e in range(2))
        none = jnp.zeros_like(one)
        vector[10 + i : 11 + i, :] = jnp.where(
            core == 0,
            jnp.concatenate([one, none, two, none], 1),
            jnp.concatenate([none, one, none, two], 1),
        )

    out_copy = remote(base + 1, osend, orecv, to_core)
    for k in range(2):
        other = lanes_at((1 - core) * block + k * 2 * block, block)
        to = slice(k * block, (k + 1) * block)
        osend[:, to] = dot(w_down[...], gd[0:inner, other], TN).astype(jnp.bfloat16)
        keep[:, to] = mid[:, own_cols(k)] + vecs[:, 9:10] + dot(
            w_down[...], gd[0:inner, own_cols(k)], TN
        )
    out_copy.start()
    serve("out")

    dm_copy.wait()
    sums[...] = jnp.zeros_like(sums)

    def middle(i, carry):
        cols = lanes_at(i * block, block)
        cot = ct[:, cols].astype(jnp.float32)
        m = mid[:, cols]
        shifted = m - jnp.sum(m, 0, keepdims=True) * (1.0 / width)
        spread = jnp.sum(shifted * shifted, 0, keepdims=True) * (1.0 / width)
        r = lax.rsqrt(spread + 1e-05)
        n = shifted * r
        d = dm[0:width, cols].astype(jnp.float32) + dm[width : 2 * width, cols].astype(jnp.float32)
        e = d * vecs[:, 7:8]
        mean_e = jnp.sum(e, 0, keepdims=True) * (1.0 / width)
        mean_en = jnp.sum(e * n, 0, keepdims=True) * (1.0 / width)
        dmid = cot + r * (e - mean_e - n * mean_en)
        mid[:, cols] = dmid
        dm[width : 2 * width, cols] = dmid.astype(jnp.bfloat16)
        sums[:, 0:1] += jnp.sum(d * n, 1, keepdims=True)
        sums[:, 1:2] += jnp.sum(d, 1, keepdims=True)
        sums[:, 2:3] += jnp.sum(cot, 1, keepdims=True)
        return carry

    lax.fori_loop(0, blocks_n, middle, 0)
    serve("middle")
    small = band // 2
    for b in range(bs):
        dm[half + b * small : half + (b + 1) * small, :] = dm[
            rows_at(width + b * band + core * small, small), :
        ]
    first_out = first_up + up_band
    for xx in range(2):
        grad = dot(dm[half:width, :], otf[xx * lanes : (xx + 1) * lanes, :], NT)
        grad = grad.astype(jnp.bfloat16)
        for b in range(bs):
            bsum[xx, b // 2, b % 2, first_out : first_out + small, :] = grad[
                b * small : (b + 1) * small, :
            ]
    dm[0:half, :] = dot(
        w_out[rows_at(core * half, half), :], dm[width : 2 * width, :], NN
    ).astype(jnp.bfloat16)
    serve("w_out")

    whole_loads = [
        local(24, w_qkv_in.at[:, 0:width], w_up.at[0:width, :]),
        local(25, w_qkv_in.at[:, width : 2 * width], w_up.at[width : 2 * width, :]),
        local(26, w_qkv_in.at[:, 2 * width : 3 * width], w_down.at[0:width, :]),
    ]
    for load in whole_loads:
        load.start()
    hand_out = remote(base + 2, hand.at[0], out.at[x], to_x)

    def give_output():
        out_copy.wait()
        for k in range(2):
            cols = slice(k * block, (k + 1) * block)
            rows = jnp.transpose(
                (keep[:, cols] + orecv[:, cols].astype(jnp.float32)).astype(jnp.bfloat16)
            )

            @pl.when(x == k)
            def _():
                out[k] = rows

            @pl.when(x != k)
            def _():
                hand[0] = rows

        hand_out.start()

    give_output()
    serve("given")

    def far_copy(h, j):
        mine = rows_at(j * width + core * half + h * 64, 64)
        return remote(
            base + 3 + h * 3 + j, gd.at[mine, :], far.at[rows_at(j * half + h * 64, 64), :], to_core
        )

    def head_back(h, slot, ksum, vsum):
        kept_load(h, slot).wait()
        qrow, krow, vrow = (rows_at(j * half + h * 64, 64) for j in range(3))
        mine = [rows_at(j * width + core * half + h * 64, 64) for j in range(3)]
        valn = jnp.transpose(qkv[vrow, :])
        grads = (dm[rows_at(h * 64, 64), :].astype(jnp.float32) * inv[h, 0:1, :]).astype(
            jnp.bfloat16
        )
        o_rows = otf[rows_at(core * half + h * 64, 64), :]
        delta = jnp.sum(grads.astype(jnp.float32) * o_rows.astype(jnp.float32), 0, keepdims=True)
        ksum[...] = jnp.zeros_like(ksum)
        vsum[...] = jnp.zeros_like(vsum)
        for p in range(pairs_n):
            before, split, after = p * wide, p * wide + block, (p + 1) * wide
            at_row = p * p * block
            cols, late = slice(before, after), slice(split, after)
            side = slice(p * block, (p + 1) * block)
            low = kept[slot, at_row : at_row + split, :]
            dprob = dot(valn[0:split, :], grads[:, cols], NN)
            dscore = (low.astype(jnp.float32) * (dprob - delta[:, cols])).astype(jnp.bfloat16)
            last = kept[slot, kept.shape[1] - block : kept.shape[1], side]
            dprob = dot(valn[late, :], grads[:, late], NN)
            dlast = (last.astype(jnp.float32) * (dprob - delta[:, late])).astype(jnp.bfloat16)
            dquery = dot(qkv[krow, 0:split], dscore, NN)
            dquery = jnp.concatenate(
                [dquery[:, :block], dquery[:, block:] + dot(qkv[krow, late], dlast, NN)], 1
            )
            gd[mine[0], cols] = (dquery * 0.125).astype(jnp.bfloat16)
            ksum[:, 0:split] += dot(qkv[qrow, cols], dscore, NT)
            vsum[:, 0:split] += dot(grads[:, cols], low, NT)
            ksum[:, late] += dot(qkv[qrow, late], dlast, NT)
            vsum[:, late] += dot(grads[:, late], last, NT)
        gd[mine[1], :] = ksum[...].astype(jnp.bfloat16)
        gd[mine[2], :] = vsum[...].astype(jnp.bfloat16)
        for j in range(3):
            far_copy(h, j).start()

        @pl.when(h + 2 < heads)
        def _():
            kept_load(h + 2, slot).start()

        for at_head in range(slot, heads, 2):

            @pl.when(h == at_head)
            def _():
                serve("head%d" % at_head)

    def back_pair(i, carry):
        for e in range(2):
            head_back(2 * i + e, e, ksum.at[e], vsum.at[e])
        return carry

    lax.fori_loop(0, heads // 2, back_pair, 0)
    own_loads = [local(18 + k, h_far.at[k], keep.at[:, k * block : (k + 1) * block]) for k in range(2)]
    for load in own_loads:
        load.start()

    for h in range(heads):
        for j in range(3):
            far_copy(h, j).wait()
    for j in range(3):
        gd[rows_at(j * width + (1 - core) * half, half), :] = far[j * half : (j + 1) * half, :]
    qkv_band = 3 * width // bs
    qkv_small = qkv_band // 2
    for b in range(bs):
        dm[b * qkv_small : (b + 1) * qkv_small, :] = gd[
            rows_at(b * qkv_band + core * qkv_small, qkv_small), :
        ]
    first_qkv = first_out + small
    for xx in range(2):
        grad = dot(dm[0 : bs * qkv_small, :], at[xx * lanes : (xx + 1) * lanes, :], NT)
        grad = grad.astype(jnp.bfloat16)
        for b in range(bs):
            bsum[xx, b // 2, b % 2, first_qkv : first_qkv + qkv_small, :] = grad[
                b * qkv_small : (b + 1) * qkv_small, :
            ]
    serve("qkv")

    for load in whole_loads + own_loads:
        load.wait()
    gpass[...] = jnp.zeros_like(gpass)
    hand_in = remote(base + 21, hand.at[1], gin.at[x], to_x)
    for k in range(2):
        mine = own_cols(k)
        da = dot(w_up[0:width, :], gd[0:width, mine], NN)
        da += dot(w_up[width : 2 * width, :], gd[width : 2 * width, mine], NN)
        da += dot(w_down[0:width, :], gd[2 * width : 3 * width, mine], NN)
        h = keep[:, k * block : (k + 1) * block]
        shifted = h - jnp.sum(h, 0, keepdims=True) * (1.0 / width)
        spread = jnp.sum(shifted * shifted, 0, keepdims=True) * (1.0 / width)
        r = lax.rsqrt(spread + 1e-05)
        n = shifted * r
        e = da * vecs[:, 5:6]
        mean_e = jnp.sum(e, 0, keepdims=True) * (1.0 / width)
        mean_en = jnp.sum(e * n, 0, keepdims=True) * (1.0 / width)
        dh = mid[:, mine] + r * (e - mean_e - n * mean_en)
        rows = jnp.transpose(dh).astype(jnp.bfloat16)

        @pl.when(x == k)
        def _():
            gin[k] = rows

        @pl.when(x != k)
        def _():
            hand[1] = rows
            hand_in.start()

        sums[:, 3:4] += jnp.sum(da * n, 1, keepdims=True)
        sums[:, 4:5] += jnp.sum(da, 1, keepdims=True)
        kind = lax.broadcasted_iota(jnp.int32, (16, block), 0).astype(jnp.float32)
        onehot = jnp.where(kind == prow[0:1, mine], 1.0, 0.0).astype(jnp.bfloat16)
        high = dh.astype(jnp.bfloat16)
        rest = dh - high.astype(jnp.float32)
        second_part = rest.astype(jnp.bfloat16)
        tail = (rest - second_part.astype(jnp.float32)).astype(jnp.bfloat16)
        gpass[...] += dot(onehot, high, NT) + dot(onehot, second_part, NT) + dot(onehot, tail, NT)
        serve("input%d" % k)

    lines = jnp.transpose(sums[...])
    vector[0:5, :] = gpass[0:5, :]
    vector[5:7, :] = lines[3:5, :]
    vector[7:10, :] = lines[0:3, :] * 0.5
    for i, peer in enumerate((to_core, to_x, to_y)):
        copy = remote(base + 22 + i, vector, vrecv.at[i], peer)
        copy.start()
        copy.wait()
        vector[...] = vector[...] + vrecv[i]
        serve("sum%d" % i)
    copies = [
        remote(base + 25 + i, vector, vrecv.at[3 + z], peer) for i, peer in enumerate(to_z)
    ]
    for copy in copies:
        copy.start()
    vrecv[3 + z] = vector[...]

    own_rows = down_recv.shape[0]
    down_copy = remote(
        base + 28, bsum.at[x, z, y, rows_at((1 - core) * own_rows, own_rows), :], down_recv, to_core
    )

    def swap_lanes(i, r0, r1):
        wide = lanes // 2
        v = bsum[x, z, y, r0:r1, :]
        stage_send[r0 - first_up : r1 - first_up, 0:wide] = jnp.where(
            core == 0, v[:, wide:lanes], v[:, 0:wide]
        )
        at_rows = slice(r0 - first_up, r1 - first_up)
        return remote(base + i, stage_send.at[at_rows, :], stage_recv.at[at_rows, :], to_core)

    def both_cores(mine, got):
        return jnp.where(core == 0, mine, got), jnp.where(core == 0, got, mine)

    def put(result, r0, r1):
        wide = lanes // 2
        v = bsum[x, z, y, r0:r1, :].astype(jnp.float32)
        mine = jnp.where(core == 0, v[:, 0:wide], v[:, wide:lanes])
        got = stage_recv[r0 - first_up : r1 - first_up, 0:wide].astype(jnp.float32)
        result[...] = jnp.transpose(jnp.concatenate(both_cores(mine, got), 0))

    serve("end0")
    down_copy.start()
    serve("end1")
    up_copy = swap_lanes(29, first_up, first_qkv)
    up_copy.start()
    serve("end2")
    qkv_copy = swap_lanes(30, first_qkv, first_qkv + qkv_small)
    qkv_copy.start()
    down_copy.wait()
    mine = bsum[x, z, y, rows_at(core * own_rows, own_rows), :].astype(jnp.float32)
    for c, piece in enumerate(both_cores(mine, down_recv[...].astype(jnp.float32))):
        for i in range(lanes // part):
            at_row = (2 * i + c) * part
            gdown[:, at_row : at_row + part] = piece[:, i * part : (i + 1) * part]
    up_copy.wait()
    put(gup, first_up, first_out)
    put(gout, first_out, first_qkv)
    for copy in copies:
        copy.wait()
    vector[...] = (vrecv[3] + vrecv[4]) + (vrecv[5] + vrecv[6])
    hand_out.wait()
    hand_in.wait()
    qkv_copy.wait()
    put(gqkv, first_qkv, first_qkv + qkv_small)


def finish_kernel(
    out_in, gin_in, vector_in, gqkv_in, gout_in, gup_in, gdown_in,
    out, gin, gpass, gain1, bias1, gqkv, gout, gain2, bias2, gup, gb_up, gdown, gb_down,
    vector, sem,
):
    pairs = (
        (out_in, out), (gin_in, gin), (gqkv_in, gqkv), (gout_in, gout), (gup_in, gup), (gdown_in, gdown),
        (vector_in, vector),
    )
    copies = [pltpu.make_async_copy(a, b, sem.at[i]) for i, (a, b) in enumerate(pairs)]
    for copy in copies:
        copy.start()
    for copy in copies:
        copy.wait()
    width = vector.shape[1]
    gpass[...] = vector[0:5, :]
    for i, ref in enumerate((gain1, bias1, gain2, bias2, gb_down)):
        ref[...] = vector[5 + i, :]
    for i in range(4):
        gb_up[pl.ds(i * width, width)] = vector[10 + i, :]


def shaped(*dims, kind=jnp.bfloat16):
    return jax.ShapeDtypeStruct(dims, kind)


shares = ((64, 80, 48), (64, 80, 48), (16, 16, 16), (48, 48, 48))
plan = {
    "down0": ((0, "start_e"),),
    "down1": ((0, "start_c"), (0, "start_a")),
    "hidden": ((0, "e1"),),
    "dm": ((0, "a2"),),
    "up0": ((0, "e2"),),
    "up1": ((1, "start"), (0, "c2")),
    "out": (),
    "middle": ((0, "e3"),),
    "w_out": ((2, "start"), (1, "e1")),
    "given": ((0, "z0"), (0, "e4"), (1, "a2")),
    "head0": (),
    "head1": ((0, "z1"), (1, "c2"), (1, "e2")),
    "head2": ((2, "e1"), (2, "a2"), (2, "c2")),
    "head3": ((0, "z2"),),
    "head4": ((1, "e3"),),
    "head5": ((1, "z0"), (2, "e2")),
    "qkv": ((3, "start"), (0, "z3"), (1, "e4")),
    "input0": ((1, "z1"), (2, "e3"), (2, "z0"), (3, "e1")),
    "input1": ((1, "z2"), (2, "e4"), (3, "a2")),
    "sum0": ((3, "e2"), (2, "z1"), (3, "c2")),
    "sum1": ((1, "z3"), (2, "z2")),
    "sum2": ((3, "e3"),),
    "end0": (),
    "end1": ((2, "z3"), (3, "z0")),
    "end2": ((3, "e4"), (3, "z1"), (3, "z2"), (3, "z3")),
}


def regrouped(
    block_input, lengths, pass_ids, pass_embed, ln1_gain, ln1_bias, w_qkv, w_out,
    ln2_gain, ln2_bias, w_up, b_up, w_down, b_down, cotangent, batch_n
):
    width = block_input.shape[2]
    total = 4 * block_input.shape[1]
    inner = w_up.shape[1]
    own_in, half, lanes = inner // 2, width // 2, width // 2
    band = inner // batch_n // 2
    z_n = batch_n // 2
    blocks_n = total // block
    kept_rows = (blocks_n // 2) ** 2 * block + block
    chunks, a0, c0, e0, r0 = [], 0, 0, 0, 0
    for ne, nc, na in shares:
        chunks.append((r0, r0 + ne, r0 + ne + nc, r0 + ne + nc + na, a0, c0, e0))
        r0, a0, c0, e0 = r0 + ne + nc + na, a0 + na, c0 + nc, e0 + ne
    down_n = 2 * width // batch_n
    anywhere = pl.BlockSpec(memory_space=pl.ANY)
    whole = pl.BlockSpec(memory_space=pltpu.VMEM)
    low, full = jnp.bfloat16, jnp.float32
    copies_n = 22 * len(chunks) + 9 + half // 64 + 31
    output, grad_input, vector, grad_qkv, grad_out, grad_up, grad_down, _, _ = pl.pallas_call(
        functools.partial(block_kernel, chunks=tuple(chunks), plan=plan),
        out_shape=[
            shaped(2, block, width),
            shaped(2, block, width),
            shaped(16, width, kind=full),
            shaped(width // 4, 3 * width // batch_n, kind=full),
            shaped(width // 4, width // batch_n, kind=full),
            shaped(width // 4, inner // batch_n, kind=full),
            shaped(width // batch_n, inner // 4, kind=full),
            shaped(half // 64, kept_rows, 2 * block),
            shaped(2, width, block, kind=full),
        ],
        in_specs=[pl.BlockSpec(memory_space=pltpu.SMEM)] + [anywhere] * 6 + [whole] * 8,
        out_specs=[whole] * 7 + [anywhere] * 2,
        scratch_shapes=[
            pltpu.VMEM((width, total), full),
            pltpu.VMEM((width, 2 * block), full),
            pltpu.VMEM((width, total), low),
            pltpu.VMEM((3 * half, total), low),
            pltpu.VMEM((width, total), low),
            pltpu.VMEM((width, total), low),
            pltpu.VMEM((width, total), low),
            pltpu.VMEM((2 * own_in, total), low),
            pltpu.VMEM((3 * half, total), low),
            pltpu.VMEM((2 * width, total), low),
            pltpu.VMEM((2, kept_rows, 2 * block), low),
            pltpu.VMEM((width, width), low),
            pltpu.VMEM((own_in, width), low),
            pltpu.VMEM((own_in, width), low),
            pltpu.VMEM((2, z_n, 2, r0, lanes), low),
            pltpu.VMEM((z_n, 2, a0, lanes), low),
            pltpu.VMEM((z_n, a0, lanes), low),
            pltpu.VMEM((2, z_n, c0, lanes), low),
            pltpu.VMEM((z_n, c0, lanes), low),
            pltpu.VMEM((2, e0, lanes), low),
            pltpu.VMEM((e0, lanes), low),
            pltpu.VMEM((z_n + 1, a0 + c0, lanes), low),
            pltpu.VMEM((z_n + 1, 2, 2, e0, lanes), low),
            pltpu.VMEM((width, 2 * block), low),
            pltpu.VMEM((width, 2 * block), low),
            pltpu.VMEM((2, block, width), low),
            pltpu.VMEM((width, 128), full),
            pltpu.VMEM((16, width), full),
            pltpu.VMEM((7, 16, width), full),
            pltpu.VMEM((2, 64, total), full),
            pltpu.VMEM((2, 64, total), full),
            pltpu.VMEM((r0 - down_n, 256), low),
            pltpu.VMEM((r0 - down_n, 256), low),
            pltpu.VMEM((down_n // 2, lanes), low),
            pltpu.VMEM((16, width), full),
            pltpu.VMEM((width, 16), full),
            pltpu.VMEM((own_in, 8), full),
            pltpu.VMEM((half // 64, 8, total), full),
            pltpu.VMEM((8, total), full),
            pltpu.VMEM((total, 16), low),
            pltpu.VMEM((16, total), low),
            pltpu.VMEM((4, 2, block), jnp.int32),
            pltpu.SemaphoreType.DMA((27,)),
            pltpu.SemaphoreType.DMA((copies_n,)),
            pltpu.SemaphoreType.DMA((copies_n,)),
        ],
        compiler_params=pltpu.CompilerParams(
            vmem_limit_bytes=63 << 20, collective_id=0, has_side_effects=True
        ),
        cost_estimate=pl.CostEstimate(flops=int(60e9), bytes_accessed=0, transcendentals=0),
        name="block",
    )(
        lengths, block_input, cotangent, w_up, w_qkv, w_out,
        w_down.reshape(batch_n, 2, band, width), pass_ids, pass_embed,
        ln1_gain, ln1_bias, ln2_gain, ln2_bias, b_up, b_down,
    )
    results = [output, grad_input, vector, grad_qkv, grad_out, grad_up, grad_down]
    line = jax.ShapeDtypeStruct((width,), full)
    done = pl.pallas_call(
        finish_kernel,
        out_shape=[
            shaped(2, block, width),
            shaped(2, block, width),
            shaped(5, width, kind=full),
            line,
            line,
            jax.ShapeDtypeStruct(grad_qkv.shape, full),
            jax.ShapeDtypeStruct(grad_out.shape, full),
            line,
            line,
            jax.ShapeDtypeStruct(grad_up.shape, full),
            jax.ShapeDtypeStruct((inner,), full),
            jax.ShapeDtypeStruct(grad_down.shape, full),
            line,
        ],
        in_specs=[anywhere] * 7,
        out_specs=[whole] * 13,
        scratch_shapes=[pltpu.VMEM((16, width), full), pltpu.SemaphoreType.DMA((7,))],
        compiler_params=pltpu.CompilerParams(vmem_limit_bytes=62 << 20),
        name="finish",
    )(*results)
    done = list(done)
    done[11] = jnp.transpose(done[11])
    return tuple(done)


def solution(mesh):
    batch_n = mesh.shape["batch"]
    few = mesh.shape["seq"] == 4 and batch_n == 8
    body = functools.partial(regrouped, batch_n=batch_n) if few else local
    return jax.shard_map(
        body,
        mesh=mesh,
        in_specs=(
            P("batch", "seq", None),
            P("batch"),
            P("batch", "seq"),
            P(),
            P(),
            P(),
            P(),
            P(),
            P(),
            P(),
            P(),
            P(),
            P(),
            P(),
            P("batch", "seq", None),
        ),
        out_specs=(
            P("batch", "seq", None),
            P("batch", "seq", None),
            P(),
            P(),
            P(),
            P("seq", "batch"),
            P("seq", "batch"),
            P(),
            P(),
            P("seq", "batch"),
            P(),
            P("seq", "batch"),
            P(),
        ),
        check_vma=False,
    )
```

```python
import functools

import jax
import jax.numpy as jnp
from jax import lax
from jax.experimental import pallas as pl
from jax.experimental.pallas import tpu as pltpu
from jax.sharding import PartitionSpec as P

H = 12


negative = -1e30
key_block = 1024
query_block = 512
highest = lax.Precision.HIGHEST


def layer_norm(hidden, gain, offset):
    centre = jnp.mean(hidden, -1, keepdims=True)
    shifted = hidden - centre
    spread = jnp.mean(shifted * shifted, -1, keepdims=True)
    return shifted * lax.rsqrt(spread + 1e-05) * gain + offset


def gelu_tanh(values):
    return jax.nn.gelu(values, approximate=True)


def visible(query_place, query_pass, key_place, key_pass, length):
    earlier = key_place[None, :] < query_place[:, None]
    allowed = earlier & (key_pass[None, :] <= query_pass[:, None]) & (key_place[None, :] < length)
    return allowed | (key_place[None, :] == query_place[:, None])


def masked_scores(query_part, key_part, factor, seen):
    raw = (
        jnp.einsum("qhd,khd->hqk", query_part, key_part, preferred_element_type=jnp.float32)
        * factor
    )
    return jnp.where(seen[None], raw, negative)


def split_blocks(arrays, block_len):
    return tuple(
        (
            array.reshape((array.shape[0] // block_len, block_len) + array.shape[1:])
            for array in arrays
        )
    )


def chance_of(query_part, key_part, log_part, seen, factor):
    scores = masked_scores(query_part, key_part, factor, seen)
    return jnp.where(seen[None], jnp.exp(scores - log_part[..., None]), 0.0)


def grad_pieces(query_part, dout_part, log_part, delta_part, key_part, value_part, seen, factor):
    chance = chance_of(query_part, key_part, log_part, seen, factor)
    dprob = jnp.einsum("qhd,khd->hqk", dout_part, value_part, preferred_element_type=jnp.float32)
    dscore = (chance * (dprob - delta_part[..., None])).astype(jnp.bfloat16)
    return (dscore, chance.astype(jnp.bfloat16))


def attend_row(queries, query_place, query_pass, key_rows, value_rows, key_pass, length):
    factor = queries.shape[-1] ** (-0.5)
    places = jnp.arange(key_rows.shape[0], dtype=jnp.int32)
    key_parts = split_blocks(
        (key_rows, value_rows, key_pass, places), min(key_block, key_rows.shape[0])
    )
    query_len = min(query_block, queries.shape[0])
    query_parts = split_blocks((queries, query_place, query_pass), query_len)

    def attend_one_block(query_args):
        query_part, place_part, pass_part = query_args

        def running(carry, key_args):
            peak, summed, total_out = carry
            key_part, value_part, kpass_part, kplace_part = key_args
            seen = visible(place_part, pass_part, kplace_part, kpass_part, length)
            scores = masked_scores(query_part, key_part, factor, seen)
            new_peak = jnp.maximum(peak, jnp.max(scores, -1))
            terms = jnp.where(seen[None], jnp.exp(scores - new_peak[..., None]), 0.0)
            rescale = jnp.exp(peak - new_peak)
            summed = summed * rescale + jnp.sum(terms, -1)
            added = jnp.einsum(
                "hqk,khd->qhd",
                terms.astype(jnp.bfloat16),
                value_part,
                preferred_element_type=jnp.float32,
            )
            total_out = total_out * rescale.T[..., None] + added
            return ((new_peak, summed, total_out), None)

        heads_n = query_part.shape[1]
        start = (
            jnp.full((heads_n, query_len), negative, jnp.float32),
            jnp.zeros((heads_n, query_len), jnp.float32),
            jnp.zeros(query_part.shape, jnp.float32),
        )
        (peak, summed, total_out), _ = lax.scan(running, start, key_parts)
        log_total = peak + jnp.log(summed)
        result = total_out / summed.T[..., None]
        return (result, log_total)

    results, log_totals = lax.map(attend_one_block, query_parts)
    heads_n = queries.shape[1]
    return (
        results.reshape(queries.shape),
        jnp.moveaxis(log_totals, 1, 0).reshape(heads_n, queries.shape[0]),
    )


def backward_row(
    queries,
    douts,
    outs_kept,
    log_totals,
    query_place,
    query_pass,
    key_rows,
    value_rows,
    key_pass,
    length,
):
    factor = queries.shape[-1] ** (-0.5)
    places = jnp.arange(key_rows.shape[0], dtype=jnp.int32)
    key_parts = split_blocks(
        (key_rows, value_rows, key_pass, places), min(key_block, key_rows.shape[0])
    )
    query_len = min(query_block, queries.shape[0])
    heads_n = queries.shape[1]
    block_count = queries.shape[0] // query_len
    log_parts = jnp.moveaxis(log_totals.reshape(heads_n, block_count, query_len), 1, 0)
    query_parts = split_blocks((queries, douts, outs_kept, query_place, query_pass), query_len)

    def backward_one_block(carry, query_args):
        query_part, dout_part, kept_part, place_part, pass_part, log_part = query_args
        delta_part = jnp.einsum("qhd,qhd->hq", dout_part.astype(jnp.float32), kept_part)

        def add_grads(dquery, key_args):
            key_part, value_part, kpass_part, kplace_part = key_args
            seen = visible(place_part, pass_part, kplace_part, kpass_part, length)
            dscore, low_chance = grad_pieces(
                query_part, dout_part, log_part, delta_part, key_part, value_part, seen, factor
            )
            dquery = dquery + factor * jnp.einsum(
                "hqk,khd->qhd", dscore, key_part, preferred_element_type=jnp.float32
            )
            dkey = factor * jnp.einsum(
                "hqk,qhd->khd", dscore, query_part, preferred_element_type=jnp.float32
            )
            dvalue = jnp.einsum(
                "hqk,qhd->khd", low_chance, dout_part, preferred_element_type=jnp.float32
            )
            return (dquery, (dkey, dvalue))

        dquery, key_terms = lax.scan(add_grads, jnp.zeros(query_part.shape, jnp.float32), key_parts)
        carry = (
            carry[0] + key_terms[0].reshape(key_rows.shape),
            carry[1] + key_terms[1].reshape(value_rows.shape),
        )
        return (carry, (dquery, delta_part))

    start = (jnp.zeros(key_rows.shape, jnp.float32), jnp.zeros(value_rows.shape, jnp.float32))
    key_sums, (dqueries, deltas) = lax.scan(backward_one_block, start, query_parts + (log_parts,))
    return (
        dqueries.reshape(queries.shape),
        jnp.moveaxis(deltas, 1, 0).reshape(heads_n, queries.shape[0]),
        key_sums,
    )


def local(
    block_input,
    lengths,
    pass_ids,
    pass_embed,
    ln1_gain,
    ln1_bias,
    w_qkv,
    w_out,
    ln2_gain,
    ln2_bias,
    w_up,
    b_up,
    w_down,
    b_down,
    cotangent,
):
    row_count, seg_len, width = block_input.shape
    heads_n = H
    head_size = width // heads_n
    onehot = (
        pass_ids[..., None] == jnp.arange(pass_embed.shape[0], dtype=jnp.int32)[None, None, :]
    ).astype(jnp.float32)
    hidden_in = block_input.astype(jnp.float32) + jnp.einsum(
        "rsp,pd->rsd", onehot, pass_embed, precision=highest
    )
    normed, norm_back = jax.vjp(layer_norm, hidden_in, ln1_gain, ln1_bias)
    normed_low = normed.astype(jnp.bfloat16)
    qkv = jnp.einsum("rsd,de->rse", normed_low, w_qkv, preferred_element_type=jnp.float32)
    queries = qkv[..., :width].astype(jnp.bfloat16)
    key_flat = qkv[..., width : 2 * width].astype(jnp.bfloat16)
    value_flat = qkv[..., 2 * width :].astype(jnp.bfloat16)
    pass_low = pass_ids.astype(jnp.bfloat16)
    key_all, value_all, pass_all = (
        lax.all_gather(key_flat, "seq", axis=1, tiled=True),
        lax.all_gather(value_flat, "seq", axis=1, tiled=True),
        lax.all_gather(pass_low, "seq", axis=1, tiled=True),
    )
    total_len = key_all.shape[1]
    key_all = key_all.reshape(row_count, total_len, heads_n, head_size)
    value_all = value_all.reshape(row_count, total_len, heads_n, head_size)
    pass_all = pass_all.astype(jnp.float32)
    offset = lax.axis_index("seq") * seg_len
    query_place = offset + jnp.arange(seg_len, dtype=jnp.int32)
    query_pass = pass_ids.astype(jnp.float32)
    query_heads = queries.reshape(row_count, seg_len, heads_n, head_size)
    attended_rows = []
    log_rows = []
    for row in range(row_count):
        attended, log_total = attend_row(
            query_heads[row],
            query_place,
            query_pass[row],
            key_all[row],
            value_all[row],
            pass_all[row],
            lengths[row],
        )
        attended_rows.append(attended)
        log_rows.append(log_total)
    attended_low = jnp.stack(attended_rows).astype(jnp.bfloat16).reshape(row_count, seg_len, width)
    branch = jnp.einsum("rsd,de->rse", attended_low, w_out, preferred_element_type=jnp.float32)
    middle = hidden_in + branch
    normed2, norm2_back = jax.vjp(layer_norm, middle, ln2_gain, ln2_bias)
    normed2_low = normed2.astype(jnp.bfloat16)
    pre_act = (
        jnp.einsum("rsd,df->rsf", normed2_low, w_up, preferred_element_type=jnp.float32) + b_up
    )
    active, active_back = jax.vjp(gelu_tanh, pre_act)
    active_low = active.astype(jnp.bfloat16)
    result = (
        middle
        + jnp.einsum("rsf,fd->rsd", active_low, w_down, preferred_element_type=jnp.float32)
        + b_down
    )
    output = result.astype(jnp.bfloat16)
    cot_f = cotangent.astype(jnp.float32)
    grad_active = jnp.einsum("rsd,fd->rsf", cotangent, w_down, preferred_element_type=jnp.float32)
    grad_w_down = jnp.einsum(
        "rsf,rsd->fd", active_low, cotangent, preferred_element_type=jnp.float32
    )
    grad_b_down = jnp.sum(cot_f, (0, 1))
    grad_pre = active_back(grad_active)[0].astype(jnp.bfloat16)
    grad_b_up = jnp.sum(grad_pre.astype(jnp.float32), (0, 1))
    grad_w_up = jnp.einsum("rsd,rsf->df", normed2_low, grad_pre, preferred_element_type=jnp.float32)
    grad_normed2 = jnp.einsum("rsf,df->rsd", grad_pre, w_up, preferred_element_type=jnp.float32)
    grad_mid_norm, grad_ln2_gain, grad_ln2_bias = norm2_back(grad_normed2)
    grad_middle = cot_f + grad_mid_norm
    grad_branch = grad_middle.astype(jnp.bfloat16)
    grad_w_out = jnp.einsum(
        "rsd,rse->de", attended_low, grad_branch, preferred_element_type=jnp.float32
    )
    grad_attended = jnp.einsum(
        "rse,de->rsd", grad_branch, w_out, preferred_element_type=jnp.float32
    ).astype(jnp.bfloat16)
    dout_heads = grad_attended.reshape(row_count, seg_len, heads_n, head_size)
    dquery_rows = []
    dkey_rows = []
    dvalue_rows = []
    for row in range(row_count):
        dquery, _, key_sums = backward_row(
            query_heads[row],
            dout_heads[row],
            attended_rows[row],
            log_rows[row],
            query_place,
            query_pass[row],
            key_all[row],
            value_all[row],
            pass_all[row],
            lengths[row],
        )
        dquery_rows.append(dquery)
        dkey_rows.append(key_sums[0].reshape(total_len, width))
        dvalue_rows.append(key_sums[1].reshape(total_len, width))
    dkey_sum, dvalue_sum = (
        lax.psum_scatter(
            jnp.stack(dkey_rows).astype(jnp.bfloat16), "seq", scatter_dimension=1, tiled=True
        ).astype(jnp.float32),
        lax.psum_scatter(
            jnp.stack(dvalue_rows).astype(jnp.bfloat16), "seq", scatter_dimension=1, tiled=True
        ).astype(jnp.float32),
    )
    dquery_all = jnp.stack(dquery_rows).reshape(row_count, seg_len, width)
    grad_qkv = jnp.concatenate(
        [
            dquery_all.astype(jnp.bfloat16),
            dkey_sum.astype(jnp.bfloat16),
            dvalue_sum.astype(jnp.bfloat16),
        ],
        -1,
    )
    grad_w_qkv = jnp.einsum("rsd,rse->de", normed_low, grad_qkv, preferred_element_type=jnp.float32)
    grad_normed = jnp.einsum("rse,de->rsd", grad_qkv, w_qkv, preferred_element_type=jnp.float32)
    grad_in_norm, grad_ln1_gain, grad_ln1_bias = norm_back(grad_normed)
    grad_hidden = grad_middle + grad_in_norm
    grad_input = grad_hidden.astype(jnp.bfloat16)
    grad_pass = jnp.einsum("rsp,rsd->pd", onehot, grad_hidden, precision=highest)
    matrices = (
        lax.psum_scatter(
            grad_w_qkv.astype(jnp.bfloat16), "seq", scatter_dimension=0, tiled=True
        ).astype(jnp.float32),
        lax.psum_scatter(
            grad_w_out.astype(jnp.bfloat16), "seq", scatter_dimension=0, tiled=True
        ).astype(jnp.float32),
        lax.psum_scatter(
            grad_w_up.astype(jnp.bfloat16), "seq", scatter_dimension=0, tiled=True
        ).astype(jnp.float32),
        lax.psum_scatter(
            grad_w_down.astype(jnp.bfloat16), "seq", scatter_dimension=0, tiled=True
        ).astype(jnp.float32),
    )
    matrices = (
        lax.psum_scatter(
            matrices[0].astype(jnp.bfloat16), "batch", scatter_dimension=1, tiled=True
        ).astype(jnp.float32),
        lax.psum_scatter(
            matrices[1].astype(jnp.bfloat16), "batch", scatter_dimension=1, tiled=True
        ).astype(jnp.float32),
        lax.psum_scatter(
            matrices[2].astype(jnp.bfloat16), "batch", scatter_dimension=1, tiled=True
        ).astype(jnp.float32),
        lax.psum_scatter(
            matrices[3].astype(jnp.bfloat16), "batch", scatter_dimension=1, tiled=True
        ).astype(jnp.float32),
    )
    vectors = lax.psum(
        (
            grad_pass,
            grad_ln1_gain,
            grad_ln1_bias,
            grad_ln2_gain,
            grad_ln2_bias,
            grad_b_up,
            grad_b_down,
        ),
        ("seq", "batch"),
    )
    return (
        output,
        grad_input,
        vectors[0],
        vectors[1],
        vectors[2],
        matrices[0],
        matrices[1],
        vectors[3],
        vectors[4],
        matrices[2],
        vectors[5],
        matrices[3],
        vectors[6],
    )


NN = (((1,), (0,)), ((), ()))
NT = (((1,), (1,)), ((), ()))
TN = (((0,), (0,)), ((), ()))
vmem_bytes = 60 << 20
block = 256


def dot(left, right, form):
    return lax.dot_general(left, right, form, preferred_element_type=jnp.float32)


mesh_ids = pl.DeviceIdType.MESH


def block_kernel(
    lengths,
    block_in, cot_in, w_up_in, w_qkv_in, w_out_in, w_down_in,
    pass_in, embed_in, gain1, bias1, gain2, bias2, b_up_in, b_down_in,
    out, gin, vector, gqkv, gout, gup, gdown,
    kept_far, h_far,
    mid, keep, at, qkv, otf, ct, mt, gd, far, dm, kept, w_out, w_up, w_down,
    bsum, r1a, r2a, r1c, r2c, r2e, r3e, rz, rze,
    osend, orecv, hand, sums, gpass, vrecv, ksum, vsum, stage_send, stage_recv, down_recv,
    params, vecs, bcol, inv, prow, kmask, qhot, passes,
    lsem, ssem, rsem,
    *, chunks, plan,
):
    seq, bat = lax.axis_index("seq"), lax.axis_index("batch")
    x, core = seq // 2, seq % 2
    z, y = bat // 2, bat % 2
    to_core, to_x, to_y = (seq + 1 - 2 * core, bat), (seq + 2 - 4 * x, bat), (seq, bat + 1 - 2 * y)
    to_cross = (3 - seq, bat)
    to_z = [(seq, ((z + i) % 4) * 2 + y) for i in (1, 2, 3)]
    up_z, low_z = (seq, bat + 2), (seq, bat - 2)

    barrier = pltpu.get_barrier_semaphore()
    for peer in [to_core, to_x, to_y, to_cross] + to_z:
        pl.semaphore_signal(barrier, inc=1, device_id=peer, device_id_type=mesh_ids)

    width, total = mid.shape
    half = width // 2
    inner = w_up.shape[0]
    blocks_n = total // block
    heads = half // 64
    bs = 8

    def rows_at(first, count):
        return pl.ds(pl.multiple_of(first, 16), count)

    def lanes_at(first, count):
        return pl.ds(pl.multiple_of(first, 128), count)

    def own_cols(k):
        return lanes_at(core * block + k * 2 * block, block)

    def local(i, src, dst):
        return pltpu.make_async_copy(src, dst, lsem.at[i])

    def remote(i, src, dst, peer):
        return pltpu.make_async_remote_copy(
            src_ref=src, dst_ref=dst, send_sem=ssem.at[i], recv_sem=rsem.at[i],
            device_id=peer, device_id_type=mesh_ids,
        )

    part = w_down_in.shape[2]
    own_x = local(0, block_in.at[x], far.at[0:block, 0:width])
    own_c = local(1, cot_in.at[x], dm.at[0:block, 0:width])
    out_load = local(2, w_out_in, w_out)
    up_loads = [
        local(3 + p, w_up_in.at[:, p * width : (p + 1) * width],
              gd.at[p * width : (p + 1) * width, 0:width])
        for p in range(4)
    ]
    down_loads = [
        local(7 + i, w_down_in.at[i, core], w_down.at[i * part : (i + 1) * part, :])
        for i in range(bs)
    ]
    qkv_loads = [
        local(15 + j, w_qkv_in.at[:, j * width : (j + 1) * width],
              gd.at[j * width : (j + 1) * width, 0:width])
        for j in range(3)
    ]
    for load in [own_x] + up_loads + [own_c, out_load] + down_loads:
        load.start()

    base = 22 * len(chunks)
    x_far = remote(base, block_in.at[1 - x], far.at[block : 2 * block, 0:width], to_x)
    x_near = remote(base + 1, block_in.at[x], far.at[2 * block : 3 * block, 0:width], to_core)
    x_cross = remote(
        base + 2, far.at[block : 2 * block, 0:width], far.at[3 * block : 4 * block, 0:width], to_core
    )
    c_far = remote(base + 3, cot_in.at[1 - x], dm.at[block : 2 * block, 0:width], to_x)
    c_near = remote(base + 4, cot_in.at[x], dm.at[2 * block : 3 * block, 0:width], to_core)
    c_cross = remote(
        base + 5, dm.at[block : 2 * block, 0:width], dm.at[3 * block : 4 * block, 0:width], to_core
    )
    p_far = remote(base + 6, pass_in, passes.at[1], to_x)
    p_near = remote(base + 7, pass_in, passes.at[2], to_core)
    p_cross = remote(base + 8, pass_in, passes.at[3], to_cross)
    base += 9
    pl.semaphore_wait(barrier, 7)
    for copy in (p_far, x_far, x_near, p_near, p_cross, c_near):
        copy.start()


    def line_copy(i, d, up, part, slots):
        slot = d if up else jnp.where(z - 1 == d, 4, d)
        return remote(i + (d if up else 4 + d), part(d), slots(slot), up_z if up else low_z)

    def line_add(d, slot, part, slots):
        here, got = part(d), slots(slot)
        here[...] = here[...] + got[...]

    def line_start(i, part, slots):
        @pl.when(z == 0)
        def _():
            for d in (3, 2, 1):
                line_copy(i, d, True, part, slots).start()

        @pl.when(z == 3)
        def _():
            for d in (0, 1, 2):
                line_copy(i, d, False, part, slots).start()

    def line_pass(i, d, up, part, slots):
        copy = line_copy(i, d, up, part, slots)
        copy.wait_recv()
        line_add(d, d, part, slots)
        copy.start()

    def line_one(i, part, slots):
        @pl.when(z == 1)
        def _():
            line_pass(i, 3, True, part, slots)

        @pl.when(z == 2)
        def _():
            line_pass(i, 0, False, part, slots)

    def line_two(i, part, slots):
        @pl.when(z == 1)
        def _():
            line_pass(i, 2, True, part, slots)
            line_pass(i, 0, False, part, slots)

        @pl.when(z == 2)
        def _():
            line_pass(i, 1, False, part, slots)
            line_pass(i, 3, True, part, slots)

    def line_last(i, part, slots):
        for d in range(4):

            @pl.when(z == d)
            def _():
                if d > 0:
                    line_copy(i, d, True, part, slots).wait_recv()
                    line_add(d, d, part, slots)
                if d < 3:
                    line_copy(i, d, False, part, slots).wait_recv()
                    line_add(d, 4, part, slots)
                for e in range(4):
                    if e > d:
                        line_copy(i, e, True, part, slots).wait_send()
                    if e < d:
                        line_copy(i, e, False, part, slots).wait_send()

    class Chunk:
        def __init__(self, k):
            r0, rc, ra, r1, a0, c0, e0 = chunks[k]
            ne, nc, na = rc - r0, ra - rc, r1 - ra
            i = 22 * k
            rows_e, rows_c, rows_a = pl.ds(r0, ne), pl.ds(rc, nc), pl.ds(ra, na)
            got_a, got_c, got_e = pl.ds(a0, na), pl.ds(c0, nc), pl.ds(e0, ne)
            sub = bsum.at
            self.one_a = remote(i, sub[1 - x, :, :, rows_a, :], r1a.at[:, :, got_a, :], to_x)
            self.one_c = remote(i + 1, sub[:, :, 1 - y, rows_c, :], r1c.at[:, :, got_c, :], to_y)
            self.two_a = remote(i + 2, sub[x, :, 1 - y, rows_a, :], r2a.at[:, got_a, :], to_y)
            self.two_c = remote(i + 3, sub[1 - x, :, y, rows_c, :], r2c.at[:, got_c, :], to_x)
            self.two_e = remote(i + 4, sub[:, z, 1 - y, rows_e, :], r2e.at[:, got_e, :], to_y)
            self.three_e = remote(i + 5, sub[1 - x, z, y, rows_e, :], r3e.at[got_e, :], to_x)
            self.adds = [
                (sub[x, :, :, rows_a, :], r1a.at[:, :, got_a, :]),
                (sub[:, :, y, rows_c, :], r1c.at[:, :, got_c, :]),
                (sub[x, :, y, rows_a, :], r2a.at[:, got_a, :]),
                (sub[x, :, y, rows_c, :], r2c.at[:, got_c, :]),
                (sub[:, z, y, rows_e, :], r2e.at[:, got_e, :]),
                (sub[x, z, y, rows_e, :], r3e.at[got_e, :]),
            ]
            both, low = pl.ds(rc, na + nc), pl.ds(a0 + c0, na + nc)
            self.line_ac = (
                i + 6, lambda d: sub[x, d, y, both, :], lambda s: rz.at[s, low, :]
            )
            self.line_e = (
                i + 14, lambda d: sub[:, d, :, rows_e, :], lambda s: rze.at[s, :, :, got_e, :]
            )

        def add(self, j):
            here, got = self.adds[j]
            here[...] = here[...] + got[...]

        def start(self):
            line_start(*self.line_e)
            self.one_c.start()
            self.one_a.start()

        def start_a(self):
            self.one_a.start()

        def start_c(self):
            self.one_c.start()

        def start_e(self):
            line_start(*self.line_e)

        def e1(self):
            line_one(*self.line_e)

        def e2(self):
            line_two(*self.line_e)

        def e3(self):
            line_last(*self.line_e)
            self.two_e.start()

        def a2(self):
            self.one_a.wait()
            self.add(0)
            self.two_a.start()

        def c2(self):
            self.one_c.wait()
            self.add(1)
            self.two_c.start()

        def e4(self):
            self.two_e.wait()
            self.add(4)
            self.three_e.start()

        def z0(self):
            self.two_a.wait()
            self.add(2)
            self.two_c.wait()
            self.add(3)
            line_start(*self.line_ac)

        def z1(self):
            line_one(*self.line_ac)

        def z2(self):
            line_two(*self.line_ac)

        def z3(self):
            line_last(*self.line_ac)
            self.three_e.wait()
            self.add(5)
    steps = [Chunk(k) for k in range(len(chunks))]

    def serve(slot):
        for k, name in plan[slot]:
            getattr(steps[k], name)()

    params[...] = jnp.zeros_like(params)
    params[0:5, :] = embed_in[...]
    for i, ref in enumerate((gain1, bias1, gain2, bias2, b_down_in)):
        params[5 + i, :] = ref[...]
    for i in range(4):
        params[10 + i, :] = b_up_in[pl.ds(i * width, width)]
    vecs[...] = jnp.transpose(params[...])
    for b in range(bs):
        i, low = 10 + b // 2, b % 2 * 2 * part
        bcol[b * part : (b + 1) * part, :] = jnp.broadcast_to(
            jnp.where(
                core == 0,
                vecs[low : low + part, i : i + 1],
                vecs[low + part : low + 2 * part, i : i + 1],
            ),
            (part, 8),
        )
    for b in range(bs):
        p, low = b // 2, b % 2 * 2 * part
        if b % 2 == 0:
            up_loads[p].wait()
        turned = jnp.transpose(gd[p * width : (p + 1) * width, low : low + 2 * part])
        w_up[b * part : (b + 1) * part, :] = jnp.where(core == 0, turned[:part], turned[part:])
    for load in qkv_loads:
        load.start()
    passes[0] = pass_in[...]
    places = (2 * x + core, 2 * (1 - x) + core, 2 * x + 1 - core, 2 * (1 - x) + 1 - core)
    length = lengths[x]
    emb = jnp.where(lax.broadcasted_iota(jnp.int32, (8, width), 0) < 5, params[0:8, :], 0.0)
    emb_a = emb.astype(jnp.bfloat16)
    rest = emb - emb_a.astype(jnp.float32)
    emb_b = rest.astype(jnp.bfloat16)
    emb_c = (rest - emb_b.astype(jnp.float32)).astype(jnp.bfloat16)

    def take(k):
        cols = lanes_at(places[k] * block, block)
        rows = rows_at(places[k] * block, block)
        got = passes[k]
        line = jnp.where(x == 0, got[0:1, :], got[1:2, :])
        prow[:, cols] = jnp.broadcast_to(line.astype(jnp.float32), (8, block))
        kind = lax.broadcasted_iota(jnp.int32, (16, block), 0)
        spot = lax.broadcasted_iota(jnp.int32, (16, block), 1) + places[k] * block
        onehot = jnp.where(kind == line, 1.0, 0.0).astype(jnp.bfloat16)
        qhot[:, cols] = onehot
        hidden = jnp.where((line > kind) | (spot >= length), negative, 0.0)
        kmask[rows, :] = jnp.transpose(hidden).astype(jnp.bfloat16)
        hot = onehot[0:8, :]
        added = dot(emb_a, hot, TN) + dot(emb_b, hot, TN) + dot(emb_c, hot, TN)
        h = jnp.transpose(far[k * block : (k + 1) * block, 0:width]).astype(jnp.float32) + added
        mid[:, cols] = h
        shifted = h - jnp.sum(h, 0, keepdims=True) * (1.0 / width)
        spread = jnp.sum(shifted * shifted, 0, keepdims=True) * (1.0 / width)
        scaled = shifted * lax.rsqrt(spread + 1e-05)
        at[:, cols] = (scaled * vecs[:, 5:6] + vecs[:, 6:7]).astype(jnp.bfloat16)
        for j in range(3):
            res = dot(
                gd[j * width : (j + 1) * width, lanes_at(core * half, half)], at[:, cols], TN
            ).astype(jnp.bfloat16)
            qkv[j * half : (j + 1) * half, cols] = res * jnp.bfloat16(0.125) if j == 0 else res

    own_x.wait()
    for load in qkv_loads:
        load.wait()
    take(0)
    x_near.wait()
    p_near.wait()
    take(2)
    p_far.wait()
    x_far.wait()
    x_cross.start()
    c_far.start()
    take(1)
    x_cross.wait()
    p_cross.wait()
    take(3)
    h_saves = [local(18 + k, mid.at[:, own_cols(k)], h_far.at[k]) for k in range(2)]
    for save in h_saves:
        save.start()

    pairs_n = blocks_n // 2
    wide = 2 * block

    def cover(first_key, first_query, queries):
        key = lax.broadcasted_iota(jnp.int32, (block, queries), 0) + first_key
        place = lax.broadcasted_iota(jnp.int32, (block, queries), 1) + first_query
        hidden = dot(
            kmask[first_key : first_key + block, :], qhot[:, first_query : first_query + queries], NN
        )
        hidden = jnp.where(key < place, hidden, negative)
        return jnp.where(key == place, 0.0, hidden)

    for p in range(pairs_n):
        keep[p * block : (p + 1) * block, :] = cover(p * wide, p * wide, wide)
        keep[wide : wide + block, p * block : (p + 1) * block] = cover(
            p * wide + block, p * wide + block, block
        )

    def kept_save(h, slot):
        return pltpu.make_async_copy(kept.at[slot], kept_far.at[h], lsem.at[20 + slot])

    def o_copy(h):
        mine = rows_at(core * half + h * 64, 64)
        return remote(base + h, otf.at[mine, :], otf.at[mine, :], to_core)

    def turn(k):
        ct[:, lanes_at(places[k] * block, block)] = jnp.transpose(
            dm[k * block : (k + 1) * block, 0:width]
        )

    def one_head(h, slot):
        @pl.when(h >= 2)
        def _():
            kept_save(h - 2, slot).wait()

        qrow, krow, vrow = (rows_at(j * half + h * 64, 64) for j in range(3))
        mine = rows_at(core * half + h * 64, 64)
        keyn = jnp.concatenate([jnp.transpose(qkv[krow, :]), kmask[...]], 1)
        query = jnp.concatenate([qkv[qrow, :], qhot[...]], 0)
        for p in range(pairs_n):
            before, split, after = p * wide, p * wide + block, (p + 1) * wide
            at_row = p * p * block
            cols, late = slice(before, after), slice(split, after)
            side = slice(p * block, (p + 1) * block)
            near = dot(keyn[before:split, 0:64], query[0:64, cols], NN)
            near = near + keep[p * block : (p + 1) * block, :]
            peak = jnp.max(near, 0, keepdims=True)
            last = dot(keyn[late, 0:64], query[0:64, late], NN) + keep[wide : wide + block, side]
            last_peak = jnp.maximum(peak[:, block:], jnp.max(last, 0, keepdims=True))
            peak = jnp.concatenate([peak[:, :block], last_peak], 1)
            if p:
                scores = dot(keyn[0:before, :], query[:, cols], NN)
                peak = jnp.maximum(peak, jnp.max(scores, 0, keepdims=True))
                expo = jnp.exp(scores - peak)
                count = jnp.sum(expo, 0, keepdims=True)
                low = expo.astype(jnp.bfloat16)
                kept[slot, at_row : at_row + before, :] = low
                result = dot(qkv[vrow, 0:before], low, NN)
            near = jnp.exp(near - peak)
            near_sum = jnp.sum(near, 0, keepdims=True)
            count = count + near_sum if p else near_sum
            low = near.astype(jnp.bfloat16)
            kept[slot, at_row + before : at_row + split, :] = low
            near_result = dot(qkv[vrow, before:split], low, NN)
            result = result + near_result if p else near_result
            last = jnp.exp(last - peak[:, block:])
            low = last.astype(jnp.bfloat16)
            kept[slot, kept.shape[1] - block : kept.shape[1], side] = low
            last_result = dot(qkv[vrow, late], low, NN)
            over = 1.0 / jnp.concatenate(
                [count[:, :block], count[:, block:] + jnp.sum(last, 0, keepdims=True)], 1
            )
            result = jnp.concatenate([result[:, :block], result[:, block:] + last_result], 1)
            inv[h, :, cols] = jnp.broadcast_to(over, (8, wide))
            otf[mine, cols] = (result * over).astype(jnp.bfloat16)
        kept_save(h, slot).start()

        @pl.when(h == heads - 2)
        def _():
            c_near.wait()
            c_far.wait()
            c_cross.start()
            own_c.wait()
            for k in (0, 2, 1):
                turn(k)

        @pl.when(h == heads - 1)
        def _():
            c_cross.wait()
            turn(3)

        o_copy(h).start()

    def head_pair(i, carry):
        for e in range(2):
            one_head(2 * i + e, e)
        return carry

    lax.fori_loop(0, heads // 2, head_pair, 0)
    kept_save(heads - 2, heads % 2).wait()
    kept_save(heads - 1, (heads - 1) % 2).wait()

    def kept_load(h, slot):
        return pltpu.make_async_copy(kept_far.at[h], kept.at[slot], lsem.at[22 + slot])

    kept_load(0, 0).start()
    kept_load(1, 1).start()
    for h in range(heads):
        o_copy(h).wait()
    base += heads

    for save in h_saves:
        save.wait()
    out_load.wait()

    def mix(i, carry):
        cols = lanes_at(i * block, block)
        m = mid[:, cols] + dot(w_out[...], otf[:, cols], TN)
        mid[:, cols] = m
        shifted = m - jnp.sum(m, 0, keepdims=True) * (1.0 / width)
        spread = jnp.sum(shifted * shifted, 0, keepdims=True) * (1.0 / width)
        scaled = shifted * lax.rsqrt(spread + 1e-05)
        mt[:, cols] = (scaled * vecs[:, 7:8] + vecs[:, 8:9]).astype(jnp.bfloat16)
        return carry

    lax.fori_loop(0, blocks_n, mix, 0)

    def hidden_at(first):
        for i in range(2):
            rows = slice(first + i * part, first + (i + 1) * part)
            below = slice(inner + first + i * part, inner + first + (i + 1) * part)
            u = dot(w_up[rows, :], mt[...], NN) + bcol[rows, 0:1]
            square = u * u
            t = jnp.tanh(u * (0.7978845608028654 + 0.035677408136300125 * square))
            gate = 0.5 + 0.5 * t
            gd[rows, :] = (u * gate).astype(jnp.bfloat16)
            slope = gate + (0.5 * u) * (1.0 - t * t) * (
                0.7978845608028654 + 0.10703222440890037 * square
            )
            gd[below, :] = slope.astype(jnp.bfloat16)

    lanes = bsum.shape[-1]
    band = width // bs
    for j in range(2):
        for xx in range(2):
            at_row = (2 * xx + j) * lanes
            hidden_at(at_row)
            grad = dot(ct[...], gd[at_row : at_row + lanes, :], NT).astype(jnp.bfloat16)
            for b in range(bs):
                bsum[xx, b // 2, b % 2, j * band : (j + 1) * band, :] = grad[
                    b * band : (b + 1) * band, :
                ]
        serve("down%d" % j)
    for load in down_loads:
        load.wait()

    for i in range(bs):
        rows = slice(i * part, (i + 1) * part)
        below = slice(inner + i * part, inner + (i + 1) * part)
        back = dot(w_down[rows, :], ct[...], NN)
        gd[below, :] = (back * gd[below, :].astype(jnp.float32)).astype(jnp.bfloat16)
    serve("hidden")

    dm_copy = remote(base, dm.at[0:width, :], dm.at[width : 2 * width, :], to_core)

    for i in range(blocks_n):
        cols = slice(i * block, (i + 1) * block)
        dm[0:width, cols] = dot(w_up[...], gd[inner : 2 * inner, cols], TN).astype(jnp.bfloat16)
    dm_copy.start()
    serve("dm")
    first_up = 2 * band
    up_band = part
    for xx in range(2):
        for i in range(2):
            low, high = inner + i * inner // 2, inner + (i + 1) * inner // 2
            grad = dot(gd[low:high, :], mt[xx * lanes : (xx + 1) * lanes, :], NT)
            grad = grad.astype(jnp.bfloat16)
            for b in range(bs // 2):
                bb = i * bs // 2 + b
                bsum[xx, bb // 2, bb % 2, first_up : first_up + up_band, :] = grad[
                    b * up_band : (b + 1) * up_band, :
                ]
        serve("up%d" % xx)
    ones = jnp.ones((8, total), jnp.bfloat16)
    up_sum = dot(ones, gd[inner : 2 * inner, :], NT)
    vector[...] = jnp.zeros_like(vector)
    for i in range(4):
        one, two = (up_sum[0:1, (2 * i + e) * part : (2 * i + e + 1) * part] for e in range(2))
        none = jnp.zeros_like(one)
        vector[10 + i : 11 + i, :] = jnp.where(
            core == 0,
            jnp.concatenate([one, none, two, none], 1),
            jnp.concatenate([none, one, none, two], 1),
        )

    out_copy = remote(base + 1, osend, orecv, to_core)
    for k in range(2):
        other = lanes_at((1 - core) * block + k * 2 * block, block)
        to = slice(k * block, (k + 1) * block)
        osend[:, to] = dot(w_down[...], gd[0:inner, other], TN).astype(jnp.bfloat16)
        keep[:, to] = mid[:, own_cols(k)] + vecs[:, 9:10] + dot(
            w_down[...], gd[0:inner, own_cols(k)], TN
        )
    out_copy.start()
    serve("out")

    dm_copy.wait()
    sums[...] = jnp.zeros_like(sums)

    def middle(i, carry):
        cols = lanes_at(i * block, block)
        cot = ct[:, cols].astype(jnp.float32)
        m = mid[:, cols]
        shifted = m - jnp.sum(m, 0, keepdims=True) * (1.0 / width)
        spread = jnp.sum(shifted * shifted, 0, keepdims=True) * (1.0 / width)
        r = lax.rsqrt(spread + 1e-05)
        n = shifted * r
        d = dm[0:width, cols].astype(jnp.float32) + dm[width : 2 * width, cols].astype(jnp.float32)
        e = d * vecs[:, 7:8]
        mean_e = jnp.sum(e, 0, keepdims=True) * (1.0 / width)
        mean_en = jnp.sum(e * n, 0, keepdims=True) * (1.0 / width)
        dmid = cot + r * (e - mean_e - n * mean_en)
        mid[:, cols] = dmid
        dm[width : 2 * width, cols] = dmid.astype(jnp.bfloat16)
        sums[:, 0:1] += jnp.sum(d * n, 1, keepdims=True)
        sums[:, 1:2] += jnp.sum(d, 1, keepdims=True)
        sums[:, 2:3] += jnp.sum(cot, 1, keepdims=True)
        return carry

    lax.fori_loop(0, blocks_n, middle, 0)
    serve("middle")
    small = band // 2
    for b in range(bs):
        dm[half + b * small : half + (b + 1) * small, :] = dm[
            rows_at(width + b * band + core * small, small), :
        ]
    first_out = first_up + up_band
    for xx in range(2):
        grad = dot(dm[half:width, :], otf[xx * lanes : (xx + 1) * lanes, :], NT)
        grad = grad.astype(jnp.bfloat16)
        for b in range(bs):
            bsum[xx, b // 2, b % 2, first_out : first_out + small, :] = grad[
                b * small : (b + 1) * small, :
            ]
    dm[0:half, :] = dot(
        w_out[rows_at(core * half, half), :], dm[width : 2 * width, :], NN
    ).astype(jnp.bfloat16)
    serve("w_out")

    whole_loads = [
        local(24, w_qkv_in.at[:, 0:width], w_up.at[0:width, :]),
        local(25, w_qkv_in.at[:, width : 2 * width], w_up.at[width : 2 * width, :]),
        local(26, w_qkv_in.at[:, 2 * width : 3 * width], w_down.at[0:width, :]),
    ]
    for load in whole_loads:
        load.start()
    hand_out = remote(base + 2, hand.at[0], out.at[x], to_x)

    def give_output():
        out_copy.wait()
        for k in range(2):
            cols = slice(k * block, (k + 1) * block)
            rows = jnp.transpose(
                (keep[:, cols] + orecv[:, cols].astype(jnp.float32)).astype(jnp.bfloat16)
            )

            @pl.when(x == k)
            def _():
                out[k] = rows

            @pl.when(x != k)
            def _():
                hand[0] = rows

        hand_out.start()

    give_output()
    serve("given")

    def far_copy(h, j):
        mine = rows_at(j * width + core * half + h * 64, 64)
        return remote(
            base + 3 + h * 3 + j, gd.at[mine, :], far.at[rows_at(j * half + h * 64, 64), :], to_core
        )

    def head_back(h, slot, ksum, vsum):
        kept_load(h, slot).wait()
        qrow, krow, vrow = (rows_at(j * half + h * 64, 64) for j in range(3))
        mine = [rows_at(j * width + core * half + h * 64, 64) for j in range(3)]
        valn = jnp.transpose(qkv[vrow, :])
        grads = (dm[rows_at(h * 64, 64), :].astype(jnp.float32) * inv[h, 0:1, :]).astype(
            jnp.bfloat16
        )
        o_rows = otf[rows_at(core * half + h * 64, 64), :]
        delta = jnp.sum(grads.astype(jnp.float32) * o_rows.astype(jnp.float32), 0, keepdims=True)
        ksum[...] = jnp.zeros_like(ksum)
        vsum[...] = jnp.zeros_like(vsum)
        for p in range(pairs_n):
            before, split, after = p * wide, p * wide + block, (p + 1) * wide
            at_row = p * p * block
            cols, late = slice(before, after), slice(split, after)
            side = slice(p * block, (p + 1) * block)
            low = kept[slot, at_row : at_row + split, :]
            dprob = dot(valn[0:split, :], grads[:, cols], NN)
            dscore = (low.astype(jnp.float32) * (dprob - delta[:, cols])).astype(jnp.bfloat16)
            last = kept[slot, kept.shape[1] - block : kept.shape[1], side]
            dprob = dot(valn[late, :], grads[:, late], NN)
            dlast = (last.astype(jnp.float32) * (dprob - delta[:, late])).astype(jnp.bfloat16)
            dquery = dot(qkv[krow, 0:split], dscore, NN)
            dquery = jnp.concatenate(
                [dquery[:, :block], dquery[:, block:] + dot(qkv[krow, late], dlast, NN)], 1
            )
            gd[mine[0], cols] = (dquery * 0.125).astype(jnp.bfloat16)
            ksum[:, 0:split] += dot(qkv[qrow, cols], dscore, NT)
            vsum[:, 0:split] += dot(grads[:, cols], low, NT)
            ksum[:, late] += dot(qkv[qrow, late], dlast, NT)
            vsum[:, late] += dot(grads[:, late], last, NT)
        gd[mine[1], :] = ksum[...].astype(jnp.bfloat16)
        gd[mine[2], :] = vsum[...].astype(jnp.bfloat16)
        for j in range(3):
            far_copy(h, j).start()

        @pl.when(h + 2 < heads)
        def _():
            kept_load(h + 2, slot).start()

        for at_head in range(slot, heads, 2):

            @pl.when(h == at_head)
            def _():
                serve("head%d" % at_head)

    def back_pair(i, carry):
        for e in range(2):
            head_back(2 * i + e, e, ksum.at[e], vsum.at[e])
        return carry

    lax.fori_loop(0, heads // 2, back_pair, 0)
    own_loads = [local(18 + k, h_far.at[k], keep.at[:, k * block : (k + 1) * block]) for k in range(2)]
    for load in own_loads:
        load.start()

    for h in range(heads):
        for j in range(3):
            far_copy(h, j).wait()
    for j in range(3):
        gd[rows_at(j * width + (1 - core) * half, half), :] = far[j * half : (j + 1) * half, :]
    qkv_band = 3 * width // bs
    qkv_small = qkv_band // 2
    for b in range(bs):
        dm[b * qkv_small : (b + 1) * qkv_small, :] = gd[
            rows_at(b * qkv_band + core * qkv_small, qkv_small), :
        ]
    first_qkv = first_out + small
    for xx in range(2):
        grad = dot(dm[0 : bs * qkv_small, :], at[xx * lanes : (xx + 1) * lanes, :], NT)
        grad = grad.astype(jnp.bfloat16)
        for b in range(bs):
            bsum[xx, b // 2, b % 2, first_qkv : first_qkv + qkv_small, :] = grad[
                b * qkv_small : (b + 1) * qkv_small, :
            ]
    serve("qkv")

    for load in whole_loads + own_loads:
        load.wait()
    gpass[...] = jnp.zeros_like(gpass)
    hand_in = remote(base + 21, hand.at[1], gin.at[x], to_x)
    for k in range(2):
        mine = own_cols(k)
        da = dot(w_up[0:width, :], gd[0:width, mine], NN)
        da += dot(w_up[width : 2 * width, :], gd[width : 2 * width, mine], NN)
        da += dot(w_down[0:width, :], gd[2 * width : 3 * width, mine], NN)
        h = keep[:, k * block : (k + 1) * block]
        shifted = h - jnp.sum(h, 0, keepdims=True) * (1.0 / width)
        spread = jnp.sum(shifted * shifted, 0, keepdims=True) * (1.0 / width)
        r = lax.rsqrt(spread + 1e-05)
        n = shifted * r
        e = da * vecs[:, 5:6]
        mean_e = jnp.sum(e, 0, keepdims=True) * (1.0 / width)
        mean_en = jnp.sum(e * n, 0, keepdims=True) * (1.0 / width)
        dh = mid[:, mine] + r * (e - mean_e - n * mean_en)
        rows = jnp.transpose(dh).astype(jnp.bfloat16)

        @pl.when(x == k)
        def _():
            gin[k] = rows

        @pl.when(x != k)
        def _():
            hand[1] = rows
            hand_in.start()

        sums[:, 3:4] += jnp.sum(da * n, 1, keepdims=True)
        sums[:, 4:5] += jnp.sum(da, 1, keepdims=True)
        kind = lax.broadcasted_iota(jnp.int32, (16, block), 0).astype(jnp.float32)
        onehot = jnp.where(kind == prow[0:1, mine], 1.0, 0.0).astype(jnp.bfloat16)
        high = dh.astype(jnp.bfloat16)
        rest = dh - high.astype(jnp.float32)
        second_part = rest.astype(jnp.bfloat16)
        tail = (rest - second_part.astype(jnp.float32)).astype(jnp.bfloat16)
        gpass[...] += dot(onehot, high, NT) + dot(onehot, second_part, NT) + dot(onehot, tail, NT)
        serve("input%d" % k)

    own_rows = down_recv.shape[0]
    wide = lanes // 2
    row_ranges = ((0, first_up), (first_up, first_out), (first_out, first_qkv),
                  (first_qkv, first_qkv + qkv_small))
    results = (gdown, gup, gout, gqkv)

    def both_cores(mine, got):
        return jnp.where(core == 0, mine, got), jnp.where(core == 0, got, mine)

    class Finish:
        def swap(self, k):
            r0, r1 = row_ranges[k]
            if k == 0:
                theirs = rows_at((1 - core) * own_rows, own_rows)
                return remote(base + 28, bsum.at[x, z, y, theirs, :], down_recv, to_core)
            rows = slice(r0 - first_up, r1 - first_up)
            return remote(base + 28 + k, stage_send.at[rows, :], stage_recv.at[rows, :], to_core)

        def send(self, k):
            r0, r1 = row_ranges[k]
            if k:
                v = bsum[x, z, y, r0:r1, :]
                stage_send[r0 - first_up : r1 - first_up, 0:wide] = jnp.where(
                    core == 0, v[:, wide:lanes], v[:, 0:wide]
                )
            self.swap(k).start()

        def put(self, k):
            self.swap(k).wait()
            if k == 0:
                mine = bsum[x, z, y, rows_at(core * own_rows, own_rows), :].astype(jnp.float32)
                for c, piece in enumerate(both_cores(mine, down_recv[...].astype(jnp.float32))):
                    for i in range(lanes // part):
                        at_row = (2 * i + c) * part
                        gdown[:, at_row : at_row + part] = piece[:, i * part : (i + 1) * part]
                return
            r0, r1 = row_ranges[k]
            v = bsum[x, z, y, r0:r1, :].astype(jnp.float32)
            mine = jnp.where(core == 0, v[:, 0:wide], v[:, wide:lanes])
            got = stage_recv[r0 - first_up : r1 - first_up, 0:wide].astype(jnp.float32)
            results[k][...] = jnp.transpose(jnp.concatenate(both_cores(mine, got), 0))

    for k in range(4):
        setattr(Finish, "f%d" % k, lambda self, k=k: self.send(k))
        setattr(Finish, "g%d" % k, lambda self, k=k: self.put(k))

    lines = jnp.transpose(sums[...])
    vector[0:5, :] = gpass[0:5, :]
    vector[5:7, :] = lines[3:5, :]
    vector[7:10, :] = lines[0:3, :] * 0.5
    hops = [
        remote(base + 22 + i, vector, vrecv.at[i], peer)
        for i, peer in enumerate((to_core, to_x, to_y))
    ]
    copies = [
        remote(base + 25 + i, vector, vrecv.at[3 + z], peer) for i, peer in enumerate(to_z)
    ]

    class Vector:
        def v0(self):
            hops[0].start()

        def take(self, i):
            hops[i].wait()
            vector[...] = vector[...] + vrecv[i]

        def v1(self):
            self.take(0)
            hops[1].start()

        def v2(self):
            self.take(1)
            hops[2].start()

        def v3(self):
            self.take(2)
            for copy in copies:
                copy.start()
            vrecv[3 + z] = vector[...]

    steps.extend((Vector(), Finish()))
    for i in range(3):
        serve("sum%d" % i)

    for i in range(3):
        serve("end%d" % i)
    for copy in copies:
        copy.wait()
    vector[...] = (vrecv[3] + vrecv[4]) + (vrecv[5] + vrecv[6])
    hand_out.wait()
    hand_in.wait()


def finish_kernel(
    out_in, gin_in, vector_in, gqkv_in, gout_in, gup_in, gdown_in,
    out, gin, gpass, gain1, bias1, gqkv, gout, gain2, bias2, gup, gb_up, gdown, gb_down,
    vector, sem,
):
    pairs = (
        (out_in, out), (gin_in, gin), (gqkv_in, gqkv), (gout_in, gout), (gup_in, gup), (gdown_in, gdown),
        (vector_in, vector),
    )
    copies = [pltpu.make_async_copy(a, b, sem.at[i]) for i, (a, b) in enumerate(pairs)]
    for copy in copies:
        copy.start()
    for copy in copies:
        copy.wait()
    width = vector.shape[1]
    gpass[...] = vector[0:5, :]
    for i, ref in enumerate((gain1, bias1, gain2, bias2, gb_down)):
        ref[...] = vector[5 + i, :]
    for i in range(4):
        gb_up[pl.ds(i * width, width)] = vector[10 + i, :]


def shaped(*dims, kind=jnp.bfloat16):
    return jax.ShapeDtypeStruct(dims, kind)


shares = ((80, 32, 80), (64, 48, 80), (16, 16, 16), (48, 32, 64))
plan = {
    "down0": ((0, "start_e"),),
    "down1": ((0, "start_c"), (0, "start_a"),),
    "hidden": ((0, "e1"),),
    "dm": (),
    "up0": ((0, "c2"),),
    "up1": ((1, "start"),),
    "out": ((0, "e2"),),
    "middle": (),
    "w_out": ((2, "start"), (0, "a2"),),
    "given": ((1, "e1"),),
    "head0": (),
    "head1": ((2, "e1"),),
    "head2": ((0, "e3"), (1, "a2"),),
    "head3": ((0, "z0"), (2, "c2"), (2, "a2"),),
    "head4": ((0, "z1"), (2, "e2"), (1, "c2"),),
    "head5": (),
    "qkv": ((3, "start"), (1, "e2"),),
    "input0": ((2, "e3"), (0, "z2"), (3, "e1"), (2, "z0"), (0, "e4"), (3, "c2"), (1, "z0"),),
    "input1": ((3, "e2"), (3, "a2"),),
    "sum0": ((1, "z1"), (2, "e4"), (1, "e3"), (4, "v0"), (1, "z2"),),
    "sum1": ((2, "z1"), (0, "z3"),),
    "sum2": ((5, "f0"), (3, "z0"), (3, "e3"), (3, "z1"), (1, "e4"), (2, "z2"),),
    "end0": ((4, "v1"), (5, "g0"), (3, "z2"),),
    "end1": ((3, "e4"), (2, "z3"), (5, "f2"), (1, "z3"),),
    "end2": ((5, "f1"), (4, "v2"), (3, "z3"), (5, "f3"), (5, "g2"), (5, "g1"), (4, "v3"), (5, "g3"),),
}


def regrouped(
    block_input, lengths, pass_ids, pass_embed, ln1_gain, ln1_bias, w_qkv, w_out,
    ln2_gain, ln2_bias, w_up, b_up, w_down, b_down, cotangent, batch_n
):
    width = block_input.shape[2]
    total = 4 * block_input.shape[1]
    inner = w_up.shape[1]
    own_in, half, lanes = inner // 2, width // 2, width // 2
    band = inner // batch_n // 2
    z_n = batch_n // 2
    blocks_n = total // block
    kept_rows = (blocks_n // 2) ** 2 * block + block
    chunks, a0, c0, e0, r0 = [], 0, 0, 0, 0
    for ne, nc, na in shares:
        chunks.append((r0, r0 + ne, r0 + ne + nc, r0 + ne + nc + na, a0, c0, e0))
        r0, a0, c0, e0 = r0 + ne + nc + na, a0 + na, c0 + nc, e0 + ne
    down_n = 2 * width // batch_n
    anywhere = pl.BlockSpec(memory_space=pl.ANY)
    whole = pl.BlockSpec(memory_space=pltpu.VMEM)
    low, full = jnp.bfloat16, jnp.float32
    copies_n = 22 * len(chunks) + 9 + half // 64 + 32
    output, grad_input, vector, grad_qkv, grad_out, grad_up, grad_down, _, _ = pl.pallas_call(
        functools.partial(block_kernel, chunks=tuple(chunks), plan=plan),
        out_shape=[
            shaped(2, block, width),
            shaped(2, block, width),
            shaped(16, width, kind=full),
            shaped(width // 4, 3 * width // batch_n, kind=full),
            shaped(width // 4, width // batch_n, kind=full),
            shaped(width // 4, inner // batch_n, kind=full),
            shaped(width // batch_n, inner // 4, kind=full),
            shaped(half // 64, kept_rows, 2 * block),
            shaped(2, width, block, kind=full),
        ],
        in_specs=[pl.BlockSpec(memory_space=pltpu.SMEM)] + [anywhere] * 6 + [whole] * 8,
        out_specs=[whole] * 7 + [anywhere] * 2,
        scratch_shapes=[
            pltpu.VMEM((width, total), full),
            pltpu.VMEM((width, 2 * block), full),
            pltpu.VMEM((width, total), low),
            pltpu.VMEM((3 * half, total), low),
            pltpu.VMEM((width, total), low),
            pltpu.VMEM((width, total), low),
            pltpu.VMEM((width, total), low),
            pltpu.VMEM((2 * own_in, total), low),
            pltpu.VMEM((3 * half, total), low),
            pltpu.VMEM((2 * width, total), low),
            pltpu.VMEM((2, kept_rows, 2 * block), low),
            pltpu.VMEM((width, width), low),
            pltpu.VMEM((own_in, width), low),
            pltpu.VMEM((own_in, width), low),
            pltpu.VMEM((2, z_n, 2, r0, lanes), low),
            pltpu.VMEM((z_n, 2, a0, lanes), low),
            pltpu.VMEM((z_n, a0, lanes), low),
            pltpu.VMEM((2, z_n, c0, lanes), low),
            pltpu.VMEM((z_n, c0, lanes), low),
            pltpu.VMEM((2, e0, lanes), low),
            pltpu.VMEM((e0, lanes), low),
            pltpu.VMEM((z_n + 1, a0 + c0, lanes), low),
            pltpu.VMEM((z_n + 1, 2, 2, e0, lanes), low),
            pltpu.VMEM((width, 2 * block), low),
            pltpu.VMEM((width, 2 * block), low),
            pltpu.VMEM((2, block, width), low),
            pltpu.VMEM((width, 128), full),
            pltpu.VMEM((16, width), full),
            pltpu.VMEM((7, 16, width), full),
            pltpu.VMEM((2, 64, total), full),
            pltpu.VMEM((2, 64, total), full),
            pltpu.VMEM((r0 - down_n, 256), low),
            pltpu.VMEM((r0 - down_n, 256), low),
            pltpu.VMEM((down_n // 2, lanes), low),
            pltpu.VMEM((16, width), full),
            pltpu.VMEM((width, 16), full),
            pltpu.VMEM((own_in, 8), full),
            pltpu.VMEM((half // 64, 8, total), full),
            pltpu.VMEM((8, total), full),
            pltpu.VMEM((total, 16), low),
            pltpu.VMEM((16, total), low),
            pltpu.VMEM((4, 2, block), jnp.int32),
            pltpu.SemaphoreType.DMA((27,)),
            pltpu.SemaphoreType.DMA((copies_n,)),
            pltpu.SemaphoreType.DMA((copies_n,)),
        ],
        compiler_params=pltpu.CompilerParams(
            vmem_limit_bytes=63 << 20, collective_id=0, has_side_effects=True
        ),
        cost_estimate=pl.CostEstimate(flops=int(60e9), bytes_accessed=0, transcendentals=0),
        name="block",
    )(
        lengths, block_input, cotangent, w_up, w_qkv, w_out,
        w_down.reshape(batch_n, 2, band, width), pass_ids, pass_embed,
        ln1_gain, ln1_bias, ln2_gain, ln2_bias, b_up, b_down,
    )
    results = [output, grad_input, vector, grad_qkv, grad_out, grad_up, grad_down]
    line = jax.ShapeDtypeStruct((width,), full)
    done = pl.pallas_call(
        finish_kernel,
        out_shape=[
            shaped(2, block, width),
            shaped(2, block, width),
            shaped(5, width, kind=full),
            line,
            line,
            jax.ShapeDtypeStruct(grad_qkv.shape, full),
            jax.ShapeDtypeStruct(grad_out.shape, full),
            line,
            line,
            jax.ShapeDtypeStruct(grad_up.shape, full),
            jax.ShapeDtypeStruct((inner,), full),
            jax.ShapeDtypeStruct(grad_down.shape, full),
            line,
        ],
        in_specs=[anywhere] * 7,
        out_specs=[whole] * 13,
        scratch_shapes=[pltpu.VMEM((16, width), full), pltpu.SemaphoreType.DMA((7,))],
        compiler_params=pltpu.CompilerParams(vmem_limit_bytes=62 << 20),
        name="finish",
    )(*results)
    done = list(done)
    done[11] = jnp.transpose(done[11])
    return tuple(done)


def solution(mesh):
    batch_n = mesh.shape["batch"]
    few = mesh.shape["seq"] == 4 and batch_n == 8
    body = functools.partial(regrouped, batch_n=batch_n) if few else local
    return jax.shard_map(
        body,
        mesh=mesh,
        in_specs=(
            P("batch", "seq", None),
            P("batch"),
            P("batch", "seq"),
            P(),
            P(),
            P(),
            P(),
            P(),
            P(),
            P(),
            P(),
            P(),
            P(),
            P(),
            P("batch", "seq", None),
        ),
        out_specs=(
            P("batch", "seq", None),
            P("batch", "seq", None),
            P(),
            P(),
            P(),
            P("seq", "batch"),
            P("seq", "batch"),
            P(),
            P(),
            P("seq", "batch"),
            P(),
            P("seq", "batch"),
            P(),
        ),
        check_vma=False,
    )
```

```python
import functools

import jax
import jax.numpy as jnp
from jax import lax
from jax.experimental import pallas as pl
from jax.experimental.pallas import tpu as pltpu
from jax.sharding import PartitionSpec as P

H = 12


negative = -1e30
key_block = 1024
query_block = 512
highest = lax.Precision.HIGHEST


def layer_norm(hidden, gain, offset):
    centre = jnp.mean(hidden, -1, keepdims=True)
    shifted = hidden - centre
    spread = jnp.mean(shifted * shifted, -1, keepdims=True)
    return shifted * lax.rsqrt(spread + 1e-05) * gain + offset


def gelu_tanh(values):
    return jax.nn.gelu(values, approximate=True)


def visible(query_place, query_pass, key_place, key_pass, length):
    earlier = key_place[None, :] < query_place[:, None]
    allowed = earlier & (key_pass[None, :] <= query_pass[:, None]) & (key_place[None, :] < length)
    return allowed | (key_place[None, :] == query_place[:, None])


def masked_scores(query_part, key_part, factor, seen):
    raw = (
        jnp.einsum("qhd,khd->hqk", query_part, key_part, preferred_element_type=jnp.float32)
        * factor
    )
    return jnp.where(seen[None], raw, negative)


def split_blocks(arrays, block_len):
    return tuple(
        (
            array.reshape((array.shape[0] // block_len, block_len) + array.shape[1:])
            for array in arrays
        )
    )


def chance_of(query_part, key_part, log_part, seen, factor):
    scores = masked_scores(query_part, key_part, factor, seen)
    return jnp.where(seen[None], jnp.exp(scores - log_part[..., None]), 0.0)


def grad_pieces(query_part, dout_part, log_part, delta_part, key_part, value_part, seen, factor):
    chance = chance_of(query_part, key_part, log_part, seen, factor)
    dprob = jnp.einsum("qhd,khd->hqk", dout_part, value_part, preferred_element_type=jnp.float32)
    dscore = (chance * (dprob - delta_part[..., None])).astype(jnp.bfloat16)
    return (dscore, chance.astype(jnp.bfloat16))


def attend_row(queries, query_place, query_pass, key_rows, value_rows, key_pass, length):
    factor = queries.shape[-1] ** (-0.5)
    places = jnp.arange(key_rows.shape[0], dtype=jnp.int32)
    key_parts = split_blocks(
        (key_rows, value_rows, key_pass, places), min(key_block, key_rows.shape[0])
    )
    query_len = min(query_block, queries.shape[0])
    query_parts = split_blocks((queries, query_place, query_pass), query_len)

    def attend_one_block(query_args):
        query_part, place_part, pass_part = query_args

        def running(carry, key_args):
            peak, summed, total_out = carry
            key_part, value_part, kpass_part, kplace_part = key_args
            seen = visible(place_part, pass_part, kplace_part, kpass_part, length)
            scores = masked_scores(query_part, key_part, factor, seen)
            new_peak = jnp.maximum(peak, jnp.max(scores, -1))
            terms = jnp.where(seen[None], jnp.exp(scores - new_peak[..., None]), 0.0)
            rescale = jnp.exp(peak - new_peak)
            summed = summed * rescale + jnp.sum(terms, -1)
            added = jnp.einsum(
                "hqk,khd->qhd",
                terms.astype(jnp.bfloat16),
                value_part,
                preferred_element_type=jnp.float32,
            )
            total_out = total_out * rescale.T[..., None] + added
            return ((new_peak, summed, total_out), None)

        heads_n = query_part.shape[1]
        start = (
            jnp.full((heads_n, query_len), negative, jnp.float32),
            jnp.zeros((heads_n, query_len), jnp.float32),
            jnp.zeros(query_part.shape, jnp.float32),
        )
        (peak, summed, total_out), _ = lax.scan(running, start, key_parts)
        log_total = peak + jnp.log(summed)
        result = total_out / summed.T[..., None]
        return (result, log_total)

    results, log_totals = lax.map(attend_one_block, query_parts)
    heads_n = queries.shape[1]
    return (
        results.reshape(queries.shape),
        jnp.moveaxis(log_totals, 1, 0).reshape(heads_n, queries.shape[0]),
    )


def backward_row(
    queries,
    douts,
    outs_kept,
    log_totals,
    query_place,
    query_pass,
    key_rows,
    value_rows,
    key_pass,
    length,
):
    factor = queries.shape[-1] ** (-0.5)
    places = jnp.arange(key_rows.shape[0], dtype=jnp.int32)
    key_parts = split_blocks(
        (key_rows, value_rows, key_pass, places), min(key_block, key_rows.shape[0])
    )
    query_len = min(query_block, queries.shape[0])
    heads_n = queries.shape[1]
    block_count = queries.shape[0] // query_len
    log_parts = jnp.moveaxis(log_totals.reshape(heads_n, block_count, query_len), 1, 0)
    query_parts = split_blocks((queries, douts, outs_kept, query_place, query_pass), query_len)

    def backward_one_block(carry, query_args):
        query_part, dout_part, kept_part, place_part, pass_part, log_part = query_args
        delta_part = jnp.einsum("qhd,qhd->hq", dout_part.astype(jnp.float32), kept_part)

        def add_grads(dquery, key_args):
            key_part, value_part, kpass_part, kplace_part = key_args
            seen = visible(place_part, pass_part, kplace_part, kpass_part, length)
            dscore, low_chance = grad_pieces(
                query_part, dout_part, log_part, delta_part, key_part, value_part, seen, factor
            )
            dquery = dquery + factor * jnp.einsum(
                "hqk,khd->qhd", dscore, key_part, preferred_element_type=jnp.float32
            )
            dkey = factor * jnp.einsum(
                "hqk,qhd->khd", dscore, query_part, preferred_element_type=jnp.float32
            )
            dvalue = jnp.einsum(
                "hqk,qhd->khd", low_chance, dout_part, preferred_element_type=jnp.float32
            )
            return (dquery, (dkey, dvalue))

        dquery, key_terms = lax.scan(add_grads, jnp.zeros(query_part.shape, jnp.float32), key_parts)
        carry = (
            carry[0] + key_terms[0].reshape(key_rows.shape),
            carry[1] + key_terms[1].reshape(value_rows.shape),
        )
        return (carry, (dquery, delta_part))

    start = (jnp.zeros(key_rows.shape, jnp.float32), jnp.zeros(value_rows.shape, jnp.float32))
    key_sums, (dqueries, deltas) = lax.scan(backward_one_block, start, query_parts + (log_parts,))
    return (
        dqueries.reshape(queries.shape),
        jnp.moveaxis(deltas, 1, 0).reshape(heads_n, queries.shape[0]),
        key_sums,
    )


def local(
    block_input,
    lengths,
    pass_ids,
    pass_embed,
    ln1_gain,
    ln1_bias,
    w_qkv,
    w_out,
    ln2_gain,
    ln2_bias,
    w_up,
    b_up,
    w_down,
    b_down,
    cotangent,
):
    row_count, seg_len, width = block_input.shape
    heads_n = H
    head_size = width // heads_n
    onehot = (
        pass_ids[..., None] == jnp.arange(pass_embed.shape[0], dtype=jnp.int32)[None, None, :]
    ).astype(jnp.float32)
    hidden_in = block_input.astype(jnp.float32) + jnp.einsum(
        "rsp,pd->rsd", onehot, pass_embed, precision=highest
    )
    normed, norm_back = jax.vjp(layer_norm, hidden_in, ln1_gain, ln1_bias)
    normed_low = normed.astype(jnp.bfloat16)
    qkv = jnp.einsum("rsd,de->rse", normed_low, w_qkv, preferred_element_type=jnp.float32)
    queries = qkv[..., :width].astype(jnp.bfloat16)
    key_flat = qkv[..., width : 2 * width].astype(jnp.bfloat16)
    value_flat = qkv[..., 2 * width :].astype(jnp.bfloat16)
    pass_low = pass_ids.astype(jnp.bfloat16)
    key_all, value_all, pass_all = (
        lax.all_gather(key_flat, "seq", axis=1, tiled=True),
        lax.all_gather(value_flat, "seq", axis=1, tiled=True),
        lax.all_gather(pass_low, "seq", axis=1, tiled=True),
    )
    total_len = key_all.shape[1]
    key_all = key_all.reshape(row_count, total_len, heads_n, head_size)
    value_all = value_all.reshape(row_count, total_len, heads_n, head_size)
    pass_all = pass_all.astype(jnp.float32)
    offset = lax.axis_index("seq") * seg_len
    query_place = offset + jnp.arange(seg_len, dtype=jnp.int32)
    query_pass = pass_ids.astype(jnp.float32)
    query_heads = queries.reshape(row_count, seg_len, heads_n, head_size)
    attended_rows = []
    log_rows = []
    for row in range(row_count):
        attended, log_total = attend_row(
            query_heads[row],
            query_place,
            query_pass[row],
            key_all[row],
            value_all[row],
            pass_all[row],
            lengths[row],
        )
        attended_rows.append(attended)
        log_rows.append(log_total)
    attended_low = jnp.stack(attended_rows).astype(jnp.bfloat16).reshape(row_count, seg_len, width)
    branch = jnp.einsum("rsd,de->rse", attended_low, w_out, preferred_element_type=jnp.float32)
    middle = hidden_in + branch
    normed2, norm2_back = jax.vjp(layer_norm, middle, ln2_gain, ln2_bias)
    normed2_low = normed2.astype(jnp.bfloat16)
    pre_act = (
        jnp.einsum("rsd,df->rsf", normed2_low, w_up, preferred_element_type=jnp.float32) + b_up
    )
    active, active_back = jax.vjp(gelu_tanh, pre_act)
    active_low = active.astype(jnp.bfloat16)
    result = (
        middle
        + jnp.einsum("rsf,fd->rsd", active_low, w_down, preferred_element_type=jnp.float32)
        + b_down
    )
    output = result.astype(jnp.bfloat16)
    cot_f = cotangent.astype(jnp.float32)
    grad_active = jnp.einsum("rsd,fd->rsf", cotangent, w_down, preferred_element_type=jnp.float32)
    grad_w_down = jnp.einsum(
        "rsf,rsd->fd", active_low, cotangent, preferred_element_type=jnp.float32
    )
    grad_b_down = jnp.sum(cot_f, (0, 1))
    grad_pre = active_back(grad_active)[0].astype(jnp.bfloat16)
    grad_b_up = jnp.sum(grad_pre.astype(jnp.float32), (0, 1))
    grad_w_up = jnp.einsum("rsd,rsf->df", normed2_low, grad_pre, preferred_element_type=jnp.float32)
    grad_normed2 = jnp.einsum("rsf,df->rsd", grad_pre, w_up, preferred_element_type=jnp.float32)
    grad_mid_norm, grad_ln2_gain, grad_ln2_bias = norm2_back(grad_normed2)
    grad_middle = cot_f + grad_mid_norm
    grad_branch = grad_middle.astype(jnp.bfloat16)
    grad_w_out = jnp.einsum(
        "rsd,rse->de", attended_low, grad_branch, preferred_element_type=jnp.float32
    )
    grad_attended = jnp.einsum(
        "rse,de->rsd", grad_branch, w_out, preferred_element_type=jnp.float32
    ).astype(jnp.bfloat16)
    dout_heads = grad_attended.reshape(row_count, seg_len, heads_n, head_size)
    dquery_rows = []
    dkey_rows = []
    dvalue_rows = []
    for row in range(row_count):
        dquery, _, key_sums = backward_row(
            query_heads[row],
            dout_heads[row],
            attended_rows[row],
            log_rows[row],
            query_place,
            query_pass[row],
            key_all[row],
            value_all[row],
            pass_all[row],
            lengths[row],
        )
        dquery_rows.append(dquery)
        dkey_rows.append(key_sums[0].reshape(total_len, width))
        dvalue_rows.append(key_sums[1].reshape(total_len, width))
    dkey_sum, dvalue_sum = (
        lax.psum_scatter(
            jnp.stack(dkey_rows).astype(jnp.bfloat16), "seq", scatter_dimension=1, tiled=True
        ).astype(jnp.float32),
        lax.psum_scatter(
            jnp.stack(dvalue_rows).astype(jnp.bfloat16), "seq", scatter_dimension=1, tiled=True
        ).astype(jnp.float32),
    )
    dquery_all = jnp.stack(dquery_rows).reshape(row_count, seg_len, width)
    grad_qkv = jnp.concatenate(
        [
            dquery_all.astype(jnp.bfloat16),
            dkey_sum.astype(jnp.bfloat16),
            dvalue_sum.astype(jnp.bfloat16),
        ],
        -1,
    )
    grad_w_qkv = jnp.einsum("rsd,rse->de", normed_low, grad_qkv, preferred_element_type=jnp.float32)
    grad_normed = jnp.einsum("rse,de->rsd", grad_qkv, w_qkv, preferred_element_type=jnp.float32)
    grad_in_norm, grad_ln1_gain, grad_ln1_bias = norm_back(grad_normed)
    grad_hidden = grad_middle + grad_in_norm
    grad_input = grad_hidden.astype(jnp.bfloat16)
    grad_pass = jnp.einsum("rsp,rsd->pd", onehot, grad_hidden, precision=highest)
    matrices = (
        lax.psum_scatter(
            grad_w_qkv.astype(jnp.bfloat16), "seq", scatter_dimension=0, tiled=True
        ).astype(jnp.float32),
        lax.psum_scatter(
            grad_w_out.astype(jnp.bfloat16), "seq", scatter_dimension=0, tiled=True
        ).astype(jnp.float32),
        lax.psum_scatter(
            grad_w_up.astype(jnp.bfloat16), "seq", scatter_dimension=0, tiled=True
        ).astype(jnp.float32),
        lax.psum_scatter(
            grad_w_down.astype(jnp.bfloat16), "seq", scatter_dimension=0, tiled=True
        ).astype(jnp.float32),
    )
    matrices = (
        lax.psum_scatter(
            matrices[0].astype(jnp.bfloat16), "batch", scatter_dimension=1, tiled=True
        ).astype(jnp.float32),
        lax.psum_scatter(
            matrices[1].astype(jnp.bfloat16), "batch", scatter_dimension=1, tiled=True
        ).astype(jnp.float32),
        lax.psum_scatter(
            matrices[2].astype(jnp.bfloat16), "batch", scatter_dimension=1, tiled=True
        ).astype(jnp.float32),
        lax.psum_scatter(
            matrices[3].astype(jnp.bfloat16), "batch", scatter_dimension=1, tiled=True
        ).astype(jnp.float32),
    )
    vectors = lax.psum(
        (
            grad_pass,
            grad_ln1_gain,
            grad_ln1_bias,
            grad_ln2_gain,
            grad_ln2_bias,
            grad_b_up,
            grad_b_down,
        ),
        ("seq", "batch"),
    )
    return (
        output,
        grad_input,
        vectors[0],
        vectors[1],
        vectors[2],
        matrices[0],
        matrices[1],
        vectors[3],
        vectors[4],
        matrices[2],
        vectors[5],
        matrices[3],
        vectors[6],
    )


NN = (((1,), (0,)), ((), ()))
NT = (((1,), (1,)), ((), ()))
TN = (((0,), (0,)), ((), ()))
vmem_bytes = 60 << 20
block = 256


def dot(left, right, form):
    return lax.dot_general(left, right, form, preferred_element_type=jnp.float32)


mesh_ids = pl.DeviceIdType.MESH


def block_kernel(
    lengths,
    block_in, cot_in, w_up_in, w_qkv_in, w_out_in, w_down_in,
    pass_in, embed_in, gain1, bias1, gain2, bias2, b_up_in, b_down_in,
    out, gin, vector, gqkv, gout, gup, gdown,
    kept_far, h_far,
    mid, keep, at, qkv, otf, ct, mt, gd, far, dm, kept, w_out, w_up, w_down,
    bsum, r1a, r2a, r1c, r2c, r2e, r3e, rz, rze,
    osend, orecv, hand, sums, gpass, vrecv, ksum, vsum, stage_send, stage_recv, down_recv,
    params, vecs, bcol, inv, prow, kmask, qhot, passes,
    lsem, ssem, rsem,
    *, chunks, plan,
):
    seq, bat = lax.axis_index("seq"), lax.axis_index("batch")
    x, core = seq // 2, seq % 2
    z, y = bat // 2, bat % 2
    to_core, to_x, to_y = (seq + 1 - 2 * core, bat), (seq + 2 - 4 * x, bat), (seq, bat + 1 - 2 * y)
    to_cross = (3 - seq, bat)
    to_z = [(seq, ((z + i) % 4) * 2 + y) for i in (1, 2, 3)]
    up_z, low_z = (seq, bat + 2), (seq, bat - 2)

    barrier = pltpu.get_barrier_semaphore()
    for peer in [to_core, to_x, to_y, to_cross] + to_z:
        pl.semaphore_signal(barrier, inc=1, device_id=peer, device_id_type=mesh_ids)

    width, total = mid.shape
    half = width // 2
    inner = w_up.shape[0]
    blocks_n = total // block
    heads = half // 64
    bs = 8

    def rows_at(first, count):
        return pl.ds(pl.multiple_of(first, 16), count)

    def lanes_at(first, count):
        return pl.ds(pl.multiple_of(first, 128), count)

    def own_cols(k):
        return lanes_at(core * block + k * 2 * block, block)

    def local(i, src, dst):
        return pltpu.make_async_copy(src, dst, lsem.at[i])

    def remote(i, src, dst, peer):
        return pltpu.make_async_remote_copy(
            src_ref=src, dst_ref=dst, send_sem=ssem.at[i], recv_sem=rsem.at[i],
            device_id=peer, device_id_type=mesh_ids,
        )

    part = w_down_in.shape[2]

    def spot(b):
        return b // 2 % 2 * 4 + b // 4 * 2 + b % 2

    def slab(b):
        return slice(spot(b) * part, (spot(b) + 1) * part)

    own_x = local(0, block_in.at[x], far.at[0:block, 0:width])
    own_c = local(1, cot_in.at[x], dm.at[0:block, 0:width])
    out_load = local(2, w_out_in, w_out)
    up_loads = [
        local(3 + p, w_up_in.at[:, p * width : (p + 1) * width],
              gd.at[p * width : (p + 1) * width, 0:width])
        for p in range(4)
    ]
    down_loads = [
        local(7 + i, w_down_in.at[i, core], w_down.at[slab(i), :])
        for i in range(bs)
    ]
    qkv_loads = [
        local(15 + j, w_qkv_in.at[:, j * width : (j + 1) * width],
              gd.at[j * width : (j + 1) * width, 0:width])
        for j in range(3)
    ]
    for load in [own_x] + up_loads + [own_c, out_load] + down_loads:
        load.start()

    base = 22 * len(chunks)
    x_far = remote(base, block_in.at[1 - x], far.at[block : 2 * block, 0:width], to_x)
    x_near = remote(base + 1, block_in.at[x], far.at[2 * block : 3 * block, 0:width], to_core)
    x_cross = remote(
        base + 2, far.at[block : 2 * block, 0:width], far.at[3 * block : 4 * block, 0:width], to_core
    )
    c_far = remote(base + 3, cot_in.at[1 - x], dm.at[block : 2 * block, 0:width], to_x)
    c_near = remote(base + 4, cot_in.at[x], dm.at[2 * block : 3 * block, 0:width], to_core)
    c_cross = remote(
        base + 5, dm.at[block : 2 * block, 0:width], dm.at[3 * block : 4 * block, 0:width], to_core
    )
    p_far = remote(base + 6, pass_in, passes.at[1], to_x)
    p_near = remote(base + 7, pass_in, passes.at[2], to_core)
    p_cross = remote(base + 8, pass_in, passes.at[3], to_cross)
    base += 9
    pl.semaphore_wait(barrier, 7)
    for copy in (p_far, x_far, x_near, p_near, p_cross, c_near):
        copy.start()


    def line_copy(i, d, up, part, slots):
        slot = d if up else jnp.where(z - 1 == d, 4, d)
        return remote(i + (d if up else 4 + d), part(d), slots(slot), up_z if up else low_z)

    def line_add(d, slot, part, slots):
        here, got = part(d), slots(slot)
        here[...] = here[...] + got[...]

    def line_start(i, part, slots):
        @pl.when(z == 0)
        def _():
            for d in (3, 2, 1):
                line_copy(i, d, True, part, slots).start()

        @pl.when(z == 3)
        def _():
            for d in (0, 1, 2):
                line_copy(i, d, False, part, slots).start()

    def line_pass(i, d, up, part, slots):
        copy = line_copy(i, d, up, part, slots)
        copy.wait_recv()
        line_add(d, d, part, slots)
        copy.start()

    def line_one(i, part, slots):
        @pl.when(z == 1)
        def _():
            line_pass(i, 3, True, part, slots)

        @pl.when(z == 2)
        def _():
            line_pass(i, 0, False, part, slots)

    def line_two(i, part, slots):
        @pl.when(z == 1)
        def _():
            line_pass(i, 2, True, part, slots)
            line_pass(i, 0, False, part, slots)

        @pl.when(z == 2)
        def _():
            line_pass(i, 1, False, part, slots)
            line_pass(i, 3, True, part, slots)

    def line_last(i, part, slots):
        for d in range(4):

            @pl.when(z == d)
            def _():
                if d > 0:
                    line_copy(i, d, True, part, slots).wait_recv()
                    line_add(d, d, part, slots)
                if d < 3:
                    line_copy(i, d, False, part, slots).wait_recv()
                    line_add(d, 4, part, slots)
                for e in range(4):
                    if e > d:
                        line_copy(i, e, True, part, slots).wait_send()
                    if e < d:
                        line_copy(i, e, False, part, slots).wait_send()

    class Chunk:
        def __init__(self, k):
            r0, rc, ra, r1, a0, c0, e0 = chunks[k]
            ne, nc, na = rc - r0, ra - rc, r1 - ra
            i = 22 * k
            rows_e, rows_c, rows_a = pl.ds(r0, ne), pl.ds(rc, nc), pl.ds(ra, na)
            got_a, got_c, got_e = pl.ds(a0, na), pl.ds(c0, nc), pl.ds(e0, ne)
            sub = bsum.at
            self.one_a = remote(i, sub[1 - x, :, :, rows_a, :], r1a.at[:, :, got_a, :], to_x)
            self.one_c = remote(i + 1, sub[:, :, 1 - y, rows_c, :], r1c.at[:, :, got_c, :], to_y)
            self.two_a = remote(i + 2, sub[x, :, 1 - y, rows_a, :], r2a.at[:, got_a, :], to_y)
            self.two_c = remote(i + 3, sub[1 - x, :, y, rows_c, :], r2c.at[:, got_c, :], to_x)
            self.two_e = remote(i + 4, sub[:, z, 1 - y, rows_e, :], r2e.at[:, got_e, :], to_y)
            self.three_e = remote(i + 5, sub[1 - x, z, y, rows_e, :], r3e.at[got_e, :], to_x)
            self.adds = [
                (sub[x, :, :, rows_a, :], r1a.at[:, :, got_a, :]),
                (sub[:, :, y, rows_c, :], r1c.at[:, :, got_c, :]),
                (sub[x, :, y, rows_a, :], r2a.at[:, got_a, :]),
                (sub[x, :, y, rows_c, :], r2c.at[:, got_c, :]),
                (sub[:, z, y, rows_e, :], r2e.at[:, got_e, :]),
                (sub[x, z, y, rows_e, :], r3e.at[got_e, :]),
            ]
            both, low = pl.ds(rc, na + nc), pl.ds(a0 + c0, na + nc)
            self.line_ac = (
                i + 6, lambda d: sub[x, d, y, both, :], lambda s: rz.at[s, low, :]
            )
            self.line_e = (
                i + 14, lambda d: sub[:, d, :, rows_e, :], lambda s: rze.at[s, :, :, got_e, :]
            )

        def add(self, j):
            here, got = self.adds[j]
            here[...] = here[...] + got[...]

        def start(self):
            line_start(*self.line_e)
            self.one_c.start()
            self.one_a.start()

        def start_a(self):
            self.one_a.start()

        def start_c(self):
            self.one_c.start()

        def start_e(self):
            line_start(*self.line_e)

        def e1(self):
            line_one(*self.line_e)

        def e2(self):
            line_two(*self.line_e)

        def e3(self):
            line_last(*self.line_e)
            self.two_e.start()

        def a2(self):
            self.one_a.wait()
            self.add(0)
            self.two_a.start()

        def c2(self):
            self.one_c.wait()
            self.add(1)
            self.two_c.start()

        def e4(self):
            self.two_e.wait()
            self.add(4)
            self.three_e.start()

        def z0(self):
            self.two_a.wait()
            self.add(2)
            self.two_c.wait()
            self.add(3)
            line_start(*self.line_ac)

        def z1(self):
            line_one(*self.line_ac)

        def z2(self):
            line_two(*self.line_ac)

        def z3(self):
            line_last(*self.line_ac)
            self.three_e.wait()
            self.add(5)
    steps = [Chunk(k) for k in range(len(chunks))]

    def serve(slot):
        for k, name in plan[slot]:
            getattr(steps[k], name)()

    params[...] = jnp.zeros_like(params)
    params[0:5, :] = embed_in[...]
    for i, ref in enumerate((gain1, bias1, gain2, bias2, b_down_in)):
        params[5 + i, :] = ref[...]
    for i in range(4):
        params[10 + i, :] = b_up_in[pl.ds(i * width, width)]
    vecs[...] = jnp.transpose(params[...])
    for b in range(bs):
        i, low = 10 + b // 2, b % 2 * 2 * part
        bcol[slab(b), :] = jnp.broadcast_to(
            jnp.where(
                core == 0,
                vecs[low : low + part, i : i + 1],
                vecs[low + part : low + 2 * part, i : i + 1],
            ),
            (part, 8),
        )
    for b in range(bs):
        p, low = b // 2, b % 2 * 2 * part
        if b % 2 == 0:
            up_loads[p].wait()
        turned = jnp.transpose(gd[p * width : (p + 1) * width, low : low + 2 * part])
        w_up[slab(b), :] = jnp.where(core == 0, turned[:part], turned[part:])
    for load in qkv_loads:
        load.start()
    passes[0] = pass_in[...]
    places = (2 * x + core, 2 * (1 - x) + core, 2 * x + 1 - core, 2 * (1 - x) + 1 - core)
    length = lengths[x]
    emb = jnp.where(lax.broadcasted_iota(jnp.int32, (8, width), 0) < 5, params[0:8, :], 0.0)
    emb_a = emb.astype(jnp.bfloat16)
    rest = emb - emb_a.astype(jnp.float32)
    emb_b = rest.astype(jnp.bfloat16)
    emb_c = (rest - emb_b.astype(jnp.float32)).astype(jnp.bfloat16)

    def take(k):
        cols = lanes_at(places[k] * block, block)
        rows = rows_at(places[k] * block, block)
        got = passes[k]
        line = jnp.where(x == 0, got[0:1, :], got[1:2, :])
        prow[:, cols] = jnp.broadcast_to(line.astype(jnp.float32), (8, block))
        kind = lax.broadcasted_iota(jnp.int32, (16, block), 0)
        spot = lax.broadcasted_iota(jnp.int32, (16, block), 1) + places[k] * block
        onehot = jnp.where(kind == line, 1.0, 0.0).astype(jnp.bfloat16)
        qhot[:, cols] = onehot
        hidden = jnp.where((line > kind) | (spot >= length), negative, 0.0)
        kmask[rows, :] = jnp.transpose(hidden).astype(jnp.bfloat16)
        hot = onehot[0:8, :]
        added = dot(emb_a, hot, TN) + dot(emb_b, hot, TN) + dot(emb_c, hot, TN)
        h = jnp.transpose(far[k * block : (k + 1) * block, 0:width]).astype(jnp.float32) + added
        mid[:, cols] = h
        shifted = h - jnp.sum(h, 0, keepdims=True) * (1.0 / width)
        spread = jnp.sum(shifted * shifted, 0, keepdims=True) * (1.0 / width)
        scaled = shifted * lax.rsqrt(spread + 1e-05)
        at[:, cols] = (scaled * vecs[:, 5:6] + vecs[:, 6:7]).astype(jnp.bfloat16)
        for j in range(3):
            res = dot(
                gd[j * width : (j + 1) * width, lanes_at(core * half, half)], at[:, cols], TN
            ).astype(jnp.bfloat16)
            qkv[j * half : (j + 1) * half, cols] = res * jnp.bfloat16(0.125) if j == 0 else res

    own_x.wait()
    for load in qkv_loads:
        load.wait()
    take(0)
    x_near.wait()
    p_near.wait()
    take(2)
    p_far.wait()
    x_far.wait()
    x_cross.start()
    c_far.start()
    take(1)
    x_cross.wait()
    p_cross.wait()
    take(3)
    h_saves = [local(18 + k, mid.at[:, own_cols(k)], h_far.at[k]) for k in range(2)]
    for save in h_saves:
        save.start()

    pairs_n = blocks_n // 2
    wide = 2 * block

    def cover(first_key, first_query, queries):
        key = lax.broadcasted_iota(jnp.int32, (block, queries), 0) + first_key
        place = lax.broadcasted_iota(jnp.int32, (block, queries), 1) + first_query
        hidden = dot(
            kmask[first_key : first_key + block, :], qhot[:, first_query : first_query + queries], NN
        )
        hidden = jnp.where(key < place, hidden, negative)
        return jnp.where(key == place, 0.0, hidden)

    for p in range(pairs_n):
        keep[p * block : (p + 1) * block, :] = cover(p * wide, p * wide, wide)
        keep[wide : wide + block, p * block : (p + 1) * block] = cover(
            p * wide + block, p * wide + block, block
        )

    def kept_save(h, slot):
        return pltpu.make_async_copy(kept.at[slot], kept_far.at[h], lsem.at[20 + slot])

    def o_copy(h):
        mine = rows_at(core * half + h * 64, 64)
        return remote(base + h, otf.at[mine, :], otf.at[mine, :], to_core)

    def turn(k):
        ct[:, lanes_at(places[k] * block, block)] = jnp.transpose(
            dm[k * block : (k + 1) * block, 0:width]
        )

    def one_head(h, slot):
        @pl.when(h >= 2)
        def _():
            kept_save(h - 2, slot).wait()

        qrow, krow, vrow = (rows_at(j * half + h * 64, 64) for j in range(3))
        mine = rows_at(core * half + h * 64, 64)
        keyn = jnp.concatenate([jnp.transpose(qkv[krow, :]), kmask[...]], 1)
        query = jnp.concatenate([qkv[qrow, :], qhot[...]], 0)
        for p in range(pairs_n):
            before, split, after = p * wide, p * wide + block, (p + 1) * wide
            at_row = p * p * block
            cols, late = slice(before, after), slice(split, after)
            side = slice(p * block, (p + 1) * block)
            near = dot(keyn[before:split, 0:64], query[0:64, cols], NN)
            near = near + keep[p * block : (p + 1) * block, :]
            peak = jnp.max(near, 0, keepdims=True)
            last = dot(keyn[late, 0:64], query[0:64, late], NN) + keep[wide : wide + block, side]
            last_peak = jnp.maximum(peak[:, block:], jnp.max(last, 0, keepdims=True))
            peak = jnp.concatenate([peak[:, :block], last_peak], 1)
            if p:
                scores = dot(keyn[0:before, :], query[:, cols], NN)
                peak = jnp.maximum(peak, jnp.max(scores, 0, keepdims=True))
                expo = jnp.exp(scores - peak)
                count = jnp.sum(expo, 0, keepdims=True)
                low = expo.astype(jnp.bfloat16)
                kept[slot, at_row : at_row + before, :] = low
                result = dot(qkv[vrow, 0:before], low, NN)
            near = jnp.exp(near - peak)
            near_sum = jnp.sum(near, 0, keepdims=True)
            count = count + near_sum if p else near_sum
            low = near.astype(jnp.bfloat16)
            kept[slot, at_row + before : at_row + split, :] = low
            near_result = dot(qkv[vrow, before:split], low, NN)
            result = result + near_result if p else near_result
            last = jnp.exp(last - peak[:, block:])
            low = last.astype(jnp.bfloat16)
            kept[slot, kept.shape[1] - block : kept.shape[1], side] = low
            last_result = dot(qkv[vrow, late], low, NN)
            over = 1.0 / jnp.concatenate(
                [count[:, :block], count[:, block:] + jnp.sum(last, 0, keepdims=True)], 1
            )
            result = jnp.concatenate([result[:, :block], result[:, block:] + last_result], 1)
            inv[h, :, cols] = jnp.broadcast_to(over, (8, wide))
            otf[mine, cols] = (result * over).astype(jnp.bfloat16)
        kept_save(h, slot).start()

        @pl.when(h == heads - 2)
        def _():
            c_near.wait()
            c_far.wait()
            c_cross.start()
            own_c.wait()
            for k in (0, 2, 1):
                turn(k)

        @pl.when(h == heads - 1)
        def _():
            c_cross.wait()
            turn(3)

        o_copy(h).start()

    def head_pair(i, carry):
        for e in range(2):
            one_head(2 * i + e, e)
        return carry

    lax.fori_loop(0, heads // 2, head_pair, 0)
    kept_save(heads - 2, heads % 2).wait()
    kept_save(heads - 1, (heads - 1) % 2).wait()

    def kept_load(h, slot):
        return pltpu.make_async_copy(kept_far.at[h], kept.at[slot], lsem.at[22 + slot])

    kept_load(0, 0).start()
    kept_load(1, 1).start()
    for h in range(heads):
        o_copy(h).wait()
    base += heads

    for save in h_saves:
        save.wait()
    out_load.wait()

    def mix(i, carry):
        cols = lanes_at(i * block, block)
        m = mid[:, cols] + dot(w_out[...], otf[:, cols], TN)
        mid[:, cols] = m
        shifted = m - jnp.sum(m, 0, keepdims=True) * (1.0 / width)
        spread = jnp.sum(shifted * shifted, 0, keepdims=True) * (1.0 / width)
        scaled = shifted * lax.rsqrt(spread + 1e-05)
        mt[:, cols] = (scaled * vecs[:, 7:8] + vecs[:, 8:9]).astype(jnp.bfloat16)
        return carry

    lax.fori_loop(0, blocks_n, mix, 0)

    def hidden_at(first):
        for i in range(4):
            rows = slice(first + i * part, first + (i + 1) * part)
            below = slice(inner + first + i * part, inner + first + (i + 1) * part)
            u = dot(w_up[rows, :], mt[...], NN) + bcol[rows, 0:1]
            square = u * u
            t = jnp.tanh(u * (0.7978845608028654 + 0.035677408136300125 * square))
            gate = 0.5 + 0.5 * t
            gd[rows, :] = (u * gate).astype(jnp.bfloat16)
            slope = gate + (0.5 * u) * (1.0 - t * t) * (
                0.7978845608028654 + 0.10703222440890037 * square
            )
            gd[below, :] = slope.astype(jnp.bfloat16)

    lanes = bsum.shape[-1]
    band = width // bs
    for j in range(2):
        hidden_at(j * width)
        grad = dot(ct[...], gd[j * width : (j + 1) * width, :], NT).astype(jnp.bfloat16)
        for xx in range(2):
            for b in range(bs):
                bsum[xx, b // 2, b % 2, j * band : (j + 1) * band, :] = grad[
                    b * band : (b + 1) * band, xx * lanes : (xx + 1) * lanes
                ]
        serve("down%d" % j)
    for load in down_loads:
        load.wait()

    for i in range(bs):
        rows = slice(i * part, (i + 1) * part)
        below = slice(inner + i * part, inner + (i + 1) * part)
        back = dot(w_down[rows, :], ct[...], NN)
        gd[below, :] = (back * gd[below, :].astype(jnp.float32)).astype(jnp.bfloat16)
    serve("hidden")

    dm_copy = remote(base, dm.at[0:width, :], dm.at[width : 2 * width, :], to_core)

    for i in range(blocks_n):
        cols = slice(i * block, (i + 1) * block)
        dm[0:width, cols] = dot(w_up[...], gd[inner : 2 * inner, cols], TN).astype(jnp.bfloat16)
    dm_copy.start()
    serve("dm")
    first_up = 2 * band
    up_band = part
    for i in range(2):
        grad = dot(gd[inner + i * width : inner + (i + 1) * width, :], mt[...], NT)
        grad = grad.astype(jnp.bfloat16)
        for b in range(bs):
            low = spot(b) * part - i * width
            if 0 <= low < width:
                for xx in range(2):
                    bsum[xx, b // 2, b % 2, first_up : first_up + up_band, :] = grad[
                        low : low + part, xx * lanes : (xx + 1) * lanes
                    ]
        serve("up%d" % i)
    ones = jnp.ones((8, total), jnp.bfloat16)
    up_sum = dot(ones, gd[inner : 2 * inner, :], NT)
    vector[...] = jnp.zeros_like(vector)
    for i in range(4):
        one, two = (up_sum[0:1, slab(2 * i + e)] for e in range(2))
        none = jnp.zeros_like(one)
        vector[10 + i : 11 + i, :] = jnp.where(
            core == 0,
            jnp.concatenate([one, none, two, none], 1),
            jnp.concatenate([none, one, none, two], 1),
        )

    out_copy = remote(base + 1, osend, orecv, to_core)
    for k in range(2):
        other = lanes_at((1 - core) * block + k * 2 * block, block)
        to = slice(k * block, (k + 1) * block)
        osend[:, to] = dot(w_down[...], gd[0:inner, other], TN).astype(jnp.bfloat16)
        keep[:, to] = mid[:, own_cols(k)] + vecs[:, 9:10] + dot(
            w_down[...], gd[0:inner, own_cols(k)], TN
        )
    out_copy.start()
    serve("out")

    dm_copy.wait()
    sums[...] = jnp.zeros_like(sums)

    def middle(i, carry):
        cols = lanes_at(i * block, block)
        cot = ct[:, cols].astype(jnp.float32)
        m = mid[:, cols]
        shifted = m - jnp.sum(m, 0, keepdims=True) * (1.0 / width)
        spread = jnp.sum(shifted * shifted, 0, keepdims=True) * (1.0 / width)
        r = lax.rsqrt(spread + 1e-05)
        n = shifted * r
        d = dm[0:width, cols].astype(jnp.float32) + dm[width : 2 * width, cols].astype(jnp.float32)
        e = d * vecs[:, 7:8]
        mean_e = jnp.sum(e, 0, keepdims=True) * (1.0 / width)
        mean_en = jnp.sum(e * n, 0, keepdims=True) * (1.0 / width)
        dmid = cot + r * (e - mean_e - n * mean_en)
        mid[:, cols] = dmid
        dm[width : 2 * width, cols] = dmid.astype(jnp.bfloat16)
        sums[:, 0:1] += jnp.sum(d * n, 1, keepdims=True)
        sums[:, 1:2] += jnp.sum(d, 1, keepdims=True)
        sums[:, 2:3] += jnp.sum(cot, 1, keepdims=True)
        return carry

    lax.fori_loop(0, blocks_n, middle, 0)
    serve("middle")
    small = band // 2
    for b in range(bs):
        dm[half + b * small : half + (b + 1) * small, :] = dm[
            rows_at(width + b * band + core * small, small), :
        ]
    first_out = first_up + up_band
    grad = dot(dm[half:width, :], otf[...], NT).astype(jnp.bfloat16)
    for xx in range(2):
        for b in range(bs):
            bsum[xx, b // 2, b % 2, first_out : first_out + small, :] = grad[
                b * small : (b + 1) * small, xx * lanes : (xx + 1) * lanes
            ]
    dm[0:half, :] = dot(
        w_out[rows_at(core * half, half), :], dm[width : 2 * width, :], NN
    ).astype(jnp.bfloat16)
    serve("w_out")

    whole_loads = [
        local(24, w_qkv_in.at[:, 0:width], w_up.at[0:width, :]),
        local(25, w_qkv_in.at[:, width : 2 * width], w_up.at[width : 2 * width, :]),
        local(26, w_qkv_in.at[:, 2 * width : 3 * width], w_down.at[0:width, :]),
    ]
    for load in whole_loads:
        load.start()
    hand_out = remote(base + 2, hand.at[0], out.at[x], to_x)

    def give_output():
        out_copy.wait()
        for k in range(2):
            cols = slice(k * block, (k + 1) * block)
            rows = jnp.transpose(
                (keep[:, cols] + orecv[:, cols].astype(jnp.float32)).astype(jnp.bfloat16)
            )

            @pl.when(x == k)
            def _():
                out[k] = rows

            @pl.when(x != k)
            def _():
                hand[0] = rows

        hand_out.start()

    give_output()
    serve("given")

    def far_copy(h, j):
        mine = rows_at(j * width + core * half + h * 64, 64)
        return remote(
            base + 3 + h * 3 + j, gd.at[mine, :], far.at[rows_at(j * half + h * 64, 64), :], to_core
        )

    def head_back(h, slot, ksum, vsum):
        kept_load(h, slot).wait()
        qrow, krow, vrow = (rows_at(j * half + h * 64, 64) for j in range(3))
        mine = [rows_at(j * width + core * half + h * 64, 64) for j in range(3)]
        valn = jnp.transpose(qkv[vrow, :])
        grads = (dm[rows_at(h * 64, 64), :].astype(jnp.float32) * inv[h, 0:1, :]).astype(
            jnp.bfloat16
        )
        o_rows = otf[rows_at(core * half + h * 64, 64), :]
        delta = jnp.sum(grads.astype(jnp.float32) * o_rows.astype(jnp.float32), 0, keepdims=True)
        ksum[...] = jnp.zeros_like(ksum)
        vsum[...] = jnp.zeros_like(vsum)
        for p in range(pairs_n):
            before, split, after = p * wide, p * wide + block, (p + 1) * wide
            at_row = p * p * block
            cols, late = slice(before, after), slice(split, after)
            side = slice(p * block, (p + 1) * block)
            low = kept[slot, at_row : at_row + split, :]
            dprob = dot(valn[0:split, :], grads[:, cols], NN)
            dscore = (low.astype(jnp.float32) * (dprob - delta[:, cols])).astype(jnp.bfloat16)
            last = kept[slot, kept.shape[1] - block : kept.shape[1], side]
            dprob = dot(valn[late, :], grads[:, late], NN)
            dlast = (last.astype(jnp.float32) * (dprob - delta[:, late])).astype(jnp.bfloat16)
            dquery = dot(qkv[krow, 0:split], dscore, NN)
            dquery = jnp.concatenate(
                [dquery[:, :block], dquery[:, block:] + dot(qkv[krow, late], dlast, NN)], 1
            )
            gd[mine[0], cols] = (dquery * 0.125).astype(jnp.bfloat16)
            ksum[:, 0:split] += dot(qkv[qrow, cols], dscore, NT)
            vsum[:, 0:split] += dot(grads[:, cols], low, NT)
            ksum[:, late] += dot(qkv[qrow, late], dlast, NT)
            vsum[:, late] += dot(grads[:, late], last, NT)
        gd[mine[1], :] = ksum[...].astype(jnp.bfloat16)
        gd[mine[2], :] = vsum[...].astype(jnp.bfloat16)
        for j in range(3):
            far_copy(h, j).start()

        @pl.when(h + 2 < heads)
        def _():
            kept_load(h + 2, slot).start()

        for at_head in range(slot, heads, 2):

            @pl.when(h == at_head)
            def _():
                serve("head%d" % at_head)

    def back_pair(i, carry):
        for e in range(2):
            head_back(2 * i + e, e, ksum.at[e], vsum.at[e])
        return carry

    lax.fori_loop(0, heads // 2, back_pair, 0)
    own_loads = [local(18 + k, h_far.at[k], keep.at[:, k * block : (k + 1) * block]) for k in range(2)]
    for load in own_loads:
        load.start()

    for h in range(heads):
        for j in range(3):
            far_copy(h, j).wait()
    for j in range(3):
        gd[rows_at(j * width + (1 - core) * half, half), :] = far[j * half : (j + 1) * half, :]
    qkv_band = 3 * width // bs
    qkv_small = qkv_band // 2
    for b in range(bs):
        dm[b * qkv_small : (b + 1) * qkv_small, :] = gd[
            rows_at(b * qkv_band + core * qkv_small, qkv_small), :
        ]
    first_qkv = first_out + small
    for i in range(2):
        grad = dot(dm[i * bs // 2 * qkv_small : (i + 1) * bs // 2 * qkv_small, :], at[...], NT)
        grad = grad.astype(jnp.bfloat16)
        for xx in range(2):
            for b in range(bs // 2):
                bb = i * bs // 2 + b
                bsum[xx, bb // 2, bb % 2, first_qkv : first_qkv + qkv_small, :] = grad[
                    b * qkv_small : (b + 1) * qkv_small, xx * lanes : (xx + 1) * lanes
                ]
    serve("qkv")

    for load in whole_loads + own_loads:
        load.wait()
    gpass[...] = jnp.zeros_like(gpass)
    hand_in = remote(base + 21, hand.at[1], gin.at[x], to_x)
    for k in range(2):
        mine = own_cols(k)
        da = dot(w_up[0:width, :], gd[0:width, mine], NN)
        da += dot(w_up[width : 2 * width, :], gd[width : 2 * width, mine], NN)
        da += dot(w_down[0:width, :], gd[2 * width : 3 * width, mine], NN)
        h = keep[:, k * block : (k + 1) * block]
        shifted = h - jnp.sum(h, 0, keepdims=True) * (1.0 / width)
        spread = jnp.sum(shifted * shifted, 0, keepdims=True) * (1.0 / width)
        r = lax.rsqrt(spread + 1e-05)
        n = shifted * r
        e = da * vecs[:, 5:6]
        mean_e = jnp.sum(e, 0, keepdims=True) * (1.0 / width)
        mean_en = jnp.sum(e * n, 0, keepdims=True) * (1.0 / width)
        dh = mid[:, mine] + r * (e - mean_e - n * mean_en)
        rows = jnp.transpose(dh).astype(jnp.bfloat16)

        @pl.when(x == k)
        def _():
            gin[k] = rows

        @pl.when(x != k)
        def _():
            hand[1] = rows
            hand_in.start()

        sums[:, 3:4] += jnp.sum(da * n, 1, keepdims=True)
        sums[:, 4:5] += jnp.sum(da, 1, keepdims=True)
        kind = lax.broadcasted_iota(jnp.int32, (16, block), 0).astype(jnp.float32)
        onehot = jnp.where(kind == prow[0:1, mine], 1.0, 0.0).astype(jnp.bfloat16)
        high = dh.astype(jnp.bfloat16)
        rest = dh - high.astype(jnp.float32)
        second_part = rest.astype(jnp.bfloat16)
        tail = (rest - second_part.astype(jnp.float32)).astype(jnp.bfloat16)
        gpass[...] += dot(onehot, high, NT) + dot(onehot, second_part, NT) + dot(onehot, tail, NT)
        serve("input%d" % k)

    own_rows = down_recv.shape[0]
    wide = lanes // 2
    row_ranges = ((0, first_up), (first_up, first_out), (first_out, first_qkv),
                  (first_qkv, first_qkv + qkv_small))
    results = (gdown, gup, gout, gqkv)

    def both_cores(mine, got):
        return jnp.where(core == 0, mine, got), jnp.where(core == 0, got, mine)

    class Finish:
        def swap(self, k):
            r0, r1 = row_ranges[k]
            if k == 0:
                theirs = rows_at((1 - core) * own_rows, own_rows)
                return remote(base + 28, bsum.at[x, z, y, theirs, :], down_recv, to_core)
            rows = slice(r0 - first_up, r1 - first_up)
            return remote(base + 28 + k, stage_send.at[rows, :], stage_recv.at[rows, :], to_core)

        def send(self, k):
            r0, r1 = row_ranges[k]
            if k:
                v = bsum[x, z, y, r0:r1, :]
                stage_send[r0 - first_up : r1 - first_up, 0:wide] = jnp.where(
                    core == 0, v[:, wide:lanes], v[:, 0:wide]
                )
            self.swap(k).start()

        def put(self, k):
            self.swap(k).wait()
            if k == 0:
                mine = bsum[x, z, y, rows_at(core * own_rows, own_rows), :].astype(jnp.float32)
                for c, piece in enumerate(both_cores(mine, down_recv[...].astype(jnp.float32))):
                    for i in range(lanes // part):
                        at_row = (2 * i + c) * part
                        gdown[:, at_row : at_row + part] = piece[:, i * part : (i + 1) * part]
                return
            r0, r1 = row_ranges[k]
            v = bsum[x, z, y, r0:r1, :].astype(jnp.float32)
            mine = jnp.where(core == 0, v[:, 0:wide], v[:, wide:lanes])
            got = stage_recv[r0 - first_up : r1 - first_up, 0:wide].astype(jnp.float32)
            results[k][...] = jnp.transpose(jnp.concatenate(both_cores(mine, got), 0))

    for k in range(4):
        setattr(Finish, "f%d" % k, lambda self, k=k: self.send(k))
        setattr(Finish, "g%d" % k, lambda self, k=k: self.put(k))

    lines = jnp.transpose(sums[...])
    vector[0:5, :] = gpass[0:5, :]
    vector[5:7, :] = lines[3:5, :]
    vector[7:10, :] = lines[0:3, :] * 0.5
    hops = [
        remote(base + 22 + i, vector, vrecv.at[i], peer)
        for i, peer in enumerate((to_core, to_x, to_y))
    ]
    copies = [
        remote(base + 25 + i, vector, vrecv.at[3 + z], peer) for i, peer in enumerate(to_z)
    ]

    class Vector:
        def v0(self):
            hops[0].start()

        def take(self, i):
            hops[i].wait()
            vector[...] = vector[...] + vrecv[i]

        def v1(self):
            self.take(0)
            hops[1].start()

        def v2(self):
            self.take(1)
            hops[2].start()

        def v3(self):
            self.take(2)
            for copy in copies:
                copy.start()
            vrecv[3 + z] = vector[...]

    steps.extend((Vector(), Finish()))
    for i in range(3):
        serve("sum%d" % i)

    for i in range(3):
        serve("end%d" % i)
    for copy in copies:
        copy.wait()
    vector[...] = (vrecv[3] + vrecv[4]) + (vrecv[5] + vrecv[6])
    hand_out.wait()
    hand_in.wait()


def finish_kernel(
    out_in, gin_in, vector_in, gqkv_in, gout_in, gup_in, gdown_in,
    out, gin, gpass, gain1, bias1, gqkv, gout, gain2, bias2, gup, gb_up, gdown, gb_down,
    vector, sem,
):
    pairs = (
        (out_in, out), (gin_in, gin), (gqkv_in, gqkv), (gout_in, gout), (gup_in, gup), (gdown_in, gdown),
        (vector_in, vector),
    )
    copies = [pltpu.make_async_copy(a, b, sem.at[i]) for i, (a, b) in enumerate(pairs)]
    for copy in copies:
        copy.start()
    for copy in copies:
        copy.wait()
    width = vector.shape[1]
    gpass[...] = vector[0:5, :]
    for i, ref in enumerate((gain1, bias1, gain2, bias2, gb_down)):
        ref[...] = vector[5 + i, :]
    for i in range(4):
        gb_up[pl.ds(i * width, width)] = vector[10 + i, :]


def shaped(*dims, kind=jnp.bfloat16):
    return jax.ShapeDtypeStruct(dims, kind)


shares = ((80, 32, 80), (64, 64, 64), (16, 16, 16), (48, 48, 48))
plan = {
    "down0": ((0, "start_e"),),
    "down1": ((0, "start_c"), (0, "start_a"),),
    "hidden": ((0, "e1"),),
    "dm": (),
    "up0": ((0, "c2"),),
    "up1": ((1, "start"),),
    "out": ((0, "e2"),),
    "middle": (),
    "w_out": ((2, "start"), (0, "a2"),),
    "given": ((1, "e1"),),
    "head0": (),
    "head1": ((2, "e1"),),
    "head2": ((0, "e3"), (1, "a2"),),
    "head3": ((0, "z0"), (2, "c2"), (2, "a2"),),
    "head4": ((0, "z1"), (2, "e2"), (1, "c2"),),
    "head5": (),
    "qkv": ((3, "start"), (1, "e2"),),
    "input0": ((2, "e3"), (0, "z2"), (3, "e1"), (2, "z0"), (0, "e4"), (3, "c2"), (1, "z0"),),
    "input1": ((3, "e2"), (3, "a2"),),
    "sum0": ((1, "z1"), (2, "e4"), (1, "e3"), (4, "v0"), (1, "z2"),),
    "sum1": ((2, "z1"), (0, "z3"),),
    "sum2": ((5, "f0"), (3, "z0"), (3, "e3"), (3, "z1"), (1, "e4"), (2, "z2"),),
    "end0": ((4, "v1"), (5, "g0"), (3, "z2"),),
    "end1": ((3, "e4"), (2, "z3"), (5, "f2"), (1, "z3"),),
    "end2": ((5, "f1"), (4, "v2"), (3, "z3"), (5, "f3"), (5, "g2"), (5, "g1"), (4, "v3"), (5, "g3"),),
}


def regrouped(
    block_input, lengths, pass_ids, pass_embed, ln1_gain, ln1_bias, w_qkv, w_out,
    ln2_gain, ln2_bias, w_up, b_up, w_down, b_down, cotangent, batch_n
):
    width = block_input.shape[2]
    total = 4 * block_input.shape[1]
    inner = w_up.shape[1]
    own_in, half, lanes = inner // 2, width // 2, width // 2
    band = inner // batch_n // 2
    z_n = batch_n // 2
    blocks_n = total // block
    kept_rows = (blocks_n // 2) ** 2 * block + block
    chunks, a0, c0, e0, r0 = [], 0, 0, 0, 0
    for ne, nc, na in shares:
        chunks.append((r0, r0 + ne, r0 + ne + nc, r0 + ne + nc + na, a0, c0, e0))
        r0, a0, c0, e0 = r0 + ne + nc + na, a0 + na, c0 + nc, e0 + ne
    down_n = 2 * width // batch_n
    anywhere = pl.BlockSpec(memory_space=pl.ANY)
    whole = pl.BlockSpec(memory_space=pltpu.VMEM)
    low, full = jnp.bfloat16, jnp.float32
    copies_n = 22 * len(chunks) + 9 + half // 64 + 32
    output, grad_input, vector, grad_qkv, grad_out, grad_up, grad_down, _, _ = pl.pallas_call(
        functools.partial(block_kernel, chunks=tuple(chunks), plan=plan),
        out_shape=[
            shaped(2, block, width),
            shaped(2, block, width),
            shaped(16, width, kind=full),
            shaped(width // 4, 3 * width // batch_n, kind=full),
            shaped(width // 4, width // batch_n, kind=full),
            shaped(width // 4, inner // batch_n, kind=full),
            shaped(width // batch_n, inner // 4, kind=full),
            shaped(half // 64, kept_rows, 2 * block),
            shaped(2, width, block, kind=full),
        ],
        in_specs=[pl.BlockSpec(memory_space=pltpu.SMEM)] + [anywhere] * 6 + [whole] * 8,
        out_specs=[whole] * 7 + [anywhere] * 2,
        scratch_shapes=[
            pltpu.VMEM((width, total), full),
            pltpu.VMEM((width, 2 * block), full),
            pltpu.VMEM((width, total), low),
            pltpu.VMEM((3 * half, total), low),
            pltpu.VMEM((width, total), low),
            pltpu.VMEM((width, total), low),
            pltpu.VMEM((width, total), low),
            pltpu.VMEM((2 * own_in, total), low),
            pltpu.VMEM((3 * half, total), low),
            pltpu.VMEM((2 * width, total), low),
            pltpu.VMEM((2, kept_rows, 2 * block), low),
            pltpu.VMEM((width, width), low),
            pltpu.VMEM((own_in, width), low),
            pltpu.VMEM((own_in, width), low),
            pltpu.VMEM((2, z_n, 2, r0, lanes), low),
            pltpu.VMEM((z_n, 2, a0, lanes), low),
            pltpu.VMEM((z_n, a0, lanes), low),
            pltpu.VMEM((2, z_n, c0, lanes), low),
            pltpu.VMEM((z_n, c0, lanes), low),
            pltpu.VMEM((2, e0, lanes), low),
            pltpu.VMEM((e0, lanes), low),
            pltpu.VMEM((z_n + 1, a0 + c0, lanes), low),
            pltpu.VMEM((z_n + 1, 2, 2, e0, lanes), low),
            pltpu.VMEM((width, 2 * block), low),
            pltpu.VMEM((width, 2 * block), low),
            pltpu.VMEM((2, block, width), low),
            pltpu.VMEM((width, 128), full),
            pltpu.VMEM((16, width), full),
            pltpu.VMEM((7, 16, width), full),
            pltpu.VMEM((2, 64, total), full),
            pltpu.VMEM((2, 64, total), full),
            pltpu.VMEM((r0 - down_n, 256), low),
            pltpu.VMEM((r0 - down_n, 256), low),
            pltpu.VMEM((down_n // 2, lanes), low),
            pltpu.VMEM((16, width), full),
            pltpu.VMEM((width, 16), full),
            pltpu.VMEM((own_in, 8), full),
            pltpu.VMEM((half // 64, 8, total), full),
            pltpu.VMEM((8, total), full),
            pltpu.VMEM((total, 16), low),
            pltpu.VMEM((16, total), low),
            pltpu.VMEM((4, 2, block), jnp.int32),
            pltpu.SemaphoreType.DMA((27,)),
            pltpu.SemaphoreType.DMA((copies_n,)),
            pltpu.SemaphoreType.DMA((copies_n,)),
        ],
        compiler_params=pltpu.CompilerParams(
            vmem_limit_bytes=63 << 20, collective_id=0, has_side_effects=True
        ),
        cost_estimate=pl.CostEstimate(flops=int(60e9), bytes_accessed=0, transcendentals=0),
        name="block",
    )(
        lengths, block_input, cotangent, w_up, w_qkv, w_out,
        w_down.reshape(batch_n, 2, band, width), pass_ids, pass_embed,
        ln1_gain, ln1_bias, ln2_gain, ln2_bias, b_up, b_down,
    )
    results = [output, grad_input, vector, grad_qkv, grad_out, grad_up, grad_down]
    line = jax.ShapeDtypeStruct((width,), full)
    done = pl.pallas_call(
        finish_kernel,
        out_shape=[
            shaped(2, block, width),
            shaped(2, block, width),
            shaped(5, width, kind=full),
            line,
            line,
            jax.ShapeDtypeStruct(grad_qkv.shape, full),
            jax.ShapeDtypeStruct(grad_out.shape, full),
            line,
            line,
            jax.ShapeDtypeStruct(grad_up.shape, full),
            jax.ShapeDtypeStruct((inner,), full),
            jax.ShapeDtypeStruct(grad_down.shape, full),
            line,
        ],
        in_specs=[anywhere] * 7,
        out_specs=[whole] * 13,
        scratch_shapes=[pltpu.VMEM((16, width), full), pltpu.SemaphoreType.DMA((7,))],
        compiler_params=pltpu.CompilerParams(vmem_limit_bytes=62 << 20),
        name="finish",
    )(*results)
    done = list(done)
    done[11] = jnp.transpose(done[11])
    return tuple(done)


def solution(mesh):
    batch_n = mesh.shape["batch"]
    few = mesh.shape["seq"] == 4 and batch_n == 8
    body = functools.partial(regrouped, batch_n=batch_n) if few else local
    return jax.shard_map(
        body,
        mesh=mesh,
        in_specs=(
            P("batch", "seq", None),
            P("batch"),
            P("batch", "seq"),
            P(),
            P(),
            P(),
            P(),
            P(),
            P(),
            P(),
            P(),
            P(),
            P(),
            P(),
            P("batch", "seq", None),
        ),
        out_specs=(
            P("batch", "seq", None),
            P("batch", "seq", None),
            P(),
            P(),
            P(),
            P("seq", "batch"),
            P("seq", "batch"),
            P(),
            P(),
            P("seq", "batch"),
            P(),
            P("seq", "batch"),
            P(),
        ),
        check_vma=False,
    )
```

```python
import functools

import jax
import jax.numpy as jnp
from jax import lax
from jax.experimental import pallas as pl
from jax.experimental.pallas import tpu as pltpu
from jax.sharding import PartitionSpec as P

H = 12


negative = -1e30
key_block = 1024
query_block = 512
highest = lax.Precision.HIGHEST


def layer_norm(hidden, gain, offset):
    centre = jnp.mean(hidden, -1, keepdims=True)
    shifted = hidden - centre
    spread = jnp.mean(shifted * shifted, -1, keepdims=True)
    return shifted * lax.rsqrt(spread + 1e-05) * gain + offset


def gelu_tanh(values):
    return jax.nn.gelu(values, approximate=True)


def visible(query_place, query_pass, key_place, key_pass, length):
    earlier = key_place[None, :] < query_place[:, None]
    allowed = earlier & (key_pass[None, :] <= query_pass[:, None]) & (key_place[None, :] < length)
    return allowed | (key_place[None, :] == query_place[:, None])


def masked_scores(query_part, key_part, factor, seen):
    raw = (
        jnp.einsum("qhd,khd->hqk", query_part, key_part, preferred_element_type=jnp.float32)
        * factor
    )
    return jnp.where(seen[None], raw, negative)


def split_blocks(arrays, block_len):
    return tuple(
        (
            array.reshape((array.shape[0] // block_len, block_len) + array.shape[1:])
            for array in arrays
        )
    )


def chance_of(query_part, key_part, log_part, seen, factor):
    scores = masked_scores(query_part, key_part, factor, seen)
    return jnp.where(seen[None], jnp.exp(scores - log_part[..., None]), 0.0)


def grad_pieces(query_part, dout_part, log_part, delta_part, key_part, value_part, seen, factor):
    chance = chance_of(query_part, key_part, log_part, seen, factor)
    dprob = jnp.einsum("qhd,khd->hqk", dout_part, value_part, preferred_element_type=jnp.float32)
    dscore = (chance * (dprob - delta_part[..., None])).astype(jnp.bfloat16)
    return (dscore, chance.astype(jnp.bfloat16))


def attend_row(queries, query_place, query_pass, key_rows, value_rows, key_pass, length):
    factor = queries.shape[-1] ** (-0.5)
    places = jnp.arange(key_rows.shape[0], dtype=jnp.int32)
    key_parts = split_blocks(
        (key_rows, value_rows, key_pass, places), min(key_block, key_rows.shape[0])
    )
    query_len = min(query_block, queries.shape[0])
    query_parts = split_blocks((queries, query_place, query_pass), query_len)

    def attend_one_block(query_args):
        query_part, place_part, pass_part = query_args

        def running(carry, key_args):
            peak, summed, total_out = carry
            key_part, value_part, kpass_part, kplace_part = key_args
            seen = visible(place_part, pass_part, kplace_part, kpass_part, length)
            scores = masked_scores(query_part, key_part, factor, seen)
            new_peak = jnp.maximum(peak, jnp.max(scores, -1))
            terms = jnp.where(seen[None], jnp.exp(scores - new_peak[..., None]), 0.0)
            rescale = jnp.exp(peak - new_peak)
            summed = summed * rescale + jnp.sum(terms, -1)
            added = jnp.einsum(
                "hqk,khd->qhd",
                terms.astype(jnp.bfloat16),
                value_part,
                preferred_element_type=jnp.float32,
            )
            total_out = total_out * rescale.T[..., None] + added
            return ((new_peak, summed, total_out), None)

        heads_n = query_part.shape[1]
        start = (
            jnp.full((heads_n, query_len), negative, jnp.float32),
            jnp.zeros((heads_n, query_len), jnp.float32),
            jnp.zeros(query_part.shape, jnp.float32),
        )
        (peak, summed, total_out), _ = lax.scan(running, start, key_parts)
        log_total = peak + jnp.log(summed)
        result = total_out / summed.T[..., None]
        return (result, log_total)

    results, log_totals = lax.map(attend_one_block, query_parts)
    heads_n = queries.shape[1]
    return (
        results.reshape(queries.shape),
        jnp.moveaxis(log_totals, 1, 0).reshape(heads_n, queries.shape[0]),
    )


def backward_row(
    queries,
    douts,
    outs_kept,
    log_totals,
    query_place,
    query_pass,
    key_rows,
    value_rows,
    key_pass,
    length,
):
    factor = queries.shape[-1] ** (-0.5)
    places = jnp.arange(key_rows.shape[0], dtype=jnp.int32)
    key_parts = split_blocks(
        (key_rows, value_rows, key_pass, places), min(key_block, key_rows.shape[0])
    )
    query_len = min(query_block, queries.shape[0])
    heads_n = queries.shape[1]
    block_count = queries.shape[0] // query_len
    log_parts = jnp.moveaxis(log_totals.reshape(heads_n, block_count, query_len), 1, 0)
    query_parts = split_blocks((queries, douts, outs_kept, query_place, query_pass), query_len)

    def backward_one_block(carry, query_args):
        query_part, dout_part, kept_part, place_part, pass_part, log_part = query_args
        delta_part = jnp.einsum("qhd,qhd->hq", dout_part.astype(jnp.float32), kept_part)

        def add_grads(dquery, key_args):
            key_part, value_part, kpass_part, kplace_part = key_args
            seen = visible(place_part, pass_part, kplace_part, kpass_part, length)
            dscore, low_chance = grad_pieces(
                query_part, dout_part, log_part, delta_part, key_part, value_part, seen, factor
            )
            dquery = dquery + factor * jnp.einsum(
                "hqk,khd->qhd", dscore, key_part, preferred_element_type=jnp.float32
            )
            dkey = factor * jnp.einsum(
                "hqk,qhd->khd", dscore, query_part, preferred_element_type=jnp.float32
            )
            dvalue = jnp.einsum(
                "hqk,qhd->khd", low_chance, dout_part, preferred_element_type=jnp.float32
            )
            return (dquery, (dkey, dvalue))

        dquery, key_terms = lax.scan(add_grads, jnp.zeros(query_part.shape, jnp.float32), key_parts)
        carry = (
            carry[0] + key_terms[0].reshape(key_rows.shape),
            carry[1] + key_terms[1].reshape(value_rows.shape),
        )
        return (carry, (dquery, delta_part))

    start = (jnp.zeros(key_rows.shape, jnp.float32), jnp.zeros(value_rows.shape, jnp.float32))
    key_sums, (dqueries, deltas) = lax.scan(backward_one_block, start, query_parts + (log_parts,))
    return (
        dqueries.reshape(queries.shape),
        jnp.moveaxis(deltas, 1, 0).reshape(heads_n, queries.shape[0]),
        key_sums,
    )


def local(
    block_input,
    lengths,
    pass_ids,
    pass_embed,
    ln1_gain,
    ln1_bias,
    w_qkv,
    w_out,
    ln2_gain,
    ln2_bias,
    w_up,
    b_up,
    w_down,
    b_down,
    cotangent,
):
    row_count, seg_len, width = block_input.shape
    heads_n = H
    head_size = width // heads_n
    onehot = (
        pass_ids[..., None] == jnp.arange(pass_embed.shape[0], dtype=jnp.int32)[None, None, :]
    ).astype(jnp.float32)
    hidden_in = block_input.astype(jnp.float32) + jnp.einsum(
        "rsp,pd->rsd", onehot, pass_embed, precision=highest
    )
    normed, norm_back = jax.vjp(layer_norm, hidden_in, ln1_gain, ln1_bias)
    normed_low = normed.astype(jnp.bfloat16)
    qkv = jnp.einsum("rsd,de->rse", normed_low, w_qkv, preferred_element_type=jnp.float32)
    queries = qkv[..., :width].astype(jnp.bfloat16)
    key_flat = qkv[..., width : 2 * width].astype(jnp.bfloat16)
    value_flat = qkv[..., 2 * width :].astype(jnp.bfloat16)
    pass_low = pass_ids.astype(jnp.bfloat16)
    key_all, value_all, pass_all = (
        lax.all_gather(key_flat, "seq", axis=1, tiled=True),
        lax.all_gather(value_flat, "seq", axis=1, tiled=True),
        lax.all_gather(pass_low, "seq", axis=1, tiled=True),
    )
    total_len = key_all.shape[1]
    key_all = key_all.reshape(row_count, total_len, heads_n, head_size)
    value_all = value_all.reshape(row_count, total_len, heads_n, head_size)
    pass_all = pass_all.astype(jnp.float32)
    offset = lax.axis_index("seq") * seg_len
    query_place = offset + jnp.arange(seg_len, dtype=jnp.int32)
    query_pass = pass_ids.astype(jnp.float32)
    query_heads = queries.reshape(row_count, seg_len, heads_n, head_size)
    attended_rows = []
    log_rows = []
    for row in range(row_count):
        attended, log_total = attend_row(
            query_heads[row],
            query_place,
            query_pass[row],
            key_all[row],
            value_all[row],
            pass_all[row],
            lengths[row],
        )
        attended_rows.append(attended)
        log_rows.append(log_total)
    attended_low = jnp.stack(attended_rows).astype(jnp.bfloat16).reshape(row_count, seg_len, width)
    branch = jnp.einsum("rsd,de->rse", attended_low, w_out, preferred_element_type=jnp.float32)
    middle = hidden_in + branch
    normed2, norm2_back = jax.vjp(layer_norm, middle, ln2_gain, ln2_bias)
    normed2_low = normed2.astype(jnp.bfloat16)
    pre_act = (
        jnp.einsum("rsd,df->rsf", normed2_low, w_up, preferred_element_type=jnp.float32) + b_up
    )
    active, active_back = jax.vjp(gelu_tanh, pre_act)
    active_low = active.astype(jnp.bfloat16)
    result = (
        middle
        + jnp.einsum("rsf,fd->rsd", active_low, w_down, preferred_element_type=jnp.float32)
        + b_down
    )
    output = result.astype(jnp.bfloat16)
    cot_f = cotangent.astype(jnp.float32)
    grad_active = jnp.einsum("rsd,fd->rsf", cotangent, w_down, preferred_element_type=jnp.float32)
    grad_w_down = jnp.einsum(
        "rsf,rsd->fd", active_low, cotangent, preferred_element_type=jnp.float32
    )
    grad_b_down = jnp.sum(cot_f, (0, 1))
    grad_pre = active_back(grad_active)[0].astype(jnp.bfloat16)
    grad_b_up = jnp.sum(grad_pre.astype(jnp.float32), (0, 1))
    grad_w_up = jnp.einsum("rsd,rsf->df", normed2_low, grad_pre, preferred_element_type=jnp.float32)
    grad_normed2 = jnp.einsum("rsf,df->rsd", grad_pre, w_up, preferred_element_type=jnp.float32)
    grad_mid_norm, grad_ln2_gain, grad_ln2_bias = norm2_back(grad_normed2)
    grad_middle = cot_f + grad_mid_norm
    grad_branch = grad_middle.astype(jnp.bfloat16)
    grad_w_out = jnp.einsum(
        "rsd,rse->de", attended_low, grad_branch, preferred_element_type=jnp.float32
    )
    grad_attended = jnp.einsum(
        "rse,de->rsd", grad_branch, w_out, preferred_element_type=jnp.float32
    ).astype(jnp.bfloat16)
    dout_heads = grad_attended.reshape(row_count, seg_len, heads_n, head_size)
    dquery_rows = []
    dkey_rows = []
    dvalue_rows = []
    for row in range(row_count):
        dquery, _, key_sums = backward_row(
            query_heads[row],
            dout_heads[row],
            attended_rows[row],
            log_rows[row],
            query_place,
            query_pass[row],
            key_all[row],
            value_all[row],
            pass_all[row],
            lengths[row],
        )
        dquery_rows.append(dquery)
        dkey_rows.append(key_sums[0].reshape(total_len, width))
        dvalue_rows.append(key_sums[1].reshape(total_len, width))
    dkey_sum, dvalue_sum = (
        lax.psum_scatter(
            jnp.stack(dkey_rows).astype(jnp.bfloat16), "seq", scatter_dimension=1, tiled=True
        ).astype(jnp.float32),
        lax.psum_scatter(
            jnp.stack(dvalue_rows).astype(jnp.bfloat16), "seq", scatter_dimension=1, tiled=True
        ).astype(jnp.float32),
    )
    dquery_all = jnp.stack(dquery_rows).reshape(row_count, seg_len, width)
    grad_qkv = jnp.concatenate(
        [
            dquery_all.astype(jnp.bfloat16),
            dkey_sum.astype(jnp.bfloat16),
            dvalue_sum.astype(jnp.bfloat16),
        ],
        -1,
    )
    grad_w_qkv = jnp.einsum("rsd,rse->de", normed_low, grad_qkv, preferred_element_type=jnp.float32)
    grad_normed = jnp.einsum("rse,de->rsd", grad_qkv, w_qkv, preferred_element_type=jnp.float32)
    grad_in_norm, grad_ln1_gain, grad_ln1_bias = norm_back(grad_normed)
    grad_hidden = grad_middle + grad_in_norm
    grad_input = grad_hidden.astype(jnp.bfloat16)
    grad_pass = jnp.einsum("rsp,rsd->pd", onehot, grad_hidden, precision=highest)
    matrices = (
        lax.psum_scatter(
            grad_w_qkv.astype(jnp.bfloat16), "seq", scatter_dimension=0, tiled=True
        ).astype(jnp.float32),
        lax.psum_scatter(
            grad_w_out.astype(jnp.bfloat16), "seq", scatter_dimension=0, tiled=True
        ).astype(jnp.float32),
        lax.psum_scatter(
            grad_w_up.astype(jnp.bfloat16), "seq", scatter_dimension=0, tiled=True
        ).astype(jnp.float32),
        lax.psum_scatter(
            grad_w_down.astype(jnp.bfloat16), "seq", scatter_dimension=0, tiled=True
        ).astype(jnp.float32),
    )
    matrices = (
        lax.psum_scatter(
            matrices[0].astype(jnp.bfloat16), "batch", scatter_dimension=1, tiled=True
        ).astype(jnp.float32),
        lax.psum_scatter(
            matrices[1].astype(jnp.bfloat16), "batch", scatter_dimension=1, tiled=True
        ).astype(jnp.float32),
        lax.psum_scatter(
            matrices[2].astype(jnp.bfloat16), "batch", scatter_dimension=1, tiled=True
        ).astype(jnp.float32),
        lax.psum_scatter(
            matrices[3].astype(jnp.bfloat16), "batch", scatter_dimension=1, tiled=True
        ).astype(jnp.float32),
    )
    vectors = lax.psum(
        (
            grad_pass,
            grad_ln1_gain,
            grad_ln1_bias,
            grad_ln2_gain,
            grad_ln2_bias,
            grad_b_up,
            grad_b_down,
        ),
        ("seq", "batch"),
    )
    return (
        output,
        grad_input,
        vectors[0],
        vectors[1],
        vectors[2],
        matrices[0],
        matrices[1],
        vectors[3],
        vectors[4],
        matrices[2],
        vectors[5],
        matrices[3],
        vectors[6],
    )


NN = (((1,), (0,)), ((), ()))
NT = (((1,), (1,)), ((), ()))
TN = (((0,), (0,)), ((), ()))
vmem_bytes = 60 << 20
block = 256


def dot(left, right, form):
    return lax.dot_general(left, right, form, preferred_element_type=jnp.float32)


mesh_ids = pl.DeviceIdType.MESH


def block_kernel(
    lengths,
    block_in, cot_in, w_up_in, w_qkv_in, w_out_in, w_down_in,
    pass_in, embed_in, gain1, bias1, gain2, bias2, b_up_in, b_down_in,
    out, gin, vector, gqkv, gout, gup, gdown,
    kept_far, h_far,
    mid, keep, at, qkv, otf, ct, mt, gd, far, dm, kept, w_out, w_up, w_down,
    bsum, r1a, r2a, r1c, r2c, r2e, r3e, rz, rze,
    osend, orecv, hand, sums, gpass, vrecv, ksum, vsum, stage_send, stage_recv, down_recv,
    params, vecs, bcol, inv, prow, kmask, qhot, passes,
    lsem, ssem, rsem,
    *, chunks, plan,
):
    seq, bat = lax.axis_index("seq"), lax.axis_index("batch")
    x, core = seq // 2, seq % 2
    z, y = bat // 2, bat % 2
    to_core, to_x, to_y = (seq + 1 - 2 * core, bat), (seq + 2 - 4 * x, bat), (seq, bat + 1 - 2 * y)
    to_cross = (3 - seq, bat)
    to_z = [(seq, ((z + i) % 4) * 2 + y) for i in (1, 2, 3)]
    up_z, low_z = (seq, bat + 2), (seq, bat - 2)

    barrier = pltpu.get_barrier_semaphore()
    for peer in [to_core, to_x, to_y, to_cross] + to_z:
        pl.semaphore_signal(barrier, inc=1, device_id=peer, device_id_type=mesh_ids)

    width, total = mid.shape
    half = width // 2
    inner = w_up.shape[0]
    blocks_n = total // block
    heads = half // 64
    bs = 8

    def rows_at(first, count):
        return pl.ds(pl.multiple_of(first, 16), count)

    def lanes_at(first, count):
        return pl.ds(pl.multiple_of(first, 128), count)

    def own_cols(k):
        return lanes_at(core * block + k * 2 * block, block)

    def local(i, src, dst):
        return pltpu.make_async_copy(src, dst, lsem.at[i])

    def remote(i, src, dst, peer):
        return pltpu.make_async_remote_copy(
            src_ref=src, dst_ref=dst, send_sem=ssem.at[i], recv_sem=rsem.at[i],
            device_id=peer, device_id_type=mesh_ids,
        )

    part = w_down_in.shape[2]

    def spot(b):
        return b // 2 % 2 * 4 + b // 4 * 2 + b % 2

    def slab(b):
        return slice(spot(b) * part, (spot(b) + 1) * part)

    own_x = local(0, block_in.at[x], far.at[0:block, 0:width])
    own_c = local(1, cot_in.at[x], dm.at[0:block, 0:width])
    out_load = local(2, w_out_in, w_out)
    up_loads = [
        local(3 + p, w_up_in.at[:, p * width : (p + 1) * width],
              gd.at[p * width : (p + 1) * width, 0:width])
        for p in range(4)
    ]
    down_loads = [
        local(7 + i, w_down_in.at[i, core], w_down.at[slab(i), :])
        for i in range(bs)
    ]
    qkv_loads = [
        local(15 + j, w_qkv_in.at[:, j * width : (j + 1) * width],
              gd.at[j * width : (j + 1) * width, 0:width])
        for j in range(3)
    ]
    for load in [own_x] + up_loads + [own_c, out_load] + down_loads:
        load.start()

    base = 22 * len(chunks)
    x_far = remote(base, block_in.at[1 - x], far.at[block : 2 * block, 0:width], to_x)
    x_near = remote(base + 1, block_in.at[x], far.at[2 * block : 3 * block, 0:width], to_core)
    x_cross = remote(
        base + 2, far.at[block : 2 * block, 0:width], far.at[3 * block : 4 * block, 0:width], to_core
    )
    c_far = remote(base + 3, cot_in.at[1 - x], dm.at[block : 2 * block, 0:width], to_x)
    c_near = remote(base + 4, cot_in.at[x], dm.at[2 * block : 3 * block, 0:width], to_core)
    c_cross = remote(
        base + 5, dm.at[block : 2 * block, 0:width], dm.at[3 * block : 4 * block, 0:width], to_core
    )
    p_far = remote(base + 6, pass_in, passes.at[1], to_x)
    p_near = remote(base + 7, pass_in, passes.at[2], to_core)
    p_cross = remote(base + 8, pass_in, passes.at[3], to_cross)
    base += 9
    pl.semaphore_wait(barrier, 7)
    for copy in (p_far, x_far, x_near, p_near, p_cross, c_near):
        copy.start()


    def line_copy(i, d, up, part, slots):
        slot = d if up else jnp.where(z - 1 == d, 4, d)
        return remote(i + (d if up else 4 + d), part(d), slots(slot), up_z if up else low_z)

    def line_add(d, slot, part, slots):
        here, got = part(d), slots(slot)
        here[...] = here[...] + got[...]

    def line_start(i, part, slots):
        @pl.when(z == 0)
        def _():
            for d in (3, 2, 1):
                line_copy(i, d, True, part, slots).start()

        @pl.when(z == 3)
        def _():
            for d in (0, 1, 2):
                line_copy(i, d, False, part, slots).start()

    def line_pass(i, d, up, part, slots):
        copy = line_copy(i, d, up, part, slots)
        copy.wait_recv()
        line_add(d, d, part, slots)
        copy.start()

    def line_one(i, part, slots):
        @pl.when(z == 1)
        def _():
            line_pass(i, 3, True, part, slots)

        @pl.when(z == 2)
        def _():
            line_pass(i, 0, False, part, slots)

    def line_two(i, part, slots):
        @pl.when(z == 1)
        def _():
            line_pass(i, 2, True, part, slots)
            line_pass(i, 0, False, part, slots)

        @pl.when(z == 2)
        def _():
            line_pass(i, 1, False, part, slots)
            line_pass(i, 3, True, part, slots)

    def line_last(i, part, slots):
        for d in range(4):

            @pl.when(z == d)
            def _():
                if d > 0:
                    line_copy(i, d, True, part, slots).wait_recv()
                    line_add(d, d, part, slots)
                if d < 3:
                    line_copy(i, d, False, part, slots).wait_recv()
                    line_add(d, 4, part, slots)
                for e in range(4):
                    if e > d:
                        line_copy(i, e, True, part, slots).wait_send()
                    if e < d:
                        line_copy(i, e, False, part, slots).wait_send()

    class Chunk:
        def __init__(self, k):
            r0, rc, ra, r1, a0, c0, e0 = chunks[k]
            ne, nc, na = rc - r0, ra - rc, r1 - ra
            i = 22 * k
            rows_e, rows_c, rows_a = pl.ds(r0, ne), pl.ds(rc, nc), pl.ds(ra, na)
            got_a, got_c, got_e = pl.ds(a0, na), pl.ds(c0, nc), pl.ds(e0, ne)
            sub = bsum.at
            self.one_a = remote(i, sub[1 - x, :, :, rows_a, :], r1a.at[:, :, got_a, :], to_x)
            self.one_c = remote(i + 1, sub[:, :, 1 - y, rows_c, :], r1c.at[:, :, got_c, :], to_y)
            self.two_a = remote(i + 2, sub[x, :, 1 - y, rows_a, :], r2a.at[:, got_a, :], to_y)
            self.two_c = remote(i + 3, sub[1 - x, :, y, rows_c, :], r2c.at[:, got_c, :], to_x)
            self.two_e = remote(i + 4, sub[:, z, 1 - y, rows_e, :], r2e.at[:, got_e, :], to_y)
            self.three_e = remote(i + 5, sub[1 - x, z, y, rows_e, :], r3e.at[got_e, :], to_x)
            self.adds = [
                (sub[x, :, :, rows_a, :], r1a.at[:, :, got_a, :]),
                (sub[:, :, y, rows_c, :], r1c.at[:, :, got_c, :]),
                (sub[x, :, y, rows_a, :], r2a.at[:, got_a, :]),
                (sub[x, :, y, rows_c, :], r2c.at[:, got_c, :]),
                (sub[:, z, y, rows_e, :], r2e.at[:, got_e, :]),
                (sub[x, z, y, rows_e, :], r3e.at[got_e, :]),
            ]
            both, low = pl.ds(rc, na + nc), pl.ds(a0 + c0, na + nc)
            self.line_ac = (
                i + 6, lambda d: sub[x, d, y, both, :], lambda s: rz.at[s, low, :]
            )
            self.line_e = (
                i + 14, lambda d: sub[:, d, :, rows_e, :], lambda s: rze.at[s, :, :, got_e, :]
            )

        def add(self, j):
            here, got = self.adds[j]
            here[...] = here[...] + got[...]

        def start(self):
            line_start(*self.line_e)
            self.one_c.start()
            self.one_a.start()

        def start_a(self):
            self.one_a.start()

        def start_c(self):
            self.one_c.start()

        def start_e(self):
            line_start(*self.line_e)

        def e1(self):
            line_one(*self.line_e)

        def e2(self):
            line_two(*self.line_e)

        def e3(self):
            line_last(*self.line_e)
            self.two_e.start()

        def a2(self):
            self.one_a.wait()
            self.add(0)
            self.two_a.start()

        def c2(self):
            self.one_c.wait()
            self.add(1)
            self.two_c.start()

        def e4(self):
            self.two_e.wait()
            self.add(4)
            self.three_e.start()

        def z0(self):
            self.two_a.wait()
            self.add(2)
            self.two_c.wait()
            self.add(3)
            line_start(*self.line_ac)

        def z1(self):
            line_one(*self.line_ac)

        def z2(self):
            line_two(*self.line_ac)

        def z3(self):
            line_last(*self.line_ac)
            self.three_e.wait()
            self.add(5)
    steps = [Chunk(k) for k in range(len(chunks))]

    def serve(slot):
        for k, name in plan[slot]:
            getattr(steps[k], name)()

    params[...] = jnp.zeros_like(params)
    params[0:5, :] = embed_in[...]
    for i, ref in enumerate((gain1, bias1, gain2, bias2, b_down_in)):
        params[5 + i, :] = ref[...]
    for i in range(4):
        params[10 + i, :] = b_up_in[pl.ds(i * width, width)]
    vecs[...] = jnp.transpose(params[...])
    for b in range(bs):
        i, low = 10 + b // 2, b % 2 * 2 * part
        bcol[slab(b), :] = jnp.broadcast_to(
            jnp.where(
                core == 0,
                vecs[low : low + part, i : i + 1],
                vecs[low + part : low + 2 * part, i : i + 1],
            ),
            (part, 8),
        )
    for b in range(bs):
        p, low = b // 2, b % 2 * 2 * part
        if b % 2 == 0:
            up_loads[p].wait()
        turned = jnp.transpose(gd[p * width : (p + 1) * width, low : low + 2 * part])
        w_up[slab(b), :] = jnp.where(core == 0, turned[:part], turned[part:])
    for load in qkv_loads:
        load.start()
    passes[0] = pass_in[...]
    places = (2 * x + core, 2 * (1 - x) + core, 2 * x + 1 - core, 2 * (1 - x) + 1 - core)
    length = lengths[x]
    emb = jnp.where(lax.broadcasted_iota(jnp.int32, (8, width), 0) < 5, params[0:8, :], 0.0)
    emb_a = emb.astype(jnp.bfloat16)
    rest = emb - emb_a.astype(jnp.float32)
    emb_b = rest.astype(jnp.bfloat16)
    emb_c = (rest - emb_b.astype(jnp.float32)).astype(jnp.bfloat16)

    def take(k):
        cols = lanes_at(places[k] * block, block)
        rows = rows_at(places[k] * block, block)
        got = passes[k]
        line = jnp.where(x == 0, got[0:1, :], got[1:2, :])
        prow[:, cols] = jnp.broadcast_to(line.astype(jnp.float32), (8, block))
        kind = lax.broadcasted_iota(jnp.int32, (16, block), 0)
        spot = lax.broadcasted_iota(jnp.int32, (16, block), 1) + places[k] * block
        onehot = jnp.where(kind == line, 1.0, 0.0).astype(jnp.bfloat16)
        qhot[:, cols] = onehot
        hidden = jnp.where((line > kind) | (spot >= length), negative, 0.0)
        kmask[rows, :] = jnp.transpose(hidden).astype(jnp.bfloat16)
        hot = onehot[0:8, :]
        added = dot(emb_a, hot, TN) + dot(emb_b, hot, TN) + dot(emb_c, hot, TN)
        h = jnp.transpose(far[k * block : (k + 1) * block, 0:width]).astype(jnp.float32) + added
        mid[:, cols] = h
        shifted = h - jnp.sum(h, 0, keepdims=True) * (1.0 / width)
        spread = jnp.sum(shifted * shifted, 0, keepdims=True) * (1.0 / width)
        scaled = shifted * lax.rsqrt(spread + 1e-05)
        at[:, cols] = (scaled * vecs[:, 5:6] + vecs[:, 6:7]).astype(jnp.bfloat16)
        for j in range(3):
            res = dot(
                gd[j * width : (j + 1) * width, lanes_at(core * half, half)], at[:, cols], TN
            ).astype(jnp.bfloat16)
            qkv[j * half : (j + 1) * half, cols] = res * jnp.bfloat16(0.125) if j == 0 else res

    own_x.wait()
    for load in qkv_loads:
        load.wait()
    take(0)
    x_near.wait()
    p_near.wait()
    take(2)
    p_far.wait()
    x_far.wait()
    x_cross.start()
    c_far.start()
    take(1)
    x_cross.wait()
    p_cross.wait()
    take(3)
    h_saves = [local(18 + k, mid.at[:, own_cols(k)], h_far.at[k]) for k in range(2)]
    for save in h_saves:
        save.start()

    pairs_n = blocks_n // 2
    wide = 2 * block

    def cover(first_key, first_query, queries):
        key = lax.broadcasted_iota(jnp.int32, (block, queries), 0) + first_key
        place = lax.broadcasted_iota(jnp.int32, (block, queries), 1) + first_query
        hidden = dot(
            kmask[first_key : first_key + block, :], qhot[:, first_query : first_query + queries], NN
        )
        hidden = jnp.where(key < place, hidden, negative)
        return jnp.where(key == place, 0.0, hidden)

    for p in range(pairs_n):
        keep[p * block : (p + 1) * block, :] = cover(p * wide, p * wide, wide)
        keep[wide : wide + block, p * block : (p + 1) * block] = cover(
            p * wide + block, p * wide + block, block
        )

    def kept_save(h, slot):
        return pltpu.make_async_copy(kept.at[slot], kept_far.at[h], lsem.at[20 + slot])

    def o_copy(h):
        mine = rows_at(core * half + h * 64, 64)
        return remote(base + h, otf.at[mine, :], otf.at[mine, :], to_core)

    def turn(k):
        ct[:, lanes_at(places[k] * block, block)] = jnp.transpose(
            dm[k * block : (k + 1) * block, 0:width]
        )

    def one_head(h, slot):
        @pl.when(h >= 2)
        def _():
            kept_save(h - 2, slot).wait()

        qrow, krow, vrow = (rows_at(j * half + h * 64, 64) for j in range(3))
        mine = rows_at(core * half + h * 64, 64)
        keyn = jnp.concatenate([jnp.transpose(qkv[krow, :]), kmask[...]], 1)
        query = jnp.concatenate([qkv[qrow, :], qhot[...]], 0)
        for p in range(pairs_n):
            before, split, after = p * wide, p * wide + block, (p + 1) * wide
            at_row = p * p * block
            cols, late = slice(before, after), slice(split, after)
            side = slice(p * block, (p + 1) * block)
            near = dot(keyn[before:split, 0:64], query[0:64, cols], NN)
            near = near + keep[p * block : (p + 1) * block, :]
            peak = jnp.max(near, 0, keepdims=True)
            last = dot(keyn[late, 0:64], query[0:64, late], NN) + keep[wide : wide + block, side]
            last_peak = jnp.maximum(peak[:, block:], jnp.max(last, 0, keepdims=True))
            peak = jnp.concatenate([peak[:, :block], last_peak], 1)
            if p:
                scores = dot(keyn[0:before, :], query[:, cols], NN)
                peak = jnp.maximum(peak, jnp.max(scores, 0, keepdims=True))
                expo = jnp.exp(scores - peak)
                count = jnp.sum(expo, 0, keepdims=True)
                low = expo.astype(jnp.bfloat16)
                kept[slot, at_row : at_row + before, :] = low
                result = dot(qkv[vrow, 0:before], low, NN)
            near = jnp.exp(near - peak)
            near_sum = jnp.sum(near, 0, keepdims=True)
            count = count + near_sum if p else near_sum
            low = near.astype(jnp.bfloat16)
            kept[slot, at_row + before : at_row + split, :] = low
            near_result = dot(qkv[vrow, before:split], low, NN)
            result = result + near_result if p else near_result
            last = jnp.exp(last - peak[:, block:])
            low = last.astype(jnp.bfloat16)
            kept[slot, kept.shape[1] - block : kept.shape[1], side] = low
            last_result = dot(qkv[vrow, late], low, NN)
            over = 1.0 / jnp.concatenate(
                [count[:, :block], count[:, block:] + jnp.sum(last, 0, keepdims=True)], 1
            )
            result = jnp.concatenate([result[:, :block], result[:, block:] + last_result], 1)
            inv[h, :, cols] = jnp.broadcast_to(over, (8, wide))
            otf[mine, cols] = (result * over).astype(jnp.bfloat16)
        kept_save(h, slot).start()

        @pl.when(h == heads - 2)
        def _():
            c_near.wait()
            c_far.wait()
            c_cross.start()
            own_c.wait()
            for k in (0, 2, 1):
                turn(k)

        @pl.when(h == heads - 1)
        def _():
            c_cross.wait()
            turn(3)

        o_copy(h).start()

    def head_pair(i, carry):
        for e in range(2):
            one_head(2 * i + e, e)
        return carry

    lax.fori_loop(0, heads // 2, head_pair, 0)
    kept_save(heads - 2, heads % 2).wait()
    kept_save(heads - 1, (heads - 1) % 2).wait()

    def kept_load(h, slot):
        return pltpu.make_async_copy(kept_far.at[h], kept.at[slot], lsem.at[22 + slot])

    kept_load(0, 0).start()
    kept_load(1, 1).start()
    for h in range(heads):
        o_copy(h).wait()
    base += heads

    for save in h_saves:
        save.wait()
    out_load.wait()

    def mix(i, carry):
        cols = lanes_at(i * block, block)
        m = mid[:, cols] + dot(w_out[...], otf[:, cols], TN)
        mid[:, cols] = m
        shifted = m - jnp.sum(m, 0, keepdims=True) * (1.0 / width)
        spread = jnp.sum(shifted * shifted, 0, keepdims=True) * (1.0 / width)
        scaled = shifted * lax.rsqrt(spread + 1e-05)
        mt[:, cols] = (scaled * vecs[:, 7:8] + vecs[:, 8:9]).astype(jnp.bfloat16)
        return carry

    lax.fori_loop(0, blocks_n, mix, 0)

    def hidden_at(first):
        for i in range(4):
            rows = slice(first + i * part, first + (i + 1) * part)
            below = slice(inner + first + i * part, inner + first + (i + 1) * part)
            u = dot(w_up[rows, :], mt[...], NN) + bcol[rows, 0:1]
            square = u * u
            t = jnp.tanh(u * (0.7978845608028654 + 0.035677408136300125 * square))
            gate = 0.5 + 0.5 * t
            gd[rows, :] = (u * gate).astype(jnp.bfloat16)
            slope = gate + (0.5 * u) * (1.0 - t * t) * (
                0.7978845608028654 + 0.10703222440890037 * square
            )
            gd[below, :] = slope.astype(jnp.bfloat16)

    lanes = bsum.shape[-1]
    band = width // bs
    for j in range(2):
        hidden_at(j * width)
        grad = dot(ct[...], gd[j * width : (j + 1) * width, :], NT).astype(jnp.bfloat16)
        for xx in range(2):
            for b in range(bs):
                bsum[xx, b // 2, b % 2, j * band : (j + 1) * band, :] = grad[
                    b * band : (b + 1) * band, xx * lanes : (xx + 1) * lanes
                ]
        serve("down%d" % j)
    for load in down_loads:
        load.wait()

    for i in range(bs):
        rows = slice(i * part, (i + 1) * part)
        below = slice(inner + i * part, inner + (i + 1) * part)
        back = dot(w_down[rows, :], ct[...], NN)
        gd[below, :] = (back * gd[below, :].astype(jnp.float32)).astype(jnp.bfloat16)
    serve("hidden")

    dm_copy = remote(base, dm.at[0:width, :], dm.at[width : 2 * width, :], to_core)

    for i in range(blocks_n):
        cols = slice(i * block, (i + 1) * block)
        dm[0:width, cols] = dot(w_up[...], gd[inner : 2 * inner, cols], TN).astype(jnp.bfloat16)
    dm_copy.start()
    serve("dm")
    first_up = 2 * band
    up_band = part
    for i in range(2):
        grad = dot(gd[inner + i * width : inner + (i + 1) * width, :], mt[...], NT)
        grad = grad.astype(jnp.bfloat16)
        for b in range(bs):
            low = spot(b) * part - i * width
            if 0 <= low < width:
                for xx in range(2):
                    bsum[xx, b // 2, b % 2, first_up : first_up + up_band, :] = grad[
                        low : low + part, xx * lanes : (xx + 1) * lanes
                    ]
        serve("up%d" % i)
    ones = jnp.ones((8, total), jnp.bfloat16)
    up_sum = dot(ones, gd[inner : 2 * inner, :], NT)
    vector[...] = jnp.zeros_like(vector)
    for i in range(4):
        one, two = (up_sum[0:1, slab(2 * i + e)] for e in range(2))
        none = jnp.zeros_like(one)
        vector[10 + i : 11 + i, :] = jnp.where(
            core == 0,
            jnp.concatenate([one, none, two, none], 1),
            jnp.concatenate([none, one, none, two], 1),
        )

    out_copy = remote(base + 1, osend, orecv, to_core)
    for k in range(2):
        other = lanes_at((1 - core) * block + k * 2 * block, block)
        to = slice(k * block, (k + 1) * block)
        osend[:, to] = dot(w_down[...], gd[0:inner, other], TN).astype(jnp.bfloat16)
        keep[:, to] = mid[:, own_cols(k)] + vecs[:, 9:10] + dot(
            w_down[...], gd[0:inner, own_cols(k)], TN
        )
    out_copy.start()
    serve("out")

    dm_copy.wait()
    sums[...] = jnp.zeros_like(sums)

    def middle(i, carry):
        cols = lanes_at(i * block, block)
        cot = ct[:, cols].astype(jnp.float32)
        m = mid[:, cols]
        shifted = m - jnp.sum(m, 0, keepdims=True) * (1.0 / width)
        spread = jnp.sum(shifted * shifted, 0, keepdims=True) * (1.0 / width)
        r = lax.rsqrt(spread + 1e-05)
        n = shifted * r
        d = dm[0:width, cols].astype(jnp.float32) + dm[width : 2 * width, cols].astype(jnp.float32)
        e = d * vecs[:, 7:8]
        mean_e = jnp.sum(e, 0, keepdims=True) * (1.0 / width)
        mean_en = jnp.sum(e * n, 0, keepdims=True) * (1.0 / width)
        dmid = cot + r * (e - mean_e - n * mean_en)
        mid[:, cols] = dmid
        dm[width : 2 * width, cols] = dmid.astype(jnp.bfloat16)
        sums[:, 0:1] += jnp.sum(d * n, 1, keepdims=True)
        sums[:, 1:2] += jnp.sum(d, 1, keepdims=True)
        sums[:, 2:3] += jnp.sum(cot, 1, keepdims=True)
        return carry

    lax.fori_loop(0, blocks_n, middle, 0)
    serve("middle")
    small = band // 2
    for b in range(bs):
        dm[half + b * small : half + (b + 1) * small, :] = dm[
            rows_at(width + b * band + core * small, small), :
        ]
    first_out = first_up + up_band
    grad = dot(dm[half:width, :], otf[...], NT).astype(jnp.bfloat16)
    for xx in range(2):
        for b in range(bs):
            bsum[xx, b // 2, b % 2, first_out : first_out + small, :] = grad[
                b * small : (b + 1) * small, xx * lanes : (xx + 1) * lanes
            ]
    dm[0:half, :] = dot(
        w_out[rows_at(core * half, half), :], dm[width : 2 * width, :], NN
    ).astype(jnp.bfloat16)
    serve("w_out")

    whole_loads = [
        local(24, w_qkv_in.at[:, 0:width], w_up.at[0:width, :]),
        local(25, w_qkv_in.at[:, width : 2 * width], w_up.at[width : 2 * width, :]),
        local(26, w_qkv_in.at[:, 2 * width : 3 * width], w_down.at[0:width, :]),
    ]
    for load in whole_loads:
        load.start()
    hand_out = remote(base + 2, hand.at[0], out.at[x], to_x)

    def give_output():
        out_copy.wait()
        for k in range(2):
            cols = slice(k * block, (k + 1) * block)
            rows = jnp.transpose(
                (keep[:, cols] + orecv[:, cols].astype(jnp.float32)).astype(jnp.bfloat16)
            )

            @pl.when(x == k)
            def _():
                out[k] = rows

            @pl.when(x != k)
            def _():
                hand[0] = rows

        hand_out.start()

    give_output()
    serve("given")

    def far_copy(h, j):
        mine = rows_at(j * width + core * half + h * 64, 64)
        return remote(
            base + 3 + h * 3 + j, gd.at[mine, :], far.at[rows_at(j * half + h * 64, 64), :], to_core
        )

    def head_back(h, slot, ksum, vsum):
        kept_load(h, slot).wait()
        qrow, krow, vrow = (rows_at(j * half + h * 64, 64) for j in range(3))
        mine = [rows_at(j * width + core * half + h * 64, 64) for j in range(3)]
        valn = jnp.transpose(qkv[vrow, :])
        grads = (dm[rows_at(h * 64, 64), :].astype(jnp.float32) * inv[h, 0:1, :]).astype(
            jnp.bfloat16
        )
        o_rows = otf[rows_at(core * half + h * 64, 64), :]
        delta = jnp.sum(grads.astype(jnp.float32) * o_rows.astype(jnp.float32), 0, keepdims=True)
        ksum[...] = jnp.zeros_like(ksum)
        vsum[...] = jnp.zeros_like(vsum)
        for p in range(pairs_n):
            before, split, after = p * wide, p * wide + block, (p + 1) * wide
            at_row = p * p * block
            cols, late = slice(before, after), slice(split, after)
            side = slice(p * block, (p + 1) * block)
            low = kept[slot, at_row : at_row + split, :]
            dprob = dot(valn[0:split, :], grads[:, cols], NN)
            dscore = (low.astype(jnp.float32) * (dprob - delta[:, cols])).astype(jnp.bfloat16)
            last = kept[slot, kept.shape[1] - block : kept.shape[1], side]
            dprob = dot(valn[late, :], grads[:, late], NN)
            dlast = (last.astype(jnp.float32) * (dprob - delta[:, late])).astype(jnp.bfloat16)
            dquery = dot(qkv[krow, 0:split], dscore, NN)
            dquery = jnp.concatenate(
                [dquery[:, :block], dquery[:, block:] + dot(qkv[krow, late], dlast, NN)], 1
            )
            gd[mine[0], cols] = (dquery * 0.125).astype(jnp.bfloat16)
            ksum[:, 0:split] += dot(qkv[qrow, cols], dscore, NT)
            vsum[:, 0:split] += dot(grads[:, cols], low, NT)
            ksum[:, late] += dot(qkv[qrow, late], dlast, NT)
            vsum[:, late] += dot(grads[:, late], last, NT)
        gd[mine[1], :] = ksum[...].astype(jnp.bfloat16)
        gd[mine[2], :] = vsum[...].astype(jnp.bfloat16)
        for j in range(3):
            far_copy(h, j).start()

        @pl.when(h + 2 < heads)
        def _():
            kept_load(h + 2, slot).start()

        for at_head in range(slot, heads, 2):

            @pl.when(h == at_head)
            def _():
                serve("head%d" % at_head)

    def back_pair(i, carry):
        for e in range(2):
            head_back(2 * i + e, e, ksum.at[e], vsum.at[e])
        return carry

    lax.fori_loop(0, heads // 2, back_pair, 0)
    own_loads = [local(18 + k, h_far.at[k], keep.at[:, k * block : (k + 1) * block]) for k in range(2)]
    for load in own_loads:
        load.start()

    for h in range(heads):
        for j in range(3):
            far_copy(h, j).wait()
    for j in range(3):
        gd[rows_at(j * width + (1 - core) * half, half), :] = far[j * half : (j + 1) * half, :]
    qkv_band = 3 * width // bs
    qkv_small = qkv_band // 2
    for b in range(bs):
        dm[b * qkv_small : (b + 1) * qkv_small, :] = gd[
            rows_at(b * qkv_band + core * qkv_small, qkv_small), :
        ]
    first_qkv = first_out + small
    for i in range(2):
        grad = dot(dm[i * bs // 2 * qkv_small : (i + 1) * bs // 2 * qkv_small, :], at[...], NT)
        grad = grad.astype(jnp.bfloat16)
        for xx in range(2):
            for b in range(bs // 2):
                bb = i * bs // 2 + b
                bsum[xx, bb // 2, bb % 2, first_qkv : first_qkv + qkv_small, :] = grad[
                    b * qkv_small : (b + 1) * qkv_small, xx * lanes : (xx + 1) * lanes
                ]
    serve("qkv")

    for load in whole_loads + own_loads:
        load.wait()
    gpass[...] = jnp.zeros_like(gpass)
    hand_in = remote(base + 21, hand.at[1], gin.at[x], to_x)
    for k in range(2):
        mine = own_cols(k)
        da = dot(w_up[0:width, :], gd[0:width, mine], NN)
        da += dot(w_up[width : 2 * width, :], gd[width : 2 * width, mine], NN)
        da += dot(w_down[0:width, :], gd[2 * width : 3 * width, mine], NN)
        h = keep[:, k * block : (k + 1) * block]
        shifted = h - jnp.sum(h, 0, keepdims=True) * (1.0 / width)
        spread = jnp.sum(shifted * shifted, 0, keepdims=True) * (1.0 / width)
        r = lax.rsqrt(spread + 1e-05)
        n = shifted * r
        e = da * vecs[:, 5:6]
        mean_e = jnp.sum(e, 0, keepdims=True) * (1.0 / width)
        mean_en = jnp.sum(e * n, 0, keepdims=True) * (1.0 / width)
        dh = mid[:, mine] + r * (e - mean_e - n * mean_en)
        rows = jnp.transpose(dh).astype(jnp.bfloat16)

        @pl.when(x == k)
        def _():
            gin[k] = rows

        @pl.when(x != k)
        def _():
            hand[1] = rows
            hand_in.start()

        sums[:, 3:4] += jnp.sum(da * n, 1, keepdims=True)
        sums[:, 4:5] += jnp.sum(da, 1, keepdims=True)
        kind = lax.broadcasted_iota(jnp.int32, (16, block), 0).astype(jnp.float32)
        onehot = jnp.where(kind == prow[0:1, mine], 1.0, 0.0).astype(jnp.bfloat16)
        high = dh.astype(jnp.bfloat16)
        rest = dh - high.astype(jnp.float32)
        second_part = rest.astype(jnp.bfloat16)
        tail = (rest - second_part.astype(jnp.float32)).astype(jnp.bfloat16)
        gpass[...] += dot(onehot, high, NT) + dot(onehot, second_part, NT) + dot(onehot, tail, NT)
        serve("input%d" % k)

    own_rows = down_recv.shape[0]
    wide = lanes // 2
    row_ranges = ((0, first_up), (first_up, first_out), (first_out, first_qkv),
                  (first_qkv, first_qkv + qkv_small))
    results = (gdown, gup, gout, gqkv)

    def both_cores(mine, got):
        return jnp.where(core == 0, mine, got), jnp.where(core == 0, got, mine)

    class Finish:
        def swap(self, k):
            r0, r1 = row_ranges[k]
            if k == 0:
                theirs = rows_at((1 - core) * own_rows, own_rows)
                return remote(base + 28, bsum.at[x, z, y, theirs, :], down_recv, to_core)
            rows = slice(r0 - first_up, r1 - first_up)
            return remote(base + 28 + k, stage_send.at[rows, :], stage_recv.at[rows, :], to_core)

        def send(self, k):
            r0, r1 = row_ranges[k]
            if k:
                v = bsum[x, z, y, r0:r1, :]
                stage_send[r0 - first_up : r1 - first_up, 0:wide] = jnp.where(
                    core == 0, v[:, wide:lanes], v[:, 0:wide]
                )
            self.swap(k).start()

        def put(self, k):
            self.swap(k).wait()
            if k == 0:
                mine = bsum[x, z, y, rows_at(core * own_rows, own_rows), :].astype(jnp.float32)
                for c, piece in enumerate(both_cores(mine, down_recv[...].astype(jnp.float32))):
                    for i in range(lanes // part):
                        at_row = (2 * i + c) * part
                        gdown[:, at_row : at_row + part] = piece[:, i * part : (i + 1) * part]
                return
            r0, r1 = row_ranges[k]
            v = bsum[x, z, y, r0:r1, :].astype(jnp.float32)
            mine = jnp.where(core == 0, v[:, 0:wide], v[:, wide:lanes])
            got = stage_recv[r0 - first_up : r1 - first_up, 0:wide].astype(jnp.float32)
            results[k][...] = jnp.transpose(jnp.concatenate(both_cores(mine, got), 0))

    for k in range(4):
        setattr(Finish, "f%d" % k, lambda self, k=k: self.send(k))
        setattr(Finish, "g%d" % k, lambda self, k=k: self.put(k))

    lines = jnp.transpose(sums[...])
    vector[0:5, :] = gpass[0:5, :]
    vector[5:7, :] = lines[3:5, :]
    vector[7:10, :] = lines[0:3, :] * 0.5
    hops = [
        remote(base + 22 + i, vector, vrecv.at[i], peer)
        for i, peer in enumerate((to_core, to_x, to_y))
    ]
    copies = [
        remote(base + 25 + i, vector, vrecv.at[3 + z], peer) for i, peer in enumerate(to_z)
    ]

    class Vector:
        def v0(self):
            hops[0].start()

        def take(self, i):
            hops[i].wait()
            vector[...] = vector[...] + vrecv[i]

        def v1(self):
            self.take(0)
            hops[1].start()

        def v2(self):
            self.take(1)
            hops[2].start()

        def v3(self):
            self.take(2)
            for copy in copies:
                copy.start()
            vrecv[3 + z] = vector[...]

    steps.extend((Vector(), Finish()))
    for i in range(3):
        serve("sum%d" % i)

    for i in range(3):
        serve("end%d" % i)
    for copy in copies:
        copy.wait()
    vector[...] = (vrecv[3] + vrecv[4]) + (vrecv[5] + vrecv[6])
    hand_out.wait()
    hand_in.wait()


def finish_kernel(
    out_in, gin_in, vector_in, gqkv_in, gout_in, gup_in, gdown_in,
    out, gin, gpass, gain1, bias1, gqkv, gout, gain2, bias2, gup, gb_up, gdown, gb_down,
    vector, sem,
):
    pairs = (
        (out_in, out), (gin_in, gin), (gqkv_in, gqkv), (gout_in, gout), (gup_in, gup), (gdown_in, gdown),
        (vector_in, vector),
    )
    copies = [pltpu.make_async_copy(a, b, sem.at[i]) for i, (a, b) in enumerate(pairs)]
    for copy in copies:
        copy.start()
    for copy in copies:
        copy.wait()
    width = vector.shape[1]
    gpass[...] = vector[0:5, :]
    for i, ref in enumerate((gain1, bias1, gain2, bias2, gb_down)):
        ref[...] = vector[5 + i, :]
    for i in range(4):
        gb_up[pl.ds(i * width, width)] = vector[10 + i, :]


def shaped(*dims, kind=jnp.bfloat16):
    return jax.ShapeDtypeStruct(dims, kind)


shares = ((80, 48, 64), (64, 64, 64), (16, 16, 16), (48, 48, 48))
plan = {
    "down0": ((0, "start_e"),),
    "down1": ((0, "start_c"), (0, "start_a"),),
    "hidden": ((0, "e1"),),
    "dm": (),
    "up0": ((0, "c2"),),
    "up1": ((1, "start"),),
    "out": ((0, "e2"),),
    "middle": (),
    "w_out": ((2, "start"), (0, "a2"),),
    "given": ((1, "e1"),),
    "head0": (),
    "head1": ((2, "e1"),),
    "head2": ((0, "e3"), (1, "a2"),),
    "head3": ((0, "z0"), (2, "c2"), (2, "a2"),),
    "head4": ((0, "z1"), (2, "e2"), (1, "c2"),),
    "head5": (),
    "qkv": ((3, "start"), (1, "e2"),),
    "input0": ((2, "e3"), (0, "z2"), (3, "e1"), (2, "z0"), (0, "e4"), (3, "c2"), (1, "z0"),),
    "input1": ((3, "e2"), (3, "a2"),),
    "sum0": ((1, "z1"), (2, "e4"), (1, "e3"), (4, "v0"), (1, "z2"),),
    "sum1": ((2, "z1"), (0, "z3"),),
    "sum2": ((5, "f0"), (3, "z0"), (3, "e3"), (3, "z1"), (1, "e4"), (2, "z2"),),
    "end0": ((4, "v1"), (5, "g0"), (3, "z2"),),
    "end1": ((3, "e4"), (2, "z3"), (5, "f2"), (1, "z3"),),
    "end2": ((5, "f1"), (4, "v2"), (3, "z3"), (5, "f3"), (5, "g2"), (5, "g1"), (4, "v3"), (5, "g3"),),
}


def regrouped(
    block_input, lengths, pass_ids, pass_embed, ln1_gain, ln1_bias, w_qkv, w_out,
    ln2_gain, ln2_bias, w_up, b_up, w_down, b_down, cotangent, batch_n
):
    width = block_input.shape[2]
    total = 4 * block_input.shape[1]
    inner = w_up.shape[1]
    own_in, half, lanes = inner // 2, width // 2, width // 2
    band = inner // batch_n // 2
    z_n = batch_n // 2
    blocks_n = total // block
    kept_rows = (blocks_n // 2) ** 2 * block + block
    chunks, a0, c0, e0, r0 = [], 0, 0, 0, 0
    for ne, nc, na in shares:
        chunks.append((r0, r0 + ne, r0 + ne + nc, r0 + ne + nc + na, a0, c0, e0))
        r0, a0, c0, e0 = r0 + ne + nc + na, a0 + na, c0 + nc, e0 + ne
    down_n = 2 * width // batch_n
    anywhere = pl.BlockSpec(memory_space=pl.ANY)
    whole = pl.BlockSpec(memory_space=pltpu.VMEM)
    low, full = jnp.bfloat16, jnp.float32
    copies_n = 22 * len(chunks) + 9 + half // 64 + 32
    output, grad_input, vector, grad_qkv, grad_out, grad_up, grad_down, _, _ = pl.pallas_call(
        functools.partial(block_kernel, chunks=tuple(chunks), plan=plan),
        out_shape=[
            shaped(2, block, width),
            shaped(2, block, width),
            shaped(16, width, kind=full),
            shaped(width // 4, 3 * width // batch_n, kind=full),
            shaped(width // 4, width // batch_n, kind=full),
            shaped(width // 4, inner // batch_n, kind=full),
            shaped(width // batch_n, inner // 4, kind=full),
            shaped(half // 64, kept_rows, 2 * block),
            shaped(2, width, block, kind=full),
        ],
        in_specs=[pl.BlockSpec(memory_space=pltpu.SMEM)] + [anywhere] * 6 + [whole] * 8,
        out_specs=[whole] * 7 + [anywhere] * 2,
        scratch_shapes=[
            pltpu.VMEM((width, total), full),
            pltpu.VMEM((width, 2 * block), full),
            pltpu.VMEM((width, total), low),
            pltpu.VMEM((3 * half, total), low),
            pltpu.VMEM((width, total), low),
            pltpu.VMEM((width, total), low),
            pltpu.VMEM((width, total), low),
            pltpu.VMEM((2 * own_in, total), low),
            pltpu.VMEM((3 * half, total), low),
            pltpu.VMEM((2 * width, total), low),
            pltpu.VMEM((2, kept_rows, 2 * block), low),
            pltpu.VMEM((width, width), low),
            pltpu.VMEM((own_in, width), low),
            pltpu.VMEM((own_in, width), low),
            pltpu.VMEM((2, z_n, 2, r0, lanes), low),
            pltpu.VMEM((z_n, 2, a0, lanes), low),
            pltpu.VMEM((z_n, a0, lanes), low),
            pltpu.VMEM((2, z_n, c0, lanes), low),
            pltpu.VMEM((z_n, c0, lanes), low),
            pltpu.VMEM((2, e0, lanes), low),
            pltpu.VMEM((e0, lanes), low),
            pltpu.VMEM((z_n + 1, a0 + c0, lanes), low),
            pltpu.VMEM((z_n + 1, 2, 2, e0, lanes), low),
            pltpu.VMEM((width, 2 * block), low),
            pltpu.VMEM((width, 2 * block), low),
            pltpu.VMEM((2, block, width), low),
            pltpu.VMEM((width, 128), full),
            pltpu.VMEM((16, width), full),
            pltpu.VMEM((7, 16, width), full),
            pltpu.VMEM((2, 64, total), full),
            pltpu.VMEM((2, 64, total), full),
            pltpu.VMEM((r0 - down_n, 256), low),
            pltpu.VMEM((r0 - down_n, 256), low),
            pltpu.VMEM((down_n // 2, lanes), low),
            pltpu.VMEM((16, width), full),
            pltpu.VMEM((width, 16), full),
            pltpu.VMEM((own_in, 8), full),
            pltpu.VMEM((half // 64, 8, total), full),
            pltpu.VMEM((8, total), full),
            pltpu.VMEM((total, 16), low),
            pltpu.VMEM((16, total), low),
            pltpu.VMEM((4, 2, block), jnp.int32),
            pltpu.SemaphoreType.DMA((27,)),
            pltpu.SemaphoreType.DMA((copies_n,)),
            pltpu.SemaphoreType.DMA((copies_n,)),
        ],
        compiler_params=pltpu.CompilerParams(
            vmem_limit_bytes=63 << 20, collective_id=0, has_side_effects=True
        ),
        cost_estimate=pl.CostEstimate(flops=int(60e9), bytes_accessed=0, transcendentals=0),
        name="block",
    )(
        lengths, block_input, cotangent, w_up, w_qkv, w_out,
        w_down.reshape(batch_n, 2, band, width), pass_ids, pass_embed,
        ln1_gain, ln1_bias, ln2_gain, ln2_bias, b_up, b_down,
    )
    results = [output, grad_input, vector, grad_qkv, grad_out, grad_up, grad_down]
    line = jax.ShapeDtypeStruct((width,), full)
    done = pl.pallas_call(
        finish_kernel,
        out_shape=[
            shaped(2, block, width),
            shaped(2, block, width),
            shaped(5, width, kind=full),
            line,
            line,
            jax.ShapeDtypeStruct(grad_qkv.shape, full),
            jax.ShapeDtypeStruct(grad_out.shape, full),
            line,
            line,
            jax.ShapeDtypeStruct(grad_up.shape, full),
            jax.ShapeDtypeStruct((inner,), full),
            jax.ShapeDtypeStruct(grad_down.shape, full),
            line,
        ],
        in_specs=[anywhere] * 7,
        out_specs=[whole] * 13,
        scratch_shapes=[pltpu.VMEM((16, width), full), pltpu.SemaphoreType.DMA((7,))],
        compiler_params=pltpu.CompilerParams(vmem_limit_bytes=62 << 20),
        name="finish",
    )(*results)
    done = list(done)
    done[11] = jnp.transpose(done[11])
    return tuple(done)


def solution(mesh):
    batch_n = mesh.shape["batch"]
    few = mesh.shape["seq"] == 4 and batch_n == 8
    body = functools.partial(regrouped, batch_n=batch_n) if few else local
    return jax.shard_map(
        body,
        mesh=mesh,
        in_specs=(
            P("batch", "seq", None),
            P("batch"),
            P("batch", "seq"),
            P(),
            P(),
            P(),
            P(),
            P(),
            P(),
            P(),
            P(),
            P(),
            P(),
            P(),
            P("batch", "seq", None),
        ),
        out_specs=(
            P("batch", "seq", None),
            P("batch", "seq", None),
            P(),
            P(),
            P(),
            P("seq", "batch"),
            P("seq", "batch"),
            P(),
            P(),
            P("seq", "batch"),
            P(),
            P("seq", "batch"),
            P(),
        ),
        check_vma=False,
    )
```
